512 devices in a mesh: seq: 32 (over z, core), expert: 8 (over y, x_hi), tensor: 2 (over x_lo).
Axes of the slice: x: 4 (x_hi: 2, x_lo: 2; x = x_hi * 2 + x_lo), y: 4, z: 16, core: 2. Of those that a mesh axis runs over, the one named last changes fastest.
Arguments:
- tokens: bfloat16 [2048, 4096], P('seq', 'expert'), may hold values from -60 to 60
- routes: int32 [2048, 2], P('seq'), may hold values from 0 to 7, as said below
- chosen_expert_weight: float32 [2048, 2], P('seq'), may hold values from 0.1 to 1
- expert_gate_weight: bfloat16 [8, 4096, 8192], P('expert', None, ('seq', 'tensor')), may hold values from -0.09375 to 0.09375
- expert_up_weight: bfloat16 [8, 4096, 8192], P('expert', None, ('seq', 'tensor')), may hold values from -0.09375 to 0.09375
- expert_down_weight: bfloat16 [8, 8192, 4096], P('expert', None, 'seq'), may hold values from -0.0625 to 0.0625
- adapter_down_weight: bfloat16 [32, 4096], P(None, 'expert'), may hold values from -0.09375 to 0.09375
- adapter_up_weight: bfloat16 [32, 4096], P(None, 'expert'), may hold values from -1.5 to 1.5
- document_task_index: int32 [1], replicated, may hold values from 0 to 1
- counts: int32 [1], replicated, may hold values from 1024 to 2048
- final_norm_scale: float32 [4096], P('expert'), may hold values from 0.25 to 1.75
Outputs:
- embedding: float32 [1, 4096], replicated
The draws below stay inside these ranges and needn't reach their ends.
Inputs may be any that keep to these rules, and one draw needn't show every extreme that they name: `routes`: within each aligned block of 64 rows the two ids of a token differ and no id is named more than 20 times; one id, the same in every block, is named exactly 20 times in every block.
All inputs are finite; a program needn't handle non-finite values.
Results may differ from the reference program's by a relative error of at most 0.0025.
Values may be sent and summed in bfloat16 or wider, within the bound.
No kernel may reach another device: no remote copies, remote signals or barrier semaphores. Data moves between devices by JAX's collectives and lax.ppermute only.
A program may use at most 64 MiB of HBM per device.

```python
import jax
import jax.numpy as jnp
from jax import lax

MODEL_WIDTH = 4096
FF = 8192
EXPERTS = 8
TOPK = 2
ADAPTER_DEPTH = 16
TASK_COUNT = 2
DOCS = 1
TOK_DEV = 64
CAP = 20
BLOCKS = 32
TOKENS = 2048
DOC_LEN = 2048
SLOTS = 640


def draw_tokens(key, part):
    key = jax.random.fold_in(key, 7)
    keys = jax.random.split(key, 3)
    row_scale = jnp.exp(jax.random.uniform(keys[0], (TOKENS, 1), jnp.float32, -1.15, 1.15))
    col_scale = jnp.exp(jax.random.uniform(keys[1], (1, MODEL_WIDTH), jnp.float32, -1.15, 1.15))
    values = jnp.clip(jax.random.normal(keys[2], (TOKENS, MODEL_WIDTH), jnp.float32), -6.0, 6.0)
    return (values * row_scale * col_scale).astype(jnp.bfloat16)


def draw_routes(key, part):
    key = jax.random.fold_in(key, 11)
    keys = jax.random.split(key, 4)
    block_count = TOKENS // TOK_DEV
    hot = jax.random.randint(keys[0], (), 0, EXPERTS)
    rotate = jax.random.randint(keys[1], (block_count, 1), 0, EXPERTS - 1)
    token = jnp.arange(TOK_DEV, dtype=jnp.int32)[None, :]
    first_index = jnp.where(token < CAP, token, CAP + 2 * (token - CAP))
    second_index = jnp.where(token < CAP, token, first_index + 1)
    first_other = (hot + 1 + (rotate + first_index) % (EXPERTS - 1)) % EXPERTS
    second = (hot + 1 + (rotate + second_index) % (EXPERTS - 1)) % EXPERTS
    first = jnp.where(token < CAP, hot, first_other)
    first = jnp.broadcast_to(first, (block_count, TOK_DEV))
    second = jnp.broadcast_to(second, (block_count, TOK_DEV))
    order = jax.vmap(lambda k: jax.random.permutation(k, TOK_DEV))(jax.random.split(keys[2], block_count))
    first = jnp.take_along_axis(first, order, axis=1)
    second = jnp.take_along_axis(second, order, axis=1)
    swapped = jax.random.randint(keys[3], (block_count, TOK_DEV), 0, 2)
    left = jnp.where(swapped == 1, second, first)
    right = jnp.where(swapped == 1, first, second)
    return jnp.stack([left, right], axis=-1).reshape(TOKENS, 2).astype(jnp.int32)


def levels(stream_key, dims, pieces, least, top_value):
    def one(position, shards_of):
        draws = jax.random.uniform(jax.random.fold_in(jax.random.fold_in(stream_key, 6), position), (shards_of,), jnp.float32, least / len(pieces), top_value / len(pieces))
        return jnp.repeat(jnp.exp(draws), dims[position] // shards_of).reshape((-1,) + (1,) * (len(dims) - position - 1))

    gain = one(*pieces[0])
    for cut in pieces[1:]:
        gain = gain * one(*cut)
    return gain


def bell_draw(rng, shape, scale, reach, shards=(), held_as=jnp.bfloat16):
    values = jax.random.normal(rng, shape, jnp.float32) * scale
    if len(shards) > 0:
        values = levels(rng, shape, shards, -0.22, 0.18) * values
    return jnp.clip(values, min=-reach, max=reach).astype(held_as)


def setup_inputs(seed: int = 0) -> dict:
    key_of = jax.random.split(jax.random.key(seed), 12)
    tokens = draw_tokens(jax.random.fold_in(key_of[11], 71), 0)
    routes = draw_routes(jax.random.fold_in(key_of[11], 71), 0)
    chosen_expert_weight = jnp.clip(0.1 + 0.9 * jax.random.uniform(key_of[2], (TOKENS, TOPK), jnp.float32) ** levels(key_of[2], (TOKENS, TOPK), ((0, 32),), -0.2, 0.2), 0.1, 1.0)
    expert_gate_weight = bell_draw(key_of[3], (EXPERTS, MODEL_WIDTH, FF), MODEL_WIDTH ** -0.5, 0.09375, ((0, 8), (2, 64)))
    expert_up_weight = bell_draw(key_of[4], (EXPERTS, MODEL_WIDTH, FF), MODEL_WIDTH ** -0.5, 0.09375, ((0, 8), (2, 64)))
    expert_down_weight = bell_draw(key_of[5], (EXPERTS, FF, MODEL_WIDTH), FF ** -0.5, 0.0625, ((0, 8), (2, 32)))
    adapter_down_weight = bell_draw(key_of[6], (TASK_COUNT * ADAPTER_DEPTH, MODEL_WIDTH), MODEL_WIDTH ** -0.5, 0.09375, ((1, 8),))
    adapter_up_weight = bell_draw(key_of[7], (TASK_COUNT * ADAPTER_DEPTH, MODEL_WIDTH), ADAPTER_DEPTH ** -0.5, 1.5, ((1, 8),))
    document_task_index = jax.random.randint(key_of[8], (DOCS,), 0, TASK_COUNT).astype(jnp.int32)
    counts = jax.random.randint(key_of[9], (DOCS,), DOC_LEN // 2, DOC_LEN + 1).astype(jnp.int32)
    final_norm_scale = jnp.clip(1.0 + 0.15 * jax.random.normal(key_of[10], (MODEL_WIDTH,), jnp.float32), 0.25, 1.75)
    return {"tokens": tokens, "routes": routes, "chosen_expert_weight": chosen_expert_weight, "expert_gate_weight": expert_gate_weight, "expert_up_weight": expert_up_weight, "expert_down_weight": expert_down_weight, "adapter_down_weight": adapter_down_weight, "adapter_up_weight": adapter_up_weight, "document_task_index": document_task_index, "counts": counts, "final_norm_scale": final_norm_scale}


adapter_scale = 0.5

def expert_block(operands):
    slots_in, gate_w, up_w, down_w = operands
    gate_act = jnp.dot(slots_in, gate_w, preferred_element_type=jnp.float32)
    up_act = jnp.dot(slots_in, up_w, preferred_element_type=jnp.float32)
    hidden = (jax.nn.silu(gate_act) * up_act).astype(jnp.bfloat16)
    return jnp.dot(hidden, down_w, preferred_element_type=jnp.float32).astype(jnp.bfloat16)

def reference(tokens, routes, chosen_expert_weight, expert_gate_weight, expert_up_weight, expert_down_weight, adapter_down_weight, adapter_up_weight, document_task_index, counts, final_norm_scale):
    pair_ids = routes.reshape(BLOCKS, TOK_DEV * TOPK)
    expert_iota = jnp.arange(EXPERTS, dtype=jnp.int32)
    one_hot = (pair_ids[:, :, None] == expert_iota[None, None, :]).astype(jnp.int32)
    slot_index = lax.optimization_barrier(jnp.sum(jnp.cumsum(one_hot, axis=1) * one_hot, axis=2)) - 1
    row_of = (jnp.arange(BLOCKS, dtype=jnp.int32)[:, None] * CAP + slot_index).reshape(-1).astype(jnp.int32)
    expert_of = pair_ids.reshape(-1).astype(jnp.int32)
    token_of = jnp.arange(TOKENS * TOPK, dtype=jnp.int32) // TOPK
    dispatched = jnp.zeros((EXPERTS, SLOTS, MODEL_WIDTH), tokens.dtype).at[expert_of, row_of].set(tokens[token_of])
    expert_out = lax.map(expert_block, (dispatched, expert_gate_weight, expert_up_weight, expert_down_weight))
    picked = expert_out[expert_of, row_of].astype(jnp.float32).reshape(TOKENS, TOPK, MODEL_WIDTH)
    expert_mixture_layer = lax.optimization_barrier(jnp.sum(picked * chosen_expert_weight[:, :, None], axis=1))
    doc_of = jnp.arange(TOKENS, dtype=jnp.int32) // DOC_LEN
    token_task_index = document_task_index[doc_of]
    narrow_all_tasks = jnp.dot(tokens, adapter_down_weight.T, preferred_element_type=jnp.float32)
    task_mask = jnp.arange(TASK_COUNT * ADAPTER_DEPTH, dtype=jnp.int32)[None, :] // ADAPTER_DEPTH == token_task_index[:, None]
    narrow_projection = jnp.where(task_mask, narrow_all_tasks, 0.0).astype(jnp.bfloat16)
    adapted_rows = jnp.dot(narrow_projection, adapter_up_weight, preferred_element_type=jnp.float32)
    expert_mixture = tokens.astype(jnp.float32) + expert_mixture_layer + adapter_scale * adapted_rows
    normed = expert_mixture * lax.rsqrt(lax.optimization_barrier(jnp.mean(expert_mixture * expert_mixture, axis=1, keepdims=True)) + 1e-05) * final_norm_scale
    within = jnp.arange(TOKENS, dtype=jnp.int32) - doc_of * DOC_LEN
    in_count = within < counts[doc_of]
    pooled = lax.optimization_barrier(jnp.sum(jnp.where(in_count[:, None], normed, 0.0).reshape(DOCS, DOC_LEN, MODEL_WIDTH), axis=1))
    return pooled * lax.rsqrt(lax.optimization_barrier(jnp.mean(pooled * pooled, axis=1, keepdims=True)) + 1e-06)
```

```python
import jax
import jax.numpy as jnp
from jax import lax
from jax.sharding import Mesh
from jax.sharding import PartitionSpec as P

TASK_COUNT = 2
ADAPTER_SCALE = 0.5

SEQ = ("z", "c")
EXPERT = ("y", "h")
GROUP = ("y", "h", "t")

BF16 = jnp.bfloat16
F16 = jnp.float16
F32 = jnp.float32
HIGH = lax.Precision.HIGHEST
LANES = 128
LEAST_EXPONENT = -40.0


def swap(x, axes):
    return lax.all_to_all(x, axes, split_axis=0, concat_axis=0, tiled=True)


def spread(x, axes):
    return swap(jnp.broadcast_to(x[None], (lax.axis_size(axes),) + x.shape), axes)


def three_parts(x):
    first = x.astype(BF16)
    rest = x - first.astype(F32)
    second = rest.astype(BF16)
    third = (rest - second.astype(F32)).astype(BF16)
    return first, second, third


def slots_of(ids, experts):
    pairs = ids.shape[1]
    one_hot = (ids[:, None, :] == jnp.arange(experts, dtype=jnp.int32)[None, :, None]).astype(BF16)
    before = (
        jnp.arange(pairs, dtype=jnp.int32)[:, None] < jnp.arange(pairs, dtype=jnp.int32)[None, :]
    ).astype(BF16)
    earlier = lax.dot_general(
        one_hot, before, (((2,), (0,)), ((), ())), preferred_element_type=F32
    )
    return jnp.sum(earlier * one_hot.astype(F32), axis=1).astype(jnp.int32)


def local(
    tokens,
    routes,
    chosen_expert_weight,
    expert_gate_weight,
    expert_up_weight,
    expert_down_weight,
    adapter_down_weight,
    adapter_up_weight,
    document_task_index,
    counts,
    final_norm_scale,
):
    rows, feats = tokens.shape
    seq = lax.axis_size(SEQ)
    experts = lax.axis_size(EXPERT)
    cores = lax.axis_size("c")
    groups = lax.axis_size(GROUP)
    tensors = lax.axis_size("t")
    chips = seq // cores
    capacity = rows * 5 // 16
    width = feats * experts
    half = feats // cores
    slice_width = width // seq
    slots = seq * capacity
    pairs = 2 * rows
    s = lax.axis_index(SEQ)
    e = lax.axis_index(EXPERT)
    t = lax.axis_index("t")
    g = lax.axis_index(GROUP)

    pair_ids = routes.reshape(1, pairs)
    target = pair_ids[0] * capacity + slots_of(pair_ids, experts)[0]
    chooser = jnp.any(
        (target[:, None] == jnp.arange(experts * capacity, dtype=jnp.int32)[None, :]).reshape(
            rows, 2, experts * capacity
        ),
        axis=1,
    ).astype(BF16)
    outgoing = lax.dot_general(
        chooser, tokens, (((0,), (0,)), ((), ())), preferred_element_type=F32
    ).astype(BF16)
    outgoing = outgoing.reshape(experts, capacity, cores, half).transpose(0, 2, 1, 3)
    received = swap(outgoing.reshape(experts * cores, capacity, half), EXPERT + ("c",))
    shard = received.reshape(experts, cores, capacity, half).transpose(1, 2, 0, 3)
    shard = shard.reshape(cores * capacity, experts * half).astype(F32)

    table = jnp.stack(
        [routes.reshape(pairs).astype(F32), chosen_expert_weight.reshape(pairs)]
    )
    tables = spread(table, SEQ)
    task_rows = adapter_down_weight.shape[0]
    params = spread(
        jnp.concatenate(
            [adapter_down_weight, adapter_up_weight]
            + [part[None] for part in three_parts(final_norm_scale)]
        ),
        EXPERT,
    )

    largest = jnp.max(jnp.abs(shard), axis=1, keepdims=True)
    exponent = jnp.maximum(
        jnp.floor(jnp.log2(jnp.maximum(largest, 1e-30)) + 1.01), LEAST_EXPONENT
    )
    scaled = (shard * jnp.exp2(15.0 - exponent)).astype(F16)
    sent = jnp.concatenate(
        [scaled, jnp.broadcast_to(exponent, (cores * capacity, LANES)).astype(F16)], axis=1
    )
    gathered = lax.all_gather(sent, SEQ, axis=0, tiled=False)
    gathered = gathered.reshape(chips, cores, cores * capacity, -1).transpose(1, 0, 2, 3)
    exponents = gathered[..., experts * half : experts * half + 1].astype(F32)
    dispatched = (
        gathered[..., : experts * half].astype(F32) * jnp.exp2(exponents - 15.0)
    ).astype(BF16)
    dispatched = dispatched.reshape(cores, slots, experts * half)
    row_exponent = jnp.max(exponents, axis=0).reshape(slots, 1)

    def reorder(weight):
        columns = weight.shape[-1]
        return (
            weight.reshape(experts, cores, half, columns)
            .transpose(1, 0, 2, 3)
            .reshape(cores, experts * half, columns)
        )

    both = ((0, 2), (0, 1)), ((), ())
    gate_act = lax.dot_general(
        dispatched, reorder(expert_gate_weight[0]), both, preferred_element_type=F32
    )
    up_act = lax.dot_general(
        dispatched, reorder(expert_up_weight[0]), both, preferred_element_type=F32
    )
    hidden = (jax.nn.silu(gate_act) * up_act).astype(BF16).astype(F32)
    hidden = (hidden * jnp.exp2(-2.0 * row_exponent - 2.0)).astype(F16)
    hidden = lax.all_gather(hidden, SEQ, axis=0, tiled=False)
    hidden_units = hidden.shape[-1]
    down = lax.dynamic_index_in_dim(
        expert_down_weight[0].reshape(seq, tensors, hidden_units, slice_width),
        t,
        axis=1,
        keepdims=False,
    )
    part = lax.dot_general(hidden.astype(BF16), down, both, preferred_element_type=F32)

    adapter_down = (
        params[:, :task_rows]
        .reshape(experts, task_rows, cores, half)
        .transpose(2, 1, 0, 3)
        .reshape(cores, task_rows, experts * half)
    )
    low_rank = lax.dot_general(
        dispatched, adapter_down, (((0, 2), (0, 2)), ((), ())), preferred_element_type=F32
    )
    task_of_row = jnp.arange(task_rows, dtype=jnp.int32) // (task_rows // TASK_COUNT)
    low_rank = jnp.where(
        task_of_row[None, :] == document_task_index[0], low_rank, 0.0
    ).astype(BF16)
    per_feature_group = feats // slice_width
    per_half = half // slice_width
    adapter_up = lax.dynamic_slice(
        params,
        (s // per_feature_group, task_rows, (s % per_feature_group) * slice_width),
        (1, task_rows, slice_width),
    )[0]
    adapted = jnp.dot(low_rank, adapter_up, preferred_element_type=F32)
    own = lax.dynamic_slice(
        dispatched,
        (
            (s // per_half) % cores,
            0,
            (s // per_feature_group) * half + (s % per_half) * slice_width,
        ),
        (1, slots, slice_width),
    )[0]
    base = own.astype(F32) + ADAPTER_SCALE * adapted

    ids = tables[:, 0].astype(jnp.int32)
    weights = tables[:, 1]
    slot_of = slots_of(ids, experts)
    is_mine = jnp.where(ids == e, slot_of, -1)
    slot_weight = jnp.sum(
        jnp.where(
            is_mine[:, None, :] == jnp.arange(capacity, dtype=jnp.int32)[None, :, None],
            weights[:, None, :],
            0.0,
        ),
        axis=2,
    ).reshape(slots, 1)
    payload = slot_weight * jnp.exp2(2.0 * row_exponent + 2.0) * part + base / (2 * tensors)
    blocks = seq // groups
    returned = swap(payload.reshape(groups, blocks * capacity, slice_width), GROUP)
    returned = jnp.sum(
        returned.reshape(experts, tensors, blocks * capacity, slice_width), axis=1
    ).reshape(experts * blocks * capacity, slice_width)

    group_ids = lax.dynamic_slice_in_dim(ids, g * blocks, blocks, axis=0)
    group_slots = lax.dynamic_slice_in_dim(slot_of, g * blocks, blocks, axis=0)
    place = (
        group_ids * (blocks * capacity)
        + jnp.arange(blocks, dtype=jnp.int32)[:, None] * capacity
        + group_slots
    )
    group_rows = blocks * rows
    combiner = jnp.any(
        place.reshape(group_rows, 2)[:, :, None]
        == jnp.arange(experts * blocks * capacity, dtype=jnp.int32)[None, None, :],
        axis=1,
    ).astype(F32)
    mixed = jnp.dot(combiner, returned, precision=HIGH)
    squares = jnp.sum(spread(jnp.sum(mixed * mixed, axis=1)[None], SEQ), axis=0)
    position = g * group_rows + jnp.arange(group_rows, dtype=jnp.int32)[None, :]
    factor = jnp.where(position < counts[0], lax.rsqrt(squares / width + 1e-05), 0.0)
    pooled = jnp.dot(factor, mixed, precision=HIGH)
    pooled = jnp.sum(spread(pooled, GROUP), axis=0)
    pooled = spread(pooled, SEQ).reshape(1, width)
    scale = jnp.sum(params[:, 2 * task_rows :].astype(F32), axis=1).reshape(1, width)
    pooled = pooled * scale
    return pooled * lax.rsqrt(jnp.mean(pooled * pooled, axis=1, keepdims=True) + 1e-06)


def solution(mesh):
    seq, experts, tensors = mesh.devices.shape
    parts = Mesh(
        mesh.devices.reshape(seq // 2, 2, experts // 2, 2, tensors), ("z", "c", "y", "h", "t")
    )
    return jax.shard_map(
        local,
        mesh=parts,
        in_specs=(
            P(SEQ, EXPERT),
            P(SEQ, None),
            P(SEQ, None),
            P(EXPERT, None, SEQ + ("t",)),
            P(EXPERT, None, SEQ + ("t",)),
            P(EXPERT, None, SEQ),
            P(None, EXPERT),
            P(None, EXPERT),
            P(),
            P(),
            P(EXPERT),
        ),
        out_specs=P(),
        check_vma=False,
    )
```

```python
import jax
import jax.numpy as jnp
from jax import lax
from jax.sharding import Mesh
from jax.sharding import PartitionSpec as P

TASK_COUNT = 2
ADAPTER_SCALE = 0.5

SEQ = ("z", "c")
EXPERT = ("y", "h")
GROUP = ("y", "h", "t")

BF16 = jnp.bfloat16
F16 = jnp.float16
F32 = jnp.float32
HIGH = lax.Precision.HIGHEST
LANES = 128
LEAST_EXPONENT = -40.0


def swap(x, axes):
    return lax.all_to_all(x, axes, split_axis=0, concat_axis=0, tiled=True)


def spread(x, axes):
    return swap(jnp.broadcast_to(x[None], (lax.axis_size(axes),) + x.shape), axes)


def rounded(x):
    return lax.reduce_precision(x, 8, 7)


def three_parts(x, step):
    first = rounded(x)
    rest = (x - first) * step
    second = rounded(rest)
    return first, second, (rest - second) * step


def slots_of(ids, experts):
    pairs = ids.shape[1]
    one_hot = (ids[:, None, :] == jnp.arange(experts, dtype=jnp.int32)[None, :, None]).astype(BF16)
    before = (
        jnp.arange(pairs, dtype=jnp.int32)[:, None] < jnp.arange(pairs, dtype=jnp.int32)[None, :]
    ).astype(BF16)
    earlier = lax.dot_general(
        one_hot, before, (((2,), (0,)), ((), ())), preferred_element_type=F32
    )
    return jnp.sum(earlier * one_hot.astype(F32), axis=1).astype(jnp.int32)


def local(
    tokens,
    routes,
    chosen_expert_weight,
    expert_gate_weight,
    expert_up_weight,
    expert_down_weight,
    adapter_down_weight,
    adapter_up_weight,
    document_task_index,
    counts,
    final_norm_scale,
):
    rows, feats = tokens.shape
    seq = lax.axis_size(SEQ)
    experts = lax.axis_size(EXPERT)
    cores = lax.axis_size("c")
    groups = lax.axis_size(GROUP)
    tensors = lax.axis_size("t")
    chips = seq // cores
    capacity = rows * 5 // 16
    width = feats * experts
    half = feats // cores
    slice_width = width // seq
    slots = seq * capacity
    pairs = 2 * rows
    s = lax.axis_index(SEQ)
    e = lax.axis_index(EXPERT)
    t = lax.axis_index("t")
    g = lax.axis_index(GROUP)

    pair_ids = routes.reshape(1, pairs)
    target = pair_ids[0] * capacity + slots_of(pair_ids, experts)[0]
    chooser = jnp.any(
        (target[:, None] == jnp.arange(experts * capacity, dtype=jnp.int32)[None, :]).reshape(
            rows, 2, experts * capacity
        ),
        axis=1,
    ).astype(BF16)
    outgoing = lax.dot_general(
        chooser, tokens, (((0,), (0,)), ((), ())), preferred_element_type=F32
    ).astype(BF16)
    outgoing = outgoing.reshape(experts, capacity, cores, half).transpose(0, 2, 1, 3)
    outgoing = outgoing.reshape(experts * cores, capacity, half)

    task_rows = adapter_down_weight.shape[0]
    own_params = jnp.concatenate(
        [adapter_down_weight, adapter_up_weight]
        + [part[None].astype(BF16) for part in three_parts(final_norm_scale, 1.0)]
    )
    outgoing, own_params = lax.optimization_barrier((outgoing, own_params))
    received = swap(outgoing, EXPERT + ("c",))
    params = spread(own_params, EXPERT)
    shard_rows = cores * capacity
    shard = received.reshape(experts, cores, capacity, half).transpose(1, 2, 0, 3)
    shard = shard.reshape(shard_rows, experts * half).astype(F32)

    largest = jnp.max(jnp.abs(shard), axis=1, keepdims=True)
    exponent = jnp.maximum(
        jnp.floor(jnp.log2(jnp.maximum(largest, 1e-30)) + 1.01), LEAST_EXPONENT
    )
    scaled = (shard * jnp.exp2(15.0 - exponent)).astype(F16)
    table = jnp.stack(
        [routes.reshape(pairs).astype(F32)]
        + list(three_parts(chosen_expert_weight.reshape(pairs), 256.0))
    ).astype(F16)
    sent = jnp.concatenate(
        [
            scaled,
            jnp.broadcast_to(exponent, (shard_rows, LANES)).astype(F16),
            jnp.pad(table, ((0, shard_rows - table.shape[0]), (0, 0))),
        ],
        axis=1,
    )
    gathered = lax.all_gather(sent, SEQ, axis=0, tiled=False)
    gathered = lax.optimization_barrier(gathered.astype(BF16))
    columns = experts * half
    tables = gathered[:, :4, columns + LANES :].astype(F32)
    gathered = gathered.reshape(chips, cores, shard_rows, -1).transpose(1, 0, 2, 3)
    dispatched = gathered[..., :columns].reshape(cores, slots, columns)
    exponents = gathered[..., columns : columns + LANES].reshape(cores, slots, LANES).astype(F32)
    row_scale = jnp.exp2(exponents - 15.0)
    row_exponent = jnp.max(exponents, axis=0)

    weights_in = jnp.concatenate([expert_gate_weight[0], expert_up_weight[0]], axis=1)
    hidden_units = expert_gate_weight.shape[2]
    weights_in = (
        weights_in.reshape(experts, cores, half, 2 * hidden_units)
        .transpose(1, 0, 2, 3)
        .reshape(cores, columns, 2 * hidden_units)
    )
    acts = lax.dot_general(
        dispatched, weights_in, (((2,), (1,)), ((0,), (0,))), preferred_element_type=F32
    )
    gate_act = jnp.sum(acts[..., :hidden_units] * row_scale, axis=0)
    up_act = jnp.sum(acts[..., hidden_units:] * row_scale, axis=0)
    hidden = rounded(jax.nn.silu(gate_act) * up_act)
    hidden = (hidden * jnp.exp2(-2.0 * row_exponent - 2.0)).astype(F16)
    hidden = lax.all_gather(hidden, SEQ, axis=0, tiled=False)
    down = lax.dynamic_index_in_dim(
        expert_down_weight[0].reshape(seq, tensors, hidden_units, slice_width),
        t,
        axis=1,
        keepdims=False,
    )
    part = lax.dot_general(
        hidden.astype(BF16), down, (((0, 2), (0, 1)), ((), ())), preferred_element_type=F32
    )

    adapter_down = (
        params[:, :task_rows]
        .reshape(experts, task_rows, cores, half)
        .transpose(2, 1, 0, 3)
        .reshape(cores, task_rows, columns)
    )
    low_rank = lax.dot_general(
        dispatched, adapter_down, (((2,), (2,)), ((0,), (0,))), preferred_element_type=F32
    )
    low_rank = jnp.sum(low_rank * row_scale[..., :task_rows], axis=0)
    task_of_row = jnp.arange(task_rows, dtype=jnp.int32) // (task_rows // TASK_COUNT)
    low_rank = jnp.where(
        task_of_row[None, :] == document_task_index[0], low_rank, 0.0
    ).astype(BF16)
    per_feature_group = feats // slice_width
    per_half = half // slice_width
    adapter_up = lax.dynamic_slice(
        params,
        (s // per_feature_group, task_rows, (s % per_feature_group) * slice_width),
        (1, task_rows, slice_width),
    )[0]
    adapted = jnp.dot(low_rank, adapter_up, preferred_element_type=F32)
    own_half = (s // per_half) % cores
    own = lax.dynamic_slice(
        dispatched,
        (own_half, 0, (s // per_feature_group) * half + (s % per_half) * slice_width),
        (1, slots, slice_width),
    )[0]
    own_scale = lax.dynamic_index_in_dim(row_scale, own_half, axis=0, keepdims=False)
    base = own.astype(F32) * own_scale + ADAPTER_SCALE * adapted

    ids = tables[:, 0].astype(jnp.int32)
    weights = tables[:, 1] + (tables[:, 2] + tables[:, 3] / 256.0) / 256.0
    slot_of = slots_of(ids, experts)
    is_mine = jnp.where(ids == e, slot_of, -1)
    slot_weight = jnp.sum(
        jnp.where(
            is_mine[:, None, :] == jnp.arange(capacity, dtype=jnp.int32)[None, :, None],
            weights[:, None, :],
            0.0,
        ),
        axis=2,
    ).reshape(slots, 1)
    payload = slot_weight * jnp.exp2(2.0 * row_exponent + 2.0) * part + base / (2 * tensors)
    blocks = seq // groups
    returned = swap(payload.reshape(groups, blocks * capacity, slice_width), GROUP)
    returned = jnp.sum(
        returned.reshape(experts, tensors, blocks * capacity, slice_width), axis=1
    ).reshape(experts * blocks * capacity, slice_width)

    group_ids = lax.dynamic_slice_in_dim(ids, g * blocks, blocks, axis=0)
    group_slots = lax.dynamic_slice_in_dim(slot_of, g * blocks, blocks, axis=0)
    place = (
        group_ids * (blocks * capacity)
        + jnp.arange(blocks, dtype=jnp.int32)[:, None] * capacity
        + group_slots
    )
    group_rows = blocks * rows
    combiner = jnp.any(
        place.reshape(group_rows, 2)[:, :, None]
        == jnp.arange(experts * blocks * capacity, dtype=jnp.int32)[None, None, :],
        axis=1,
    ).astype(F32)
    mixed = jnp.dot(combiner, returned, precision=HIGH)
    squares = jnp.sum(spread(jnp.sum(mixed * mixed, axis=1)[None], SEQ), axis=0)
    position = g * group_rows + jnp.arange(group_rows, dtype=jnp.int32)[None, :]
    factor = jnp.where(position < counts[0], lax.rsqrt(squares / width + 1e-05), 0.0)
    pooled = jnp.dot(factor, mixed, precision=HIGH)
    pooled = jnp.sum(spread(pooled, GROUP), axis=0)
    pooled = spread(pooled, SEQ).reshape(1, width)
    scale = jnp.sum(params[:, 2 * task_rows :].astype(F32), axis=1).reshape(1, width)
    pooled = pooled * scale
    return pooled * lax.rsqrt(jnp.mean(pooled * pooled, axis=1, keepdims=True) + 1e-06)


def solution(mesh):
    seq, experts, tensors = mesh.devices.shape
    parts = Mesh(
        mesh.devices.reshape(seq // 2, 2, experts // 2, 2, tensors), ("z", "c", "y", "h", "t")
    )
    return jax.shard_map(
        local,
        mesh=parts,
        in_specs=(
            P(SEQ, EXPERT),
            P(SEQ, None),
            P(SEQ, None),
            P(EXPERT, None, SEQ + ("t",)),
            P(EXPERT, None, SEQ + ("t",)),
            P(EXPERT, None, SEQ),
            P(None, EXPERT),
            P(None, EXPERT),
            P(),
            P(),
            P(EXPERT),
        ),
        out_specs=P(),
        check_vma=False,
    )
```

```python
import jax
import jax.numpy as jnp
from jax import lax
from jax.sharding import Mesh
from jax.sharding import PartitionSpec as P

TASK_COUNT = 2
ADAPTER_SCALE = 0.5

SEQ = ("z", "c")
EXPERT = ("y", "h")
GROUP = ("y", "h", "t")

BF16 = jnp.bfloat16
F16 = jnp.float16
F32 = jnp.float32
HIGH = lax.Precision.HIGHEST
LANES = 128
LEAST_EXPONENT = -40.0
LOW_STEP = 2.0**28


def swap(x, axes):
    return lax.all_to_all(x, axes, split_axis=0, concat_axis=0, tiled=True)


def spread(x, axes):
    return swap(jnp.broadcast_to(x[None], (lax.axis_size(axes),) + x.shape), axes)


def rounded(x):
    return lax.reduce_precision(x, 8, 7)


def three_parts(x, step):
    first = rounded(x)
    rest = (x - first) * step
    second = rounded(rest)
    return first, second, (rest - second) * step


def slots_of(ids, experts):
    pairs = ids.shape[1]
    one_hot = (ids[:, None, :] == jnp.arange(experts, dtype=jnp.int32)[None, :, None]).astype(BF16)
    before = (
        jnp.arange(pairs, dtype=jnp.int32)[:, None] < jnp.arange(pairs, dtype=jnp.int32)[None, :]
    ).astype(BF16)
    earlier = lax.dot_general(
        one_hot, before, (((2,), (0,)), ((), ())), preferred_element_type=F32
    )
    return jnp.sum(earlier * one_hot.astype(F32), axis=1).astype(jnp.int32)


def local(
    tokens,
    routes,
    chosen_expert_weight,
    expert_gate_weight,
    expert_up_weight,
    expert_down_weight,
    adapter_down_weight,
    adapter_up_weight,
    document_task_index,
    counts,
    final_norm_scale,
):
    rows, feats = tokens.shape
    seq = lax.axis_size(SEQ)
    experts = lax.axis_size(EXPERT)
    cores = lax.axis_size("c")
    groups = lax.axis_size(GROUP)
    tensors = lax.axis_size("t")
    chips = seq // cores
    capacity = rows * 5 // 16
    width = feats * experts
    half = feats // cores
    slice_width = width // seq
    slots = seq * capacity
    pairs = 2 * rows
    s = lax.axis_index(SEQ)
    e = lax.axis_index(EXPERT)
    t = lax.axis_index("t")
    g = lax.axis_index(GROUP)

    pair_ids = routes.reshape(1, pairs)
    target = pair_ids[0] * capacity + slots_of(pair_ids, experts)[0]
    chooser = jnp.any(
        (target[:, None] == jnp.arange(experts * capacity, dtype=jnp.int32)[None, :]).reshape(
            rows, 2, experts * capacity
        ),
        axis=1,
    ).astype(BF16)
    outgoing = lax.dot_general(
        chooser, tokens, (((0,), (0,)), ((), ())), preferred_element_type=F32
    ).astype(BF16)
    outgoing = outgoing.reshape(experts, capacity, cores, half).transpose(0, 2, 1, 3)
    outgoing = outgoing.reshape(experts * cores, capacity, half)

    task_rows = adapter_down_weight.shape[0]
    column = (s % (feats // slice_width)) * slice_width
    low_part = lax.dot_general(
        tokens, adapter_down_weight, (((1,), (1,)), ((), ())), preferred_element_type=F32
    )
    low_lines = rows * task_rows // LANES
    own_params = jnp.concatenate(
        [
            low_part.reshape(low_lines, LANES),
            lax.dynamic_slice_in_dim(adapter_up_weight, column, slice_width, axis=1).astype(F32),
            lax.dynamic_slice_in_dim(final_norm_scale, column, slice_width)[None],
        ]
    )
    own_params, _ = lax.optimization_barrier((own_params, outgoing))
    received = swap(outgoing, EXPERT + ("c",))
    params = spread(own_params, EXPERT)
    holder = lax.dynamic_index_in_dim(
        params[:, low_lines:], s // (feats // slice_width), axis=0, keepdims=False
    )
    adapter_up = holder[:task_rows].astype(BF16)
    norm_scale = holder[task_rows:]
    task_of_lane = (
        jnp.arange(LANES, dtype=jnp.int32) % task_rows // (task_rows // TASK_COUNT)
    )
    low_rank = rounded(
        jnp.where(
            task_of_lane[None, :] == document_task_index[0],
            jnp.sum(params[:, :low_lines], axis=0),
            0.0,
        )
    )
    low_first = lax.reduce_precision(low_rank, 5, 10)
    low_second = (low_rank - low_first) * LOW_STEP
    shard_rows = cores * capacity
    shard = received.reshape(experts, cores, capacity, half).transpose(1, 2, 0, 3)
    shard = shard.reshape(shard_rows, experts * half).astype(F32)

    largest = jnp.max(jnp.abs(shard), axis=1, keepdims=True)
    exponent = jnp.maximum(
        jnp.floor(jnp.log2(jnp.maximum(largest, 1e-30)) + 1.01), LEAST_EXPONENT
    )
    scaled = (shard * jnp.exp2(15.0 - exponent)).astype(F16)
    table = jnp.stack(
        [routes.reshape(pairs).astype(F32)]
        + list(three_parts(chosen_expert_weight.reshape(pairs), 256.0))
    )
    table = jnp.concatenate([table, low_first, low_second]).astype(F16)
    sent = jnp.concatenate(
        [
            scaled,
            jnp.broadcast_to(exponent, (shard_rows, LANES)).astype(F16),
            jnp.pad(table, ((0, shard_rows - table.shape[0]), (0, 0))),
        ],
        axis=1,
    )
    gathered = lax.all_gather(sent, SEQ, axis=0, tiled=False)
    gathered = lax.optimization_barrier(gathered.astype(BF16))
    columns = experts * half
    tables = gathered[:, : 4 + 2 * low_lines, columns + LANES :].astype(F32)
    gathered = gathered.reshape(chips, cores, shard_rows, -1).transpose(1, 0, 2, 3)
    dispatched = gathered[..., :columns].reshape(cores, slots, columns)
    exponents = gathered[..., columns : columns + LANES].reshape(cores, slots, LANES).astype(F32)
    row_scale = jnp.exp2(exponents - 15.0)
    row_exponent = jnp.max(exponents, axis=0)

    weights_in = jnp.concatenate([expert_gate_weight[0], expert_up_weight[0]], axis=1)
    hidden_units = expert_gate_weight.shape[2]
    weights_in = (
        weights_in.reshape(experts, cores, half, 2 * hidden_units)
        .transpose(1, 0, 2, 3)
        .reshape(cores, columns, 2 * hidden_units)
    )
    acts = lax.dot_general(
        dispatched, weights_in, (((2,), (1,)), ((0,), (0,))), preferred_element_type=F32
    )
    gate_act = jnp.sum(acts[..., :hidden_units] * row_scale, axis=0)
    up_act = jnp.sum(acts[..., hidden_units:] * row_scale, axis=0)
    hidden = rounded(jax.nn.silu(gate_act) * up_act)
    hidden = (hidden * jnp.exp2(-2.0 * row_exponent - 2.0)).astype(F16)
    hidden = lax.all_gather(hidden, SEQ, axis=0, tiled=False)
    down = lax.dynamic_index_in_dim(
        expert_down_weight[0].reshape(seq, tensors, hidden_units, slice_width),
        t,
        axis=1,
        keepdims=False,
    )
    part = lax.dot_general(
        hidden.astype(BF16), down, (((0, 2), (0, 1)), ((), ())), preferred_element_type=F32
    )

    per_half = half // slice_width
    own_half = (s // per_half) % cores
    own = lax.dynamic_slice(
        dispatched,
        (
            own_half,
            0,
            (s // (feats // slice_width)) * half + (s % per_half) * slice_width,
        ),
        (1, slots, slice_width),
    )[0]
    own_scale = lax.dynamic_index_in_dim(row_scale, own_half, axis=0, keepdims=False)
    base = own.astype(F32) * own_scale

    ids = tables[:, 0].astype(jnp.int32)
    weights = tables[:, 1] + (tables[:, 2] + tables[:, 3] / 256.0) / 256.0
    slot_of = slots_of(ids, experts)
    is_mine = jnp.where(ids == e, slot_of, -1)
    slot_weight = jnp.sum(
        jnp.where(
            is_mine[:, None, :] == jnp.arange(capacity, dtype=jnp.int32)[None, :, None],
            weights[:, None, :],
            0.0,
        ),
        axis=2,
    ).reshape(slots, 1)
    payload = slot_weight * jnp.exp2(2.0 * row_exponent + 2.0) * part + base / (2 * tensors)
    blocks = seq // groups
    returned = swap(payload.reshape(groups, blocks * capacity, slice_width), GROUP)
    returned = jnp.sum(
        returned.reshape(experts, tensors, blocks * capacity, slice_width), axis=1
    ).reshape(experts * blocks * capacity, slice_width)

    group_ids = lax.dynamic_slice_in_dim(ids, g * blocks, blocks, axis=0)
    group_slots = lax.dynamic_slice_in_dim(slot_of, g * blocks, blocks, axis=0)
    place = (
        group_ids * (blocks * capacity)
        + jnp.arange(blocks, dtype=jnp.int32)[:, None] * capacity
        + group_slots
    )
    group_rows = blocks * rows
    combiner = jnp.any(
        place.reshape(group_rows, 2)[:, :, None]
        == jnp.arange(experts * blocks * capacity, dtype=jnp.int32)[None, None, :],
        axis=1,
    ).astype(F32)
    group_low = lax.dynamic_slice_in_dim(tables, g * blocks, blocks, axis=0)[:, 4:]
    group_low = group_low[:, :low_lines] + group_low[:, low_lines:] / LOW_STEP
    adapted = jnp.dot(
        group_low.reshape(group_rows, task_rows).astype(BF16),
        adapter_up,
        preferred_element_type=F32,
    )
    mixed = jnp.dot(combiner, returned, precision=HIGH) + ADAPTER_SCALE * adapted
    squares = jnp.sum(spread(jnp.sum(mixed * mixed, axis=1)[None], SEQ), axis=0)
    position = g * group_rows + jnp.arange(group_rows, dtype=jnp.int32)[None, :]
    factor = jnp.where(position < counts[0], lax.rsqrt(squares / width + 1e-05), 0.0)
    pooled = jnp.dot(factor, mixed, precision=HIGH) * norm_scale
    pooled = jnp.sum(spread(pooled, GROUP), axis=0)
    pooled = spread(pooled, SEQ).reshape(1, width)
    return pooled * lax.rsqrt(jnp.mean(pooled * pooled, axis=1, keepdims=True) + 1e-06)


def solution(mesh):
    seq, experts, tensors = mesh.devices.shape
    parts = Mesh(
        mesh.devices.reshape(seq // 2, 2, experts // 2, 2, tensors), ("z", "c", "y", "h", "t")
    )
    return jax.shard_map(
        local,
        mesh=parts,
        in_specs=(
            P(SEQ, EXPERT),
            P(SEQ, None),
            P(SEQ, None),
            P(EXPERT, None, SEQ + ("t",)),
            P(EXPERT, None, SEQ + ("t",)),
            P(EXPERT, None, SEQ),
            P(None, EXPERT),
            P(None, EXPERT),
            P(),
            P(),
            P(EXPERT),
        ),
        out_specs=P(),
        check_vma=False,
    )
```

```python
import functools

import jax
import jax.numpy as jnp
from jax import lax
from jax.experimental import pallas as pl
from jax.experimental.pallas import tpu as pltpu
from jax.sharding import Mesh
from jax.sharding import PartitionSpec as P

TASK_COUNT = 2
ADAPTER_SCALE = 0.5

SEQ = ("z", "c")
EXPERT = ("y", "h")
GROUP = ("y", "h", "t")

BF16 = jnp.bfloat16
F16 = jnp.float16
F32 = jnp.float32
HIGH = lax.Precision.HIGHEST
LANES = 128
LEAST_EXPONENT = -40.0
LOW_STEP = 2.0**28


def swap(x, axes):
    return lax.all_to_all(x, axes, split_axis=0, concat_axis=0, tiled=True)


def spread(x, axes):
    return swap(jnp.broadcast_to(x[None], (lax.axis_size(axes),) + x.shape), axes)


def rounded(x):
    return lax.reduce_precision(x, 8, 7)


def three_parts(x, step):
    first = rounded(x)
    rest = (x - first) * step
    second = rounded(rest)
    return first, second, (rest - second) * step


def slots_of(ids, experts):
    pairs = ids.shape[1]
    one_hot = (ids[:, None, :] == jnp.arange(experts, dtype=jnp.int32)[None, :, None]).astype(BF16)
    before = (
        jnp.arange(pairs, dtype=jnp.int32)[:, None] < jnp.arange(pairs, dtype=jnp.int32)[None, :]
    ).astype(BF16)
    earlier = lax.dot_general(
        one_hot, before, (((2,), (0,)), ((), ())), preferred_element_type=F32
    )
    return jnp.sum(earlier * one_hot.astype(F32), axis=1).astype(jnp.int32)


def expert_kernel(
    shard_rows, own_ref, x_ref, gate_ref, up_ref, hidden_ref, scale_ref, base_ref, weight_ref
):
    columns = weight_ref.shape[0]
    units = gate_ref.shape[1]
    halves = 2
    half = 256
    for block in range(columns // half):
        for c in range(halves):
            source = pl.ds((block * halves + c) * half, half)
            target = pl.ds(block * half, half)
            weight_ref[target, pl.ds(c * 2 * units, units)] = gate_ref[source, :]
            weight_ref[target, pl.ds((c * 2 + 1) * units, units)] = up_ref[source, :]
    chips = 4
    step_rows = chips * halves * shard_rows
    shape = (chips, halves, shard_rows, units)
    own_half = own_ref[0]
    own_column = pl.multiple_of(own_ref[1], LANES)

    def step(i, carry):
        rows = pl.ds(pl.multiple_of(i * step_rows, step_rows), step_rows)
        out_rows = pl.ds(
            pl.multiple_of(i * chips * shard_rows, chips * shard_rows), chips * shard_rows
        )
        acts = jnp.dot(
            x_ref[rows, pl.ds(0, columns)], weight_ref[...], preferred_element_type=F32
        )
        acts = acts.reshape(chips, halves, shard_rows, 4 * units)
        exponents = x_ref[rows, pl.ds(columns, LANES)].astype(F32).reshape(shape)
        own = x_ref[rows, pl.ds(own_column, LANES)].astype(F32).reshape(shape)
        first, second = exponents[:, 0], exponents[:, 1]
        first_scale, second_scale = jnp.exp2(first - 15.0), jnp.exp2(second - 15.0)
        gate_act = (
            acts[:, 0, :, :units] * first_scale
            + acts[:, 1, :, 2 * units : 3 * units] * second_scale
        )
        up_act = (
            acts[:, 0, :, units : 2 * units] * first_scale
            + acts[:, 1, :, 3 * units :] * second_scale
        )
        hidden = (gate_act / (1.0 + jnp.exp(-gate_act)) * up_act).astype(BF16).astype(F32)
        row_exponent = jnp.maximum(first, second)
        flat = (chips * shard_rows, units)
        hidden_ref[out_rows, :] = (hidden * jnp.exp2(-2.0 * row_exponent - 2.0)).reshape(flat)
        scale_ref[out_rows, :] = jnp.exp2(2.0 * row_exponent + 2.0).reshape(flat)
        base_ref[out_rows, :] = jnp.where(
            own_half == 0, own[:, 0] * first_scale, own[:, 1] * second_scale
        ).reshape(flat)
        return carry

    lax.fori_loop(0, x_ref.shape[0] // step_rows, step, 0)


def expert_layer(gathered, gate_weight, up_weight, own_half, own_column, shard_rows):
    rows = gathered.shape[0]
    columns = gathered.shape[1] - LANES
    units = gate_weight.shape[1]
    out = jax.ShapeDtypeStruct((rows // 2, units), F32)
    vmem = pl.BlockSpec(memory_space=pltpu.VMEM)
    return pl.pallas_call(
        functools.partial(expert_kernel, shard_rows),
        out_shape=(out, out, out),
        in_specs=[pl.BlockSpec(memory_space=pltpu.SMEM), vmem, vmem, vmem],
        out_specs=(vmem, vmem, vmem),
        scratch_shapes=[pltpu.VMEM((columns, 4 * units), BF16)],
        compiler_params=pltpu.CompilerParams(vmem_limit_bytes=32 * 2**20),
        cost_estimate=pl.CostEstimate(
            flops=8 * rows * columns * units,
            bytes_accessed=2 * rows * columns + 8 * columns * units,
            transcendentals=2 * rows * units,
        ),
    )(jnp.stack([own_half, own_column]), gathered, gate_weight, up_weight)


def local(
    tokens,
    routes,
    chosen_expert_weight,
    expert_gate_weight,
    expert_up_weight,
    expert_down_weight,
    adapter_down_weight,
    adapter_up_weight,
    document_task_index,
    counts,
    final_norm_scale,
):
    rows, feats = tokens.shape
    seq = lax.axis_size(SEQ)
    experts = lax.axis_size(EXPERT)
    cores = lax.axis_size("c")
    groups = lax.axis_size(GROUP)
    tensors = lax.axis_size("t")
    capacity = rows * 5 // 16
    width = feats * experts
    half = feats // cores
    slice_width = width // seq
    slots = seq * capacity
    pairs = 2 * rows
    s = lax.axis_index(SEQ)
    e = lax.axis_index(EXPERT)
    t = lax.axis_index("t")
    g = lax.axis_index(GROUP)

    pair_ids = routes.reshape(1, pairs)
    target = pair_ids[0] * capacity + slots_of(pair_ids, experts)[0]
    chooser = jnp.any(
        (target[:, None] == jnp.arange(experts * capacity, dtype=jnp.int32)[None, :]).reshape(
            rows, 2, experts * capacity
        ),
        axis=1,
    ).astype(BF16)
    outgoing = lax.dot_general(
        chooser, tokens, (((0,), (0,)), ((), ())), preferred_element_type=F32
    ).astype(BF16)
    outgoing = outgoing.reshape(experts, capacity, cores, half).transpose(0, 2, 1, 3)
    outgoing = outgoing.reshape(experts * cores, capacity, half)

    task_rows = adapter_down_weight.shape[0]
    column = (s % (feats // slice_width)) * slice_width
    low_part = lax.dot_general(
        tokens, adapter_down_weight, (((1,), (1,)), ((), ())), preferred_element_type=F32
    )
    low_lines = rows * task_rows // LANES
    own_params = jnp.concatenate(
        [
            low_part.reshape(low_lines, LANES),
            lax.dynamic_slice_in_dim(adapter_up_weight, column, slice_width, axis=1).astype(F32),
            lax.dynamic_slice_in_dim(final_norm_scale, column, slice_width)[None],
        ]
    )
    own_params, _ = lax.optimization_barrier((own_params, outgoing))
    received = swap(outgoing, EXPERT + ("c",))
    params = spread(own_params, EXPERT)
    holder = lax.dynamic_index_in_dim(
        params[:, low_lines:], s // (feats // slice_width), axis=0, keepdims=False
    )
    adapter_up = holder[:task_rows].astype(BF16)
    norm_scale = holder[task_rows:]
    task_of_lane = (
        jnp.arange(LANES, dtype=jnp.int32) % task_rows // (task_rows // TASK_COUNT)
    )
    low_rank = rounded(
        jnp.where(
            task_of_lane[None, :] == document_task_index[0],
            jnp.sum(params[:, :low_lines], axis=0),
            0.0,
        )
    )
    low_first = lax.reduce_precision(low_rank, 5, 10)
    low_second = (low_rank - low_first) * LOW_STEP
    shard_rows = cores * capacity
    shard = received.reshape(experts, cores, capacity, half).transpose(1, 2, 0, 3)
    shard = shard.reshape(shard_rows, experts * half).astype(F32)

    largest = jnp.max(jnp.abs(shard), axis=1, keepdims=True)
    exponent = jnp.maximum(
        jnp.floor(jnp.log2(jnp.maximum(largest, 1e-30)) + 1.01), LEAST_EXPONENT
    )
    scaled = (shard * jnp.exp2(15.0 - exponent)).astype(F16)
    notes = jnp.stack(
        [routes.reshape(pairs).astype(F32)]
        + list(three_parts(chosen_expert_weight.reshape(pairs), 256.0))
    )
    notes = jnp.concatenate([notes, low_first, low_second])
    notes = jnp.pad(notes, ((0, -notes.shape[0] % 8), (0, 0))).astype(F16)
    sent = jnp.concatenate(
        [
            scaled,
            jnp.broadcast_to(exponent, (shard_rows, LANES)).astype(F16),
        ],
        axis=1,
    )
    gathered = lax.all_gather(sent, SEQ, axis=0, tiled=False)
    columns = experts * half
    gathered = gathered.astype(BF16).reshape(seq * shard_rows, columns + LANES)
    per_half = half // slice_width
    hidden, return_scale, base = expert_layer(
        gathered,
        expert_gate_weight[0],
        expert_up_weight[0],
        (s // per_half) % cores,
        (s // (feats // slice_width)) * half + (s % per_half) * slice_width,
        shard_rows,
    )

    hidden = lax.all_gather(
        jnp.concatenate([hidden.astype(F16), notes]), SEQ, axis=0, tiled=False
    )
    tables = hidden[:, slots : slots + 4 + 2 * low_lines].astype(F32)
    hidden = hidden[:, :slots]
    hidden_units = hidden.shape[-1]
    down = lax.dynamic_index_in_dim(
        expert_down_weight[0].reshape(seq, tensors, hidden_units, slice_width),
        t,
        axis=1,
        keepdims=False,
    )
    part = lax.dot_general(
        hidden.astype(BF16), down, (((0, 2), (0, 1)), ((), ())), preferred_element_type=F32
    )

    ids = tables[:, 0].astype(jnp.int32)
    weights = tables[:, 1] + (tables[:, 2] + tables[:, 3] / 256.0) / 256.0
    slot_of = slots_of(ids, experts)
    is_mine = jnp.where(ids == e, slot_of, -1)
    slot_weight = jnp.sum(
        jnp.where(
            is_mine[:, None, :] == jnp.arange(capacity, dtype=jnp.int32)[None, :, None],
            weights[:, None, :],
            0.0,
        ),
        axis=2,
    ).reshape(slots, 1)
    payload = slot_weight * return_scale * part + base / (2 * tensors)
    blocks = seq // groups
    returned = swap(payload.reshape(groups, blocks * capacity, slice_width), GROUP)
    returned = jnp.sum(
        returned.reshape(experts, tensors, blocks * capacity, slice_width), axis=1
    ).reshape(experts * blocks * capacity, slice_width)

    group_ids = lax.dynamic_slice_in_dim(ids, g * blocks, blocks, axis=0)
    group_slots = lax.dynamic_slice_in_dim(slot_of, g * blocks, blocks, axis=0)
    place = (
        group_ids * (blocks * capacity)
        + jnp.arange(blocks, dtype=jnp.int32)[:, None] * capacity
        + group_slots
    )
    group_rows = blocks * rows
    combiner = jnp.any(
        place.reshape(group_rows, 2)[:, :, None]
        == jnp.arange(experts * blocks * capacity, dtype=jnp.int32)[None, None, :],
        axis=1,
    ).astype(F32)
    group_low = lax.dynamic_slice_in_dim(tables, g * blocks, blocks, axis=0)[:, 4:]
    group_low = group_low[:, :low_lines] + group_low[:, low_lines:] / LOW_STEP
    adapted = jnp.dot(
        group_low.reshape(group_rows, task_rows).astype(BF16),
        adapter_up,
        preferred_element_type=F32,
    )
    mixed = jnp.dot(combiner, returned, precision=HIGH) + ADAPTER_SCALE * adapted
    squares = jnp.sum(spread(jnp.sum(mixed * mixed, axis=1)[None], SEQ), axis=0)
    position = g * group_rows + jnp.arange(group_rows, dtype=jnp.int32)[None, :]
    factor = jnp.where(position < counts[0], lax.rsqrt(squares / width + 1e-05), 0.0)
    pooled = jnp.dot(factor, mixed, precision=HIGH) * norm_scale
    pooled = jnp.sum(spread(pooled, GROUP), axis=0)
    pooled = spread(pooled, SEQ).reshape(1, width)
    return pooled * lax.rsqrt(jnp.mean(pooled * pooled, axis=1, keepdims=True) + 1e-06)


def solution(mesh):
    seq, experts, tensors = mesh.devices.shape
    parts = Mesh(
        mesh.devices.reshape(seq // 2, 2, experts // 2, 2, tensors), ("z", "c", "y", "h", "t")
    )
    return jax.shard_map(
        local,
        mesh=parts,
        in_specs=(
            P(SEQ, EXPERT),
            P(SEQ, None),
            P(SEQ, None),
            P(EXPERT, None, SEQ + ("t",)),
            P(EXPERT, None, SEQ + ("t",)),
            P(EXPERT, None, SEQ),
            P(None, EXPERT),
            P(None, EXPERT),
            P(),
            P(),
            P(EXPERT),
        ),
        out_specs=P(),
        check_vma=False,
    )
```

```python
import functools

import jax
import jax.numpy as jnp
from jax import lax
from jax.experimental import pallas as pl
from jax.experimental.pallas import tpu as pltpu
from jax.sharding import Mesh
from jax.sharding import PartitionSpec as P

TASK_COUNT = 2
ADAPTER_SCALE = 0.5

SEQ = ("z", "c")
EXPERT = ("y", "h")
GROUP = ("y", "h", "t")
HALVES = 2

BF16 = jnp.bfloat16
F16 = jnp.float16
F32 = jnp.float32
HIGH = lax.Precision.HIGHEST
LANES = 128
LEAST_EXPONENT = -40.0
NOTE_ROWS = 16
PART_STEP = 256.0
PARAM_ROWS = 128


def swap(x, axes):
    return lax.all_to_all(x, axes, split_axis=0, concat_axis=0, tiled=True)


def spread(x, axes):
    return swap(jnp.broadcast_to(x[None], (lax.axis_size(axes),) + x.shape), axes)


def three_parts(x, step):
    first = lax.reduce_precision(x, 8, 7)
    rest = (x - first) * step
    second = lax.reduce_precision(rest, 8, 7)
    return first, second, (rest - second) * step


def earlier_in_block(lanes, block):
    i = lax.broadcasted_iota(jnp.int32, (lanes, lanes), 0)
    j = lax.broadcasted_iota(jnp.int32, (lanes, lanes), 1)
    return ((i < j) & (i // block == j // block)).astype(F32).astype(BF16)


def positions(named, block, capacity):
    lanes = named.shape[1]
    before = jnp.dot(
        named.astype(F32).astype(BF16),
        earlier_in_block(lanes, block),
        preferred_element_type=F32,
    )
    first = (lax.broadcasted_iota(jnp.int32, named.shape, 1) // block * capacity).astype(F32)
    return jnp.where(named, before + first, -1.0)


def expert_kernel(
    shard_rows,
    own_ref,
    x_ref,
    gate_ref,
    up_ref,
    params_ref,
    hidden_ref,
    scale_ref,
    base_ref,
    weight_ref,
    adapter_ref,
):
    columns = weight_ref.shape[0]
    units = gate_ref.shape[1]
    task_rows = adapter_ref.shape[0] // HALVES
    groups = params_ref.shape[0]
    half = columns // groups
    for block in range(groups):
        target = pl.ds(block * half, half)
        for c in range(HALVES):
            source = pl.ds((block * HALVES + c) * half, half)
            weight_ref[target, pl.ds(c * 2 * units, units)] = gate_ref[source, :]
            weight_ref[target, pl.ds((c * 2 + 1) * units, units)] = up_ref[source, :]
            adapter_ref[pl.ds(c * task_rows, task_rows), target] = params_ref[
                block, pl.ds(0, task_rows), pl.ds(c * half, half)
            ]
    chips = 4
    step_rows = chips * HALVES * shard_rows
    shape = (chips, HALVES, shard_rows, units)
    flat = (chips * shard_rows, units)
    own_half = own_ref[0]
    own_column = pl.multiple_of(own_ref[1], LANES)
    own_group = own_ref[2]
    group_column = pl.multiple_of(own_ref[3], LANES)
    task = own_ref[4]
    adapter_up = params_ref[own_group, pl.ds(task_rows, task_rows), pl.ds(group_column, units)]
    task_of_lane = lax.broadcasted_iota(
        jnp.int32, (flat[0], task_rows), 1
    ) // (task_rows // TASK_COUNT)

    def step(i, carry):
        rows = pl.ds(pl.multiple_of(i * step_rows, step_rows), step_rows)
        out_rows = pl.ds(pl.multiple_of(i * flat[0], flat[0]), flat[0])
        x = x_ref[rows, pl.ds(0, columns)]
        acts = jnp.dot(x, weight_ref[...], preferred_element_type=F32)
        acts = acts.reshape(chips, HALVES, shard_rows, 4 * units)
        low = lax.dot_general(
            x, adapter_ref[...], (((1,), (1,)), ((), ())), preferred_element_type=F32
        ).reshape(chips, HALVES, shard_rows, HALVES * task_rows)
        exponents = x_ref[rows, pl.ds(columns, LANES)].astype(F32).reshape(shape)
        own = x_ref[rows, pl.ds(own_column, LANES)].astype(F32).reshape(shape)
        first, second = exponents[:, 0], exponents[:, 1]
        first_scale, second_scale = jnp.exp2(first - 15.0), jnp.exp2(second - 15.0)
        gate_act = (
            acts[:, 0, :, :units] * first_scale
            + acts[:, 1, :, 2 * units : 3 * units] * second_scale
        )
        up_act = (
            acts[:, 0, :, units : 2 * units] * first_scale
            + acts[:, 1, :, 3 * units :] * second_scale
        )
        hidden = (gate_act / (1.0 + jnp.exp(-gate_act)) * up_act).astype(BF16).astype(F32)
        row_exponent = jnp.maximum(first, second)
        hidden_ref[out_rows, :] = (hidden * jnp.exp2(-2.0 * row_exponent - 2.0)).reshape(flat)
        scale_ref[out_rows, :] = jnp.exp2(2.0 * row_exponent + 2.0).reshape(flat)
        low = (
            low[:, 0, :, :task_rows] * first_scale[..., :task_rows]
            + low[:, 1, :, task_rows:] * second_scale[..., :task_rows]
        ).reshape(flat[0], task_rows)
        low = jnp.where(task_of_lane == task, low, 0.0).astype(BF16)
        adapted = jnp.dot(low, adapter_up, preferred_element_type=F32)
        residual = jnp.where(
            own_half == 0, own[:, 0] * first_scale, own[:, 1] * second_scale
        ).reshape(flat)
        base_ref[out_rows, :] = residual + ADAPTER_SCALE * adapted
        return carry

    lax.fori_loop(0, x_ref.shape[0] // step_rows, step, 0)


def expert_layer(gathered, gate_weight, up_weight, params, own, shard_rows, task_rows):
    rows = gathered.shape[0]
    columns = gathered.shape[1] - LANES
    units = gate_weight.shape[1]
    out = jax.ShapeDtypeStruct((rows // HALVES, units), F32)
    vmem = pl.BlockSpec(memory_space=pltpu.VMEM)
    return pl.pallas_call(
        functools.partial(expert_kernel, shard_rows),
        out_shape=(out, out, out),
        in_specs=[pl.BlockSpec(memory_space=pltpu.SMEM), vmem, vmem, vmem, vmem],
        out_specs=(vmem, vmem, vmem),
        scratch_shapes=[
            pltpu.VMEM((columns, 4 * units), BF16),
            pltpu.VMEM((HALVES * task_rows, columns), BF16),
        ],
        compiler_params=pltpu.CompilerParams(vmem_limit_bytes=32 * 2**20),
        cost_estimate=pl.CostEstimate(
            flops=8 * rows * columns * units,
            bytes_accessed=2 * rows * columns + 8 * columns * units,
            transcendentals=2 * rows * units,
        ),
    )(own, gathered, gate_weight, up_weight, params)


def return_kernel(block, capacity, own_ref, h_ref, down_ref, scale_ref, base_ref, out_ref, note_ref):
    seq, rows, units = h_ref.shape
    slots = rows - NOTE_ROWS
    tensor = own_ref[0]
    expert = own_ref[1]
    group = own_ref[2]
    tensors = down_ref.shape[0] // (seq * units)
    cores = HALVES
    pair_rows = cores * capacity
    notes = h_ref[:, pl.ds(slots, NOTE_ROWS), :].astype(F32)
    notes = notes.reshape(seq // cores, cores, NOTE_ROWS, units).sum(axis=1)
    first, second = notes[:, 0, :].astype(jnp.int32), notes[:, 1, :].astype(jnp.int32)
    parts = notes[:, 2:8, :]
    weight = [
        parts[:, k, :] + (parts[:, k + 2, :] + parts[:, k + 4, :] / PART_STEP) / PART_STEP
        for k in range(2)
    ]
    place = positions((first == expert) | (second == expert), block, capacity)
    weight = jnp.where(first == expert, weight[0], weight[1])
    note_ref[...] = h_ref[group * cores, pl.ds(slots, NOTE_ROWS), :].astype(F32) + h_ref[
        group * cores + 1, pl.ds(slots, NOTE_ROWS), :
    ].astype(F32)

    width = 4
    out_ref[...] = jnp.zeros_like(out_ref)

    def step(i, carry):
        lhs = jnp.concatenate(
            [h_ref[i * width + k, pl.ds(0, slots), :] for k in range(width)], axis=1
        )
        rhs = jnp.concatenate(
            [
                down_ref[
                    pl.ds(
                        pl.multiple_of(((i * width + k) * tensors + tensor) * units, units), units
                    ),
                    :,
                ]
                for k in range(width)
            ],
            axis=0,
        )
        out_ref[...] += jnp.dot(lhs, rhs, preferred_element_type=F32)
        return carry

    lax.fori_loop(0, seq // width, step, 0)
    row = lax.broadcasted_iota(jnp.int32, (pair_rows, units), 0).astype(F32)
    for chip in range(seq // cores):
        at = pl.ds(chip * pair_rows, pair_rows)
        slot_weight = jnp.sum(
            jnp.where(place[chip : chip + 1, :] == row, weight[chip : chip + 1, :], 0.0),
            axis=1,
            keepdims=True,
        )
        out_ref[at, :] = slot_weight * (scale_ref[at, :] * out_ref[at, :]) + base_ref[at, :] / (
            2 * tensors
        )


def return_layer(hidden, down_weight, scale, base, own, block, capacity):
    seq, rows, units = hidden.shape
    slots = rows - NOTE_ROWS
    vmem = pl.BlockSpec(memory_space=pltpu.VMEM)
    return pl.pallas_call(
        functools.partial(return_kernel, block, capacity),
        out_shape=(
            jax.ShapeDtypeStruct((slots, units), F32),
            jax.ShapeDtypeStruct((NOTE_ROWS, units), F32),
        ),
        in_specs=[pl.BlockSpec(memory_space=pltpu.SMEM), vmem, vmem, vmem, vmem],
        out_specs=(vmem, vmem),
        compiler_params=pltpu.CompilerParams(vmem_limit_bytes=32 * 2**20),
        cost_estimate=pl.CostEstimate(
            flops=2 * seq * slots * units * units,
            bytes_accessed=2 * seq * slots * units + 2 * down_weight.size,
            transcendentals=0,
        ),
    )(own, hidden, down_weight, scale, base)


def local(
    tokens,
    routes,
    chosen_expert_weight,
    expert_gate_weight,
    expert_up_weight,
    expert_down_weight,
    adapter_down_weight,
    adapter_up_weight,
    document_task_index,
    counts,
    final_norm_scale,
):
    rows, feats = tokens.shape
    seq = lax.axis_size(SEQ)
    experts = lax.axis_size(EXPERT)
    cores = lax.axis_size("c")
    groups = lax.axis_size(GROUP)
    capacity = rows * 5 // 16
    shard_rows = cores * capacity
    width = feats * experts
    half = feats // cores
    columns = experts * half
    slice_width = width // seq
    slots = seq * capacity
    task_rows = adapter_down_weight.shape[0]
    s = lax.axis_index(SEQ)
    g = lax.axis_index(GROUP)
    per_feature_group = feats // slice_width
    own_group = s // per_feature_group
    group_column = (s % per_feature_group) * slice_width

    params = jnp.concatenate(
        [adapter_down_weight, adapter_up_weight]
        + [part[None].astype(BF16) for part in three_parts(final_norm_scale, 1.0)]
    )
    params = jnp.pad(params, ((0, PARAM_ROWS - params.shape[0]), (0, 0)))
    params = lax.all_gather(params, EXPERT, axis=0, tiled=False)

    ids = routes.T
    expert_ids = jnp.arange(experts, dtype=jnp.int32)[:, None]
    place = positions((ids[:1] == expert_ids) | (ids[1:] == expert_ids), rows, capacity)
    chooser = (
        place[:, None, :] == jnp.arange(capacity, dtype=jnp.int32).astype(F32)[None, :, None]
    ).astype(BF16)
    outgoing = jnp.dot(
        chooser.reshape(experts * capacity, rows), tokens, preferred_element_type=F32
    ).astype(BF16)
    outgoing = outgoing.reshape(experts, capacity, cores, half).transpose(0, 2, 1, 3)
    received = swap(outgoing.reshape(experts * cores, capacity, half), EXPERT + ("c",))
    shard = received.reshape(experts, cores, capacity, half).transpose(1, 2, 0, 3)
    shard = shard.reshape(shard_rows, columns).astype(F32)

    largest = jnp.max(jnp.abs(shard), axis=1, keepdims=True)
    exponent = jnp.maximum(
        jnp.floor(jnp.log2(jnp.maximum(largest, 1e-30)) + 1.01), LEAST_EXPONENT
    )
    scaled = (shard * jnp.exp2(15.0 - exponent)).astype(F16)
    sent = jnp.concatenate(
        [scaled, jnp.broadcast_to(exponent, (shard_rows, LANES)).astype(F16)], axis=1
    )
    gathered = lax.all_gather(sent, SEQ, axis=0, tiled=False)
    gathered = gathered.astype(BF16).reshape(seq * shard_rows, columns + LANES)
    per_half = half // slice_width
    own = jnp.stack(
        [
            (s // per_half) % cores,
            own_group * half + (s % per_half) * slice_width,
            own_group,
            group_column,
            document_task_index[0],
        ]
    )
    hidden, return_scale, base = expert_layer(
        gathered,
        expert_gate_weight[0],
        expert_up_weight[0],
        params,
        own,
        shard_rows,
        task_rows,
    )

    notes = jnp.concatenate(
        [ids.astype(F32)] + list(three_parts(chosen_expert_weight.T, PART_STEP))
    )
    core = lax.axis_index("c")
    notes = jnp.concatenate([jnp.where(core == k, notes, 0.0) for k in range(cores)], axis=1)
    notes = jnp.pad(notes, ((0, NOTE_ROWS - notes.shape[0]), (0, 0)))
    hidden = lax.all_gather(
        jnp.concatenate([hidden.astype(F16), notes.astype(F16)]), SEQ, axis=0, tiled=False
    )
    payload, group_notes = return_layer(
        hidden.astype(BF16),
        expert_down_weight[0],
        return_scale,
        base,
        jnp.stack([lax.axis_index("t"), lax.axis_index(EXPERT), g]),
        rows,
        capacity,
    )

    returned = swap(payload.reshape(groups, shard_rows, slice_width), GROUP)
    returned = jnp.sum(returned.reshape(experts, -1, shard_rows, slice_width), axis=1)
    returned = returned.reshape(experts * shard_rows, slice_width)

    group_ids = group_notes[:2].astype(jnp.int32)
    group_place = positions(
        (group_ids[:1] == expert_ids) | (group_ids[1:] == expert_ids), rows, capacity
    )
    group_rows = cores * rows
    combiner = (
        group_place[:, None, :]
        == jnp.arange(shard_rows, dtype=jnp.int32).astype(F32)[None, :, None]
    ).astype(F32)
    mixed = lax.dot_general(
        combiner.reshape(experts * shard_rows, group_rows),
        returned,
        (((0,), (0,)), ((), ())),
        precision=HIGH,
    )
    squares = jnp.sum(spread(jnp.sum(mixed * mixed, axis=1)[None], SEQ), axis=0)
    position = g * group_rows + jnp.arange(group_rows, dtype=jnp.int32)[None, :]
    factor = jnp.where(position < counts[0], lax.rsqrt(squares / width + 1e-05), 0.0)
    norm_scale = lax.dynamic_slice(
        params, (own_group, 2 * task_rows, group_column), (1, 3, slice_width)
    )
    norm_scale = jnp.sum(norm_scale.astype(F32), axis=1)
    pooled = jnp.dot(factor, mixed, precision=HIGH) * norm_scale
    pooled = jnp.sum(spread(pooled, GROUP), axis=0)
    pooled = spread(pooled, SEQ).reshape(1, width)
    return pooled * lax.rsqrt(jnp.mean(pooled * pooled, axis=1, keepdims=True) + 1e-06)


def solution(mesh):
    seq, experts, tensors = mesh.devices.shape
    parts = Mesh(
        mesh.devices.reshape(seq // 2, 2, experts // 2, 2, tensors), ("z", "c", "y", "h", "t")
    )
    return jax.shard_map(
        local,
        mesh=parts,
        in_specs=(
            P(SEQ, EXPERT),
            P(SEQ, None),
            P(SEQ, None),
            P(EXPERT, None, SEQ + ("t",)),
            P(EXPERT, None, SEQ + ("t",)),
            P(EXPERT, None, SEQ),
            P(None, EXPERT),
            P(None, EXPERT),
            P(),
            P(),
            P(EXPERT),
        ),
        out_specs=P(),
        check_vma=False,
    )
```

```python
import functools

import jax
import jax.numpy as jnp
from jax import lax
from jax.experimental import pallas as pl
from jax.experimental.pallas import tpu as pltpu
from jax.sharding import Mesh
from jax.sharding import PartitionSpec as P

TASK_COUNT = 2
ADAPTER_SCALE = 0.5

SEQ = ("z", "c")
EXPERT = ("y", "h")
GROUP = ("y", "h", "t")
HALVES = 2

BF16 = jnp.bfloat16
F16 = jnp.float16
F32 = jnp.float32
HIGH = lax.Precision.HIGHEST
LANES = 128
LEAST_EXPONENT = -40.0
NOTE_ROWS = 16
PART_STEP = 256.0
LOW_LANES = 32


def swap(x, axes):
    return lax.all_to_all(x, axes, split_axis=0, concat_axis=0, tiled=True)


def spread(x, axes):
    return swap(jnp.broadcast_to(x[None], (lax.axis_size(axes),) + x.shape), axes)


def three_parts(x, step):
    first = lax.reduce_precision(x, 8, 7)
    rest = (x - first) * step
    second = lax.reduce_precision(rest, 8, 7)
    return first, second, (rest - second) * step


def earlier_in_block(lanes, block):
    i = lax.broadcasted_iota(jnp.int32, (lanes, lanes), 0)
    j = lax.broadcasted_iota(jnp.int32, (lanes, lanes), 1)
    return ((i < j) & (i // block == j // block)).astype(F32).astype(BF16)


def positions(named, block, capacity):
    lanes = named.shape[1]
    before = jnp.dot(
        named.astype(F32).astype(BF16),
        earlier_in_block(lanes, block),
        preferred_element_type=F32,
    )
    first = (lax.broadcasted_iota(jnp.int32, named.shape, 1) // block * capacity).astype(F32)
    return jnp.where(named, before + first, -1.0)


def dispatch_kernel(
    capacity, own_ref, routes_ref, tokens_ref, down_ref, up_ref, norm_ref, out_ref
):
    targets, _, out_lanes = out_ref.shape
    experts = targets // HALVES
    rows, feats = tokens_ref.shape
    half = feats // HALVES
    ranks = down_ref.shape[0] // HALVES
    core = own_ref[0]
    ids = routes_ref[...]
    expert = lax.broadcasted_iota(jnp.int32, (experts, rows), 0)
    place = positions((ids[:1] == expert) | (ids[1:] == expert), rows, capacity)
    padded = -(-capacity // 16) * 16
    slot = lax.broadcasted_iota(jnp.int32, (padded, rows), 0).astype(F32)
    chooser = jnp.concatenate(
        [(place[e : e + 1] == slot).astype(F32) for e in range(experts)], axis=0
    ).astype(BF16)
    for c in range(HALVES):
        lanes = pl.ds(c * half, half)
        x = tokens_ref[:, lanes]
        low = lax.dot_general(
            x, down_ref[:, lanes], (((1,), (1,)), ((), ())), preferred_element_type=F32
        )
        first = low.astype(BF16)
        rest = low - first.astype(F32)
        second = rest.astype(BF16)
        third = (rest - second.astype(F32)).astype(BF16)
        x = jnp.concatenate([x, jnp.zeros_like(first), first, second, third], axis=1)
        chosen = jnp.dot(chooser, x, preferred_element_type=F32).astype(BF16).astype(F32)
        column = pl.multiple_of(own_ref[1 + c], LANES)
        norm = norm_ref[:, pl.ds(column, LANES)]
        norm_first = norm.astype(BF16).astype(F32)
        norm_rest = norm - norm_first
        norm_second = norm_rest.astype(BF16).astype(F32)
        up_rows = up_ref[pl.ds(pl.multiple_of(core * ranks, ranks), ranks), pl.ds(column, LANES)]
        small = jnp.concatenate(
            [
                up_rows.astype(F32),
                norm_first,
                norm_second,
                norm_rest - norm_second,
                jnp.zeros((capacity - ranks - 3, LANES), F32),
            ],
            axis=0,
        ).astype(BF16)
        for e in range(experts):
            out_ref[e * HALVES + c, :, pl.ds(0, out_lanes - LANES)] = chosen[
                e * padded : e * padded + capacity
            ].astype(BF16)
            out_ref[e * HALVES + c, :, pl.ds(out_lanes - LANES, LANES)] = small


def dispatch_layer(own, routes, tokens, adapter_down, adapter_up, norm_scale, experts, capacity):
    rows, feats = tokens.shape
    vmem = pl.BlockSpec(memory_space=pltpu.VMEM)
    lanes = feats // HALVES + 2 * LANES
    return pl.pallas_call(
        functools.partial(dispatch_kernel, capacity),
        out_shape=jax.ShapeDtypeStruct((experts * HALVES, capacity, lanes), BF16),
        in_specs=[pl.BlockSpec(memory_space=pltpu.SMEM)] + [vmem] * 5,
        out_specs=vmem,
        compiler_params=pltpu.CompilerParams(vmem_limit_bytes=16 * 2**20),
        cost_estimate=pl.CostEstimate(
            flops=4 * rows * feats * experts * capacity,
            bytes_accessed=2 * rows * feats + 2 * experts * HALVES * capacity * lanes,
            transcendentals=0,
        ),
    )(own, routes, tokens, adapter_down, adapter_up, norm_scale)


def expert_kernel(
    shard_rows,
    own_ref,
    x_ref,
    gate_ref,
    up_ref,
    adapter_ref,
    hidden_ref,
    scale_ref,
    base_ref,
    weight_ref,
):
    columns = weight_ref.shape[0]
    units = gate_ref.shape[1]
    task_rows = adapter_ref.shape[0]
    half = 2 * LANES
    for block in range(columns // half):
        target = pl.ds(block * half, half)
        for c in range(HALVES):
            source = pl.ds((block * HALVES + c) * half, half)
            weight_ref[target, pl.ds(c * 2 * units, units)] = gate_ref[source, :]
            weight_ref[target, pl.ds((c * 2 + 1) * units, units)] = up_ref[source, :]
    chips = 4
    step_rows = chips * HALVES * shard_rows
    shape = (chips, HALVES, shard_rows, units)
    flat = (chips * shard_rows, units)
    own_half = own_ref[0]
    own_column = pl.multiple_of(own_ref[1], LANES)
    task = own_ref[2]
    task_of_lane = lax.broadcasted_iota(
        jnp.int32, (flat[0], task_rows), 1
    ) // (task_rows // TASK_COUNT)

    def step(i, carry):
        rows = pl.ds(pl.multiple_of(i * step_rows, step_rows), step_rows)
        out_rows = pl.ds(pl.multiple_of(i * flat[0], flat[0]), flat[0])
        x = x_ref[rows, pl.ds(0, columns)]
        acts = jnp.dot(x, weight_ref[...], preferred_element_type=F32)
        acts = acts.reshape(chips, HALVES, shard_rows, 4 * units)
        beside = x_ref[rows, pl.ds(columns, LANES)].astype(F32)
        exponent = beside[:, :LOW_LANES]
        low = beside[:, LOW_LANES : 2 * LOW_LANES] + (
            beside[:, 2 * LOW_LANES : 3 * LOW_LANES]
            + beside[:, 3 * LOW_LANES :] / PART_STEP
        ) / PART_STEP
        low = (low * jnp.exp2(exponent - 7.0)).reshape(chips, HALVES, shard_rows, LOW_LANES)
        exponents = jnp.concatenate([exponent] * (LANES // LOW_LANES), axis=1).reshape(shape)
        own = x_ref[rows, pl.ds(own_column, LANES)].astype(F32).reshape(shape)
        first, second = exponents[:, 0], exponents[:, 1]
        first_scale, second_scale = jnp.exp2(first - 15.0), jnp.exp2(second - 15.0)
        gate_act = (
            acts[:, 0, :, :units] * first_scale
            + acts[:, 1, :, 2 * units : 3 * units] * second_scale
        )
        up_act = (
            acts[:, 0, :, units : 2 * units] * first_scale
            + acts[:, 1, :, 3 * units :] * second_scale
        )
        hidden = (gate_act / (1.0 + jnp.exp(-gate_act)) * up_act).astype(BF16).astype(F32)
        row_exponent = jnp.maximum(first, second)
        hidden_ref[out_rows, :] = (hidden * jnp.exp2(-2.0 * row_exponent - 2.0)).reshape(flat)
        scale_ref[out_rows, :] = jnp.exp2(2.0 * row_exponent + 2.0).reshape(flat)
        low = (low[:, 0] + low[:, 1]).reshape(flat[0], LOW_LANES)
        low = jnp.where(task_of_lane == task, low, 0.0).astype(BF16)
        adapted = jnp.dot(low, adapter_ref[...], preferred_element_type=F32)
        residual = jnp.where(
            own_half == 0, own[:, 0] * first_scale, own[:, 1] * second_scale
        ).reshape(flat)
        base_ref[out_rows, :] = residual + ADAPTER_SCALE * adapted
        return carry

    lax.fori_loop(0, x_ref.shape[0] // step_rows, step, 0)


def expert_layer(gathered, gate_weight, up_weight, adapter_up, own, shard_rows):
    rows = gathered.shape[0]
    columns = gathered.shape[1] - LANES
    units = gate_weight.shape[1]
    out = jax.ShapeDtypeStruct((rows // HALVES, units), F32)
    vmem = pl.BlockSpec(memory_space=pltpu.VMEM)
    return pl.pallas_call(
        functools.partial(expert_kernel, shard_rows),
        out_shape=(out, out, out),
        in_specs=[pl.BlockSpec(memory_space=pltpu.SMEM), vmem, vmem, vmem, vmem],
        out_specs=(vmem, vmem, vmem),
        scratch_shapes=[pltpu.VMEM((columns, 4 * units), BF16)],
        compiler_params=pltpu.CompilerParams(vmem_limit_bytes=24 * 2**20),
        cost_estimate=pl.CostEstimate(
            flops=8 * rows * columns * units,
            bytes_accessed=2 * rows * columns + 8 * columns * units,
            transcendentals=2 * rows * units,
        ),
    )(own, gathered, gate_weight, up_weight, adapter_up)


def return_kernel(
    block,
    capacity,
    own_ref,
    h_ref,
    down_ref,
    scale_ref,
    base_ref,
    out_ref,
    note_ref,
    weight_ref,
):
    seq, rows, units = h_ref.shape
    slots = rows - NOTE_ROWS
    tensor = own_ref[0]
    expert = own_ref[1]
    group = own_ref[2]
    tensors = down_ref.shape[0] // (seq * units)
    cores = HALVES
    pair_rows = cores * capacity
    notes = h_ref[:, pl.ds(slots, NOTE_ROWS), :].astype(F32)
    notes = notes.reshape(seq // cores, cores, NOTE_ROWS, units).sum(axis=1)
    first, second = notes[:, 0, :].astype(jnp.int32), notes[:, 1, :].astype(jnp.int32)
    parts = notes[:, 2:8, :]
    weight = [
        parts[:, k, :] + (parts[:, k + 2, :] + parts[:, k + 4, :] / PART_STEP) / PART_STEP
        for k in range(2)
    ]
    place = positions((first == expert) | (second == expert), block, capacity)
    weight = jnp.where(first == expert, weight[0], weight[1])
    note_ref[...] = h_ref[group * cores, pl.ds(slots, NOTE_ROWS), :].astype(F32) + h_ref[
        group * cores + 1, pl.ds(slots, NOTE_ROWS), :
    ].astype(F32)

    for k in range(seq):
        source = pl.multiple_of((k * tensors + tensor) * units, units)
        weight_ref[pl.ds(k * units, units), :] = down_ref[pl.ds(source, units), :]
    step_rows = slots // 2

    def step(i, carry):
        at = pl.ds(pl.multiple_of(i * step_rows, step_rows), step_rows)
        lhs = jnp.concatenate([h_ref[k, at, :] for k in range(seq)], axis=1)
        out_ref[at, :] = jnp.dot(lhs, weight_ref[...], preferred_element_type=F32)
        return carry

    lax.fori_loop(0, slots // step_rows, step, 0)
    row = lax.broadcasted_iota(jnp.int32, (pair_rows, units), 0).astype(F32)
    for chip in range(seq // cores):
        at = pl.ds(chip * pair_rows, pair_rows)
        slot_weight = jnp.sum(
            jnp.where(place[chip : chip + 1, :] == row, weight[chip : chip + 1, :], 0.0),
            axis=1,
            keepdims=True,
        )
        out_ref[at, :] = slot_weight * (scale_ref[at, :] * out_ref[at, :]) + base_ref[at, :] / (
            2 * tensors
        )


def return_layer(hidden, down_weight, scale, base, own, block, capacity):
    seq, rows, units = hidden.shape
    slots = rows - NOTE_ROWS
    vmem = pl.BlockSpec(memory_space=pltpu.VMEM)
    return pl.pallas_call(
        functools.partial(return_kernel, block, capacity),
        out_shape=(
            jax.ShapeDtypeStruct((slots, units), F32),
            jax.ShapeDtypeStruct((NOTE_ROWS, units), F32),
        ),
        in_specs=[pl.BlockSpec(memory_space=pltpu.SMEM), vmem, vmem, vmem, vmem],
        out_specs=(vmem, vmem),
        scratch_shapes=[pltpu.VMEM((seq * units, units), BF16)],
        compiler_params=pltpu.CompilerParams(vmem_limit_bytes=24 * 2**20),
        cost_estimate=pl.CostEstimate(
            flops=2 * seq * slots * units * units,
            bytes_accessed=2 * seq * slots * units + 2 * down_weight.size,
            transcendentals=0,
        ),
    )(own, hidden, down_weight, scale, base)


def local(
    tokens,
    routes,
    chosen_expert_weight,
    expert_gate_weight,
    expert_up_weight,
    expert_down_weight,
    adapter_down_weight,
    adapter_up_weight,
    document_task_index,
    counts,
    final_norm_scale,
):
    rows, feats = tokens.shape
    seq = lax.axis_size(SEQ)
    experts = lax.axis_size(EXPERT)
    cores = lax.axis_size("c")
    groups = lax.axis_size(GROUP)
    capacity = rows * 5 // 16
    shard_rows = cores * capacity
    width = feats * experts
    half = feats // cores
    columns = experts * half
    slice_width = width // seq
    slots = seq * capacity
    task_rows = adapter_down_weight.shape[0]
    s = lax.axis_index(SEQ)
    g = lax.axis_index(GROUP)
    per_feature_group = feats // slice_width
    own_group = s // per_feature_group

    core = lax.axis_index("c")
    ids = routes.T
    outgoing = dispatch_layer(
        jnp.stack(
            [core] + [(s - core + k) % per_feature_group * slice_width for k in range(cores)]
        ),
        ids,
        tokens,
        adapter_down_weight,
        adapter_up_weight,
        final_norm_scale[None],
        experts,
        capacity,
    )
    received = swap(outgoing, EXPERT + ("c",)).reshape(experts, cores, capacity, -1)
    shard = received[..., :half].transpose(1, 2, 0, 3)
    shard = shard.reshape(shard_rows, columns).astype(F32)
    low = jnp.sum(received[..., half + LOW_LANES : half + LANES].astype(F32), axis=0)
    low = low.reshape(shard_rows, 3, LOW_LANES).sum(axis=1)
    small = lax.dynamic_index_in_dim(received, own_group, axis=0, keepdims=False)
    small = small[..., half + LANES :]
    adapter_up = small[:, : task_rows // cores].reshape(task_rows, slice_width)
    norm_scale = jnp.sum(
        small[:1, task_rows // cores : task_rows // cores + 3].astype(F32), axis=1
    )

    largest = jnp.max(jnp.abs(shard), axis=1, keepdims=True)
    exponent = jnp.maximum(
        jnp.floor(jnp.log2(jnp.maximum(largest, 1e-30)) + 1.01), LEAST_EXPONENT
    )
    scaled = (shard * jnp.exp2(15.0 - exponent)).astype(F16)
    sent = jnp.concatenate(
        [scaled, jnp.broadcast_to(exponent, (shard_rows, LOW_LANES)).astype(F16)]
        + [part.astype(F16) for part in three_parts(low * jnp.exp2(7.0 - exponent), PART_STEP)],
        axis=1,
    )
    gathered = lax.all_gather(sent, SEQ, axis=0, tiled=False)
    gathered = gathered.astype(BF16).reshape(seq * shard_rows, columns + LANES)
    per_half = half // slice_width
    own = jnp.stack(
        [
            (s // per_half) % cores,
            own_group * half + (s % per_half) * slice_width,
            document_task_index[0],
        ]
    )
    hidden, return_scale, base = expert_layer(
        gathered,
        expert_gate_weight[0],
        expert_up_weight[0],
        adapter_up,
        own,
        shard_rows,
    )

    notes = jnp.concatenate(
        [ids.astype(F32)] + list(three_parts(chosen_expert_weight.T, PART_STEP))
    )
    notes = jnp.concatenate([jnp.where(core == k, notes, 0.0) for k in range(cores)], axis=1)
    notes = jnp.pad(notes, ((0, NOTE_ROWS - notes.shape[0]), (0, 0)))
    hidden = lax.all_gather(
        jnp.concatenate([hidden.astype(F16), notes.astype(F16)]), SEQ, axis=0, tiled=False
    )
    payload, group_notes = return_layer(
        hidden.astype(BF16),
        expert_down_weight[0],
        return_scale,
        base,
        jnp.stack([lax.axis_index("t"), lax.axis_index(EXPERT), g]),
        rows,
        capacity,
    )

    returned = swap(payload.reshape(groups, shard_rows, slice_width), GROUP)
    returned = jnp.sum(returned.reshape(experts, -1, shard_rows, slice_width), axis=1)
    returned = returned.reshape(experts * shard_rows, slice_width)

    expert_ids = jnp.arange(experts, dtype=jnp.int32)[:, None]
    group_ids = group_notes[:2].astype(jnp.int32)
    group_place = positions(
        (group_ids[:1] == expert_ids) | (group_ids[1:] == expert_ids), rows, capacity
    )
    group_rows = cores * rows
    combiner = (
        group_place[:, None, :]
        == jnp.arange(shard_rows, dtype=jnp.int32).astype(F32)[None, :, None]
    ).astype(F32)
    mixed = lax.dot_general(
        combiner.reshape(experts * shard_rows, group_rows),
        returned,
        (((0,), (0,)), ((), ())),
        precision=HIGH,
    )
    squares = jnp.sum(spread(jnp.sum(mixed * mixed, axis=1)[None], SEQ), axis=0)
    position = g * group_rows + jnp.arange(group_rows, dtype=jnp.int32)[None, :]
    factor = jnp.where(position < counts[0], lax.rsqrt(squares / width + 1e-05), 0.0)
    pooled = jnp.dot(factor, mixed, precision=HIGH) * norm_scale
    pooled = jnp.sum(spread(pooled, GROUP), axis=0)
    pooled = spread(pooled, SEQ).reshape(1, width)
    return pooled * lax.rsqrt(jnp.mean(pooled * pooled, axis=1, keepdims=True) + 1e-06)


def solution(mesh):
    seq, experts, tensors = mesh.devices.shape
    parts = Mesh(
        mesh.devices.reshape(seq // 2, 2, experts // 2, 2, tensors), ("z", "c", "y", "h", "t")
    )
    return jax.shard_map(
        local,
        mesh=parts,
        in_specs=(
            P(SEQ, EXPERT),
            P(SEQ, None),
            P(SEQ, None),
            P(EXPERT, None, SEQ + ("t",)),
            P(EXPERT, None, SEQ + ("t",)),
            P(EXPERT, None, SEQ),
            P(None, EXPERT),
            P(None, EXPERT),
            P(),
            P(),
            P(EXPERT),
        ),
        out_specs=P(),
        check_vma=False,
    )
```

```python
import functools

import jax
import jax.numpy as jnp
from jax import lax
from jax.experimental import pallas as pl
from jax.experimental.pallas import tpu as pltpu
from jax.sharding import Mesh
from jax.sharding import PartitionSpec as P

TASK_COUNT = 2
ADAPTER_SCALE = 0.5

SEQ = ("z", "c")
EXPERT = ("y", "h")
GROUP = ("y", "h", "t")
HALVES = 2

BF16 = jnp.bfloat16
F16 = jnp.float16
F32 = jnp.float32
HIGH = lax.Precision.HIGHEST
LANES = 128
LEAST_EXPONENT = -40.0
NOTE_ROWS = 16
PART_STEP = 256.0
LOW_LANES = 32


def swap(x, axes):
    return lax.all_to_all(x, axes, split_axis=0, concat_axis=0, tiled=True)


def spread(x, axes):
    return swap(jnp.broadcast_to(x[None], (lax.axis_size(axes),) + x.shape), axes)


def three_parts(x, step):
    first = lax.reduce_precision(x, 8, 7)
    rest = (x - first) * step
    second = lax.reduce_precision(rest, 8, 7)
    return first, second, (rest - second) * step


def earlier_in_block(lanes, block):
    i = lax.broadcasted_iota(jnp.int32, (lanes, lanes), 0)
    j = lax.broadcasted_iota(jnp.int32, (lanes, lanes), 1)
    return ((i < j) & (i // block == j // block)).astype(F32).astype(BF16)


def slots_of(named, block):
    before = jnp.dot(
        named.astype(F32).astype(BF16),
        earlier_in_block(named.shape[1], block),
        preferred_element_type=F32,
    )
    return jnp.where(named, before, -1.0)


def block_of(shape, block):
    return (lax.broadcasted_iota(jnp.int32, shape, 1) // block).astype(F32)


def dispatch_kernel(own_ref, *refs):
    out_ref, held, sem = refs[5], refs[6:11], refs[11]
    copies = [pltpu.make_async_copy(refs[k], held[k], sem.at[k]) for k in range(5)]
    for copy in copies:
        copy.start()
    for copy in copies:
        copy.wait()
    routes_ref, tokens_ref, down_ref, up_ref, norm_ref = held
    targets, set_slots, _ = out_ref.shape
    experts = targets // HALVES
    rows, feats = tokens_ref.shape
    half = feats // HALVES
    ranks = down_ref.shape[0] // HALVES
    core = own_ref[0]
    first_slot = (own_ref[3] * set_slots).astype(F32)
    ids = routes_ref[...]
    expert = lax.broadcasted_iota(jnp.int32, (experts, rows), 0)
    place = slots_of((ids[:1] == expert) | (ids[1:] == expert), rows)
    padded = 16
    row = lax.broadcasted_iota(jnp.int32, (padded, rows), 0)
    slot = jnp.where(row < set_slots, row.astype(F32) + first_slot, -2.0)
    chooser = jnp.concatenate(
        [(place[e : e + 1] == slot).astype(F32) for e in range(experts)], axis=0
    ).astype(BF16)
    for c in range(HALVES):
        lanes = pl.ds(c * half, half)
        x = tokens_ref[:, lanes]
        low = lax.dot_general(
            x, down_ref[:, lanes], (((1,), (1,)), ((), ())), preferred_element_type=F32
        )
        first = low.astype(BF16)
        rest = low - first.astype(F32)
        second = rest.astype(BF16)
        third = (rest - second.astype(F32)).astype(BF16)
        x = jnp.concatenate([x, jnp.zeros_like(first), first, second, third], axis=1)
        chosen = jnp.dot(chooser, x, preferred_element_type=F32)
        column = pl.multiple_of(own_ref[1 + c], LANES)
        norm = norm_ref[:, pl.ds(column, LANES)]
        norm_first = norm.astype(BF16).astype(F32)
        norm_rest = norm - norm_first
        norm_second = norm_rest.astype(BF16).astype(F32)
        up_rows = up_ref[pl.ds(pl.multiple_of(core * ranks, ranks), ranks), pl.ds(column, LANES)]
        up_rows = up_rows.astype(F32)
        small = [
            up_rows[:set_slots],
            jnp.concatenate(
                [
                    up_rows[set_slots:],
                    norm_first,
                    norm_second,
                    norm_rest - norm_second,
                    jnp.zeros((2 * set_slots - ranks - 3, LANES), F32),
                ],
                axis=0,
            ),
        ]
        small = jnp.concatenate(small, axis=1).astype(BF16)
        for e in range(experts):
            out_ref[e * HALVES + c, :, pl.ds(0, half + LANES)] = chosen[
                e * padded : e * padded + set_slots
            ].astype(BF16)
            out_ref[e * HALVES + c, :, pl.ds(half + LANES, 2 * LANES)] = small


def dispatch_layer(own, routes, tokens, adapter_down, adapter_up, norm_scale, experts, set_slots):
    rows, feats = tokens.shape
    lanes = feats // HALVES + 3 * LANES
    operands = (routes, tokens, adapter_down, adapter_up, norm_scale)
    return pl.pallas_call(
        dispatch_kernel,
        out_shape=jax.ShapeDtypeStruct((experts * HALVES, set_slots, lanes), BF16),
        in_specs=[pl.BlockSpec(memory_space=pltpu.SMEM)]
        + [pl.BlockSpec(memory_space=pl.ANY)] * len(operands),
        out_specs=pl.BlockSpec(memory_space=pltpu.VMEM),
        scratch_shapes=[pltpu.VMEM(x.shape, x.dtype) for x in operands]
        + [pltpu.SemaphoreType.DMA((len(operands),))],
        compiler_params=pltpu.CompilerParams(vmem_limit_bytes=16 * 2**20),
        cost_estimate=pl.CostEstimate(
            flops=4 * rows * feats * experts * set_slots,
            bytes_accessed=2 * rows * feats + 2 * experts * HALVES * set_slots * lanes,
            transcendentals=0,
        ),
    )(own, *operands)


def expert_kernel(
    shard_rows,
    own_ref,
    x_ref,
    gate_ref,
    up_ref,
    far_gate_ref,
    far_up_ref,
    adapter_ref,
    hidden_ref,
    scale_ref,
    base_ref,
    weight_ref,
):
    quarters, columns, _ = weight_ref.shape
    units = gate_ref.shape[1]
    task_rows = adapter_ref.shape[0]
    half = 2 * LANES
    blocks = columns // half
    for c in range(HALVES):
        for q in range(HALVES):
            for block in range(blocks):
                source = pl.ds(((q * blocks + block) * HALVES + c) * half, half)
                target = pl.ds(block * half, half)
                for k, ref in enumerate((gate_ref, up_ref, far_gate_ref, far_up_ref)):
                    weight_ref[c * HALVES + q, target, pl.ds(k * units, units)] = ref[source, :]
    rows = shard_rows // HALVES
    group = -(-rows // 8) * 8
    chips = x_ref.shape[0] // (HALVES * shard_rows)
    flat = chips * group
    own_core, own_quarter = own_ref[0], own_ref[1]
    own_column = pl.multiple_of(own_ref[2], LANES)
    task = own_ref[3]
    tensor = own_ref[4]

    def part(value, c, q):
        value = value.reshape(chips, HALVES, shard_rows, value.shape[-1])[:, c]
        value = value[:, :group] if q == 0 else value[:, shard_rows - group :]
        return value.reshape(flat, value.shape[-1])

    def aligned(value, q):
        return value if q == 0 else pltpu.roll(value, flat - (group - rows), 0)

    x = x_ref[:, pl.ds(0, columns)].astype(F32)
    own = x_ref[:, pl.ds(own_column, LANES)].astype(F32)
    beside = x_ref[:, pl.ds(columns, LANES)].astype(F32)
    acts = jnp.zeros((flat, 4 * units), F32)
    low = jnp.zeros((flat, LOW_LANES), F32)
    residual = jnp.zeros((flat, units), F32)
    row_exponent = None
    for c in range(HALVES):
        tile = part(beside, c, 0)
        exponent = tile[:, :LOW_LANES]
        low_part = tile[:, LOW_LANES : 2 * LOW_LANES] + (
            tile[:, 2 * LOW_LANES : 3 * LOW_LANES] + tile[:, 3 * LOW_LANES :] / PART_STEP
        ) / PART_STEP
        low += low_part * jnp.exp2(exponent - 7.0)
        exponent = jnp.concatenate([exponent] * (LANES // LOW_LANES), axis=1)
        scale = jnp.exp2(exponent - 15.0)
        row_exponent = exponent if c == 0 else jnp.maximum(row_exponent, exponent)
        half_acts = jnp.zeros((flat, 4 * units), F32)
        for q in range(HALVES):
            product = jnp.dot(
                part(x, c, q).astype(BF16),
                weight_ref[c * HALVES + q],
                preferred_element_type=F32,
            )
            half_acts += aligned(product, q)
            mine = (own_core == c) & (own_quarter == q)
            residual += jnp.where(mine, aligned(part(own, c, q), q) * scale, 0.0)
        acts += half_acts * jnp.concatenate([scale] * 4, axis=1)
    low_lane = lax.broadcasted_iota(jnp.int32, low.shape, 1) // (task_rows // TASK_COUNT)
    low = jnp.where(low_lane == task, low, 0.0).astype(BF16)
    base = residual + ADAPTER_SCALE * jnp.dot(
        low, adapter_ref[...], preferred_element_type=F32
    )
    down_scale = jnp.exp2(-2.0 * row_exponent - 2.0)
    up_scale = jnp.exp2(2.0 * row_exponent + 2.0)

    def hidden(gate_act, up_act):
        value = (gate_act / (1.0 + jnp.exp(-gate_act)) * up_act).astype(BF16).astype(F32)
        return value * down_scale

    near = hidden(acts[:, :units], acts[:, units : 2 * units])
    far = hidden(acts[:, 2 * units : 3 * units], acts[:, 3 * units :])
    pair = (jnp.where(tensor == 0, near, far), jnp.where(tensor == 0, far, near))
    for chip in range(chips):
        source = slice(chip * group, chip * group + rows)
        for k in range(2):
            hidden_ref[pl.ds((k * chips + chip) * rows, rows), :] = pair[k][source]
        scale_ref[pl.ds(chip * rows, rows), :] = up_scale[source]
        base_ref[pl.ds(chip * rows, rows), :] = base[source]


def expert_layer(gathered, weights, adapter_up, own, shard_rows):
    rows = gathered.shape[0]
    columns = gathered.shape[1] - LANES
    units = weights[0].shape[1]
    out = jax.ShapeDtypeStruct((rows // 4, units), F32)
    vmem = pl.BlockSpec(memory_space=pltpu.VMEM)
    return pl.pallas_call(
        functools.partial(expert_kernel, shard_rows),
        out_shape=(jax.ShapeDtypeStruct((rows // 2, units), F32), out, out),
        in_specs=[pl.BlockSpec(memory_space=pltpu.SMEM)] + [vmem] * 6,
        out_specs=(vmem, vmem, vmem),
        scratch_shapes=[pltpu.VMEM((2 * HALVES, columns, 4 * units), BF16)],
        compiler_params=pltpu.CompilerParams(vmem_limit_bytes=32 * 2**20),
        cost_estimate=pl.CostEstimate(
            flops=8 * rows * columns * units,
            bytes_accessed=2 * rows * columns + 8 * columns * units,
            transcendentals=2 * rows * units,
        ),
    )(own, gathered, *weights, adapter_up)


def return_kernel(
    block, set_slots, own_ref, h_ref, down_ref, scale_ref, base_ref, out_ref, note_ref
):
    seq, rows, units = h_ref.shape
    slots = (rows - NOTE_ROWS) // 2
    tensor = own_ref[0]
    expert = own_ref[1]
    group = own_ref[2]
    cores = HALVES
    at_notes = pl.ds(2 * slots, NOTE_ROWS)
    notes = h_ref[:, at_notes, :].astype(F32)
    notes = notes.reshape(seq // cores, cores, NOTE_ROWS, units).sum(axis=1)
    first, second = notes[:, 0, :].astype(jnp.int32), notes[:, 1, :].astype(jnp.int32)
    parts = notes[:, 2:8, :]
    weight = [
        parts[:, k, :] + (parts[:, k + 2, :] + parts[:, k + 4, :] / PART_STEP) / PART_STEP
        for k in range(2)
    ]
    slot = slots_of((first == expert) | (second == expert), block)
    slot = slot - (tensor * set_slots).astype(F32)
    in_set = (slot >= 0.0) & (slot < set_slots)
    place = jnp.where(in_set, slot + set_slots * block_of(slot.shape, block), -1000.0)
    weight = jnp.where(first == expert, weight[0], weight[1])
    note_ref[...] = (
        h_ref[group * cores, at_notes, :].astype(F32)
        + h_ref[group * cores + 1, at_notes, :].astype(F32)
    )

    lhs = jnp.concatenate(
        [h_ref[k, pl.ds(i * slots, slots), :] for k in range(seq) for i in range(2)], axis=1
    )
    out_ref[...] = jnp.dot(lhs, down_ref[...], preferred_element_type=F32)
    chip_rows = cores * set_slots
    pair_rows = 2 * chip_rows
    row = lax.broadcasted_iota(jnp.int32, (pair_rows, units), 0).astype(F32)
    for pair in range(seq // cores // 2):
        at = pl.ds(pair * pair_rows, pair_rows)
        one, two = slice(2 * pair, 2 * pair + 1), slice(2 * pair + 1, 2 * pair + 2)
        slot_weight = jnp.sum(
            jnp.where(place[one] == row, weight[one], 0.0)
            + jnp.where(place[two] + chip_rows == row, weight[two], 0.0),
            axis=1,
            keepdims=True,
        )
        out_ref[at, :] = slot_weight * (scale_ref[at, :] * out_ref[at, :]) + 0.5 * base_ref[at, :]


def return_layer(hidden, down_weight, scale, base, own, block, set_slots):
    seq, rows, units = hidden.shape
    slots = (rows - NOTE_ROWS) // 2
    vmem = pl.BlockSpec(memory_space=pltpu.VMEM)
    return pl.pallas_call(
        functools.partial(return_kernel, block, set_slots),
        out_shape=(
            jax.ShapeDtypeStruct((slots, units), F32),
            jax.ShapeDtypeStruct((NOTE_ROWS, units), F32),
        ),
        in_specs=[pl.BlockSpec(memory_space=pltpu.SMEM), vmem, vmem, vmem, vmem],
        out_specs=(vmem, vmem),
        compiler_params=pltpu.CompilerParams(vmem_limit_bytes=24 * 2**20),
        cost_estimate=pl.CostEstimate(
            flops=4 * seq * slots * units * units,
            bytes_accessed=4 * seq * slots * units + 2 * down_weight.size,
            transcendentals=0,
        ),
    )(own, hidden, down_weight, scale, base)


def norm_kernel(x_ref, out_ref):
    x = x_ref[:, 0, :]
    mean = jnp.sum(jnp.sum(x * x, axis=1, keepdims=True), axis=0, keepdims=True) / x.size
    x = x * lax.rsqrt(mean + 1e-06)
    for k in range(x.shape[0]):
        out_ref[:, pl.ds(k * LANES, LANES)] = x[k : k + 1, :]


def norm_layer(pooled):
    return pl.pallas_call(
        norm_kernel,
        out_shape=jax.ShapeDtypeStruct((1, pooled.size), F32),
        in_specs=[pl.BlockSpec(memory_space=pltpu.VMEM)],
        out_specs=pl.BlockSpec(memory_space=pltpu.VMEM),
    )(pooled)


def local(
    tokens,
    routes,
    chosen_expert_weight,
    expert_gate_weight,
    expert_up_weight,
    expert_down_weight,
    adapter_down_weight,
    adapter_up_weight,
    document_task_index,
    counts,
    final_norm_scale,
):
    rows, feats = tokens.shape
    seq = lax.axis_size(SEQ)
    experts = lax.axis_size(EXPERT)
    cores = lax.axis_size("c")
    groups = lax.axis_size(GROUP)
    tensors = lax.axis_size("t")
    capacity = rows * 5 // 16
    set_slots = capacity // tensors
    chip_rows = cores * set_slots
    shard_rows = HALVES * chip_rows
    width = feats * experts
    half = feats // cores
    columns = experts * half // HALVES
    slice_width = width // seq
    task_rows = adapter_down_weight.shape[0]
    s = lax.axis_index(SEQ)
    t = lax.axis_index("t")
    g = lax.axis_index(GROUP)
    per_feature_group = feats // slice_width
    own_group = s // per_feature_group

    core = lax.axis_index("c")
    ids = routes.T
    outgoing = dispatch_layer(
        jnp.stack(
            [core] + [(s - core + k) % per_feature_group * slice_width for k in range(cores)] + [t]
        ),
        ids,
        tokens,
        adapter_down_weight,
        adapter_up_weight,
        final_norm_scale[None],
        experts,
        set_slots,
    )
    far_weights, _ = lax.optimization_barrier(
        ((expert_gate_weight[0], expert_up_weight[0]), outgoing)
    )
    other = [(k, tensors - 1 - k) for k in range(tensors)]
    far_weights = [lax.ppermute(w, "t", other) for w in far_weights]
    received = swap(outgoing, EXPERT + ("c",)).reshape(experts, cores, set_slots, -1)
    shard = received[..., :half].transpose(1, 2, 0, 3).reshape(chip_rows, experts * half)
    low = jnp.sum(received[..., half + LOW_LANES : half + LANES].astype(F32), axis=0)
    low = low.reshape(chip_rows, 3, LOW_LANES).sum(axis=1)
    small = lax.dynamic_index_in_dim(received, own_group, axis=0, keepdims=False)
    small = jnp.concatenate(
        [small[..., half + LANES : half + 2 * LANES], small[..., half + 2 * LANES :]], axis=1
    )
    adapter_up = small[:, : task_rows // cores].reshape(task_rows, slice_width)
    norm_scale = jnp.sum(
        small[:1, task_rows // cores : task_rows // cores + 3].astype(F32), axis=1
    )

    shard = shard.astype(F32)
    largest = jnp.max(jnp.abs(shard), axis=1, keepdims=True)
    exponent = jnp.maximum(
        jnp.floor(jnp.log2(jnp.maximum(largest, 1e-30)) + 1.01), LEAST_EXPONENT
    )
    scaled = (shard * jnp.exp2(15.0 - exponent)).astype(F16)
    beside = jnp.concatenate(
        [jnp.broadcast_to(exponent, (chip_rows, LOW_LANES))]
        + list(three_parts(low * jnp.exp2(7.0 - exponent), PART_STEP)),
        axis=1,
    ).astype(F16)
    sent = jnp.concatenate(
        [
            jnp.concatenate([scaled[:, q * columns : (q + 1) * columns], beside], axis=1)
            for q in range(HALVES)
        ]
    )
    gathered = lax.all_gather(sent, SEQ, axis=0, tiled=False)
    gathered = gathered.astype(BF16).reshape(seq * shard_rows, columns + LANES)
    per_half = half // slice_width
    own_column = own_group * half + (s % per_half) * slice_width
    hidden, return_scale, base = expert_layer(
        gathered,
        [expert_gate_weight[0], expert_up_weight[0]] + far_weights,
        adapter_up,
        jnp.stack(
            [
                (s // per_half) % cores,
                own_column // columns,
                own_column % columns,
                document_task_index[0],
                t,
            ]
        ),
        shard_rows,
    )

    notes = jnp.concatenate(
        [ids.astype(F32)] + list(three_parts(chosen_expert_weight.T, PART_STEP))
    )
    notes = jnp.concatenate([jnp.where(core == k, notes, 0.0) for k in range(cores)], axis=1)
    notes = jnp.pad(notes, ((0, NOTE_ROWS - notes.shape[0]), (0, 0)))
    hidden = lax.all_gather(
        jnp.concatenate([hidden.astype(F16), notes.astype(F16)]), SEQ, axis=0, tiled=False
    )
    payload, group_notes = return_layer(
        hidden.astype(BF16),
        expert_down_weight[0],
        return_scale,
        base,
        jnp.stack([t, lax.axis_index(EXPERT), g]),
        rows,
        set_slots,
    )

    returned = swap(payload.reshape(groups, chip_rows, slice_width), GROUP)

    expert_ids = jnp.arange(experts, dtype=jnp.int32)[:, None]
    group_ids = group_notes[:2].astype(jnp.int32)
    slot = slots_of((group_ids[:1] == expert_ids) | (group_ids[1:] == expert_ids), rows)
    slot_set = jnp.floor(slot / set_slots)
    place = jnp.where(
        slot >= 0.0,
        slot + slot_set * (chip_rows - set_slots) + set_slots * block_of(slot.shape, rows),
        -1.0,
    )
    group_rows = cores * rows
    combiner = (
        place[:, None, :]
        == jnp.arange(tensors * chip_rows, dtype=jnp.int32).astype(F32)[None, :, None]
    ).astype(F32)
    mixed = lax.dot_general(
        combiner.reshape(groups * chip_rows, group_rows),
        returned.reshape(groups * chip_rows, slice_width),
        (((0,), (0,)), ((), ())),
        precision=HIGH,
    )
    squares = jnp.sum(spread(jnp.sum(mixed * mixed, axis=1)[None], SEQ), axis=0)
    position = g * group_rows + jnp.arange(group_rows, dtype=jnp.int32)[None, :]
    factor = jnp.where(position < counts[0], lax.rsqrt(squares / width + 1e-05), 0.0)
    pooled = jnp.dot(factor, mixed, precision=HIGH) * norm_scale
    pooled = jnp.sum(spread(pooled, GROUP), axis=0)
    return norm_layer(spread(pooled, SEQ))


def solution(mesh):
    seq, experts, tensors = mesh.devices.shape
    parts = Mesh(
        mesh.devices.reshape(seq // 2, 2, experts // 2, 2, tensors), ("z", "c", "y", "h", "t")
    )
    return jax.shard_map(
        local,
        mesh=parts,
        in_specs=(
            P(SEQ, EXPERT),
            P(SEQ, None),
            P(SEQ, None),
            P(EXPERT, None, SEQ + ("t",)),
            P(EXPERT, None, SEQ + ("t",)),
            P(EXPERT, None, SEQ),
            P(None, EXPERT),
            P(None, EXPERT),
            P(),
            P(),
            P(EXPERT),
        ),
        out_specs=P(),
        check_vma=False,
    )
```

```python
import functools

import jax
import jax.numpy as jnp
from jax import lax
from jax.experimental import pallas as pl
from jax.experimental.pallas import tpu as pltpu
from jax.sharding import Mesh
from jax.sharding import PartitionSpec as P

TASK_COUNT = 2
ADAPTER_SCALE = 0.5

SEQ = ("z", "c")
EXPERT = ("y", "h")
GROUP = ("y", "h", "t")
HALVES = 2

BF16 = jnp.bfloat16
F16 = jnp.float16
F32 = jnp.float32
HIGH = lax.Precision.HIGHEST
LANES = 128
LEAST_EXPONENT = -40.0
NOTE_ROWS = 16
PART_STEP = 256.0
LOW_LANES = 32


def swap(x, axes):
    return lax.all_to_all(x, axes, split_axis=0, concat_axis=0, tiled=True)


def spread(x, axes):
    return swap(jnp.broadcast_to(x[None], (lax.axis_size(axes),) + x.shape), axes)


def three_parts(x, step):
    first = lax.reduce_precision(x, 8, 7)
    rest = (x - first) * step
    second = lax.reduce_precision(rest, 8, 7)
    return first, second, (rest - second) * step


def earlier_in_block(lanes, block):
    i = lax.broadcasted_iota(jnp.int32, (lanes, lanes), 0)
    j = lax.broadcasted_iota(jnp.int32, (lanes, lanes), 1)
    return ((i < j) & (i // block == j // block)).astype(F32).astype(BF16)


def slots_of(named, block):
    before = jnp.dot(
        named.astype(F32).astype(BF16),
        earlier_in_block(named.shape[1], block),
        preferred_element_type=F32,
    )
    return jnp.where(named, before, -1.0)


def block_of(shape, block):
    return (lax.broadcasted_iota(jnp.int32, shape, 1) // block).astype(F32)


def dispatch_kernel(own_ref, *refs):
    out_ref, held, sem = refs[5], refs[6:11], refs[11]
    copies = [pltpu.make_async_copy(refs[k], held[k], sem.at[k]) for k in range(5)]
    for copy in copies:
        copy.start()
    for copy in copies:
        copy.wait()
    routes_ref, tokens_ref, down_ref, up_ref, norm_ref = held
    targets, set_slots, _ = out_ref.shape
    experts = targets // HALVES
    rows, feats = tokens_ref.shape
    half = feats // HALVES
    ranks = down_ref.shape[0] // HALVES
    core = own_ref[0]
    first_slot = (own_ref[3] * set_slots).astype(F32)
    ids = routes_ref[...]
    expert = lax.broadcasted_iota(jnp.int32, (experts, rows), 0)
    place = slots_of((ids[:1] == expert) | (ids[1:] == expert), rows)
    padded = 16
    row = lax.broadcasted_iota(jnp.int32, (padded, rows), 0)
    slot = jnp.where(row < set_slots, row.astype(F32) + first_slot, -2.0)
    chooser = jnp.concatenate(
        [(place[e : e + 1] == slot).astype(F32) for e in range(experts)], axis=0
    ).astype(BF16)
    for c in range(HALVES):
        lanes = pl.ds(c * half, half)
        x = tokens_ref[:, lanes]
        low = lax.dot_general(
            x, down_ref[:, lanes], (((1,), (1,)), ((), ())), preferred_element_type=F32
        )
        first = low.astype(BF16)
        rest = low - first.astype(F32)
        second = rest.astype(BF16)
        third = (rest - second.astype(F32)).astype(BF16)
        x = jnp.concatenate([x, jnp.zeros_like(first), first, second, third], axis=1)
        chosen = jnp.dot(chooser, x, preferred_element_type=F32)
        column = pl.multiple_of(own_ref[1 + c], LANES)
        norm = norm_ref[:, pl.ds(column, LANES)]
        norm_first = norm.astype(BF16).astype(F32)
        norm_rest = norm - norm_first
        norm_second = norm_rest.astype(BF16).astype(F32)
        up_rows = up_ref[pl.ds(pl.multiple_of(core * ranks, ranks), ranks), pl.ds(column, LANES)]
        up_rows = up_rows.astype(F32)
        small = [
            up_rows[:set_slots],
            jnp.concatenate(
                [
                    up_rows[set_slots:],
                    norm_first,
                    norm_second,
                    norm_rest - norm_second,
                    jnp.zeros((2 * set_slots - ranks - 3, LANES), F32),
                ],
                axis=0,
            ),
        ]
        small = jnp.concatenate(small, axis=1).astype(BF16)
        for e in range(experts):
            out_ref[e * HALVES + c, :, pl.ds(0, half + LANES)] = chosen[
                e * padded : e * padded + set_slots
            ].astype(BF16)
            out_ref[e * HALVES + c, :, pl.ds(half + LANES, 2 * LANES)] = small


def dispatch_layer(own, routes, tokens, adapter_down, adapter_up, norm_scale, experts, set_slots):
    rows, feats = tokens.shape
    lanes = feats // HALVES + 3 * LANES
    operands = (routes, tokens, adapter_down, adapter_up, norm_scale)
    return pl.pallas_call(
        dispatch_kernel,
        out_shape=jax.ShapeDtypeStruct((experts * HALVES, set_slots, lanes), BF16),
        in_specs=[pl.BlockSpec(memory_space=pltpu.SMEM)]
        + [pl.BlockSpec(memory_space=pltpu.HBM)] * len(operands),
        out_specs=pl.BlockSpec(memory_space=pltpu.VMEM),
        scratch_shapes=[pltpu.VMEM(x.shape, x.dtype) for x in operands]
        + [pltpu.SemaphoreType.DMA((len(operands),))],
        compiler_params=pltpu.CompilerParams(vmem_limit_bytes=60 * 2**20),
        cost_estimate=pl.CostEstimate(
            flops=4 * rows * feats * experts * set_slots,
            bytes_accessed=2 * rows * feats + 2 * experts * HALVES * set_slots * lanes,
            transcendentals=0,
        ),
    )(own, *operands)


def expert_kernel(
    shard_rows,
    own_ref,
    x_ref,
    gate_ref,
    up_ref,
    far_gate_ref,
    far_up_ref,
    adapter_ref,
    hidden_ref,
    scale_ref,
    base_ref,
    weight_ref,
):
    quarters, columns, _ = weight_ref.shape
    units = gate_ref.shape[1]
    task_rows = adapter_ref.shape[0]
    half = 2 * LANES
    blocks = columns // half
    for c in range(HALVES):
        for q in range(HALVES):
            for block in range(blocks):
                source = pl.ds(((q * blocks + block) * HALVES + c) * half, half)
                target = pl.ds(block * half, half)
                for k, ref in enumerate((gate_ref, up_ref, far_gate_ref, far_up_ref)):
                    weight_ref[c * HALVES + q, target, pl.ds(k * units, units)] = ref[source, :]
    rows = shard_rows // HALVES
    group = -(-rows // 8) * 8
    chips = x_ref.shape[0] // (HALVES * shard_rows)
    flat = chips * group
    own_core, own_quarter = own_ref[0], own_ref[1]
    own_column = pl.multiple_of(own_ref[2], LANES)
    task = own_ref[3]
    tensor = own_ref[4]

    def part(value, c, q):
        value = value.reshape(chips, HALVES, shard_rows, value.shape[-1])[:, c]
        value = value[:, :group] if q == 0 else value[:, shard_rows - group :]
        return value.reshape(flat, value.shape[-1])

    def aligned(value, q):
        return value if q == 0 else pltpu.roll(value, flat - (group - rows), 0)

    x = x_ref[:, pl.ds(0, columns)].astype(F32)
    own = x_ref[:, pl.ds(own_column, LANES)].astype(F32)
    beside = x_ref[:, pl.ds(columns, LANES)].astype(F32)
    acts = jnp.zeros((flat, 4 * units), F32)
    low = jnp.zeros((flat, LOW_LANES), F32)
    residual = jnp.zeros((flat, units), F32)
    row_exponent = None
    for c in range(HALVES):
        tile = part(beside, c, 0)
        exponent = tile[:, :LOW_LANES]
        low_part = tile[:, LOW_LANES : 2 * LOW_LANES] + (
            tile[:, 2 * LOW_LANES : 3 * LOW_LANES] + tile[:, 3 * LOW_LANES :] / PART_STEP
        ) / PART_STEP
        low += low_part * jnp.exp2(exponent - 7.0)
        exponent = jnp.concatenate([exponent] * (LANES // LOW_LANES), axis=1)
        scale = jnp.exp2(exponent - 15.0)
        row_exponent = exponent if c == 0 else jnp.maximum(row_exponent, exponent)
        half_acts = jnp.zeros((flat, 4 * units), F32)
        for q in range(HALVES):
            product = jnp.dot(
                part(x, c, q).astype(BF16),
                weight_ref[c * HALVES + q],
                preferred_element_type=F32,
            )
            half_acts += aligned(product, q)
            mine = (own_core == c) & (own_quarter == q)
            residual += jnp.where(mine, aligned(part(own, c, q), q) * scale, 0.0)
        acts += half_acts * jnp.concatenate([scale] * 4, axis=1)
    low_lane = lax.broadcasted_iota(jnp.int32, low.shape, 1) // (task_rows // TASK_COUNT)
    low = jnp.where(low_lane == task, low, 0.0).astype(BF16)
    base = residual + ADAPTER_SCALE * jnp.dot(
        low, adapter_ref[...], preferred_element_type=F32
    )
    down_scale = jnp.exp2(-2.0 * row_exponent - 2.0)
    up_scale = jnp.exp2(2.0 * row_exponent + 2.0)

    def hidden(gate_act, up_act):
        value = (gate_act / (1.0 + jnp.exp(-gate_act)) * up_act).astype(BF16).astype(F32)
        return value * down_scale

    near = hidden(acts[:, :units], acts[:, units : 2 * units])
    far = hidden(acts[:, 2 * units : 3 * units], acts[:, 3 * units :])
    pair = (jnp.where(tensor == 0, near, far), jnp.where(tensor == 0, far, near))
    for chip in range(chips):
        source = slice(chip * group, chip * group + rows)
        for k in range(2):
            hidden_ref[pl.ds((k * chips + chip) * rows, rows), :] = pair[k][source]
        scale_ref[pl.ds(chip * rows, rows), :] = up_scale[source]
        base_ref[pl.ds(chip * rows, rows), :] = base[source]


def expert_layer(gathered, weights, adapter_up, own, shard_rows):
    rows = gathered.shape[0]
    columns = gathered.shape[1] - LANES
    units = weights[0].shape[1]
    out = jax.ShapeDtypeStruct((rows // 4, units), F32)
    vmem = pl.BlockSpec(memory_space=pltpu.VMEM)
    return pl.pallas_call(
        functools.partial(expert_kernel, shard_rows),
        out_shape=(jax.ShapeDtypeStruct((rows // 2, units), F32), out, out),
        in_specs=[pl.BlockSpec(memory_space=pltpu.SMEM)] + [vmem] * 6,
        out_specs=(vmem, vmem, vmem),
        scratch_shapes=[pltpu.VMEM((2 * HALVES, columns, 4 * units), BF16)],
        compiler_params=pltpu.CompilerParams(vmem_limit_bytes=32 * 2**20),
        cost_estimate=pl.CostEstimate(
            flops=8 * rows * columns * units,
            bytes_accessed=2 * rows * columns + 8 * columns * units,
            transcendentals=2 * rows * units,
        ),
    )(own, gathered, *weights, adapter_up)


def return_kernel(
    block,
    set_slots,
    own_ref,
    h_ref,
    down_ref,
    scale_ref,
    base_ref,
    out_ref,
    note_ref,
):
    seq, rows, units = h_ref.shape
    slots = (rows - NOTE_ROWS) // 2
    tensor = own_ref[0]
    expert = own_ref[1]
    group = own_ref[2]
    cores = HALVES
    at_notes = pl.ds(2 * slots, NOTE_ROWS)
    notes = h_ref[:, at_notes, :].astype(F32)
    notes = notes.reshape(seq // cores, cores, NOTE_ROWS, units).sum(axis=1)
    first, second = notes[:, 0, :].astype(jnp.int32), notes[:, 1, :].astype(jnp.int32)
    parts = notes[:, 2:8, :]
    weight = [
        parts[:, k, :] + (parts[:, k + 2, :] + parts[:, k + 4, :] / PART_STEP) / PART_STEP
        for k in range(2)
    ]
    slot = slots_of((first == expert) | (second == expert), block)
    slot = slot - (tensor * set_slots).astype(F32)
    in_set = (slot >= 0.0) & (slot < set_slots)
    place = jnp.where(in_set, slot + set_slots * block_of(slot.shape, block), -1000.0)
    weight = jnp.where(first == expert, weight[0], weight[1])
    note_ref[...] = (
        h_ref[group * cores, at_notes, :].astype(F32)
        + h_ref[group * cores + 1, at_notes, :].astype(F32)
    )

    lhs = jnp.concatenate(
        [h_ref[k, pl.ds(i * slots, slots), :] for k in range(seq) for i in range(2)], axis=1
    )
    out = jnp.dot(lhs, down_ref[...], preferred_element_type=F32)
    chip_rows = cores * set_slots
    pair_rows = 2 * chip_rows
    row = lax.broadcasted_iota(jnp.int32, (pair_rows, units), 0).astype(F32)
    for pair in range(seq // cores // 2):
        at = slice(pair * pair_rows, (pair + 1) * pair_rows)
        one, two = slice(2 * pair, 2 * pair + 1), slice(2 * pair + 1, 2 * pair + 2)
        slot_weight = jnp.sum(
            jnp.where(place[one] == row, weight[one], 0.0)
            + jnp.where(place[two] + chip_rows == row, weight[two], 0.0),
            axis=1,
            keepdims=True,
        )
        value = slot_weight * (scale_ref[at, :] * out[at]) + 0.5 * base_ref[at, :]
        out_ref[2 * pair] = value[:chip_rows]
        out_ref[2 * pair + 1] = value[chip_rows:]


def return_layer(hidden, down_weight, scale, base, own, block, set_slots):
    seq, rows, units = hidden.shape
    slots = (rows - NOTE_ROWS) // 2
    vmem = pl.BlockSpec(memory_space=pltpu.VMEM)
    return pl.pallas_call(
        functools.partial(return_kernel, block, set_slots),
        out_shape=(
            jax.ShapeDtypeStruct((seq // HALVES, HALVES * set_slots, units), F32),
            jax.ShapeDtypeStruct((NOTE_ROWS, units), F32),
        ),
        in_specs=[pl.BlockSpec(memory_space=pltpu.SMEM), vmem, vmem, vmem, vmem],
        out_specs=(vmem, vmem),
        compiler_params=pltpu.CompilerParams(vmem_limit_bytes=24 * 2**20),
        cost_estimate=pl.CostEstimate(
            flops=4 * seq * slots * units * units,
            bytes_accessed=4 * seq * slots * units + 2 * down_weight.size,
            transcendentals=0,
        ),
    )(own, hidden, down_weight, scale, base)


def local(
    tokens,
    routes,
    chosen_expert_weight,
    expert_gate_weight,
    expert_up_weight,
    expert_down_weight,
    adapter_down_weight,
    adapter_up_weight,
    document_task_index,
    counts,
    final_norm_scale,
):
    rows, feats = tokens.shape
    seq = lax.axis_size(SEQ)
    experts = lax.axis_size(EXPERT)
    cores = lax.axis_size("c")
    groups = lax.axis_size(GROUP)
    tensors = lax.axis_size("t")
    capacity = rows * 5 // 16
    set_slots = capacity // tensors
    chip_rows = cores * set_slots
    shard_rows = HALVES * chip_rows
    width = feats * experts
    half = feats // cores
    columns = experts * half // HALVES
    slice_width = width // seq
    task_rows = adapter_down_weight.shape[0]
    s = lax.axis_index(SEQ)
    t = lax.axis_index("t")
    g = lax.axis_index(GROUP)
    per_feature_group = feats // slice_width
    own_group = s // per_feature_group

    core = lax.axis_index("c")
    ids = routes.T
    outgoing = dispatch_layer(
        jnp.stack(
            [core] + [(s - core + k) % per_feature_group * slice_width for k in range(cores)] + [t]
        ),
        ids,
        tokens,
        adapter_down_weight,
        adapter_up_weight,
        final_norm_scale[None],
        experts,
        set_slots,
    )
    later_up, _ = lax.optimization_barrier((expert_up_weight[0], outgoing))
    other = [(k, tensors - 1 - k) for k in range(tensors)]
    far_weights = [lax.ppermute(w, "t", other) for w in (expert_gate_weight[0], later_up)]
    received = swap(outgoing, EXPERT + ("c",)).reshape(experts, cores, set_slots, -1)
    shard = received[..., :half].transpose(1, 2, 0, 3).reshape(chip_rows, experts * half)
    low = jnp.sum(received[..., half + LOW_LANES : half + LANES].astype(F32), axis=0)
    low = low.reshape(chip_rows, 3, LOW_LANES).sum(axis=1)
    small = lax.dynamic_index_in_dim(received, own_group, axis=0, keepdims=False)
    small = jnp.concatenate(
        [small[..., half + LANES : half + 2 * LANES], small[..., half + 2 * LANES :]], axis=1
    )
    adapter_up = small[:, : task_rows // cores].reshape(task_rows, slice_width)
    norm_scale = jnp.sum(
        small[:1, task_rows // cores : task_rows // cores + 3].astype(F32), axis=1
    )

    shard = shard.astype(F32)
    largest = jnp.max(jnp.abs(shard), axis=1, keepdims=True)
    exponent = jnp.maximum(
        jnp.floor(jnp.log2(jnp.maximum(largest, 1e-30)) + 1.01), LEAST_EXPONENT
    )
    scaled = (shard * jnp.exp2(15.0 - exponent)).astype(F16)
    beside = jnp.concatenate(
        [jnp.broadcast_to(exponent, (chip_rows, LOW_LANES))]
        + list(three_parts(low * jnp.exp2(7.0 - exponent), PART_STEP)),
        axis=1,
    ).astype(F16)
    sent = jnp.concatenate(
        [
            jnp.concatenate([scaled[:, q * columns : (q + 1) * columns], beside], axis=1)
            for q in range(HALVES)
        ]
    )
    gathered = lax.all_gather(sent, SEQ, axis=0, tiled=False)
    gathered = gathered.astype(BF16).reshape(seq * shard_rows, columns + LANES)
    per_half = half // slice_width
    own_column = own_group * half + (s % per_half) * slice_width
    hidden, return_scale, base = expert_layer(
        gathered,
        [expert_gate_weight[0], expert_up_weight[0]] + far_weights,
        adapter_up,
        jnp.stack(
            [
                (s // per_half) % cores,
                own_column // columns,
                own_column % columns,
                document_task_index[0],
                t,
            ]
        ),
        shard_rows,
    )

    notes = jnp.concatenate(
        [ids.astype(F32)] + list(three_parts(chosen_expert_weight.T, PART_STEP))
    )
    notes = jnp.concatenate([jnp.where(core == k, notes, 0.0) for k in range(cores)], axis=1)
    notes = jnp.pad(notes, ((0, NOTE_ROWS - notes.shape[0]), (0, 0)))
    hidden = lax.all_gather(
        jnp.concatenate([hidden.astype(F16), notes.astype(F16)]), SEQ, axis=0, tiled=False
    )
    payload, group_notes = return_layer(
        hidden.astype(BF16),
        expert_down_weight[0],
        return_scale,
        base,
        jnp.stack([t, lax.axis_index(EXPERT), g]),
        rows,
        set_slots,
    )

    returned = swap(payload, GROUP)

    expert_ids = jnp.arange(experts, dtype=jnp.int32)[:, None]
    group_ids = group_notes[:2].astype(jnp.int32)
    slot = slots_of((group_ids[:1] == expert_ids) | (group_ids[1:] == expert_ids), rows)
    slot_set = jnp.floor(slot / set_slots)
    place = jnp.where(
        slot >= 0.0,
        slot + slot_set * (chip_rows - set_slots) + set_slots * block_of(slot.shape, rows),
        -1.0,
    )
    group_rows = cores * rows
    combiner = (
        place[:, None, :]
        == jnp.arange(tensors * chip_rows, dtype=jnp.int32).astype(F32)[None, :, None]
    ).astype(F32)
    mixed = lax.dot_general(
        combiner.reshape(groups * chip_rows, group_rows),
        returned.reshape(groups * chip_rows, slice_width),
        (((0,), (0,)), ((), ())),
        precision=HIGH,
    )
    squares = jnp.sum(spread(jnp.sum(mixed * mixed, axis=1)[None], SEQ), axis=0)
    position = g * group_rows + jnp.arange(group_rows, dtype=jnp.int32)[None, :]
    factor = jnp.where(position < counts[0], lax.rsqrt(squares / width + 1e-05), 0.0)
    pooled = jnp.dot(factor, mixed, precision=HIGH) * norm_scale
    pooled = jnp.sum(spread(pooled, GROUP), axis=0)
    own_squares = jnp.sum(pooled * pooled, axis=1, keepdims=True)
    pooled = spread(
        jnp.concatenate([pooled, jnp.broadcast_to(own_squares, pooled.shape)]), SEQ
    )
    inverse = lax.rsqrt(jnp.sum(pooled[:, 1:], axis=0, keepdims=True) / width + 1e-06)
    return (pooled[:, :1] * inverse).reshape(1, width)


def solution(mesh):
    seq, experts, tensors = mesh.devices.shape
    parts = Mesh(
        mesh.devices.reshape(seq // 2, 2, experts // 2, 2, tensors), ("z", "c", "y", "h", "t")
    )
    return jax.shard_map(
        local,
        mesh=parts,
        in_specs=(
            P(SEQ, EXPERT),
            P(SEQ, None),
            P(SEQ, None),
            P(EXPERT, None, SEQ + ("t",)),
            P(EXPERT, None, SEQ + ("t",)),
            P(EXPERT, None, SEQ),
            P(None, EXPERT),
            P(None, EXPERT),
            P(),
            P(),
            P(EXPERT),
        ),
        out_specs=P(),
        check_vma=False,
    )
```

```python
import functools

import jax
import jax.numpy as jnp
from jax import lax
from jax.experimental import pallas as pl
from jax.experimental.pallas import tpu as pltpu
from jax.sharding import Mesh
from jax.sharding import PartitionSpec as P

TASK_COUNT = 2
ADAPTER_SCALE = 0.5

SEQ = ("z", "c")
EXPERT = ("y", "h")
GROUP = ("y", "h", "t")
HALVES = 2

BF16 = jnp.bfloat16
F16 = jnp.float16
F32 = jnp.float32
HIGH = lax.Precision.HIGHEST
LANES = 128
LEAST_EXPONENT = -40.0
NOTE_ROWS = 8
PART_STEP = 256.0
LOW_LANES = 32


def swap(x, axes):
    return lax.all_to_all(x, axes, split_axis=0, concat_axis=0, tiled=True)


def spread(x, axes):
    return swap(jnp.broadcast_to(x[None], (lax.axis_size(axes),) + x.shape), axes)


def three_parts(x, step):
    first = lax.reduce_precision(x, 8, 7)
    rest = (x - first) * step
    second = lax.reduce_precision(rest, 8, 7)
    return first, second, (rest - second) * step


def earlier_in_block(lanes, block):
    i = lax.broadcasted_iota(jnp.int32, (lanes, lanes), 0)
    j = lax.broadcasted_iota(jnp.int32, (lanes, lanes), 1)
    return ((i < j) & (i // block == j // block)).astype(F32).astype(BF16)


def slots_of(named, block):
    before = jnp.dot(
        named.astype(F32).astype(BF16),
        earlier_in_block(named.shape[1], block),
        preferred_element_type=F32,
    )
    return jnp.where(named, before, -1.0)


def block_of(shape, block):
    return (lax.broadcasted_iota(jnp.int32, shape, 1) // block).astype(F32)


def dispatch_kernel(own_ref, *refs):
    out_ref, held, sem = refs[5], refs[6:11], refs[11]
    copies = [pltpu.make_async_copy(refs[k], held[k], sem.at[k]) for k in range(5)]
    for copy in copies:
        copy.start()
    for copy in copies:
        copy.wait()
    routes_ref, tokens_ref, down_ref, up_ref, norm_ref = held
    targets, set_slots, _ = out_ref.shape
    experts = targets // HALVES
    rows, feats = tokens_ref.shape
    half = feats // HALVES
    ranks = down_ref.shape[0] // HALVES
    core = own_ref[0]
    first_slot = (own_ref[3] * set_slots).astype(F32)
    ids = routes_ref[...]
    expert = lax.broadcasted_iota(jnp.int32, (experts, rows), 0)
    place = slots_of((ids[:1] == expert) | (ids[1:] == expert), rows)
    padded = 16
    row = lax.broadcasted_iota(jnp.int32, (padded, rows), 0)
    slot = jnp.where(row < set_slots, row.astype(F32) + first_slot, -2.0)
    chooser = jnp.concatenate(
        [(place[e : e + 1] == slot).astype(F32) for e in range(experts)], axis=0
    ).astype(BF16)
    for c in range(HALVES):
        lanes = pl.ds(c * half, half)
        x = tokens_ref[:, lanes]
        low = lax.dot_general(
            x, down_ref[:, lanes], (((1,), (1,)), ((), ())), preferred_element_type=F32
        )
        first = low.astype(BF16)
        rest = low - first.astype(F32)
        second = rest.astype(BF16)
        third = (rest - second.astype(F32)).astype(BF16)
        x = jnp.concatenate([x, jnp.zeros_like(first), first, second, third], axis=1)
        chosen = jnp.dot(chooser, x, preferred_element_type=F32)
        column = pl.multiple_of(own_ref[1 + c], LANES)
        norm = norm_ref[:, pl.ds(column, LANES)]
        norm_first = norm.astype(BF16).astype(F32)
        norm_rest = norm - norm_first
        norm_second = norm_rest.astype(BF16).astype(F32)
        up_rows = up_ref[pl.ds(pl.multiple_of(core * ranks, ranks), ranks), pl.ds(column, LANES)]
        up_rows = up_rows.astype(F32)
        small = [
            up_rows[:set_slots],
            jnp.concatenate(
                [
                    up_rows[set_slots:],
                    norm_first,
                    norm_second,
                    norm_rest - norm_second,
                    jnp.zeros((2 * set_slots - ranks - 3, LANES), F32),
                ],
                axis=0,
            ),
        ]
        small = jnp.concatenate(small, axis=1).astype(BF16)
        for e in range(experts):
            out_ref[e * HALVES + c, :, pl.ds(0, half + LANES)] = chosen[
                e * padded : e * padded + set_slots
            ].astype(BF16)
            out_ref[e * HALVES + c, :, pl.ds(half + LANES, 2 * LANES)] = small


def dispatch_layer(own, routes, tokens, adapter_down, adapter_up, norm_scale, experts, set_slots):
    rows, feats = tokens.shape
    lanes = feats // HALVES + 3 * LANES
    operands = (routes, tokens, adapter_down, adapter_up, norm_scale)
    return pl.pallas_call(
        dispatch_kernel,
        out_shape=jax.ShapeDtypeStruct((experts * HALVES, set_slots, lanes), BF16),
        in_specs=[pl.BlockSpec(memory_space=pltpu.SMEM)]
        + [pl.BlockSpec(memory_space=pltpu.HBM)] * len(operands),
        out_specs=pl.BlockSpec(memory_space=pltpu.VMEM),
        scratch_shapes=[pltpu.VMEM(x.shape, x.dtype) for x in operands]
        + [pltpu.SemaphoreType.DMA((len(operands),))],
        compiler_params=pltpu.CompilerParams(vmem_limit_bytes=60 * 2**20),
        cost_estimate=pl.CostEstimate(
            flops=4 * rows * feats * experts * set_slots,
            bytes_accessed=2 * rows * feats + 2 * experts * HALVES * set_slots * lanes,
            transcendentals=0,
        ),
    )(own, *operands)


def expert_kernel(
    shard_rows,
    block,
    own_ref,
    x_ref,
    gate_ref,
    up_ref,
    far_gate_ref,
    far_up_ref,
    adapter_ref,
    hidden_ref,
    factor_ref,
    base_ref,
    note_ref,
    weight_ref,
):
    quarters, columns, _ = weight_ref.shape
    units = gate_ref.shape[1]
    task_rows = adapter_ref.shape[0]
    half = 2 * LANES
    blocks = columns // half
    for c in range(HALVES):
        for q in range(HALVES):
            for n in range(blocks):
                source = pl.ds(((q * blocks + n) * HALVES + c) * half, half)
                target = pl.ds(n * half, half)
                for k, ref in enumerate((gate_ref, up_ref, far_gate_ref, far_up_ref)):
                    weight_ref[c * HALVES + q, target, pl.ds(k * units, units)] = ref[source, :]
    rows = shard_rows // HALVES
    group = -(-rows // 8) * 8
    chips = x_ref.shape[0] // (HALVES * shard_rows)
    flat = chips * group
    own_core, own_quarter = own_ref[0], own_ref[1]
    own_column = pl.multiple_of(own_ref[2], LANES)
    task = own_ref[3]
    tensor = own_ref[4]

    def part(value, c, q):
        value = value.reshape(chips, HALVES, shard_rows, value.shape[-1])[:, c]
        value = value[:, :group] if q == 0 else value[:, shard_rows - group :]
        return value.reshape(flat, value.shape[-1])

    def aligned(value, q):
        return value if q == 0 else pltpu.roll(value, flat - (group - rows), 0)

    x = x_ref[:, pl.ds(0, columns)].astype(F32)
    own = x_ref[:, pl.ds(own_column, LANES)].astype(F32)
    beside = x_ref[:, pl.ds(columns, LANES)].astype(F32)
    acts = jnp.zeros((flat, 4 * units), F32)
    low = jnp.zeros((flat, LOW_LANES), F32)
    residual = jnp.zeros((flat, units), F32)
    row_exponent = None
    for c in range(HALVES):
        tile = part(beside, c, 0)
        exponent = tile[:, :LOW_LANES]
        low_part = tile[:, LOW_LANES : 2 * LOW_LANES] + (
            tile[:, 2 * LOW_LANES : 3 * LOW_LANES] + tile[:, 3 * LOW_LANES :] / PART_STEP
        ) / PART_STEP
        low += low_part * jnp.exp2(exponent - 7.0)
        exponent = jnp.concatenate([exponent] * (LANES // LOW_LANES), axis=1)
        scale = jnp.exp2(exponent - 15.0)
        row_exponent = exponent if c == 0 else jnp.maximum(row_exponent, exponent)
        half_acts = jnp.zeros((flat, 4 * units), F32)
        for q in range(HALVES):
            product = jnp.dot(
                part(x, c, q).astype(BF16),
                weight_ref[c * HALVES + q],
                preferred_element_type=F32,
            )
            half_acts += aligned(product, q)
            mine = (own_core == c) & (own_quarter == q)
            residual += jnp.where(mine, aligned(part(own, c, q), q) * scale, 0.0)
        acts += half_acts * jnp.concatenate([scale] * 4, axis=1)
    low_lane = lax.broadcasted_iota(jnp.int32, low.shape, 1) // (task_rows // TASK_COUNT)
    low = jnp.where(low_lane == task, low, 0.0).astype(BF16)
    base = residual + ADAPTER_SCALE * jnp.dot(
        low, adapter_ref[...], preferred_element_type=F32
    )
    down_scale = jnp.exp2(-2.0 * row_exponent - 2.0)
    up_scale = jnp.exp2(2.0 * row_exponent + 2.0)

    notes = sum(aligned(part(beside, c, 1), 1) for c in range(HALVES))
    notes = notes.reshape(chips, group, LANES)[:, :NOTE_ROWS]
    note_ref[...] = notes
    first, second = notes[:, 0, :].astype(jnp.int32), notes[:, 1, :].astype(jnp.int32)
    weight = [
        notes[:, k + 2, :] + (notes[:, k + 4, :] + notes[:, k + 6, :] / PART_STEP) / PART_STEP
        for k in range(2)
    ]
    expert = own_ref[5]
    set_slots = rows // HALVES
    slot = slots_of((first == expert) | (second == expert), block)
    slot = slot - (tensor * set_slots).astype(F32)
    in_set = (slot >= 0.0) & (slot < set_slots)
    place = jnp.where(in_set, slot + set_slots * block_of(slot.shape, block), -1.0)
    weight = jnp.where(first == expert, weight[0], weight[1])
    row = lax.broadcasted_iota(jnp.int32, (group, LANES), 0).astype(F32)

    def hidden(gate_act, up_act):
        value = (gate_act / (1.0 + jnp.exp(-gate_act)) * up_act).astype(BF16).astype(F32)
        return value * down_scale

    near = hidden(acts[:, :units], acts[:, units : 2 * units])
    far = hidden(acts[:, 2 * units : 3 * units], acts[:, 3 * units :])
    pair = (jnp.where(tensor == 0, near, far), jnp.where(tensor == 0, far, near))
    for chip in range(chips):
        source = slice(chip * group, chip * group + rows)
        for k in range(2):
            hidden_ref[pl.ds((k * chips + chip) * rows, rows), :] = pair[k][source]
        slot_weight = jnp.sum(
            jnp.where(place[chip : chip + 1] == row, weight[chip : chip + 1], 0.0),
            axis=1,
            keepdims=True,
        )[:rows]
        factor_ref[pl.ds(chip * rows, rows), :] = slot_weight * up_scale[source]
        base_ref[pl.ds(chip * rows, rows), :] = 0.5 * base[source]


def expert_layer(gathered, weights, adapter_up, own, shard_rows, block):
    rows = gathered.shape[0]
    columns = gathered.shape[1] - LANES
    units = weights[0].shape[1]
    out = jax.ShapeDtypeStruct((rows // 4, units), F32)
    vmem = pl.BlockSpec(memory_space=pltpu.VMEM)
    return pl.pallas_call(
        functools.partial(expert_kernel, shard_rows, block),
        out_shape=(
            jax.ShapeDtypeStruct((rows // 2, units), F32),
            out,
            out,
            jax.ShapeDtypeStruct((rows // (2 * shard_rows), NOTE_ROWS, LANES), F32),
        ),
        in_specs=[pl.BlockSpec(memory_space=pltpu.SMEM)] + [vmem] * 6,
        out_specs=(vmem, vmem, vmem, vmem),
        scratch_shapes=[pltpu.VMEM((2 * HALVES, columns, 4 * units), BF16)],
        compiler_params=pltpu.CompilerParams(vmem_limit_bytes=32 * 2**20),
        cost_estimate=pl.CostEstimate(
            flops=8 * rows * columns * units,
            bytes_accessed=2 * rows * columns + 8 * columns * units,
            transcendentals=2 * rows * units,
        ),
    )(own, gathered, *weights, adapter_up)


def local(
    tokens,
    routes,
    chosen_expert_weight,
    expert_gate_weight,
    expert_up_weight,
    expert_down_weight,
    adapter_down_weight,
    adapter_up_weight,
    document_task_index,
    counts,
    final_norm_scale,
):
    rows, feats = tokens.shape
    seq = lax.axis_size(SEQ)
    experts = lax.axis_size(EXPERT)
    cores = lax.axis_size("c")
    groups = lax.axis_size(GROUP)
    tensors = lax.axis_size("t")
    capacity = rows * 5 // 16
    set_slots = capacity // tensors
    chip_rows = cores * set_slots
    shard_rows = HALVES * chip_rows
    width = feats * experts
    half = feats // cores
    columns = experts * half // HALVES
    slice_width = width // seq
    task_rows = adapter_down_weight.shape[0]
    s = lax.axis_index(SEQ)
    t = lax.axis_index("t")
    g = lax.axis_index(GROUP)
    per_feature_group = feats // slice_width
    own_group = s // per_feature_group

    core = lax.axis_index("c")
    ids = routes.T
    outgoing = dispatch_layer(
        jnp.stack(
            [core] + [(s - core + k) % per_feature_group * slice_width for k in range(cores)] + [t]
        ),
        ids,
        tokens,
        adapter_down_weight,
        adapter_up_weight,
        final_norm_scale[None],
        experts,
        set_slots,
    )
    later_up, _ = lax.optimization_barrier((expert_up_weight[0], outgoing))
    other = [(k, tensors - 1 - k) for k in range(tensors)]
    far_weights = [lax.ppermute(w, "t", other) for w in (expert_gate_weight[0], later_up)]
    received = swap(outgoing, EXPERT + ("c",)).reshape(experts, cores, set_slots, -1)
    shard = received[..., :half].transpose(1, 2, 0, 3).reshape(chip_rows, experts * half)
    low = jnp.sum(received[..., half + LOW_LANES : half + LANES].astype(F32), axis=0)
    low = low.reshape(chip_rows, 3, LOW_LANES).sum(axis=1)
    small = lax.dynamic_index_in_dim(received, own_group, axis=0, keepdims=False)
    small = jnp.concatenate(
        [small[..., half + LANES : half + 2 * LANES], small[..., half + 2 * LANES :]], axis=1
    )
    adapter_up = small[:, : task_rows // cores].reshape(task_rows, slice_width)
    norm_scale = jnp.sum(
        small[:1, task_rows // cores : task_rows // cores + 3].astype(F32), axis=1
    )

    shard = shard.astype(F32)
    largest = jnp.max(jnp.abs(shard), axis=1, keepdims=True)
    exponent = jnp.maximum(
        jnp.floor(jnp.log2(jnp.maximum(largest, 1e-30)) + 1.01), LEAST_EXPONENT
    )
    scaled = (shard * jnp.exp2(15.0 - exponent)).astype(F16)
    beside = jnp.concatenate(
        [jnp.broadcast_to(exponent, (chip_rows, LOW_LANES))]
        + list(three_parts(low * jnp.exp2(7.0 - exponent), PART_STEP)),
        axis=1,
    ).astype(F16)
    notes = jnp.concatenate(
        [ids.astype(F32)] + list(three_parts(chosen_expert_weight.T, PART_STEP))
    )
    notes = jnp.concatenate([jnp.where(core == k, notes, 0.0) for k in range(cores)], axis=1)
    notes = jnp.pad(notes, ((0, chip_rows - NOTE_ROWS), (0, 0))).astype(F16)
    sent = jnp.concatenate(
        [
            jnp.concatenate([scaled[:, q * columns : (q + 1) * columns], tile], axis=1)
            for q, tile in enumerate((beside, notes))
        ]
    )
    gathered = lax.all_gather(sent, SEQ, axis=0, tiled=False)
    gathered = gathered.astype(BF16).reshape(seq * shard_rows, columns + LANES)
    per_half = half // slice_width
    own_column = own_group * half + (s % per_half) * slice_width
    hidden, factor, base, notes = expert_layer(
        gathered,
        [expert_gate_weight[0], expert_up_weight[0]] + far_weights,
        adapter_up,
        jnp.stack(
            [
                (s // per_half) % cores,
                own_column // columns,
                own_column % columns,
                document_task_index[0],
                t,
                lax.axis_index(EXPERT),
            ]
        ),
        shard_rows,
        rows,
    )

    units = hidden.shape[-1]
    hidden = lax.all_gather(hidden.astype(F16), SEQ, axis=0, tiled=False)
    part = lax.dot_general(
        hidden.reshape(seq * tensors, -1, units).astype(BF16),
        expert_down_weight[0].reshape(seq * tensors, units, slice_width),
        (((0, 2), (0, 1)), ((), ())),
        preferred_element_type=F32,
    )
    payload = (part * factor + base).reshape(groups, chip_rows, slice_width)

    returned = swap(payload, GROUP)

    expert_ids = jnp.arange(experts, dtype=jnp.int32)[:, None]
    group_ids = lax.dynamic_index_in_dim(notes, g, axis=0, keepdims=False)
    group_ids = group_ids[:2].astype(jnp.int32)
    slot = slots_of((group_ids[:1] == expert_ids) | (group_ids[1:] == expert_ids), rows)
    slot_set = jnp.floor(slot / set_slots)
    place = jnp.where(
        slot >= 0.0,
        slot + slot_set * (chip_rows - set_slots) + set_slots * block_of(slot.shape, rows),
        -1.0,
    )
    group_rows = cores * rows
    combiner = (
        place[:, None, :]
        == jnp.arange(tensors * chip_rows, dtype=jnp.int32).astype(F32)[None, :, None]
    ).astype(F32)
    mixed = lax.dot_general(
        combiner.reshape(groups * chip_rows, group_rows),
        returned.reshape(groups * chip_rows, slice_width),
        (((0,), (0,)), ((), ())),
        precision=HIGH,
    )
    squares = jnp.sum(spread(jnp.sum(mixed * mixed, axis=1)[None], SEQ), axis=0)
    position = g * group_rows + jnp.arange(group_rows, dtype=jnp.int32)[None, :]
    factor = jnp.where(position < counts[0], lax.rsqrt(squares / width + 1e-05), 0.0)
    pooled = jnp.dot(factor, mixed, precision=HIGH) * norm_scale
    pooled = jnp.sum(spread(pooled, GROUP), axis=0)
    pooled = spread(pooled, SEQ).reshape(1, width)
    return pooled * lax.rsqrt(jnp.mean(pooled * pooled, axis=1, keepdims=True) + 1e-06)


def solution(mesh):
    seq, experts, tensors = mesh.devices.shape
    parts = Mesh(
        mesh.devices.reshape(seq // 2, 2, experts // 2, 2, tensors), ("z", "c", "y", "h", "t")
    )
    return jax.shard_map(
        local,
        mesh=parts,
        in_specs=(
            P(SEQ, EXPERT),
            P(SEQ, None),
            P(SEQ, None),
            P(EXPERT, None, SEQ + ("t",)),
            P(EXPERT, None, SEQ + ("t",)),
            P(EXPERT, None, SEQ),
            P(None, EXPERT),
            P(None, EXPERT),
            P(),
            P(),
            P(EXPERT),
        ),
        out_specs=P(),
        check_vma=False,
    )
```

```python
import functools

import jax
import jax.numpy as jnp
from jax import lax
from jax.experimental import pallas as pl
from jax.experimental.pallas import tpu as pltpu
from jax.sharding import Mesh
from jax.sharding import PartitionSpec as P

TASK_COUNT = 2
ADAPTER_SCALE = 0.5

SEQ = ("z", "c")
EXPERT = ("y", "h")
GROUP = ("y", "h", "t")
HALVES = 2

BF16 = jnp.bfloat16
F16 = jnp.float16
F32 = jnp.float32
HIGH = lax.Precision.HIGHEST
LANES = 128
LEAST_EXPONENT = -40.0
NOTE_ROWS = 8
PART_STEP = 256.0
LOW_LANES = 32


def swap(x, axes):
    return lax.all_to_all(x, axes, split_axis=0, concat_axis=0, tiled=True)


def spread(x, axes):
    return swap(jnp.broadcast_to(x[None], (lax.axis_size(axes),) + x.shape), axes)


def rounded_parts(x):
    first = x.astype(BF16).astype(F32)
    rest = (x - first) * PART_STEP
    second = rest.astype(BF16).astype(F32)
    return first, second, (rest - second) * PART_STEP


def earlier_in_block(lanes, block):
    i = lax.broadcasted_iota(jnp.int32, (lanes, lanes), 0)
    j = lax.broadcasted_iota(jnp.int32, (lanes, lanes), 1)
    return ((i < j) & (i // block == j // block)).astype(F32).astype(BF16)


def slots_of(named, block):
    before = jnp.dot(
        named.astype(F32).astype(BF16),
        earlier_in_block(named.shape[1], block),
        preferred_element_type=F32,
    )
    return jnp.where(named, before, -1.0)


def block_of(shape, block):
    return (lax.broadcasted_iota(jnp.int32, shape, 1) // block).astype(F32)


def dispatch_kernel(own_ref, *refs):
    out_ref, note_ref, held, sem = refs[6], refs[7], refs[8:14], refs[14]
    copies = [pltpu.make_async_copy(refs[k], held[k], sem.at[k]) for k in range(6)]
    for copy in copies:
        copy.start()
    for copy in copies:
        copy.wait()
    routes_ref, chosen_ref, tokens_ref, down_ref, up_ref, norm_ref = held
    targets, set_slots, _ = out_ref.shape
    experts = targets // HALVES
    rows, feats = tokens_ref.shape
    half = feats // HALVES
    ranks = down_ref.shape[0] // HALVES
    core = own_ref[0]
    first_slot = (own_ref[3] * set_slots).astype(F32)
    ids = routes_ref[...]
    notes = jnp.concatenate([ids.astype(F32)] + list(rounded_parts(chosen_ref[...])), axis=0)
    notes = jnp.concatenate([jnp.where(core == k, notes, 0.0) for k in range(HALVES)], axis=1)
    note_ref[...] = jnp.zeros_like(note_ref)
    note_ref[pl.ds(0, NOTE_ROWS), :] = notes
    expert = lax.broadcasted_iota(jnp.int32, (experts, rows), 0)
    place = slots_of((ids[:1] == expert) | (ids[1:] == expert), rows)
    padded = 16
    row = lax.broadcasted_iota(jnp.int32, (padded, rows), 0)
    slot = jnp.where(row < set_slots, row.astype(F32) + first_slot, -2.0)
    chooser = jnp.concatenate(
        [(place[e : e + 1] == slot).astype(F32) for e in range(experts)], axis=0
    ).astype(BF16)
    for c in range(HALVES):
        lanes = pl.ds(c * half, half)
        x = tokens_ref[:, lanes]
        low = lax.dot_general(
            x, down_ref[:, lanes], (((1,), (1,)), ((), ())), preferred_element_type=F32
        )
        first = low.astype(BF16)
        rest = low - first.astype(F32)
        second = rest.astype(BF16)
        third = (rest - second.astype(F32)).astype(BF16)
        x = jnp.concatenate([x, jnp.zeros_like(first), first, second, third], axis=1)
        chosen = jnp.dot(chooser, x, preferred_element_type=F32)
        column = pl.multiple_of(own_ref[1 + c], LANES)
        norm = norm_ref[:, pl.ds(column, LANES)]
        norm_first = norm.astype(BF16).astype(F32)
        norm_rest = norm - norm_first
        norm_second = norm_rest.astype(BF16).astype(F32)
        up_rows = up_ref[pl.ds(pl.multiple_of(core * ranks, ranks), ranks), pl.ds(column, LANES)]
        up_rows = up_rows.astype(F32)
        small = [
            up_rows[:set_slots],
            jnp.concatenate(
                [
                    up_rows[set_slots:],
                    norm_first,
                    norm_second,
                    norm_rest - norm_second,
                    jnp.zeros((2 * set_slots - ranks - 3, LANES), F32),
                ],
                axis=0,
            ),
        ]
        small = jnp.concatenate(small, axis=1).astype(BF16)
        for e in range(experts):
            out_ref[e * HALVES + c, :, pl.ds(0, half + LANES)] = chosen[
                e * padded : e * padded + set_slots
            ].astype(BF16)
            out_ref[e * HALVES + c, :, pl.ds(half + LANES, 2 * LANES)] = small


def dispatch_layer(
    own, routes, chosen, tokens, adapter_down, adapter_up, norm_scale, experts, set_slots
):
    rows, feats = tokens.shape
    lanes = feats // HALVES + 3 * LANES
    operands = (routes, chosen, tokens, adapter_down, adapter_up, norm_scale)
    return pl.pallas_call(
        dispatch_kernel,
        out_shape=(
            jax.ShapeDtypeStruct((experts * HALVES, set_slots, lanes), BF16),
            jax.ShapeDtypeStruct((HALVES * set_slots, LANES), F32),
        ),
        in_specs=[pl.BlockSpec(memory_space=pltpu.SMEM)]
        + [pl.BlockSpec(memory_space=pltpu.HBM)] * len(operands),
        out_specs=(pl.BlockSpec(memory_space=pltpu.VMEM),) * 2,
        scratch_shapes=[pltpu.VMEM(x.shape, x.dtype) for x in operands]
        + [pltpu.SemaphoreType.DMA((len(operands),))],
        compiler_params=pltpu.CompilerParams(vmem_limit_bytes=60 * 2**20),
        cost_estimate=pl.CostEstimate(
            flops=4 * rows * feats * experts * set_slots,
            bytes_accessed=2 * rows * feats + 2 * experts * HALVES * set_slots * lanes,
            transcendentals=0,
        ),
    )(own, *operands)


def rows_kernel(own_ref, received_ref, note_ref, sent_ref, adapter_ref, norm_ref):
    messages, set_slots, _ = received_ref.shape
    groups = messages // HALVES
    half = 2 * LANES
    rows = HALVES * set_slots
    columns = sent_ref.shape[1] - LANES
    ranks = adapter_ref.shape[0] // HALVES

    def both(e, first, lanes):
        return jnp.concatenate(
            [
                received_ref[e * HALVES + c, :, pl.ds(first, lanes)].astype(F32)
                for c in range(HALVES)
            ],
            axis=0,
        )

    x = jnp.concatenate([both(e, 0, half) for e in range(groups)], axis=1)
    largest = jnp.max(jnp.abs(x), axis=1, keepdims=True)
    exponent = jnp.maximum(
        jnp.floor(jnp.log2(jnp.maximum(largest, 1e-30)) + 1.01), LEAST_EXPONENT
    )
    x = x * jnp.exp2(15.0 - exponent)
    low = sum(both(e, half, LANES) for e in range(groups))
    low = sum(low[:, k * LOW_LANES : (k + 1) * LOW_LANES] for k in range(1, 4))
    low = low * jnp.exp2(7.0 - exponent)
    sent_ref[pl.ds(0, rows), pl.ds(0, columns)] = x[:, :columns]
    sent_ref[pl.ds(rows, rows), pl.ds(0, columns)] = x[:, columns:]
    sent_ref[pl.ds(0, rows), pl.ds(columns, LANES)] = jnp.concatenate(
        [jnp.broadcast_to(exponent, low.shape)] + list(rounded_parts(low)), axis=1
    )
    sent_ref[pl.ds(rows, rows), pl.ds(columns, LANES)] = note_ref[...]

    adapter = []
    for c in range(HALVES):
        small = received_ref[own_ref[0] * HALVES + c, :, pl.ds(half + LANES, 2 * LANES)]
        small = small.astype(F32)
        small = jnp.concatenate([small[:, :LANES], small[:, LANES:]], axis=0)
        adapter.append(small[:ranks])
        if c == 0:
            norm_ref[...] = (
                small[ranks : ranks + 1] + small[ranks + 1 : ranks + 2]
            ) + small[ranks + 2 : ranks + 3]
    adapter_ref[...] = jnp.concatenate(adapter, axis=0).astype(BF16)


def rows_layer(own_group, received, notes, task_rows):
    messages, set_slots, _ = received.shape
    rows = HALVES * set_slots
    vmem = pl.BlockSpec(memory_space=pltpu.VMEM)
    columns = messages // HALVES * 2 * LANES // HALVES
    return pl.pallas_call(
        rows_kernel,
        out_shape=(
            jax.ShapeDtypeStruct((HALVES * rows, columns + LANES), F32),
            jax.ShapeDtypeStruct((task_rows, LANES), BF16),
            jax.ShapeDtypeStruct((1, LANES), F32),
        ),
        in_specs=[pl.BlockSpec(memory_space=pltpu.SMEM), vmem, vmem],
        out_specs=(vmem, vmem, vmem),
        compiler_params=pltpu.CompilerParams(vmem_limit_bytes=16 * 2**20),
        cost_estimate=pl.CostEstimate(
            flops=8 * rows * columns, bytes_accessed=8 * rows * columns, transcendentals=4 * rows
        ),
    )(own_group[None], received, notes)


def expert_kernel(
    shard_rows,
    block,
    own_ref,
    x_ref,
    gate_ref,
    up_ref,
    far_gate_ref,
    far_up_ref,
    adapter_ref,
    hidden_ref,
    factor_ref,
    base_ref,
    note_ref,
    weight_ref,
):
    quarters, columns, _ = weight_ref.shape
    units = gate_ref.shape[1]
    task_rows = adapter_ref.shape[0]
    half = 2 * LANES
    blocks = columns // half
    for c in range(HALVES):
        for q in range(HALVES):
            for n in range(blocks):
                source = pl.ds(((q * blocks + n) * HALVES + c) * half, half)
                target = pl.ds(n * half, half)
                for k, ref in enumerate((gate_ref, up_ref, far_gate_ref, far_up_ref)):
                    weight_ref[c * HALVES + q, target, pl.ds(k * units, units)] = ref[source, :]
    rows = shard_rows // HALVES
    group = -(-rows // 8) * 8
    chips = x_ref.shape[0] // (HALVES * shard_rows)
    flat = chips * group
    own_core, own_quarter = own_ref[0], own_ref[1]
    own_column = pl.multiple_of(own_ref[2], LANES)
    task = own_ref[3]
    tensor = own_ref[4]

    def part(value, c, q):
        value = value.reshape(chips, HALVES, shard_rows, value.shape[-1])[:, c]
        value = value[:, :group] if q == 0 else value[:, shard_rows - group :]
        return value.reshape(flat, value.shape[-1])

    def aligned(value, q):
        return value if q == 0 else pltpu.roll(value, flat - (group - rows), 0)

    x = x_ref[:, pl.ds(0, columns)].astype(F32)
    own = x_ref[:, pl.ds(own_column, LANES)].astype(F32)
    beside = x_ref[:, pl.ds(columns, LANES)].astype(F32)
    acts = jnp.zeros((flat, 4 * units), F32)
    low = jnp.zeros((flat, LOW_LANES), F32)
    residual = jnp.zeros((flat, units), F32)
    row_exponent = None
    for c in range(HALVES):
        tile = part(beside, c, 0)
        exponent = tile[:, :LOW_LANES]
        low_part = tile[:, LOW_LANES : 2 * LOW_LANES] + (
            tile[:, 2 * LOW_LANES : 3 * LOW_LANES] + tile[:, 3 * LOW_LANES :] / PART_STEP
        ) / PART_STEP
        low += low_part * jnp.exp2(exponent - 7.0)
        exponent = jnp.concatenate([exponent] * (LANES // LOW_LANES), axis=1)
        scale = jnp.exp2(exponent - 15.0)
        row_exponent = exponent if c == 0 else jnp.maximum(row_exponent, exponent)
        half_acts = jnp.zeros((flat, 4 * units), F32)
        for q in range(HALVES):
            product = jnp.dot(
                part(x, c, q).astype(BF16),
                weight_ref[c * HALVES + q],
                preferred_element_type=F32,
            )
            half_acts += aligned(product, q)
            mine = (own_core == c) & (own_quarter == q)
            residual += jnp.where(mine, aligned(part(own, c, q), q) * scale, 0.0)
        acts += half_acts * jnp.concatenate([scale] * 4, axis=1)
    low_lane = lax.broadcasted_iota(jnp.int32, low.shape, 1) // (task_rows // TASK_COUNT)
    low = jnp.where(low_lane == task, low, 0.0).astype(BF16)
    base = residual + ADAPTER_SCALE * jnp.dot(
        low, adapter_ref[...], preferred_element_type=F32
    )
    down_scale = jnp.exp2(-2.0 * row_exponent - 2.0)
    up_scale = jnp.exp2(2.0 * row_exponent + 2.0)

    notes = sum(aligned(part(beside, c, 1), 1) for c in range(HALVES))
    notes = notes.reshape(chips, group, LANES)[:, :NOTE_ROWS]
    note_ref[...] = notes
    first, second = notes[:, 0, :].astype(jnp.int32), notes[:, 1, :].astype(jnp.int32)
    weight = [
        notes[:, k + 2, :] + (notes[:, k + 4, :] + notes[:, k + 6, :] / PART_STEP) / PART_STEP
        for k in range(2)
    ]
    expert = own_ref[5]
    set_slots = rows // HALVES
    slot = slots_of((first == expert) | (second == expert), block)
    slot = slot - (tensor * set_slots).astype(F32)
    in_set = (slot >= 0.0) & (slot < set_slots)
    place = jnp.where(in_set, slot + set_slots * block_of(slot.shape, block), -1.0)
    weight = jnp.where(first == expert, weight[0], weight[1])
    row = lax.broadcasted_iota(jnp.int32, (group, LANES), 0).astype(F32)

    def hidden(gate_act, up_act):
        value = (gate_act / (1.0 + jnp.exp(-gate_act)) * up_act).astype(BF16).astype(F32)
        return value * down_scale

    near = hidden(acts[:, :units], acts[:, units : 2 * units])
    far = hidden(acts[:, 2 * units : 3 * units], acts[:, 3 * units :])
    pair = (jnp.where(tensor == 0, near, far), jnp.where(tensor == 0, far, near))
    for chip in range(chips):
        source = slice(chip * group, chip * group + rows)
        for k in range(2):
            hidden_ref[pl.ds((k * chips + chip) * rows, rows), :] = pair[k][source]
        slot_weight = jnp.sum(
            jnp.where(place[chip : chip + 1] == row, weight[chip : chip + 1], 0.0),
            axis=1,
            keepdims=True,
        )[:rows]
        factor_ref[pl.ds(chip * rows, rows), :] = slot_weight * up_scale[source]
        base_ref[pl.ds(chip * rows, rows), :] = 0.5 * base[source]


def expert_layer(gathered, weights, adapter_up, own, shard_rows, block):
    rows = gathered.shape[0]
    columns = gathered.shape[1] - LANES
    units = weights[0].shape[1]
    out = jax.ShapeDtypeStruct((rows // 4, units), F32)
    vmem = pl.BlockSpec(memory_space=pltpu.VMEM)
    return pl.pallas_call(
        functools.partial(expert_kernel, shard_rows, block),
        out_shape=(
            jax.ShapeDtypeStruct((rows // 2, units), F32),
            out,
            out,
            jax.ShapeDtypeStruct((rows // (2 * shard_rows), NOTE_ROWS, LANES), F32),
        ),
        in_specs=[pl.BlockSpec(memory_space=pltpu.SMEM)] + [vmem] * 6,
        out_specs=(vmem, vmem, vmem, vmem),
        scratch_shapes=[pltpu.VMEM((2 * HALVES, columns, 4 * units), BF16)],
        compiler_params=pltpu.CompilerParams(vmem_limit_bytes=32 * 2**20),
        cost_estimate=pl.CostEstimate(
            flops=8 * rows * columns * units,
            bytes_accessed=2 * rows * columns + 8 * columns * units,
            transcendentals=2 * rows * units,
        ),
    )(own, gathered, *weights, adapter_up)


def local(
    tokens,
    routes,
    chosen_expert_weight,
    expert_gate_weight,
    expert_up_weight,
    expert_down_weight,
    adapter_down_weight,
    adapter_up_weight,
    document_task_index,
    counts,
    final_norm_scale,
):
    rows, feats = tokens.shape
    seq = lax.axis_size(SEQ)
    experts = lax.axis_size(EXPERT)
    cores = lax.axis_size("c")
    groups = lax.axis_size(GROUP)
    tensors = lax.axis_size("t")
    capacity = rows * 5 // 16
    set_slots = capacity // tensors
    chip_rows = cores * set_slots
    shard_rows = HALVES * chip_rows
    width = feats * experts
    half = feats // cores
    columns = experts * half // HALVES
    slice_width = width // seq
    task_rows = adapter_down_weight.shape[0]
    s = lax.axis_index(SEQ)
    t = lax.axis_index("t")
    g = lax.axis_index(GROUP)
    per_feature_group = feats // slice_width
    own_group = s // per_feature_group

    core = lax.axis_index("c")
    ids = routes.T
    outgoing, notes = dispatch_layer(
        jnp.stack(
            [core] + [(s - core + k) % per_feature_group * slice_width for k in range(cores)] + [t]
        ),
        ids,
        chosen_expert_weight.T,
        tokens,
        adapter_down_weight,
        adapter_up_weight,
        final_norm_scale[None],
        experts,
        set_slots,
    )
    later_up, _ = lax.optimization_barrier((expert_up_weight[0], outgoing))
    other = [(k, tensors - 1 - k) for k in range(tensors)]
    far_weights = [lax.ppermute(w, "t", other) for w in (expert_gate_weight[0], later_up)]
    received = swap(outgoing, EXPERT + ("c",))

    sent, adapter_up, norm_scale = rows_layer(own_group, received, notes, task_rows)
    sent = sent.astype(F16)
    gathered = lax.all_gather(sent, SEQ, axis=0, tiled=False)
    gathered = gathered.astype(BF16).reshape(seq * shard_rows, columns + LANES)
    per_half = half // slice_width
    own_column = own_group * half + (s % per_half) * slice_width
    hidden, factor, base, notes = expert_layer(
        gathered,
        [expert_gate_weight[0], expert_up_weight[0]] + far_weights,
        adapter_up,
        jnp.stack(
            [
                (s // per_half) % cores,
                own_column // columns,
                own_column % columns,
                document_task_index[0],
                t,
                lax.axis_index(EXPERT),
            ]
        ),
        shard_rows,
        rows,
    )

    units = hidden.shape[-1]
    hidden = lax.all_gather(hidden.astype(F16), SEQ, axis=0, tiled=False)
    part = lax.dot_general(
        hidden.reshape(seq * tensors, -1, units).astype(BF16),
        expert_down_weight[0].reshape(seq * tensors, units, slice_width),
        (((0, 2), (0, 1)), ((), ())),
        preferred_element_type=F32,
    )
    payload = (part * factor + base).reshape(groups, chip_rows, slice_width)

    returned = swap(payload, GROUP)

    expert_ids = jnp.arange(experts, dtype=jnp.int32)[:, None]
    group_ids = lax.dynamic_index_in_dim(notes, g, axis=0, keepdims=False)
    group_ids = group_ids[:2].astype(jnp.int32)
    slot = slots_of((group_ids[:1] == expert_ids) | (group_ids[1:] == expert_ids), rows)
    slot_set = jnp.floor(slot / set_slots)
    place = jnp.where(
        slot >= 0.0,
        slot + slot_set * (chip_rows - set_slots) + set_slots * block_of(slot.shape, rows),
        -1.0,
    )
    group_rows = cores * rows
    combiner = (
        place[:, None, :]
        == jnp.arange(tensors * chip_rows, dtype=jnp.int32).astype(F32)[None, :, None]
    ).astype(F32)
    mixed = lax.dot_general(
        combiner.reshape(groups * chip_rows, group_rows),
        returned.reshape(groups * chip_rows, slice_width),
        (((0,), (0,)), ((), ())),
        precision=HIGH,
    )
    squares = jnp.sum(spread(jnp.sum(mixed * mixed, axis=1)[None], SEQ), axis=0)
    position = g * group_rows + jnp.arange(group_rows, dtype=jnp.int32)[None, :]
    factor = jnp.where(position < counts[0], lax.rsqrt(squares / width + 1e-05), 0.0)
    pooled = jnp.dot(factor, mixed, precision=HIGH) * norm_scale
    pooled = jnp.sum(spread(pooled, GROUP), axis=0)
    pooled = spread(pooled, SEQ).reshape(1, width)
    return pooled * lax.rsqrt(jnp.mean(pooled * pooled, axis=1, keepdims=True) + 1e-06)


def solution(mesh):
    seq, experts, tensors = mesh.devices.shape
    parts = Mesh(
        mesh.devices.reshape(seq // 2, 2, experts // 2, 2, tensors), ("z", "c", "y", "h", "t")
    )
    return jax.shard_map(
        local,
        mesh=parts,
        in_specs=(
            P(SEQ, EXPERT),
            P(SEQ, None),
            P(SEQ, None),
            P(EXPERT, None, SEQ + ("t",)),
            P(EXPERT, None, SEQ + ("t",)),
            P(EXPERT, None, SEQ),
            P(None, EXPERT),
            P(None, EXPERT),
            P(),
            P(),
            P(EXPERT),
        ),
        out_specs=P(),
        check_vma=False,
    )
```

```python
import functools

import jax
import jax.numpy as jnp
from jax import lax
from jax.experimental import pallas as pl
from jax.experimental.pallas import tpu as pltpu
from jax.sharding import Mesh
from jax.sharding import PartitionSpec as P

TASK_COUNT = 2
ADAPTER_SCALE = 0.5

SEQ = ("z", "c")
EXPERT = ("y", "h")
GROUP = ("y", "h", "t")
HALVES = 2

BF16 = jnp.bfloat16
F16 = jnp.float16
F32 = jnp.float32
HIGH = lax.Precision.HIGHEST
LANES = 128
LEAST_EXPONENT = -40.0
NOTE_ROWS = 8
PART_STEP = 256.0
LOW_LANES = 32


def swap(x, axes):
    return lax.all_to_all(x, axes, split_axis=0, concat_axis=0, tiled=True)


def spread(x, axes):
    return swap(jnp.broadcast_to(x[None], (lax.axis_size(axes),) + x.shape), axes)


def rounded_parts(x):
    first = x.astype(BF16).astype(F32)
    rest = (x - first) * PART_STEP
    second = rest.astype(BF16).astype(F32)
    return first, second, (rest - second) * PART_STEP


def earlier_in_block(lanes, block):
    i = lax.broadcasted_iota(jnp.int32, (lanes, lanes), 0)
    j = lax.broadcasted_iota(jnp.int32, (lanes, lanes), 1)
    return ((i < j) & (i // block == j // block)).astype(F32).astype(BF16)


def slots_of(named, block):
    before = jnp.dot(
        named.astype(F32).astype(BF16),
        earlier_in_block(named.shape[1], block),
        preferred_element_type=F32,
    )
    return jnp.where(named, before, -1.0)


def block_of(shape, block):
    return (lax.broadcasted_iota(jnp.int32, shape, 1) // block).astype(F32)


def dispatch_kernel(*refs):
    out_ref, note_ref, held, sem = refs[6], refs[7], refs[8:14], refs[14]
    core, chip = lax.axis_index("c"), lax.axis_index("z")
    copies = [pltpu.make_async_copy(refs[k], held[k], sem.at[k]) for k in range(6)]
    for copy in copies:
        copy.start()
    for copy in copies:
        copy.wait()
    routes_ref, chosen_ref, tokens_ref, down_ref, up_ref, norm_ref = held
    targets, set_slots, _ = out_ref.shape
    experts = targets // HALVES
    rows, feats = tokens_ref.shape
    half = feats // HALVES
    ranks = down_ref.shape[0] // HALVES
    first_slot = (lax.axis_index("t") * set_slots).astype(F32)
    ids = routes_ref[...]
    notes = jnp.concatenate([ids.astype(F32)] + list(rounded_parts(chosen_ref[...])), axis=0)
    notes = jnp.concatenate([jnp.where(core == k, notes, 0.0) for k in range(HALVES)], axis=1)
    note_ref[...] = jnp.zeros_like(note_ref)
    note_ref[pl.ds(0, NOTE_ROWS), :] = notes
    expert = lax.broadcasted_iota(jnp.int32, (experts, rows), 0)
    place = slots_of((ids[:1] == expert) | (ids[1:] == expert), rows)
    padded = 16
    row = lax.broadcasted_iota(jnp.int32, (padded, rows), 0)
    slot = jnp.where(row < set_slots, row.astype(F32) + first_slot, -2.0)
    chooser = jnp.concatenate(
        [(place[e : e + 1] == slot).astype(F32) for e in range(experts)], axis=0
    ).astype(BF16)
    for c in range(HALVES):
        lanes = pl.ds(c * half, half)
        x = tokens_ref[:, lanes]
        low = lax.dot_general(
            x, down_ref[:, lanes], (((1,), (1,)), ((), ())), preferred_element_type=F32
        )
        first = low.astype(BF16)
        rest = low - first.astype(F32)
        second = rest.astype(BF16)
        third = (rest - second.astype(F32)).astype(BF16)
        x = jnp.concatenate([x, jnp.zeros_like(first), first, second, third], axis=1)
        chosen = jnp.dot(chooser, x, preferred_element_type=F32)
        column = pl.multiple_of((chip * HALVES + c) % (feats // LANES) * LANES, LANES)
        norm = norm_ref[:, pl.ds(column, LANES)]
        norm_first = norm.astype(BF16).astype(F32)
        norm_rest = norm - norm_first
        norm_second = norm_rest.astype(BF16).astype(F32)
        up_rows = up_ref[pl.ds(pl.multiple_of(core * ranks, ranks), ranks), pl.ds(column, LANES)]
        up_rows = up_rows.astype(F32)
        small = [
            up_rows[:set_slots],
            jnp.concatenate(
                [
                    up_rows[set_slots:],
                    norm_first,
                    norm_second,
                    norm_rest - norm_second,
                    jnp.zeros((2 * set_slots - ranks - 3, LANES), F32),
                ],
                axis=0,
            ),
        ]
        small = jnp.concatenate(small, axis=1).astype(BF16)
        for e in range(experts):
            out_ref[e * HALVES + c, :, pl.ds(0, half + LANES)] = chosen[
                e * padded : e * padded + set_slots
            ].astype(BF16)
            out_ref[e * HALVES + c, :, pl.ds(half + LANES, 2 * LANES)] = small


def dispatch_layer(
    routes, chosen, tokens, adapter_down, adapter_up, norm_scale, experts, set_slots
):
    rows, feats = tokens.shape
    lanes = feats // HALVES + 3 * LANES
    operands = (routes, chosen, tokens, adapter_down, adapter_up, norm_scale)
    return pl.pallas_call(
        dispatch_kernel,
        out_shape=(
            jax.ShapeDtypeStruct((experts * HALVES, set_slots, lanes), BF16),
            jax.ShapeDtypeStruct((HALVES * set_slots, LANES), F32),
        ),
        in_specs=[pl.BlockSpec(memory_space=pltpu.HBM)] * len(operands),
        out_specs=(pl.BlockSpec(memory_space=pltpu.VMEM),) * 2,
        scratch_shapes=[pltpu.VMEM(x.shape, x.dtype) for x in operands]
        + [pltpu.SemaphoreType.DMA((len(operands),))],
        compiler_params=pltpu.CompilerParams(vmem_limit_bytes=60 * 2**20),
        cost_estimate=pl.CostEstimate(
            flops=4 * rows * feats * experts * set_slots,
            bytes_accessed=2 * rows * feats + 2 * experts * HALVES * set_slots * lanes,
            transcendentals=0,
        ),
    )(*operands)


def rows_kernel(own_ref, received_ref, sent_ref, adapter_ref, norm_ref):
    messages, set_slots, _ = received_ref.shape
    groups = messages // HALVES
    half = 2 * LANES
    rows = HALVES * set_slots
    columns = sent_ref.shape[1] - LANES
    ranks = adapter_ref.shape[0] // HALVES

    def both(e, first, lanes):
        return jnp.concatenate(
            [
                received_ref[e * HALVES + c, :, pl.ds(first, lanes)].astype(F32)
                for c in range(HALVES)
            ],
            axis=0,
        )

    x = jnp.concatenate([both(e, 0, half) for e in range(groups)], axis=1)
    largest = jnp.max(jnp.abs(x), axis=1, keepdims=True)
    exponent = jnp.maximum(
        jnp.floor(jnp.log2(jnp.maximum(largest, 1e-30)) + 1.01), LEAST_EXPONENT
    )
    x = x * jnp.exp2(15.0 - exponent)
    low = sum(both(e, half, LANES) for e in range(groups))
    low = sum(low[:, k * LOW_LANES : (k + 1) * LOW_LANES] for k in range(1, 4))
    low = low * jnp.exp2(7.0 - exponent)
    sent_ref[pl.ds(0, rows), pl.ds(0, columns)] = x[:, :columns]
    sent_ref[pl.ds(rows, rows), pl.ds(0, columns)] = x[:, columns:]
    sent_ref[pl.ds(0, rows), pl.ds(columns, LANES)] = jnp.concatenate(
        [jnp.broadcast_to(exponent, low.shape)] + list(rounded_parts(low)), axis=1
    )
    sent_ref[pl.ds(rows, rows), pl.ds(columns, LANES)] = jnp.zeros((rows, LANES), F32)

    adapter = []
    for c in range(HALVES):
        small = received_ref[own_ref[0] * HALVES + c, :, pl.ds(half + LANES, 2 * LANES)]
        small = small.astype(F32)
        small = jnp.concatenate([small[:, :LANES], small[:, LANES:]], axis=0)
        adapter.append(small[:ranks])
        if c == 0:
            norm_ref[...] = (
                small[ranks : ranks + 1] + small[ranks + 1 : ranks + 2]
            ) + small[ranks + 2 : ranks + 3]
    adapter_ref[...] = jnp.concatenate(adapter, axis=0).astype(BF16)


def rows_layer(own_group, received, task_rows):
    messages, set_slots, _ = received.shape
    rows = HALVES * set_slots
    vmem = pl.BlockSpec(memory_space=pltpu.VMEM)
    columns = messages // HALVES * 2 * LANES // HALVES
    return pl.pallas_call(
        rows_kernel,
        out_shape=(
            jax.ShapeDtypeStruct((HALVES * rows, columns + LANES), F32),
            jax.ShapeDtypeStruct((task_rows, LANES), BF16),
            jax.ShapeDtypeStruct((1, LANES), F32),
        ),
        in_specs=[pl.BlockSpec(memory_space=pltpu.SMEM), vmem],
        out_specs=(vmem, vmem, vmem),
        compiler_params=pltpu.CompilerParams(vmem_limit_bytes=8 * 2**20),
        cost_estimate=pl.CostEstimate(
            flops=8 * rows * columns, bytes_accessed=8 * rows * columns, transcendentals=4 * rows
        ),
    )(own_group[None], received)


class Rows:
    def __init__(self, x_ref, shard_rows):
        self.x_ref = x_ref
        self.shard_rows = shard_rows
        self.rows = shard_rows // HALVES
        self.group = -(-self.rows // 8) * 8
        self.chips = x_ref.shape[0] // (HALVES * shard_rows)
        self.flat = self.chips * self.group
        self.columns = x_ref.shape[1] - LANES
        self.x = x_ref[:, pl.ds(0, self.columns)].astype(F32)
        self.beside = x_ref[:, pl.ds(self.columns, LANES)].astype(F32)
        exponents = [self.part(self.beside, c, 0)[:, :LOW_LANES] for c in range(HALVES)]
        exponents = [jnp.concatenate([e] * (LANES // LOW_LANES), axis=1) for e in exponents]
        self.scales = [jnp.exp2(e - 15.0) for e in exponents]
        self.row_exponent = jnp.maximum(*exponents)

    def part(self, value, c, q):
        value = value.reshape(self.chips, HALVES, self.shard_rows, value.shape[-1])[:, c]
        value = value[:, : self.group] if q == 0 else value[:, self.shard_rows - self.group :]
        return value.reshape(self.flat, value.shape[-1])

    def aligned(self, value, q):
        return value if q == 0 else pltpu.roll(value, self.flat - (self.group - self.rows), 0)

    def hidden(self, weight_ref, gate_ref, up_ref):
        units = gate_ref.shape[1]
        half = 2 * LANES
        blocks = self.columns // half
        acts = jnp.zeros((self.flat, 2 * units), F32)
        for c in range(HALVES):
            half_acts = jnp.zeros((self.flat, 2 * units), F32)
            for q in range(HALVES):
                for n in range(blocks):
                    source = pl.ds(((q * blocks + n) * HALVES + c) * half, half)
                    target = pl.ds(n * half, half)
                    for k, ref in enumerate((gate_ref, up_ref)):
                        weight_ref[c * HALVES + q, target, pl.ds(k * units, units)] = ref[source, :]
                product = jnp.dot(
                    self.part(self.x, c, q).astype(BF16),
                    weight_ref[c * HALVES + q],
                    preferred_element_type=F32,
                )
                half_acts += self.aligned(product, q)
            acts += half_acts * jnp.concatenate([self.scales[c]] * 2, axis=1)
        gate_act, up_act = acts[:, :units], acts[:, units:]
        value = (gate_act / (1.0 + jnp.exp(-gate_act)) * up_act).astype(BF16).astype(F32)
        return value * jnp.exp2(-2.0 * self.row_exponent - 2.0)

    def of_chip(self, chip):
        source = slice(chip * self.group, chip * self.group + self.rows)
        return source, pl.ds(chip * self.rows, self.rows)


def near_kernel(
    shard_rows,
    block,
    own_ref,
    x_ref,
    gate_ref,
    up_ref,
    adapter_ref,
    hidden_ref,
    factor_ref,
    base_ref,
    note_ref,
    weight_ref,
):
    r = Rows(x_ref, shard_rows)
    task_rows = adapter_ref.shape[0]
    own_core, own_quarter = own_ref[0], own_ref[1]
    own_column = pl.multiple_of(own_ref[2], LANES)
    task, tensor, expert = own_ref[3], own_ref[4], own_ref[5]
    hidden = r.hidden(weight_ref, gate_ref, up_ref)

    own = x_ref[:, pl.ds(own_column, LANES)].astype(F32)
    low = jnp.zeros((r.flat, LOW_LANES), F32)
    residual = jnp.zeros((r.flat, LANES), F32)
    for c in range(HALVES):
        tile = r.part(r.beside, c, 0)
        low_part = tile[:, LOW_LANES : 2 * LOW_LANES] + (
            tile[:, 2 * LOW_LANES : 3 * LOW_LANES] + tile[:, 3 * LOW_LANES :] / PART_STEP
        ) / PART_STEP
        low += low_part * jnp.exp2(tile[:, :LOW_LANES] - 7.0)
        for q in range(HALVES):
            mine = (own_core == c) & (own_quarter == q)
            residual += jnp.where(mine, r.aligned(r.part(own, c, q), q) * r.scales[c], 0.0)
    low_lane = lax.broadcasted_iota(jnp.int32, low.shape, 1) // (task_rows // TASK_COUNT)
    low = jnp.where(low_lane == task, low, 0.0).astype(BF16)
    base = residual + ADAPTER_SCALE * jnp.dot(
        low, adapter_ref[...], preferred_element_type=F32
    )
    up_scale = jnp.exp2(2.0 * r.row_exponent + 2.0)

    notes = sum(r.aligned(r.part(r.beside, c, 1), 1) for c in range(HALVES))
    notes = notes.reshape(r.chips, r.group, LANES)[:, :NOTE_ROWS]
    note_ref[...] = notes
    first, second = notes[:, 0, :].astype(jnp.int32), notes[:, 1, :].astype(jnp.int32)
    weight = [
        notes[:, k + 2, :] + (notes[:, k + 4, :] + notes[:, k + 6, :] / PART_STEP) / PART_STEP
        for k in range(2)
    ]
    set_slots = r.rows // HALVES
    slot = slots_of((first == expert) | (second == expert), block)
    slot = slot - (tensor * set_slots).astype(F32)
    in_set = (slot >= 0.0) & (slot < set_slots)
    place = jnp.where(in_set, slot + set_slots * block_of(slot.shape, block), -1.0)
    weight = jnp.where(first == expert, weight[0], weight[1])
    row = lax.broadcasted_iota(jnp.int32, (r.group, LANES), 0).astype(F32)
    for chip in range(r.chips):
        source, target = r.of_chip(chip)
        slot_weight = jnp.sum(
            jnp.where(place[chip : chip + 1] == row, weight[chip : chip + 1], 0.0),
            axis=1,
            keepdims=True,
        )[: r.rows]
        hidden_ref[target, :] = hidden[source]
        factor_ref[target, :] = slot_weight * up_scale[source]
        base_ref[target, :] = 0.5 * base[source]


def far_kernel(
    shard_rows, own_ref, x_ref, gate_ref, up_ref, near_ref, hidden_ref, weight_ref
):
    r = Rows(x_ref, shard_rows)
    far = r.hidden(weight_ref, gate_ref, up_ref)
    slots = r.chips * r.rows
    near_at = own_ref[0] * slots
    far_at = slots - near_at
    hidden_ref[pl.ds(pl.multiple_of(near_at, 8), slots), :] = near_ref[...]
    for chip in range(0, r.chips, 2):
        one, two = r.of_chip(chip)[0], r.of_chip(chip + 1)[0]
        start = pl.multiple_of(far_at + chip * r.rows, 8)
        hidden_ref[pl.ds(start, 2 * r.rows), :] = jnp.concatenate([far[one], far[two]], axis=0)


def near_layer(gathered, weights, adapter_up, own, shard_rows, block):
    rows = gathered.shape[0]
    columns = gathered.shape[1] - LANES
    units = weights[0].shape[1]
    out = jax.ShapeDtypeStruct((rows // 4, units), F32)
    vmem = pl.BlockSpec(memory_space=pltpu.VMEM)
    return pl.pallas_call(
        functools.partial(near_kernel, shard_rows, block),
        out_shape=(
            out,
            out,
            out,
            jax.ShapeDtypeStruct((rows // (2 * shard_rows), NOTE_ROWS, LANES), F32),
        ),
        in_specs=[pl.BlockSpec(memory_space=pltpu.SMEM)] + [vmem] * 4,
        out_specs=(vmem, vmem, vmem, vmem),
        scratch_shapes=[pltpu.VMEM((2 * HALVES, columns, 2 * units), BF16)],
        compiler_params=pltpu.CompilerParams(vmem_limit_bytes=24 * 2**20),
        cost_estimate=pl.CostEstimate(
            flops=4 * rows * columns * units,
            bytes_accessed=2 * rows * columns + 4 * columns * units,
            transcendentals=2 * rows * units,
        ),
    )(own, gathered, *weights, adapter_up)


def far_layer(gathered, weights, near, tensor, shard_rows):
    rows = gathered.shape[0]
    columns = gathered.shape[1] - LANES
    units = weights[0].shape[1]
    vmem = pl.BlockSpec(memory_space=pltpu.VMEM)
    return pl.pallas_call(
        functools.partial(far_kernel, shard_rows),
        out_shape=jax.ShapeDtypeStruct((rows // 2, units), F32),
        in_specs=[pl.BlockSpec(memory_space=pltpu.SMEM)] + [vmem] * 4,
        out_specs=vmem,
        scratch_shapes=[pltpu.VMEM((2 * HALVES, columns, 2 * units), BF16)],
        compiler_params=pltpu.CompilerParams(vmem_limit_bytes=24 * 2**20),
        cost_estimate=pl.CostEstimate(
            flops=4 * rows * columns * units,
            bytes_accessed=2 * rows * columns + 4 * columns * units,
            transcendentals=2 * rows * units,
        ),
    )(tensor[None], gathered, *weights, near)


def local(
    tokens,
    routes,
    chosen_expert_weight,
    expert_gate_weight,
    expert_up_weight,
    expert_down_weight,
    adapter_down_weight,
    adapter_up_weight,
    document_task_index,
    counts,
    final_norm_scale,
):
    rows, feats = tokens.shape
    seq = lax.axis_size(SEQ)
    experts = lax.axis_size(EXPERT)
    cores = lax.axis_size("c")
    groups = lax.axis_size(GROUP)
    tensors = lax.axis_size("t")
    capacity = rows * 5 // 16
    set_slots = capacity // tensors
    chip_rows = cores * set_slots
    shard_rows = HALVES * chip_rows
    width = feats * experts
    half = feats // cores
    columns = experts * half // HALVES
    slice_width = width // seq
    task_rows = adapter_down_weight.shape[0]
    s = lax.axis_index(SEQ)
    t = lax.axis_index("t")
    g = lax.axis_index(GROUP)
    per_feature_group = feats // slice_width
    own_group = s // per_feature_group

    ids = routes.T
    outgoing, notes = dispatch_layer(
        ids,
        chosen_expert_weight.T,
        tokens,
        adapter_down_weight,
        adapter_up_weight,
        final_norm_scale[None],
        experts,
        set_slots,
    )
    later_up, _ = lax.optimization_barrier((expert_up_weight[0], outgoing))
    other = [(k, tensors - 1 - k) for k in range(tensors)]
    far_weights = [lax.ppermute(w, "t", other) for w in (expert_gate_weight[0], later_up)]
    received = swap(outgoing, EXPERT + ("c",))

    sent, adapter_up, norm_scale = rows_layer(own_group, received, task_rows)
    sent = (sent + jnp.pad(notes, ((chip_rows, 0), (columns, 0)))).astype(F16)
    gathered = lax.all_gather(sent, SEQ, axis=0, tiled=False)
    gathered = gathered.astype(BF16).reshape(seq * shard_rows, columns + LANES)
    per_half = half // slice_width
    own_column = own_group * half + (s % per_half) * slice_width
    near, factor, base, notes = near_layer(
        gathered,
        (expert_gate_weight[0], expert_up_weight[0]),
        adapter_up,
        jnp.stack(
            [
                (s // per_half) % cores,
                own_column // columns,
                own_column % columns,
                document_task_index[0],
                t,
                lax.axis_index(EXPERT),
            ]
        ),
        shard_rows,
        rows,
    )
    hidden = far_layer(gathered, far_weights, near, t, shard_rows)

    units = hidden.shape[-1]
    hidden = lax.all_gather(hidden.astype(F16), SEQ, axis=0, tiled=False)
    part = lax.dot_general(
        hidden.reshape(seq * tensors, -1, units).astype(BF16),
        expert_down_weight[0].reshape(seq * tensors, units, slice_width),
        (((0, 2), (0, 1)), ((), ())),
        preferred_element_type=F32,
    )
    payload = (part * factor + base).reshape(groups, chip_rows, slice_width)

    returned = swap(payload, GROUP)

    expert_ids = jnp.arange(experts, dtype=jnp.int32)[:, None]
    group_ids = lax.dynamic_index_in_dim(notes, g, axis=0, keepdims=False)
    group_ids = group_ids[:2].astype(jnp.int32)
    slot = slots_of((group_ids[:1] == expert_ids) | (group_ids[1:] == expert_ids), rows)
    slot_set = jnp.floor(slot / set_slots)
    place = jnp.where(
        slot >= 0.0,
        slot + slot_set * (chip_rows - set_slots) + set_slots * block_of(slot.shape, rows),
        -1.0,
    )
    group_rows = cores * rows
    combiner = (
        place[:, None, :]
        == jnp.arange(tensors * chip_rows, dtype=jnp.int32).astype(F32)[None, :, None]
    ).astype(F32)
    mixed = lax.dot_general(
        combiner.reshape(groups * chip_rows, group_rows),
        returned.reshape(groups * chip_rows, slice_width),
        (((0,), (0,)), ((), ())),
        precision=HIGH,
    )
    squares = jnp.sum(spread(jnp.sum(mixed * mixed, axis=1)[None], SEQ), axis=0)
    position = g * group_rows + jnp.arange(group_rows, dtype=jnp.int32)[None, :]
    factor = jnp.where(position < counts[0], lax.rsqrt(squares / width + 1e-05), 0.0)
    pooled = jnp.dot(factor, mixed, precision=HIGH) * norm_scale
    pooled = jnp.sum(spread(pooled, GROUP), axis=0)
    pooled = spread(pooled, SEQ).reshape(1, width)
    return pooled * lax.rsqrt(jnp.mean(pooled * pooled, axis=1, keepdims=True) + 1e-06)


def solution(mesh):
    seq, experts, tensors = mesh.devices.shape
    parts = Mesh(
        mesh.devices.reshape(seq // 2, 2, experts // 2, 2, tensors), ("z", "c", "y", "h", "t")
    )
    return jax.shard_map(
        local,
        mesh=parts,
        in_specs=(
            P(SEQ, EXPERT),
            P(SEQ, None),
            P(SEQ, None),
            P(EXPERT, None, SEQ + ("t",)),
            P(EXPERT, None, SEQ + ("t",)),
            P(EXPERT, None, SEQ),
            P(None, EXPERT),
            P(None, EXPERT),
            P(),
            P(),
            P(EXPERT),
        ),
        out_specs=P(),
        check_vma=False,
    )
```

```python
import functools

import jax
import jax.numpy as jnp
from jax import lax
from jax.experimental import pallas as pl
from jax.experimental.pallas import tpu as pltpu
from jax.sharding import Mesh
from jax.sharding import PartitionSpec as P

TASK_COUNT = 2
ADAPTER_SCALE = 0.5

SEQ = ("z", "c")
EXPERT = ("y", "h")
GROUP = ("y", "h", "t")
HALVES = 2

BF16 = jnp.bfloat16
F16 = jnp.float16
F32 = jnp.float32
HIGH = lax.Precision.HIGHEST
LANES = 128
LEAST_EXPONENT = -40.0
NOTE_ROWS = 8
PART_STEP = 256.0
LOW_LANES = 32


def swap(x, axes):
    return lax.all_to_all(x, axes, split_axis=0, concat_axis=0, tiled=True)


def spread(x, axes):
    return swap(jnp.broadcast_to(x[None], (lax.axis_size(axes),) + x.shape), axes)


def rounded_parts(x):
    first = x.astype(BF16).astype(F32)
    rest = (x - first) * PART_STEP
    second = rest.astype(BF16).astype(F32)
    return first, second, (rest - second) * PART_STEP


def earlier_in_block(lanes, block):
    i = lax.broadcasted_iota(jnp.int32, (lanes, lanes), 0)
    j = lax.broadcasted_iota(jnp.int32, (lanes, lanes), 1)
    return ((i < j) & (i // block == j // block)).astype(F32).astype(BF16)


def slots_of(named, block):
    before = jnp.dot(
        named.astype(F32).astype(BF16),
        earlier_in_block(named.shape[1], block),
        preferred_element_type=F32,
    )
    return jnp.where(named, before, -1.0)


def block_of(shape, block):
    return (lax.broadcasted_iota(jnp.int32, shape, 1) // block).astype(F32)


def dispatch_kernel(*refs):
    out_ref, note_ref, held, sem = refs[6], refs[7], refs[8:14], refs[14]
    core, chip = lax.axis_index("c"), lax.axis_index("z")
    copies = [pltpu.make_async_copy(refs[k], held[k], sem.at[k]) for k in range(6)]
    for copy in copies:
        copy.start()
    for copy in copies:
        copy.wait()
    routes_ref, chosen_ref, tokens_ref, down_ref, up_ref, norm_ref = held
    targets, set_slots, _ = out_ref.shape
    experts = targets // HALVES
    rows, feats = tokens_ref.shape
    half = feats // HALVES
    ranks = down_ref.shape[0] // HALVES
    first_slot = (lax.axis_index("t") * set_slots).astype(F32)
    ids = routes_ref[...]
    notes = jnp.concatenate([ids.astype(F32)] + list(rounded_parts(chosen_ref[...])), axis=0)
    notes = jnp.concatenate([jnp.where(core == k, notes, 0.0) for k in range(HALVES)], axis=1)
    note_ref[...] = jnp.zeros_like(note_ref)
    note_ref[pl.ds(0, NOTE_ROWS), :] = notes
    expert = lax.broadcasted_iota(jnp.int32, (experts, rows), 0)
    place = slots_of((ids[:1] == expert) | (ids[1:] == expert), rows)
    padded = 16
    row = lax.broadcasted_iota(jnp.int32, (padded, rows), 0)
    slot = jnp.where(row < set_slots, row.astype(F32) + first_slot, -2.0)
    chooser = jnp.concatenate(
        [(place[e : e + 1] == slot).astype(F32) for e in range(experts)], axis=0
    ).astype(BF16)
    for c in range(HALVES):
        lanes = pl.ds(c * half, half)
        x = tokens_ref[:, lanes]
        low = lax.dot_general(
            x, down_ref[:, lanes], (((1,), (1,)), ((), ())), preferred_element_type=F32
        )
        first = low.astype(BF16)
        rest = low - first.astype(F32)
        second = rest.astype(BF16)
        third = (rest - second.astype(F32)).astype(BF16)
        x = jnp.concatenate([x, jnp.zeros_like(first), first, second, third], axis=1)
        chosen = jnp.dot(chooser, x, preferred_element_type=F32)
        column = pl.multiple_of((chip * HALVES + c) % (feats // LANES) * LANES, LANES)
        norm = norm_ref[:, pl.ds(column, LANES)]
        norm_first = norm.astype(BF16).astype(F32)
        norm_rest = norm - norm_first
        norm_second = norm_rest.astype(BF16).astype(F32)
        up_rows = up_ref[pl.ds(pl.multiple_of(core * ranks, ranks), ranks), pl.ds(column, LANES)]
        up_rows = up_rows.astype(F32)
        small = [
            up_rows[:set_slots],
            jnp.concatenate(
                [
                    up_rows[set_slots:],
                    norm_first,
                    norm_second,
                    norm_rest - norm_second,
                    jnp.zeros((2 * set_slots - ranks - 3, LANES), F32),
                ],
                axis=0,
            ),
        ]
        small = jnp.concatenate(small, axis=1).astype(BF16)
        for e in range(experts):
            out_ref[e * HALVES + c, :, pl.ds(0, half + LANES)] = chosen[
                e * padded : e * padded + set_slots
            ].astype(BF16)
            out_ref[e * HALVES + c, :, pl.ds(half + LANES, 2 * LANES)] = small


def dispatch_layer(
    routes, chosen, tokens, adapter_down, adapter_up, norm_scale, experts, set_slots
):
    rows, feats = tokens.shape
    lanes = feats // HALVES + 3 * LANES
    operands = (routes, chosen, tokens, adapter_down, adapter_up, norm_scale)
    return pl.pallas_call(
        dispatch_kernel,
        out_shape=(
            jax.ShapeDtypeStruct((experts * HALVES, set_slots, lanes), BF16),
            jax.ShapeDtypeStruct((HALVES * set_slots, LANES), F32),
        ),
        in_specs=[pl.BlockSpec(memory_space=pltpu.HBM)] * len(operands),
        out_specs=(pl.BlockSpec(memory_space=pltpu.VMEM),) * 2,
        scratch_shapes=[pltpu.VMEM(x.shape, x.dtype) for x in operands]
        + [pltpu.SemaphoreType.DMA((len(operands),))],
        compiler_params=pltpu.CompilerParams(vmem_limit_bytes=60 * 2**20),
        cost_estimate=pl.CostEstimate(
            flops=4 * rows * feats * experts * set_slots,
            bytes_accessed=2 * rows * feats + 2 * experts * HALVES * set_slots * lanes,
            transcendentals=0,
        ),
    )(*operands)


def rows_kernel(own_ref, received_ref, sent_ref, adapter_ref, norm_ref):
    messages, set_slots, _ = received_ref.shape
    groups = messages // HALVES
    half = 2 * LANES
    rows = HALVES * set_slots
    columns = sent_ref.shape[1] - LANES
    ranks = adapter_ref.shape[0] // HALVES

    def both(e, first, lanes):
        return jnp.concatenate(
            [
                received_ref[e * HALVES + c, :, pl.ds(first, lanes)].astype(F32)
                for c in range(HALVES)
            ],
            axis=0,
        )

    x = jnp.concatenate([both(e, 0, half) for e in range(groups)], axis=1)
    largest = jnp.max(jnp.abs(x), axis=1, keepdims=True)
    exponent = jnp.maximum(
        jnp.floor(jnp.log2(jnp.maximum(largest, 1e-30)) + 1.01), LEAST_EXPONENT
    )
    x = x * jnp.exp2(15.0 - exponent)
    low = sum(both(e, half, LANES) for e in range(groups))
    low = sum(low[:, k * LOW_LANES : (k + 1) * LOW_LANES] for k in range(1, 4))
    low = low * jnp.exp2(7.0 - exponent)
    sent_ref[pl.ds(0, rows), pl.ds(0, columns)] = x[:, :columns]
    sent_ref[pl.ds(rows, rows), pl.ds(0, columns)] = x[:, columns:]
    sent_ref[pl.ds(0, rows), pl.ds(columns, LANES)] = jnp.concatenate(
        [jnp.broadcast_to(exponent, low.shape)] + list(rounded_parts(low)), axis=1
    )
    sent_ref[pl.ds(rows, rows), pl.ds(columns, LANES)] = jnp.zeros((rows, LANES), F32)

    adapter = []
    for c in range(HALVES):
        small = received_ref[own_ref[0] * HALVES + c, :, pl.ds(half + LANES, 2 * LANES)]
        small = small.astype(F32)
        small = jnp.concatenate([small[:, :LANES], small[:, LANES:]], axis=0)
        adapter.append(small[:ranks])
        if c == 0:
            norm_ref[...] = (
                small[ranks : ranks + 1] + small[ranks + 1 : ranks + 2]
            ) + small[ranks + 2 : ranks + 3]
    adapter_ref[...] = jnp.concatenate(adapter, axis=0).astype(BF16)


def rows_layer(own_group, received, task_rows):
    messages, set_slots, _ = received.shape
    rows = HALVES * set_slots
    vmem = pl.BlockSpec(memory_space=pltpu.VMEM)
    columns = messages // HALVES * 2 * LANES // HALVES
    return pl.pallas_call(
        rows_kernel,
        out_shape=(
            jax.ShapeDtypeStruct((HALVES * rows, columns + LANES), F32),
            jax.ShapeDtypeStruct((task_rows, LANES), BF16),
            jax.ShapeDtypeStruct((1, LANES), F32),
        ),
        in_specs=[pl.BlockSpec(memory_space=pltpu.SMEM), vmem],
        out_specs=(vmem, vmem, vmem),
        compiler_params=pltpu.CompilerParams(vmem_limit_bytes=8 * 2**20),
        cost_estimate=pl.CostEstimate(
            flops=8 * rows * columns, bytes_accessed=8 * rows * columns, transcendentals=4 * rows
        ),
    )(own_group[None], received)


class Rows:
    def __init__(self, x_ref, shard_rows):
        self.x_ref = x_ref
        self.shard_rows = shard_rows
        self.rows = shard_rows // HALVES
        self.group = -(-self.rows // 8) * 8
        self.chips = x_ref.shape[0] // (HALVES * shard_rows)
        self.flat = self.chips * self.group
        self.columns = x_ref.shape[1] - LANES
        self.x = x_ref[:, pl.ds(0, self.columns)].astype(F32)
        self.beside = x_ref[:, pl.ds(self.columns, LANES)].astype(F32)
        exponents = [self.part(self.beside, c, 0)[:, :LOW_LANES] for c in range(HALVES)]
        exponents = [jnp.concatenate([e] * (LANES // LOW_LANES), axis=1) for e in exponents]
        self.scales = [jnp.exp2(e - 15.0) for e in exponents]
        self.row_exponent = jnp.maximum(*exponents)

    def part(self, value, c, q):
        value = value.reshape(self.chips, HALVES, self.shard_rows, value.shape[-1])[:, c]
        value = value[:, : self.group] if q == 0 else value[:, self.shard_rows - self.group :]
        return value.reshape(self.flat, value.shape[-1])

    def aligned(self, value, q):
        return value if q == 0 else pltpu.roll(value, self.flat - (self.group - self.rows), 0)

    def hidden(self, weight_ref, gate_ref, up_ref):
        units = gate_ref.shape[1]
        half = 2 * LANES
        blocks = self.columns // half
        acts = jnp.zeros((self.flat, 2 * units), F32)
        for c in range(HALVES):
            half_acts = jnp.zeros((self.flat, 2 * units), F32)
            for q in range(HALVES):
                for n in range(blocks):
                    source = pl.ds(((q * blocks + n) * HALVES + c) * half, half)
                    target = pl.ds(n * half, half)
                    for k, ref in enumerate((gate_ref, up_ref)):
                        weight_ref[c * HALVES + q, target, pl.ds(k * units, units)] = ref[source, :]
                product = jnp.dot(
                    self.part(self.x, c, q).astype(BF16),
                    weight_ref[c * HALVES + q],
                    preferred_element_type=F32,
                )
                half_acts += self.aligned(product, q)
            acts += half_acts * jnp.concatenate([self.scales[c]] * 2, axis=1)
        gate_act, up_act = acts[:, :units], acts[:, units:]
        value = (gate_act / (1.0 + jnp.exp(-gate_act)) * up_act).astype(BF16).astype(F32)
        return value * jnp.exp2(-2.0 * self.row_exponent - 2.0)

    def of_chip(self, chip):
        source = slice(chip * self.group, chip * self.group + self.rows)
        return source, pl.ds(chip * self.rows, self.rows)


def near_kernel(
    shard_rows,
    block,
    own_ref,
    x_ref,
    gate_ref,
    up_ref,
    adapter_ref,
    hidden_ref,
    factor_ref,
    base_ref,
    note_ref,
    weight_ref,
):
    r = Rows(x_ref, shard_rows)
    task_rows = adapter_ref.shape[0]
    own_core, own_quarter = own_ref[0], own_ref[1]
    own_column = pl.multiple_of(own_ref[2], LANES)
    task, tensor, expert = own_ref[3], own_ref[4], own_ref[5]
    hidden = r.hidden(weight_ref, gate_ref, up_ref)

    own = x_ref[:, pl.ds(own_column, LANES)].astype(F32)
    low = jnp.zeros((r.flat, LOW_LANES), F32)
    residual = jnp.zeros((r.flat, LANES), F32)
    for c in range(HALVES):
        tile = r.part(r.beside, c, 0)
        low_part = tile[:, LOW_LANES : 2 * LOW_LANES] + (
            tile[:, 2 * LOW_LANES : 3 * LOW_LANES] + tile[:, 3 * LOW_LANES :] / PART_STEP
        ) / PART_STEP
        low += low_part * jnp.exp2(tile[:, :LOW_LANES] - 7.0)
        for q in range(HALVES):
            mine = (own_core == c) & (own_quarter == q)
            residual += jnp.where(mine, r.aligned(r.part(own, c, q), q) * r.scales[c], 0.0)
    low_lane = lax.broadcasted_iota(jnp.int32, low.shape, 1) // (task_rows // TASK_COUNT)
    low = jnp.where(low_lane == task, low, 0.0).astype(BF16)
    base = residual + ADAPTER_SCALE * jnp.dot(
        low, adapter_ref[...], preferred_element_type=F32
    )
    up_scale = jnp.exp2(2.0 * r.row_exponent + 2.0)

    notes = sum(r.aligned(r.part(r.beside, c, 1), 1) for c in range(HALVES))
    notes = notes.reshape(r.chips, r.group, LANES)[:, :NOTE_ROWS]
    note_ref[...] = notes
    first, second = notes[:, 0, :].astype(jnp.int32), notes[:, 1, :].astype(jnp.int32)
    weight = [
        notes[:, k + 2, :] + (notes[:, k + 4, :] + notes[:, k + 6, :] / PART_STEP) / PART_STEP
        for k in range(2)
    ]
    set_slots = r.rows // HALVES
    slot = slots_of((first == expert) | (second == expert), block)
    slot = slot - (tensor * set_slots).astype(F32)
    in_set = (slot >= 0.0) & (slot < set_slots)
    place = jnp.where(in_set, slot + set_slots * block_of(slot.shape, block), -1.0)
    weight = jnp.where(first == expert, weight[0], weight[1])
    row = lax.broadcasted_iota(jnp.int32, (r.group, LANES), 0).astype(F32)
    for chip in range(r.chips):
        source, target = r.of_chip(chip)
        slot_weight = jnp.sum(
            jnp.where(place[chip : chip + 1] == row, weight[chip : chip + 1], 0.0),
            axis=1,
            keepdims=True,
        )[: r.rows]
        hidden_ref[target, :] = hidden[source]
        factor_ref[target, :] = slot_weight * up_scale[source]
        base_ref[target, :] = 0.5 * base[source]


def far_kernel(
    shard_rows, own_ref, x_ref, gate_ref, up_ref, near_ref, hidden_ref, weight_ref
):
    r = Rows(x_ref, shard_rows)
    far = r.hidden(weight_ref, gate_ref, up_ref)
    slots = r.chips * r.rows
    near_at = own_ref[0] * slots
    far_at = slots - near_at
    hidden_ref[pl.ds(pl.multiple_of(near_at, 8), slots), :] = near_ref[...]
    for chip in range(0, r.chips, 2):
        one, two = r.of_chip(chip)[0], r.of_chip(chip + 1)[0]
        start = pl.multiple_of(far_at + chip * r.rows, 8)
        hidden_ref[pl.ds(start, 2 * r.rows), :] = jnp.concatenate([far[one], far[two]], axis=0)


def near_layer(gathered, weights, adapter_up, own, shard_rows, block):
    rows = gathered.shape[0]
    columns = gathered.shape[1] - LANES
    units = weights[0].shape[1]
    out = jax.ShapeDtypeStruct((rows // 4, units), F32)
    vmem = pl.BlockSpec(memory_space=pltpu.VMEM)
    return pl.pallas_call(
        functools.partial(near_kernel, shard_rows, block),
        out_shape=(
            out,
            out,
            out,
            jax.ShapeDtypeStruct((rows // (2 * shard_rows), NOTE_ROWS, LANES), F32),
        ),
        in_specs=[pl.BlockSpec(memory_space=pltpu.SMEM)] + [vmem] * 4,
        out_specs=(vmem, vmem, vmem, vmem),
        scratch_shapes=[pltpu.VMEM((2 * HALVES, columns, 2 * units), BF16)],
        compiler_params=pltpu.CompilerParams(vmem_limit_bytes=24 * 2**20),
        cost_estimate=pl.CostEstimate(
            flops=4 * rows * columns * units,
            bytes_accessed=2 * rows * columns + 4 * columns * units,
            transcendentals=2 * rows * units,
        ),
    )(own, gathered, *weights, adapter_up)


def far_layer(gathered, weights, near, tensor, shard_rows):
    rows = gathered.shape[0]
    columns = gathered.shape[1] - LANES
    units = weights[0].shape[1]
    vmem = pl.BlockSpec(memory_space=pltpu.VMEM)
    return pl.pallas_call(
        functools.partial(far_kernel, shard_rows),
        out_shape=jax.ShapeDtypeStruct((rows // 2, units), F32),
        in_specs=[pl.BlockSpec(memory_space=pltpu.SMEM)] + [vmem] * 4,
        out_specs=vmem,
        scratch_shapes=[pltpu.VMEM((2 * HALVES, columns, 2 * units), BF16)],
        compiler_params=pltpu.CompilerParams(vmem_limit_bytes=24 * 2**20),
        cost_estimate=pl.CostEstimate(
            flops=4 * rows * columns * units,
            bytes_accessed=2 * rows * columns + 4 * columns * units,
            transcendentals=2 * rows * units,
        ),
    )(tensor[None], gathered, *weights, near)


def norm_kernel(x_ref, out_ref):
    x = x_ref[...]
    mean = jnp.sum(jnp.sum(x * x, axis=0, keepdims=True), axis=1, keepdims=True) / x.size
    x = x * lax.rsqrt(mean + 1e-06)
    for k in range(x.shape[0]):
        out_ref[:, pl.ds(k * LANES, LANES)] = x[k : k + 1, :]


def norm_layer(pooled):
    vmem = pl.BlockSpec(memory_space=pltpu.VMEM)
    return pl.pallas_call(
        norm_kernel,
        out_shape=jax.ShapeDtypeStruct((1, pooled.size), F32),
        in_specs=[vmem],
        out_specs=vmem,
        compiler_params=pltpu.CompilerParams(vmem_limit_bytes=4 * 2**20),
    )(pooled)


def local(
    tokens,
    routes,
    chosen_expert_weight,
    expert_gate_weight,
    expert_up_weight,
    expert_down_weight,
    adapter_down_weight,
    adapter_up_weight,
    document_task_index,
    counts,
    final_norm_scale,
):
    rows, feats = tokens.shape
    seq = lax.axis_size(SEQ)
    experts = lax.axis_size(EXPERT)
    cores = lax.axis_size("c")
    groups = lax.axis_size(GROUP)
    tensors = lax.axis_size("t")
    capacity = rows * 5 // 16
    set_slots = capacity // tensors
    chip_rows = cores * set_slots
    shard_rows = HALVES * chip_rows
    width = feats * experts
    half = feats // cores
    columns = experts * half // HALVES
    slice_width = width // seq
    task_rows = adapter_down_weight.shape[0]
    s = lax.axis_index(SEQ)
    t = lax.axis_index("t")
    g = lax.axis_index(GROUP)
    per_feature_group = feats // slice_width
    own_group = s // per_feature_group

    ids = routes.T
    outgoing, notes = dispatch_layer(
        ids,
        chosen_expert_weight.T,
        tokens,
        adapter_down_weight,
        adapter_up_weight,
        final_norm_scale[None],
        experts,
        set_slots,
    )
    later_up, _ = lax.optimization_barrier((expert_up_weight[0], outgoing))
    notes = jnp.pad(notes, ((chip_rows, 0), (columns, 0))).astype(F16)
    notes, later_up = lax.optimization_barrier((notes, later_up))
    other = [(k, tensors - 1 - k) for k in range(tensors)]
    far_weights = [lax.ppermute(w, "t", other) for w in (expert_gate_weight[0], later_up)]
    received = swap(outgoing, EXPERT + ("c",))

    sent, adapter_up, norm_scale = rows_layer(own_group, received, task_rows)
    sent = sent.astype(F16) + notes
    gathered = lax.all_gather(sent, SEQ, axis=0, tiled=False)
    gathered = gathered.astype(BF16).reshape(seq * shard_rows, columns + LANES)
    per_half = half // slice_width
    own_column = own_group * half + (s % per_half) * slice_width
    near, factor, base, notes = near_layer(
        gathered,
        (expert_gate_weight[0], expert_up_weight[0]),
        adapter_up,
        jnp.stack(
            [
                (s // per_half) % cores,
                own_column // columns,
                own_column % columns,
                document_task_index[0],
                t,
                lax.axis_index(EXPERT),
            ]
        ),
        shard_rows,
        rows,
    )
    hidden = far_layer(gathered, far_weights, near, t, shard_rows)

    units = hidden.shape[-1]
    hidden = lax.all_gather(hidden.astype(F16), SEQ, axis=0, tiled=False)
    part = lax.dot_general(
        hidden.reshape(seq * tensors, -1, units).astype(BF16),
        expert_down_weight[0].reshape(seq * tensors, units, slice_width),
        (((0, 2), (0, 1)), ((), ())),
        preferred_element_type=F32,
    )
    payload = (part * factor + base).reshape(groups, chip_rows, slice_width)

    expert_ids = jnp.arange(experts, dtype=jnp.int32)[:, None]
    group_ids = lax.dynamic_index_in_dim(notes, g, axis=0, keepdims=False)
    group_ids = group_ids[:2].astype(jnp.int32)
    slot = slots_of((group_ids[:1] == expert_ids) | (group_ids[1:] == expert_ids), rows)
    slot_set = jnp.floor(slot / set_slots)
    place = jnp.where(
        slot >= 0.0,
        slot + slot_set * (chip_rows - set_slots) + set_slots * block_of(slot.shape, rows),
        -1.0,
    )
    group_rows = cores * rows
    combiner = (
        place[:, None, :]
        == jnp.arange(tensors * chip_rows, dtype=jnp.int32).astype(F32)[None, :, None]
    ).astype(F32)
    combiner = combiner.reshape(groups * chip_rows, group_rows)
    position = g * group_rows + jnp.arange(group_rows, dtype=jnp.int32)[None, :]
    counted = (position < counts[0]).astype(F32)
    payload, combiner, counted, norm_scale = lax.optimization_barrier(
        (payload, combiner, counted, norm_scale)
    )

    returned = swap(payload, GROUP)
    mixed = lax.dot_general(
        combiner,
        returned.reshape(groups * chip_rows, slice_width),
        (((0,), (0,)), ((), ())),
        precision=HIGH,
    )
    squares = jnp.sum(spread(jnp.sum(mixed * mixed, axis=1)[None], SEQ), axis=0)
    factor = counted * lax.rsqrt(squares / width + 1e-05)
    pooled = jnp.dot(factor, mixed, precision=HIGH) * norm_scale
    pooled = jnp.sum(spread(pooled, GROUP), axis=0)
    return norm_layer(spread(pooled, SEQ).reshape(seq, slice_width))


def solution(mesh):
    seq, experts, tensors = mesh.devices.shape
    parts = Mesh(
        mesh.devices.reshape(seq // 2, 2, experts // 2, 2, tensors), ("z", "c", "y", "h", "t")
    )
    return jax.shard_map(
        local,
        mesh=parts,
        in_specs=(
            P(SEQ, EXPERT),
            P(SEQ, None),
            P(SEQ, None),
            P(EXPERT, None, SEQ + ("t",)),
            P(EXPERT, None, SEQ + ("t",)),
            P(EXPERT, None, SEQ),
            P(None, EXPERT),
            P(None, EXPERT),
            P(),
            P(),
            P(EXPERT),
        ),
        out_specs=P(),
        check_vma=False,
    )
```

```python
import functools

import jax
import jax.numpy as jnp
from jax import lax
from jax.experimental import pallas as pl
from jax.experimental.pallas import tpu as pltpu
from jax.sharding import Mesh
from jax.sharding import PartitionSpec as P

TASK_COUNT = 2
ADAPTER_SCALE = 0.5

SEQ = ("z", "c")
EXPERT = ("y", "h")
GROUP = ("y", "h", "t")
HALVES = 2

BF16 = jnp.bfloat16
F16 = jnp.float16
F32 = jnp.float32
HIGH = lax.Precision.HIGHEST
LANES = 128
LEAST_EXPONENT = -40.0
NOTE_ROWS = 8
PART_STEP = 256.0
LOW_LANES = 32


def swap(x, axes):
    return lax.all_to_all(x, axes, split_axis=0, concat_axis=0, tiled=True)


def spread(x, axes):
    return swap(jnp.broadcast_to(x[None], (lax.axis_size(axes),) + x.shape), axes)


def rounded_parts(x):
    first = x.astype(BF16).astype(F32)
    rest = (x - first) * PART_STEP
    second = rest.astype(BF16).astype(F32)
    return first, second, (rest - second) * PART_STEP


def earlier_in_block(lanes, block):
    i = lax.broadcasted_iota(jnp.int32, (lanes, lanes), 0)
    j = lax.broadcasted_iota(jnp.int32, (lanes, lanes), 1)
    return ((i < j) & (i // block == j // block)).astype(F32).astype(BF16)


def slots_of(named, block):
    before = jnp.dot(
        named.astype(F32).astype(BF16),
        earlier_in_block(named.shape[1], block),
        preferred_element_type=F32,
    )
    return jnp.where(named, before, -1.0)


def block_of(shape, block):
    return (lax.broadcasted_iota(jnp.int32, shape, 1) // block).astype(F32)


def dispatch_kernel(*refs):
    out_ref, note_ref, held, sem = refs[6], refs[7], refs[8:14], refs[14]
    core, chip = lax.axis_index("c"), lax.axis_index("z")
    copies = [pltpu.make_async_copy(refs[k], held[k], sem.at[k]) for k in range(6)]
    for copy in copies:
        copy.start()
    for copy in copies:
        copy.wait()
    routes_ref, chosen_ref, tokens_ref, down_ref, up_ref, norm_ref = held
    targets, set_slots, _ = out_ref.shape
    experts = targets // HALVES
    rows, feats = tokens_ref.shape
    half = feats // HALVES
    ranks = down_ref.shape[0] // HALVES
    first_slot = (lax.axis_index("t") * set_slots).astype(F32)
    ids = routes_ref[...]
    notes = jnp.concatenate([ids.astype(F32)] + list(rounded_parts(chosen_ref[...])), axis=0)
    notes = jnp.concatenate([jnp.where(core == k, notes, 0.0) for k in range(HALVES)], axis=1)
    note_ref[...] = jnp.zeros_like(note_ref)
    note_ref[pl.ds(0, NOTE_ROWS), :] = notes
    expert = lax.broadcasted_iota(jnp.int32, (experts, rows), 0)
    place = slots_of((ids[:1] == expert) | (ids[1:] == expert), rows)
    padded = 16
    row = lax.broadcasted_iota(jnp.int32, (padded, rows), 0)
    slot = jnp.where(row < set_slots, row.astype(F32) + first_slot, -2.0)
    chooser = jnp.concatenate(
        [(place[e : e + 1] == slot).astype(F32) for e in range(experts)], axis=0
    ).astype(BF16)
    for c in range(HALVES):
        lanes = pl.ds(c * half, half)
        x = tokens_ref[:, lanes]
        low = lax.dot_general(
            x, down_ref[:, lanes], (((1,), (1,)), ((), ())), preferred_element_type=F32
        )
        first = low.astype(BF16)
        rest = low - first.astype(F32)
        second = rest.astype(BF16)
        third = (rest - second.astype(F32)).astype(BF16)
        x = jnp.concatenate([x, jnp.zeros_like(first), first, second, third], axis=1)
        chosen = jnp.dot(chooser, x, preferred_element_type=F32)
        column = pl.multiple_of((chip * HALVES + c) % (feats // LANES) * LANES, LANES)
        norm = norm_ref[:, pl.ds(column, LANES)]
        norm_first = norm.astype(BF16).astype(F32)
        norm_rest = norm - norm_first
        norm_second = norm_rest.astype(BF16).astype(F32)
        up_rows = up_ref[pl.ds(pl.multiple_of(core * ranks, ranks), ranks), pl.ds(column, LANES)]
        up_rows = up_rows.astype(F32)
        small = [
            up_rows[:set_slots],
            jnp.concatenate(
                [
                    up_rows[set_slots:],
                    norm_first,
                    norm_second,
                    norm_rest - norm_second,
                    jnp.zeros((2 * set_slots - ranks - 3, LANES), F32),
                ],
                axis=0,
            ),
        ]
        small = jnp.concatenate(small, axis=1).astype(BF16)
        for e in range(experts):
            out_ref[e * HALVES + c, :, pl.ds(0, half + LANES)] = chosen[
                e * padded : e * padded + set_slots
            ].astype(BF16)
            out_ref[e * HALVES + c, :, pl.ds(half + LANES, 2 * LANES)] = small


def dispatch_layer(
    routes, chosen, tokens, adapter_down, adapter_up, norm_scale, experts, set_slots
):
    rows, feats = tokens.shape
    lanes = feats // HALVES + 3 * LANES
    operands = (routes, chosen, tokens, adapter_down, adapter_up, norm_scale)
    return pl.pallas_call(
        dispatch_kernel,
        out_shape=(
            jax.ShapeDtypeStruct((experts * HALVES, set_slots, lanes), BF16),
            jax.ShapeDtypeStruct((HALVES * set_slots, LANES), F32),
        ),
        in_specs=[pl.BlockSpec(memory_space=pltpu.HBM)] * len(operands),
        out_specs=(pl.BlockSpec(memory_space=pltpu.VMEM),) * 2,
        scratch_shapes=[pltpu.VMEM(x.shape, x.dtype) for x in operands]
        + [pltpu.SemaphoreType.DMA((len(operands),))],
        compiler_params=pltpu.CompilerParams(vmem_limit_bytes=60 * 2**20),
        cost_estimate=pl.CostEstimate(
            flops=4 * rows * feats * experts * set_slots,
            bytes_accessed=2 * rows * feats + 2 * experts * HALVES * set_slots * lanes,
            transcendentals=0,
        ),
    )(*operands)


def rows_kernel(own_ref, received_ref, sent_ref, adapter_ref, norm_ref):
    messages, set_slots, _ = received_ref.shape
    groups = messages // HALVES
    half = 2 * LANES
    rows = HALVES * set_slots
    columns = sent_ref.shape[1] - LANES
    ranks = adapter_ref.shape[0] // HALVES

    def both(e, first, lanes):
        return jnp.concatenate(
            [
                received_ref[e * HALVES + c, :, pl.ds(first, lanes)].astype(F32)
                for c in range(HALVES)
            ],
            axis=0,
        )

    x = jnp.concatenate([both(e, 0, half) for e in range(groups)], axis=1)
    largest = jnp.max(jnp.abs(x), axis=1, keepdims=True)
    exponent = jnp.maximum(
        jnp.floor(jnp.log2(jnp.maximum(largest, 1e-30)) + 1.01), LEAST_EXPONENT
    )
    x = x * jnp.exp2(15.0 - exponent)
    low = sum(both(e, half, LANES) for e in range(groups))
    low = sum(low[:, k * LOW_LANES : (k + 1) * LOW_LANES] for k in range(1, 4))
    low = low * jnp.exp2(7.0 - exponent)
    sent_ref[pl.ds(0, rows), pl.ds(0, columns)] = x[:, :columns]
    sent_ref[pl.ds(rows, rows), pl.ds(0, columns)] = x[:, columns:]
    sent_ref[pl.ds(0, rows), pl.ds(columns, LANES)] = jnp.concatenate(
        [jnp.broadcast_to(exponent, low.shape)] + list(rounded_parts(low)), axis=1
    )
    sent_ref[pl.ds(rows, rows), pl.ds(columns, LANES)] = jnp.zeros((rows, LANES), F32)

    adapter = []
    for c in range(HALVES):
        small = received_ref[own_ref[0] * HALVES + c, :, pl.ds(half + LANES, 2 * LANES)]
        small = small.astype(F32)
        small = jnp.concatenate([small[:, :LANES], small[:, LANES:]], axis=0)
        adapter.append(small[:ranks])
        if c == 0:
            norm_ref[...] = (
                small[ranks : ranks + 1] + small[ranks + 1 : ranks + 2]
            ) + small[ranks + 2 : ranks + 3]
    adapter_ref[...] = jnp.concatenate(adapter, axis=0).astype(BF16)


def rows_layer(own_group, received, task_rows):
    messages, set_slots, _ = received.shape
    rows = HALVES * set_slots
    vmem = pl.BlockSpec(memory_space=pltpu.VMEM)
    columns = messages // HALVES * 2 * LANES // HALVES
    return pl.pallas_call(
        rows_kernel,
        out_shape=(
            jax.ShapeDtypeStruct((HALVES * rows, columns + LANES), F32),
            jax.ShapeDtypeStruct((task_rows, LANES), BF16),
            jax.ShapeDtypeStruct((1, LANES), F32),
        ),
        in_specs=[pl.BlockSpec(memory_space=pltpu.SMEM), vmem],
        out_specs=(vmem, vmem, vmem),
        compiler_params=pltpu.CompilerParams(vmem_limit_bytes=8 * 2**20),
        cost_estimate=pl.CostEstimate(
            flops=8 * rows * columns, bytes_accessed=8 * rows * columns, transcendentals=4 * rows
        ),
    )(own_group[None], received)


def hidden_rows(parts, scales, shrink, shift, weight_ref, gate_ref, up_ref):
    units = gate_ref.shape[1]
    half = 2 * LANES
    flat, columns = parts[0].shape
    blocks = columns // half
    acts = jnp.zeros((flat, 2 * units), F32)
    for c in range(HALVES):
        half_acts = jnp.zeros((flat, 2 * units), F32)
        for q in range(HALVES):
            for n in range(blocks):
                source = pl.ds(((q * blocks + n) * HALVES + c) * half, half)
                target = pl.ds(n * half, half)
                for k, ref in enumerate((gate_ref, up_ref)):
                    weight_ref[c * HALVES + q, target, pl.ds(k * units, units)] = ref[source, :]
            product = jnp.dot(
                parts[c * HALVES + q],
                weight_ref[c * HALVES + q],
                preferred_element_type=F32,
            )
            half_acts += product if q == 0 else pltpu.roll(product, flat - shift, 0)
        acts += half_acts * jnp.concatenate([scales[c]] * 2, axis=1)
    gate_act, up_act = acts[:, :units], acts[:, units:]
    value = (gate_act / (1.0 + jnp.exp(-gate_act)) * up_act).astype(BF16).astype(F32)
    return value * shrink


class Rows:
    def __init__(self, x_ref, shard_rows):
        self.x_ref = x_ref
        self.shard_rows = shard_rows
        self.rows = shard_rows // HALVES
        self.group = -(-self.rows // 8) * 8
        self.chips = x_ref.shape[0] // (HALVES * shard_rows)
        self.flat = self.chips * self.group
        self.columns = x_ref.shape[1] - LANES
        x = x_ref[:, pl.ds(0, self.columns)].astype(F32)
        self.parts = [
            self.part(x, c, q).astype(BF16) for c in range(HALVES) for q in range(HALVES)
        ]
        self.beside = x_ref[:, pl.ds(self.columns, LANES)].astype(F32)
        exponents = [self.part(self.beside, c, 0)[:, :LOW_LANES] for c in range(HALVES)]
        exponents = [jnp.concatenate([e] * (LANES // LOW_LANES), axis=1) for e in exponents]
        self.scales = [jnp.exp2(e - 15.0) for e in exponents]
        self.row_exponent = jnp.maximum(*exponents)

    def part(self, value, c, q):
        value = value.reshape(self.chips, HALVES, self.shard_rows, value.shape[-1])[:, c]
        value = value[:, : self.group] if q == 0 else value[:, self.shard_rows - self.group :]
        return value.reshape(self.flat, value.shape[-1])

    def aligned(self, value, q):
        return value if q == 0 else pltpu.roll(value, self.flat - (self.group - self.rows), 0)

    def of_chip(self, chip):
        source = slice(chip * self.group, chip * self.group + self.rows)
        return source, pl.ds(chip * self.rows, self.rows)


def near_kernel(
    shard_rows,
    block,
    own_ref,
    x_ref,
    gate_ref,
    up_ref,
    adapter_ref,
    hidden_ref,
    factor_ref,
    base_ref,
    note_ref,
    part_ref,
    row_ref,
    weight_ref,
):
    r = Rows(x_ref, shard_rows)
    task_rows = adapter_ref.shape[0]
    own_core, own_quarter = own_ref[0], own_ref[1]
    own_column = pl.multiple_of(own_ref[2], LANES)
    task, tensor, expert = own_ref[3], own_ref[4], own_ref[5]
    shrink = jnp.exp2(-2.0 * r.row_exponent - 2.0)
    for k in range(len(r.parts)):
        part_ref[k] = r.parts[k]
    for k, value in enumerate(r.scales + [shrink]):
        row_ref[k] = value
    hidden = hidden_rows(
        r.parts, r.scales, shrink, r.group - r.rows, weight_ref, gate_ref, up_ref
    )

    own = x_ref[:, pl.ds(own_column, LANES)].astype(F32)
    low = jnp.zeros((r.flat, LOW_LANES), F32)
    residual = jnp.zeros((r.flat, LANES), F32)
    for c in range(HALVES):
        tile = r.part(r.beside, c, 0)
        low_part = tile[:, LOW_LANES : 2 * LOW_LANES] + (
            tile[:, 2 * LOW_LANES : 3 * LOW_LANES] + tile[:, 3 * LOW_LANES :] / PART_STEP
        ) / PART_STEP
        low += low_part * jnp.exp2(tile[:, :LOW_LANES] - 7.0)
        for q in range(HALVES):
            mine = (own_core == c) & (own_quarter == q)
            residual += jnp.where(mine, r.aligned(r.part(own, c, q), q) * r.scales[c], 0.0)
    low_lane = lax.broadcasted_iota(jnp.int32, low.shape, 1) // (task_rows // TASK_COUNT)
    low = jnp.where(low_lane == task, low, 0.0).astype(BF16)
    base = residual + ADAPTER_SCALE * jnp.dot(
        low, adapter_ref[...], preferred_element_type=F32
    )
    up_scale = jnp.exp2(2.0 * r.row_exponent + 2.0)

    notes = sum(r.aligned(r.part(r.beside, c, 1), 1) for c in range(HALVES))
    notes = notes.reshape(r.chips, r.group, LANES)[:, :NOTE_ROWS]
    note_ref[...] = notes
    first, second = notes[:, 0, :].astype(jnp.int32), notes[:, 1, :].astype(jnp.int32)
    weight = [
        notes[:, k + 2, :] + (notes[:, k + 4, :] + notes[:, k + 6, :] / PART_STEP) / PART_STEP
        for k in range(2)
    ]
    set_slots = r.rows // HALVES
    slot = slots_of((first == expert) | (second == expert), block)
    slot = slot - (tensor * set_slots).astype(F32)
    in_set = (slot >= 0.0) & (slot < set_slots)
    place = jnp.where(in_set, slot + set_slots * block_of(slot.shape, block), -1.0)
    weight = jnp.where(first == expert, weight[0], weight[1])
    row = lax.broadcasted_iota(jnp.int32, (r.group, LANES), 0).astype(F32)
    for chip in range(r.chips):
        source, target = r.of_chip(chip)
        slot_weight = jnp.sum(
            jnp.where(place[chip : chip + 1] == row, weight[chip : chip + 1], 0.0),
            axis=1,
            keepdims=True,
        )[: r.rows]
        hidden_ref[target, :] = hidden[source]
        factor_ref[target, :] = slot_weight * up_scale[source]
        base_ref[target, :] = 0.5 * base[source]


def far_kernel(
    rows, group, own_ref, part_ref, row_ref, gate_ref, up_ref, near_ref, hidden_ref, weight_ref
):
    parts = [part_ref[k] for k in range(part_ref.shape[0])]
    scales = [row_ref[k] for k in range(HALVES)]
    far = hidden_rows(
        parts, scales, row_ref[HALVES], group - rows, weight_ref, gate_ref, up_ref
    )
    chips = far.shape[0] // group
    slots = chips * rows
    near_at = own_ref[0] * slots
    far_at = slots - near_at
    hidden_ref[pl.ds(pl.multiple_of(near_at, 8), slots), :] = near_ref[...]
    for chip in range(0, chips, 2):
        pair = [far[k * group : k * group + rows] for k in (chip, chip + 1)]
        start = pl.multiple_of(far_at + chip * rows, 8)
        hidden_ref[pl.ds(start, 2 * rows), :] = jnp.concatenate(pair, axis=0)


def near_layer(gathered, weights, adapter_up, own, shard_rows, block):
    rows = gathered.shape[0]
    columns = gathered.shape[1] - LANES
    units = weights[0].shape[1]
    chips = rows // (HALVES * shard_rows)
    flat = chips * (-(-shard_rows // HALVES // 8) * 8)
    out = jax.ShapeDtypeStruct((rows // 4, units), F32)
    vmem = pl.BlockSpec(memory_space=pltpu.VMEM)
    return pl.pallas_call(
        functools.partial(near_kernel, shard_rows, block),
        out_shape=(
            out,
            out,
            out,
            jax.ShapeDtypeStruct((chips, NOTE_ROWS, LANES), F32),
            jax.ShapeDtypeStruct((2 * HALVES, flat, columns), BF16),
            jax.ShapeDtypeStruct((HALVES + 1, flat, LANES), F32),
        ),
        in_specs=[pl.BlockSpec(memory_space=pltpu.SMEM)] + [vmem] * 4,
        out_specs=(vmem,) * 6,
        scratch_shapes=[pltpu.VMEM((2 * HALVES, columns, 2 * units), BF16)],
        compiler_params=pltpu.CompilerParams(vmem_limit_bytes=24 * 2**20),
        cost_estimate=pl.CostEstimate(
            flops=4 * rows * columns * units,
            bytes_accessed=4 * rows * columns + 4 * columns * units,
            transcendentals=2 * rows * units,
        ),
    )(own, gathered, *weights, adapter_up)


def far_layer(parts, row_scales, weights, near, tensor, shard_rows):
    _, flat, columns = parts.shape
    slots, units = near.shape
    rows = shard_rows // HALVES
    vmem = pl.BlockSpec(memory_space=pltpu.VMEM)
    return pl.pallas_call(
        functools.partial(far_kernel, rows, flat * rows // slots),
        out_shape=jax.ShapeDtypeStruct((2 * slots, units), F32),
        in_specs=[pl.BlockSpec(memory_space=pltpu.SMEM)] + [vmem] * 5,
        out_specs=vmem,
        scratch_shapes=[pltpu.VMEM((2 * HALVES, columns, 2 * units), BF16)],
        compiler_params=pltpu.CompilerParams(vmem_limit_bytes=24 * 2**20),
        cost_estimate=pl.CostEstimate(
            flops=16 * flat * columns * units,
            bytes_accessed=8 * flat * columns + 16 * columns * units,
            transcendentals=2 * flat * units,
        ),
    )(tensor[None], parts, row_scales, *weights, near)


def norm_kernel(x_ref, out_ref):
    x = x_ref[...]
    mean = jnp.sum(jnp.sum(x * x, axis=0, keepdims=True), axis=1, keepdims=True) / x.size
    x = x * lax.rsqrt(mean + 1e-06)
    for k in range(x.shape[0]):
        out_ref[:, pl.ds(k * LANES, LANES)] = x[k : k + 1, :]


def norm_layer(pooled):
    vmem = pl.BlockSpec(memory_space=pltpu.VMEM)
    return pl.pallas_call(
        norm_kernel,
        out_shape=jax.ShapeDtypeStruct((1, pooled.size), F32),
        in_specs=[vmem],
        out_specs=vmem,
        compiler_params=pltpu.CompilerParams(vmem_limit_bytes=4 * 2**20),
    )(pooled)


def local(
    tokens,
    routes,
    chosen_expert_weight,
    expert_gate_weight,
    expert_up_weight,
    expert_down_weight,
    adapter_down_weight,
    adapter_up_weight,
    document_task_index,
    counts,
    final_norm_scale,
):
    rows, feats = tokens.shape
    seq = lax.axis_size(SEQ)
    experts = lax.axis_size(EXPERT)
    cores = lax.axis_size("c")
    groups = lax.axis_size(GROUP)
    tensors = lax.axis_size("t")
    capacity = rows * 5 // 16
    set_slots = capacity // tensors
    chip_rows = cores * set_slots
    shard_rows = HALVES * chip_rows
    width = feats * experts
    half = feats // cores
    columns = experts * half // HALVES
    slice_width = width // seq
    task_rows = adapter_down_weight.shape[0]
    s = lax.axis_index(SEQ)
    t = lax.axis_index("t")
    g = lax.axis_index(GROUP)
    per_feature_group = feats // slice_width
    own_group = s // per_feature_group

    ids = routes.T
    outgoing, notes = dispatch_layer(
        ids,
        chosen_expert_weight.T,
        tokens,
        adapter_down_weight,
        adapter_up_weight,
        final_norm_scale[None],
        experts,
        set_slots,
    )
    later_up, _ = lax.optimization_barrier((expert_up_weight[0], outgoing))
    other = [(k, tensors - 1 - k) for k in range(tensors)]
    far_weights = [lax.ppermute(w, "t", other) for w in (expert_gate_weight[0], later_up)]
    received = swap(outgoing, EXPERT + ("c",))

    sent, adapter_up, norm_scale = rows_layer(own_group, received, task_rows)
    sent = (sent + jnp.pad(notes, ((chip_rows, 0), (columns, 0)))).astype(F16)
    gathered = lax.all_gather(sent, SEQ, axis=0, tiled=False)
    gathered = gathered.astype(BF16).reshape(seq * shard_rows, columns + LANES)
    per_half = half // slice_width
    own_column = own_group * half + (s % per_half) * slice_width
    near, factor, base, notes, parts, row_scales = near_layer(
        gathered,
        (expert_gate_weight[0], expert_up_weight[0]),
        adapter_up,
        jnp.stack(
            [
                (s // per_half) % cores,
                own_column // columns,
                own_column % columns,
                document_task_index[0],
                t,
                lax.axis_index(EXPERT),
            ]
        ),
        shard_rows,
        rows,
    )
    hidden = far_layer(parts, row_scales, far_weights, near, t, shard_rows)

    units = hidden.shape[-1]
    hidden = hidden.astype(F16).reshape(tensors, -1, units)
    hidden = lax.all_gather(hidden, SEQ, axis=0, tiled=True)
    part = lax.dot_general(
        hidden.astype(BF16),
        expert_down_weight[0].reshape(seq * tensors, units, slice_width),
        (((0, 2), (0, 1)), ((), ())),
        preferred_element_type=F32,
    )
    payload = (part * factor + base).reshape(groups, chip_rows, slice_width)

    expert_ids = jnp.arange(experts, dtype=jnp.int32)[:, None]
    group_ids = lax.dynamic_index_in_dim(notes, g, axis=0, keepdims=False)
    group_ids = group_ids[:2].astype(jnp.int32)
    slot = slots_of((group_ids[:1] == expert_ids) | (group_ids[1:] == expert_ids), rows)
    slot_set = jnp.floor(slot / set_slots)
    place = jnp.where(
        slot >= 0.0,
        slot + slot_set * (chip_rows - set_slots) + set_slots * block_of(slot.shape, rows),
        -1.0,
    )
    group_rows = cores * rows
    combiner = (
        place[:, None, :]
        == jnp.arange(tensors * chip_rows, dtype=jnp.int32).astype(F32)[None, :, None]
    ).astype(F32)
    combiner = combiner.reshape(groups * chip_rows, group_rows)
    position = g * group_rows + jnp.arange(group_rows, dtype=jnp.int32)[None, :]
    counted = (position < counts[0]).astype(F32)
    payload, combiner, counted, norm_scale = lax.optimization_barrier(
        (payload, combiner, counted, norm_scale)
    )

    returned = swap(payload, GROUP)
    mixed = lax.dot_general(
        combiner,
        returned.reshape(groups * chip_rows, slice_width),
        (((0,), (0,)), ((), ())),
        precision=HIGH,
    )
    squares = jnp.sum(spread(jnp.sum(mixed * mixed, axis=1)[None], SEQ), axis=0)
    factor = counted * lax.rsqrt(squares / width + 1e-05)
    pooled = jnp.dot(factor, mixed, precision=HIGH) * norm_scale
    pooled = jnp.sum(spread(pooled, GROUP), axis=0)
    return norm_layer(spread(pooled, SEQ).reshape(seq, slice_width))


def solution(mesh):
    seq, experts, tensors = mesh.devices.shape
    parts = Mesh(
        mesh.devices.reshape(seq // 2, 2, experts // 2, 2, tensors), ("z", "c", "y", "h", "t")
    )
    return jax.shard_map(
        local,
        mesh=parts,
        in_specs=(
            P(SEQ, EXPERT),
            P(SEQ, None),
            P(SEQ, None),
            P(EXPERT, None, SEQ + ("t",)),
            P(EXPERT, None, SEQ + ("t",)),
            P(EXPERT, None, SEQ),
            P(None, EXPERT),
            P(None, EXPERT),
            P(),
            P(),
            P(EXPERT),
        ),
        out_specs=P(),
        check_vma=False,
    )
```

```python
import functools

import jax
import jax.numpy as jnp
from jax import lax
from jax.experimental import pallas as pl
from jax.experimental.pallas import tpu as pltpu
from jax.sharding import Mesh
from jax.sharding import PartitionSpec as P

TASK_COUNT = 2
ADAPTER_SCALE = 0.5

SEQ = ("z", "c")
EXPERT = ("y", "h")
GROUP = ("y", "h", "t")
HALVES = 2

BF16 = jnp.bfloat16
F16 = jnp.float16
F32 = jnp.float32
HIGH = lax.Precision.HIGHEST
LANES = 128
LEAST_EXPONENT = -40.0
NOTE_ROWS = 8
PART_STEP = 256.0
LOW_LANES = 32


def swap(x, axes):
    return lax.all_to_all(x, axes, split_axis=0, concat_axis=0, tiled=True)


def spread(x, axes):
    return swap(jnp.broadcast_to(x[None], (lax.axis_size(axes),) + x.shape), axes)


def rounded_parts(x):
    first = x.astype(BF16).astype(F32)
    rest = (x - first) * PART_STEP
    second = rest.astype(BF16).astype(F32)
    return first, second, (rest - second) * PART_STEP


def earlier_in_block(lanes, block):
    i = lax.broadcasted_iota(jnp.int32, (lanes, lanes), 0)
    j = lax.broadcasted_iota(jnp.int32, (lanes, lanes), 1)
    return ((i < j) & (i // block == j // block)).astype(F32).astype(BF16)


def slots_of(named, block):
    before = jnp.dot(
        named.astype(F32).astype(BF16),
        earlier_in_block(named.shape[1], block),
        preferred_element_type=F32,
    )
    return jnp.where(named, before, -1.0)


def block_of(shape, block):
    return (lax.broadcasted_iota(jnp.int32, shape, 1) // block).astype(F32)


def dispatch_kernel(*refs):
    out_ref, note_ref, held, sem = refs[6], refs[7], refs[8:14], refs[14]
    core, chip = lax.axis_index("c"), lax.axis_index("z")
    copies = [pltpu.make_async_copy(refs[k], held[k], sem.at[k]) for k in range(6)]
    for copy in copies:
        copy.start()
    for copy in copies:
        copy.wait()
    routes_ref, chosen_ref, tokens_ref, down_ref, up_ref, norm_ref = held
    targets, set_slots, _ = out_ref.shape
    experts = targets // HALVES
    rows, feats = tokens_ref.shape
    half = feats // HALVES
    ranks = down_ref.shape[0] // HALVES
    first_slot = (lax.axis_index("t") * set_slots).astype(F32)
    ids = routes_ref[...]
    notes = jnp.concatenate([ids.astype(F32)] + list(rounded_parts(chosen_ref[...])), axis=0)
    notes = jnp.concatenate([jnp.where(core == k, notes, 0.0) for k in range(HALVES)], axis=1)
    note_ref[...] = jnp.zeros_like(note_ref)
    note_ref[pl.ds(0, NOTE_ROWS), :] = notes
    expert = lax.broadcasted_iota(jnp.int32, (experts, rows), 0)
    place = slots_of((ids[:1] == expert) | (ids[1:] == expert), rows)
    padded = 16
    row = lax.broadcasted_iota(jnp.int32, (padded, rows), 0)
    slot = jnp.where(row < set_slots, row.astype(F32) + first_slot, -2.0)
    chooser = jnp.concatenate(
        [(place[e : e + 1] == slot).astype(F32) for e in range(experts)], axis=0
    ).astype(BF16)
    for c in range(HALVES):
        lanes = pl.ds(c * half, half)
        x = tokens_ref[:, lanes]
        low = lax.dot_general(
            x, down_ref[:, lanes], (((1,), (1,)), ((), ())), preferred_element_type=F32
        )
        first = low.astype(BF16)
        rest = low - first.astype(F32)
        second = rest.astype(BF16)
        third = (rest - second.astype(F32)).astype(BF16)
        x = jnp.concatenate([x, jnp.zeros_like(first), first, second, third], axis=1)
        chosen = jnp.dot(chooser, x, preferred_element_type=F32)
        column = pl.multiple_of((chip * HALVES + c) % (feats // LANES) * LANES, LANES)
        norm = norm_ref[:, pl.ds(column, LANES)]
        norm_first = norm.astype(BF16).astype(F32)
        norm_rest = norm - norm_first
        norm_second = norm_rest.astype(BF16).astype(F32)
        up_rows = up_ref[pl.ds(pl.multiple_of(core * ranks, ranks), ranks), pl.ds(column, LANES)]
        up_rows = up_rows.astype(F32)
        small = [
            up_rows[:set_slots],
            jnp.concatenate(
                [
                    up_rows[set_slots:],
                    norm_first,
                    norm_second,
                    norm_rest - norm_second,
                    jnp.zeros((2 * set_slots - ranks - 3, LANES), F32),
                ],
                axis=0,
            ),
        ]
        small = jnp.concatenate(small, axis=1).astype(BF16)
        for e in range(experts):
            out_ref[e * HALVES + c, :, pl.ds(0, half + LANES)] = chosen[
                e * padded : e * padded + set_slots
            ].astype(BF16)
            out_ref[e * HALVES + c, :, pl.ds(half + LANES, 2 * LANES)] = small


def dispatch_layer(
    routes, chosen, tokens, adapter_down, adapter_up, norm_scale, experts, set_slots
):
    rows, feats = tokens.shape
    lanes = feats // HALVES + 3 * LANES
    operands = (routes, chosen, tokens, adapter_down, adapter_up, norm_scale)
    return pl.pallas_call(
        dispatch_kernel,
        out_shape=(
            jax.ShapeDtypeStruct((experts * HALVES, set_slots, lanes), BF16),
            jax.ShapeDtypeStruct((HALVES * set_slots, LANES), F32),
        ),
        in_specs=[pl.BlockSpec(memory_space=pltpu.HBM)] * len(operands),
        out_specs=(pl.BlockSpec(memory_space=pltpu.VMEM),) * 2,
        scratch_shapes=[pltpu.VMEM(x.shape, x.dtype) for x in operands]
        + [pltpu.SemaphoreType.DMA((len(operands),))],
        compiler_params=pltpu.CompilerParams(vmem_limit_bytes=57 * 2**20),
        cost_estimate=pl.CostEstimate(
            flops=4 * rows * feats * experts * set_slots,
            bytes_accessed=2 * rows * feats + 2 * experts * HALVES * set_slots * lanes,
            transcendentals=0,
        ),
    )(*operands)


def rows_kernel(own_ref, received_ref, sent_ref, adapter_ref, norm_ref):
    messages, set_slots, _ = received_ref.shape
    groups = messages // HALVES
    half = 2 * LANES
    rows = HALVES * set_slots
    columns = sent_ref.shape[1] - LANES
    ranks = adapter_ref.shape[0] // HALVES

    def both(e, first, lanes):
        return jnp.concatenate(
            [
                received_ref[e * HALVES + c, :, pl.ds(first, lanes)].astype(F32)
                for c in range(HALVES)
            ],
            axis=0,
        )

    x = jnp.concatenate([both(e, 0, half) for e in range(groups)], axis=1)
    largest = jnp.max(jnp.abs(x), axis=1, keepdims=True)
    exponent = jnp.maximum(
        jnp.floor(jnp.log2(jnp.maximum(largest, 1e-30)) + 1.01), LEAST_EXPONENT
    )
    x = x * jnp.exp2(15.0 - exponent)
    low = sum(both(e, half, LANES) for e in range(groups))
    low = sum(low[:, k * LOW_LANES : (k + 1) * LOW_LANES] for k in range(1, 4))
    low = low * jnp.exp2(7.0 - exponent)
    sent_ref[pl.ds(0, rows), pl.ds(0, columns)] = x[:, :columns]
    sent_ref[pl.ds(rows, rows), pl.ds(0, columns)] = x[:, columns:]
    sent_ref[pl.ds(0, rows), pl.ds(columns, LANES)] = jnp.concatenate(
        [jnp.broadcast_to(exponent, low.shape)] + list(rounded_parts(low)), axis=1
    )
    sent_ref[pl.ds(rows, rows), pl.ds(columns, LANES)] = jnp.zeros((rows, LANES), F32)

    adapter = []
    for c in range(HALVES):
        small = received_ref[own_ref[0] * HALVES + c, :, pl.ds(half + LANES, 2 * LANES)]
        small = small.astype(F32)
        small = jnp.concatenate([small[:, :LANES], small[:, LANES:]], axis=0)
        adapter.append(small[:ranks])
        if c == 0:
            norm_ref[...] = (
                small[ranks : ranks + 1] + small[ranks + 1 : ranks + 2]
            ) + small[ranks + 2 : ranks + 3]
    adapter_ref[...] = jnp.concatenate(adapter, axis=0).astype(BF16)


def rows_layer(own_group, received, task_rows):
    messages, set_slots, _ = received.shape
    rows = HALVES * set_slots
    vmem = pl.BlockSpec(memory_space=pltpu.VMEM)
    columns = messages // HALVES * 2 * LANES // HALVES
    return pl.pallas_call(
        rows_kernel,
        out_shape=(
            jax.ShapeDtypeStruct((HALVES * rows, columns + LANES), F32),
            jax.ShapeDtypeStruct((task_rows, LANES), BF16),
            jax.ShapeDtypeStruct((1, LANES), F32),
        ),
        in_specs=[pl.BlockSpec(memory_space=pltpu.SMEM), vmem],
        out_specs=(vmem, vmem, vmem),
        compiler_params=pltpu.CompilerParams(vmem_limit_bytes=8 * 2**20),
        cost_estimate=pl.CostEstimate(
            flops=8 * rows * columns, bytes_accessed=8 * rows * columns, transcendentals=4 * rows
        ),
    )(own_group[None], received)


def hidden_rows(parts, scales, shrink, shift, weight_ref, gate_ref, up_ref):
    units = gate_ref.shape[1]
    half = 2 * LANES
    flat, columns = parts[0].shape
    blocks = columns // half
    acts = jnp.zeros((flat, 2 * units), F32)
    for c in range(HALVES):
        half_acts = jnp.zeros((flat, 2 * units), F32)
        for q in range(HALVES):
            for n in range(blocks):
                source = pl.ds(((q * blocks + n) * HALVES + c) * half, half)
                target = pl.ds(n * half, half)
                for k, ref in enumerate((gate_ref, up_ref)):
                    weight_ref[c * HALVES + q, target, pl.ds(k * units, units)] = ref[source, :]
            product = jnp.dot(
                parts[c * HALVES + q],
                weight_ref[c * HALVES + q],
                preferred_element_type=F32,
            )
            half_acts += product if q == 0 else pltpu.roll(product, flat - shift, 0)
        acts += half_acts * jnp.concatenate([scales[c]] * 2, axis=1)
    gate_act, up_act = acts[:, :units], acts[:, units:]
    value = (gate_act / (1.0 + jnp.exp(-gate_act)) * up_act).astype(BF16).astype(F32)
    return value * shrink


class Rows:
    def __init__(self, x_ref, shard_rows):
        self.x_ref = x_ref
        self.shard_rows = shard_rows
        self.rows = shard_rows // HALVES
        self.group = -(-self.rows // 8) * 8
        self.chips = x_ref.shape[0] // (HALVES * shard_rows)
        self.flat = self.chips * self.group
        self.columns = x_ref.shape[1] - LANES
        x = x_ref[:, pl.ds(0, self.columns)].astype(F32)
        self.parts = [
            self.part(x, c, q).astype(BF16) for c in range(HALVES) for q in range(HALVES)
        ]
        self.beside = x_ref[:, pl.ds(self.columns, LANES)].astype(F32)
        exponents = [self.part(self.beside, c, 0)[:, :LOW_LANES] for c in range(HALVES)]
        exponents = [jnp.concatenate([e] * (LANES // LOW_LANES), axis=1) for e in exponents]
        self.scales = [jnp.exp2(e - 15.0) for e in exponents]
        self.row_exponent = jnp.maximum(*exponents)

    def part(self, value, c, q):
        value = value.reshape(self.chips, HALVES, self.shard_rows, value.shape[-1])[:, c]
        value = value[:, : self.group] if q == 0 else value[:, self.shard_rows - self.group :]
        return value.reshape(self.flat, value.shape[-1])

    def aligned(self, value, q):
        return value if q == 0 else pltpu.roll(value, self.flat - (self.group - self.rows), 0)

    def of_chip(self, chip):
        source = slice(chip * self.group, chip * self.group + self.rows)
        return source, pl.ds(chip * self.rows, self.rows)


def near_kernel(
    shard_rows,
    block,
    own_ref,
    x_ref,
    gate_ref,
    up_ref,
    adapter_ref,
    hidden_ref,
    factor_ref,
    base_ref,
    combiner_ref,
    part_ref,
    row_ref,
    weight_ref,
    note_ref,
):
    r = Rows(x_ref, shard_rows)
    task_rows = adapter_ref.shape[0]
    own_core, own_quarter = own_ref[0], own_ref[1]
    own_column = pl.multiple_of(own_ref[2], LANES)
    task, tensor, expert = own_ref[3], own_ref[4], own_ref[5]
    shrink = jnp.exp2(-2.0 * r.row_exponent - 2.0)
    for k in range(len(r.parts)):
        part_ref[k] = r.parts[k]
    for k, value in enumerate(r.scales + [shrink]):
        row_ref[k] = value
    hidden = hidden_rows(
        r.parts, r.scales, shrink, r.group - r.rows, weight_ref, gate_ref, up_ref
    )

    own = x_ref[:, pl.ds(own_column, LANES)].astype(F32)
    low = jnp.zeros((r.flat, LOW_LANES), F32)
    residual = jnp.zeros((r.flat, LANES), F32)
    for c in range(HALVES):
        tile = r.part(r.beside, c, 0)
        low_part = tile[:, LOW_LANES : 2 * LOW_LANES] + (
            tile[:, 2 * LOW_LANES : 3 * LOW_LANES] + tile[:, 3 * LOW_LANES :] / PART_STEP
        ) / PART_STEP
        low += low_part * jnp.exp2(tile[:, :LOW_LANES] - 7.0)
        for q in range(HALVES):
            mine = (own_core == c) & (own_quarter == q)
            residual += jnp.where(mine, r.aligned(r.part(own, c, q), q) * r.scales[c], 0.0)
    low_lane = lax.broadcasted_iota(jnp.int32, low.shape, 1) // (task_rows // TASK_COUNT)
    low = jnp.where(low_lane == task, low, 0.0).astype(BF16)
    base = residual + ADAPTER_SCALE * jnp.dot(
        low, adapter_ref[...], preferred_element_type=F32
    )
    up_scale = jnp.exp2(2.0 * r.row_exponent + 2.0)

    notes = sum(r.aligned(r.part(r.beside, c, 1), 1) for c in range(HALVES))
    notes = notes.reshape(r.chips, r.group, LANES)[:, :NOTE_ROWS]
    note_ref[...] = notes
    first, second = notes[:, 0, :].astype(jnp.int32), notes[:, 1, :].astype(jnp.int32)
    weight = [
        notes[:, k + 2, :] + (notes[:, k + 4, :] + notes[:, k + 6, :] / PART_STEP) / PART_STEP
        for k in range(2)
    ]
    set_slots = r.rows // HALVES
    slot = slots_of((first == expert) | (second == expert), block)
    slot = slot - (tensor * set_slots).astype(F32)
    in_set = (slot >= 0.0) & (slot < set_slots)
    place = jnp.where(in_set, slot + set_slots * block_of(slot.shape, block), -1.0)
    weight = jnp.where(first == expert, weight[0], weight[1])
    row = lax.broadcasted_iota(jnp.int32, (r.group, LANES), 0).astype(F32)
    for chip in range(r.chips):
        source, target = r.of_chip(chip)
        slot_weight = jnp.sum(
            jnp.where(place[chip : chip + 1] == row, weight[chip : chip + 1], 0.0),
            axis=1,
            keepdims=True,
        )[: r.rows]
        hidden_ref[target, :] = hidden[source]
        factor_ref[target, :] = slot_weight * up_scale[source]
        base_ref[target, :] = 0.5 * base[source]

    ids = note_ref[own_ref[6]][:2].astype(jnp.int32)
    experts = combiner_ref.shape[0] // (2 * r.rows)
    named = lax.broadcasted_iota(jnp.int32, (experts, LANES), 0)
    slot = slots_of((ids[:1] == named) | (ids[1:] == named), block)
    slot_set = jnp.floor(slot / set_slots)
    place = jnp.where(
        slot >= 0.0,
        slot + slot_set * (r.rows - set_slots) + set_slots * block_of(slot.shape, block),
        -1.0,
    )
    row = lax.broadcasted_iota(jnp.int32, (2 * r.rows, LANES), 0).astype(F32)
    for e in range(experts):
        combiner_ref[pl.ds(e * 2 * r.rows, 2 * r.rows), :] = (place[e : e + 1] == row).astype(F32)


def far_kernel(
    rows, group, own_ref, part_ref, row_ref, gate_ref, up_ref, near_ref, hidden_ref, weight_ref
):
    parts = [part_ref[k] for k in range(part_ref.shape[0])]
    scales = [row_ref[k] for k in range(HALVES)]
    far = hidden_rows(
        parts, scales, row_ref[HALVES], group - rows, weight_ref, gate_ref, up_ref
    )
    chips = far.shape[0] // group
    slots = chips * rows
    near_at = own_ref[0] * slots
    far_at = slots - near_at
    hidden_ref[pl.ds(pl.multiple_of(near_at, 8), slots), :] = near_ref[...]
    for chip in range(0, chips, 2):
        pair = [far[k * group : k * group + rows] for k in (chip, chip + 1)]
        start = pl.multiple_of(far_at + chip * rows, 8)
        hidden_ref[pl.ds(start, 2 * rows), :] = jnp.concatenate(pair, axis=0)


def near_layer(gathered, weights, adapter_up, own, shard_rows, block, experts):
    rows = gathered.shape[0]
    columns = gathered.shape[1] - LANES
    units = weights[0].shape[1]
    chips = rows // (HALVES * shard_rows)
    flat = chips * (-(-shard_rows // HALVES // 8) * 8)
    out = jax.ShapeDtypeStruct((rows // 4, units), F32)
    vmem = pl.BlockSpec(memory_space=pltpu.VMEM)
    return pl.pallas_call(
        functools.partial(near_kernel, shard_rows, block),
        out_shape=(
            out,
            out,
            out,
            jax.ShapeDtypeStruct((experts * shard_rows, LANES), F32),
            jax.ShapeDtypeStruct((2 * HALVES, flat, columns), BF16),
            jax.ShapeDtypeStruct((HALVES + 1, flat, LANES), F32),
        ),
        in_specs=[pl.BlockSpec(memory_space=pltpu.SMEM)] + [vmem] * 4,
        out_specs=(vmem,) * 6,
        scratch_shapes=[
            pltpu.VMEM((2 * HALVES, columns, 2 * units), BF16),
            pltpu.VMEM((chips, NOTE_ROWS, LANES), F32),
        ],
        compiler_params=pltpu.CompilerParams(vmem_limit_bytes=24 * 2**20),
        cost_estimate=pl.CostEstimate(
            flops=4 * rows * columns * units,
            bytes_accessed=4 * rows * columns + 4 * columns * units,
            transcendentals=2 * rows * units,
        ),
    )(own, gathered, *weights, adapter_up)


def far_layer(parts, row_scales, weights, near, tensor, shard_rows):
    _, flat, columns = parts.shape
    slots, units = near.shape
    rows = shard_rows // HALVES
    vmem = pl.BlockSpec(memory_space=pltpu.VMEM)
    return pl.pallas_call(
        functools.partial(far_kernel, rows, flat * rows // slots),
        out_shape=jax.ShapeDtypeStruct((2 * slots, units), F32),
        in_specs=[pl.BlockSpec(memory_space=pltpu.SMEM)] + [vmem] * 5,
        out_specs=vmem,
        scratch_shapes=[pltpu.VMEM((2 * HALVES, columns, 2 * units), BF16)],
        compiler_params=pltpu.CompilerParams(vmem_limit_bytes=24 * 2**20),
        cost_estimate=pl.CostEstimate(
            flops=16 * flat * columns * units,
            bytes_accessed=8 * flat * columns + 16 * columns * units,
            transcendentals=2 * flat * units,
        ),
    )(tensor[None], parts, row_scales, *weights, near)


def norm_kernel(x_ref, out_ref):
    x = x_ref[...]
    mean = jnp.sum(jnp.sum(x * x, axis=0, keepdims=True), axis=1, keepdims=True) / x.size
    x = x * lax.rsqrt(mean + 1e-06)
    for k in range(x.shape[0]):
        out_ref[:, pl.ds(k * LANES, LANES)] = x[k : k + 1, :]


def norm_layer(pooled):
    vmem = pl.BlockSpec(memory_space=pltpu.VMEM)
    return pl.pallas_call(
        norm_kernel,
        out_shape=jax.ShapeDtypeStruct((1, pooled.size), F32),
        in_specs=[vmem],
        out_specs=vmem,
        compiler_params=pltpu.CompilerParams(vmem_limit_bytes=4 * 2**20),
    )(pooled)


def local(
    tokens,
    routes,
    chosen_expert_weight,
    expert_gate_weight,
    expert_up_weight,
    expert_down_weight,
    adapter_down_weight,
    adapter_up_weight,
    document_task_index,
    counts,
    final_norm_scale,
):
    rows, feats = tokens.shape
    seq = lax.axis_size(SEQ)
    experts = lax.axis_size(EXPERT)
    cores = lax.axis_size("c")
    groups = lax.axis_size(GROUP)
    tensors = lax.axis_size("t")
    capacity = rows * 5 // 16
    set_slots = capacity // tensors
    chip_rows = cores * set_slots
    shard_rows = HALVES * chip_rows
    width = feats * experts
    half = feats // cores
    columns = experts * half // HALVES
    slice_width = width // seq
    task_rows = adapter_down_weight.shape[0]
    s = lax.axis_index(SEQ)
    t = lax.axis_index("t")
    g = lax.axis_index(GROUP)
    per_feature_group = feats // slice_width
    own_group = s // per_feature_group

    ids = routes.T
    outgoing, notes = dispatch_layer(
        ids,
        chosen_expert_weight.T,
        tokens,
        adapter_down_weight,
        adapter_up_weight,
        final_norm_scale[None],
        experts,
        set_slots,
    )
    later_up, _ = lax.optimization_barrier((expert_up_weight[0], outgoing))
    other = [(k, tensors - 1 - k) for k in range(tensors)]
    far_weights = [lax.ppermute(w, "t", other) for w in (expert_gate_weight[0], later_up)]
    received = swap(outgoing, EXPERT + ("c",))

    sent, adapter_up, norm_scale = rows_layer(own_group, received, task_rows)
    sent = (sent + jnp.pad(notes, ((chip_rows, 0), (columns, 0)))).astype(F16)
    gathered = lax.all_gather(sent, SEQ, axis=0, tiled=False)
    gathered = gathered.astype(BF16).reshape(seq * shard_rows, columns + LANES)
    per_half = half // slice_width
    own_column = own_group * half + (s % per_half) * slice_width
    near, factor, base, combiner, parts, row_scales = near_layer(
        gathered,
        (expert_gate_weight[0], expert_up_weight[0]),
        adapter_up,
        jnp.stack(
            [
                (s // per_half) % cores,
                own_column // columns,
                own_column % columns,
                document_task_index[0],
                t,
                lax.axis_index(EXPERT),
                g,
            ]
        ),
        shard_rows,
        rows,
        experts,
    )
    hidden = far_layer(parts, row_scales, far_weights, near, t, shard_rows)

    units = hidden.shape[-1]
    hidden = hidden.astype(F16).reshape(tensors, -1, units)
    hidden = lax.all_gather(hidden, SEQ, axis=0, tiled=True)
    part = lax.dot_general(
        hidden.astype(BF16),
        expert_down_weight[0].reshape(seq * tensors, units, slice_width),
        (((0, 2), (0, 1)), ((), ())),
        preferred_element_type=F32,
    )
    payload = (part * factor + base).reshape(groups, chip_rows, slice_width)

    group_rows = cores * rows
    position = g * group_rows + jnp.arange(group_rows, dtype=jnp.int32)[None, :]
    counted = (position < counts[0]).astype(F32)
    payload, combiner, counted, norm_scale = lax.optimization_barrier(
        (payload, combiner, counted, norm_scale)
    )

    returned = swap(payload, GROUP)
    mixed = lax.dot_general(
        combiner,
        returned.reshape(groups * chip_rows, slice_width),
        (((0,), (0,)), ((), ())),
        precision=HIGH,
    )
    squares = jnp.sum(spread(jnp.sum(mixed * mixed, axis=1)[None], SEQ), axis=0)
    factor = counted * lax.rsqrt(squares / width + 1e-05)
    pooled = jnp.dot(factor, mixed, precision=HIGH) * norm_scale
    pooled = jnp.sum(spread(pooled, GROUP), axis=0)
    return norm_layer(spread(pooled, SEQ).reshape(seq, slice_width))


def solution(mesh):
    seq, experts, tensors = mesh.devices.shape
    parts = Mesh(
        mesh.devices.reshape(seq // 2, 2, experts // 2, 2, tensors), ("z", "c", "y", "h", "t")
    )
    return jax.shard_map(
        local,
        mesh=parts,
        in_specs=(
            P(SEQ, EXPERT),
            P(SEQ, None),
            P(SEQ, None),
            P(EXPERT, None, SEQ + ("t",)),
            P(EXPERT, None, SEQ + ("t",)),
            P(EXPERT, None, SEQ),
            P(None, EXPERT),
            P(None, EXPERT),
            P(),
            P(),
            P(EXPERT),
        ),
        out_specs=P(),
        check_vma=False,
    )
```

```python
import functools

import jax
import jax.numpy as jnp
from jax import lax
from jax.experimental import pallas as pl
from jax.experimental.pallas import tpu as pltpu
from jax.sharding import Mesh
from jax.sharding import PartitionSpec as P

TASK_COUNT = 2
ADAPTER_SCALE = 0.5

SEQ = ("z", "c")
EXPERT = ("y", "h")
GROUP = ("y", "h", "t")
HALVES = 2

BF16 = jnp.bfloat16
F16 = jnp.float16
F32 = jnp.float32
HIGH = lax.Precision.HIGHEST
LANES = 128
LEAST_EXPONENT = -40.0
NOTE_ROWS = 8
PART_STEP = 256.0
LOW_LANES = 32


def swap(x, axes):
    return lax.all_to_all(x, axes, split_axis=0, concat_axis=0, tiled=True)


def spread(x, axes):
    return swap(jnp.broadcast_to(x[None], (lax.axis_size(axes),) + x.shape), axes)


def rounded_parts(x):
    first = x.astype(BF16).astype(F32)
    rest = (x - first) * PART_STEP
    second = rest.astype(BF16).astype(F32)
    return first, second, (rest - second) * PART_STEP


def earlier_in_block(lanes, block):
    i = lax.broadcasted_iota(jnp.int32, (lanes, lanes), 0)
    j = lax.broadcasted_iota(jnp.int32, (lanes, lanes), 1)
    return ((i < j) & (i // block == j // block)).astype(F32).astype(BF16)


def slots_of(named, block):
    before = jnp.dot(
        named.astype(F32).astype(BF16),
        earlier_in_block(named.shape[1], block),
        preferred_element_type=F32,
    )
    return jnp.where(named, before, -1.0)


def block_of(shape, block):
    return (lax.broadcasted_iota(jnp.int32, shape, 1) // block).astype(F32)


def dispatch_kernel(*refs):
    out_ref, note_ref, held, sem = refs[6], refs[7], refs[8:14], refs[14]
    core, chip = lax.axis_index("c"), lax.axis_index("z")
    copies = [pltpu.make_async_copy(refs[k], held[k], sem.at[k]) for k in range(6)]
    for copy in copies:
        copy.start()
    for copy in copies:
        copy.wait()
    routes_ref, chosen_ref, tokens_ref, down_ref, up_ref, norm_ref = held
    targets, set_slots, _ = out_ref.shape
    experts = targets // HALVES
    rows, feats = tokens_ref.shape
    half = feats // HALVES
    ranks = down_ref.shape[0] // HALVES
    first_slot = (lax.axis_index("t") * set_slots).astype(F32)
    ids = routes_ref[...]
    notes = jnp.concatenate([ids.astype(F32)] + list(rounded_parts(chosen_ref[...])), axis=0)
    notes = jnp.concatenate([jnp.where(core == k, notes, 0.0) for k in range(HALVES)], axis=1)
    note_ref[...] = jnp.zeros_like(note_ref)
    note_ref[pl.ds(0, NOTE_ROWS), :] = notes
    expert = lax.broadcasted_iota(jnp.int32, (experts, rows), 0)
    place = slots_of((ids[:1] == expert) | (ids[1:] == expert), rows)
    padded = 16
    row = lax.broadcasted_iota(jnp.int32, (padded, rows), 0)
    slot = jnp.where(row < set_slots, row.astype(F32) + first_slot, -2.0)
    chooser = jnp.concatenate(
        [(place[e : e + 1] == slot).astype(F32) for e in range(experts)], axis=0
    ).astype(BF16)
    for c in range(HALVES):
        lanes = pl.ds(c * half, half)
        x = tokens_ref[:, lanes]
        low = lax.dot_general(
            x, down_ref[:, lanes], (((1,), (1,)), ((), ())), preferred_element_type=F32
        )
        first = low.astype(BF16)
        rest = low - first.astype(F32)
        second = rest.astype(BF16)
        third = (rest - second.astype(F32)).astype(BF16)
        x = jnp.concatenate([x, jnp.zeros_like(first), first, second, third], axis=1)
        chosen = jnp.dot(chooser, x, preferred_element_type=F32)
        column = pl.multiple_of((chip * HALVES + c) % (feats // LANES) * LANES, LANES)
        norm = norm_ref[:, pl.ds(column, LANES)]
        norm_first = norm.astype(BF16).astype(F32)
        norm_rest = norm - norm_first
        norm_second = norm_rest.astype(BF16).astype(F32)
        up_rows = up_ref[pl.ds(pl.multiple_of(core * ranks, ranks), ranks), pl.ds(column, LANES)]
        up_rows = up_rows.astype(F32)
        small = [
            up_rows[:set_slots],
            jnp.concatenate(
                [
                    up_rows[set_slots:],
                    norm_first,
                    norm_second,
                    norm_rest - norm_second,
                    jnp.zeros((2 * set_slots - ranks - 3, LANES), F32),
                ],
                axis=0,
            ),
        ]
        small = jnp.concatenate(small, axis=1).astype(BF16)
        for e in range(experts):
            out_ref[e * HALVES + c, :, pl.ds(0, half + LANES)] = chosen[
                e * padded : e * padded + set_slots
            ].astype(BF16)
            out_ref[e * HALVES + c, :, pl.ds(half + LANES, 2 * LANES)] = small


def dispatch_layer(
    routes, chosen, tokens, adapter_down, adapter_up, norm_scale, experts, set_slots
):
    rows, feats = tokens.shape
    lanes = feats // HALVES + 3 * LANES
    operands = (routes, chosen, tokens, adapter_down, adapter_up, norm_scale)
    return pl.pallas_call(
        dispatch_kernel,
        out_shape=(
            jax.ShapeDtypeStruct((experts * HALVES, set_slots, lanes), BF16),
            jax.ShapeDtypeStruct((HALVES * set_slots, LANES), F32),
        ),
        in_specs=[pl.BlockSpec(memory_space=pltpu.HBM)] * len(operands),
        out_specs=(pl.BlockSpec(memory_space=pltpu.VMEM),) * 2,
        scratch_shapes=[pltpu.VMEM(x.shape, x.dtype) for x in operands]
        + [pltpu.SemaphoreType.DMA((len(operands),))],
        compiler_params=pltpu.CompilerParams(vmem_limit_bytes=57 * 2**20),
        cost_estimate=pl.CostEstimate(
            flops=4 * rows * feats * experts * set_slots,
            bytes_accessed=2 * rows * feats + 2 * experts * HALVES * set_slots * lanes,
            transcendentals=0,
        ),
    )(*operands)


def rows_kernel(own_ref, received_ref, sent_ref, adapter_ref, norm_ref):
    messages, set_slots, _ = received_ref.shape
    groups = messages // HALVES
    half = 2 * LANES
    rows = HALVES * set_slots
    columns = sent_ref.shape[1] - LANES
    ranks = adapter_ref.shape[0] // HALVES

    def both(e, first, lanes):
        return jnp.concatenate(
            [
                received_ref[e * HALVES + c, :, pl.ds(first, lanes)].astype(F32)
                for c in range(HALVES)
            ],
            axis=0,
        )

    x = jnp.concatenate([both(e, 0, half) for e in range(groups)], axis=1)
    largest = jnp.max(jnp.abs(x), axis=1, keepdims=True)
    exponent = jnp.maximum(
        jnp.floor(jnp.log2(jnp.maximum(largest, 1e-30)) + 1.01), LEAST_EXPONENT
    )
    x = x * jnp.exp2(15.0 - exponent)
    low = sum(both(e, half, LANES) for e in range(groups))
    low = sum(low[:, k * LOW_LANES : (k + 1) * LOW_LANES] for k in range(1, 4))
    low = low * jnp.exp2(7.0 - exponent)
    sent_ref[pl.ds(0, rows), pl.ds(0, columns)] = x[:, :columns]
    sent_ref[pl.ds(rows, rows), pl.ds(0, columns)] = x[:, columns:]
    sent_ref[pl.ds(0, rows), pl.ds(columns, LANES)] = jnp.concatenate(
        [jnp.broadcast_to(exponent, low.shape)] + list(rounded_parts(low)), axis=1
    )
    sent_ref[pl.ds(rows, rows), pl.ds(columns, LANES)] = jnp.zeros((rows, LANES), F32)

    adapter = []
    for c in range(HALVES):
        small = received_ref[own_ref[0] * HALVES + c, :, pl.ds(half + LANES, 2 * LANES)]
        small = small.astype(F32)
        small = jnp.concatenate([small[:, :LANES], small[:, LANES:]], axis=0)
        adapter.append(small[:ranks])
        if c == 0:
            norm_ref[...] = (
                small[ranks : ranks + 1] + small[ranks + 1 : ranks + 2]
            ) + small[ranks + 2 : ranks + 3]
    adapter_ref[...] = jnp.concatenate(adapter, axis=0).astype(BF16)


def rows_layer(own_group, received, task_rows):
    messages, set_slots, _ = received.shape
    rows = HALVES * set_slots
    vmem = pl.BlockSpec(memory_space=pltpu.VMEM)
    columns = messages // HALVES * 2 * LANES // HALVES
    return pl.pallas_call(
        rows_kernel,
        out_shape=(
            jax.ShapeDtypeStruct((HALVES * rows, columns + LANES), F32),
            jax.ShapeDtypeStruct((task_rows, LANES), BF16),
            jax.ShapeDtypeStruct((1, LANES), F32),
        ),
        in_specs=[pl.BlockSpec(memory_space=pltpu.SMEM), vmem],
        out_specs=(vmem, vmem, vmem),
        compiler_params=pltpu.CompilerParams(vmem_limit_bytes=8 * 2**20),
        cost_estimate=pl.CostEstimate(
            flops=8 * rows * columns, bytes_accessed=8 * rows * columns, transcendentals=4 * rows
        ),
    )(own_group[None], received)


def hidden_rows(parts, scales, shrink, shift, weight_ref, gate_ref, up_ref):
    units = gate_ref.shape[1]
    half = 2 * LANES
    flat, columns = parts[0].shape
    blocks = columns // half
    acts = jnp.zeros((flat, 2 * units), F32)
    for c in range(HALVES):
        half_acts = jnp.zeros((flat, 2 * units), F32)
        for q in range(HALVES):
            for n in range(blocks):
                source = pl.ds(((q * blocks + n) * HALVES + c) * half, half)
                target = pl.ds(n * half, half)
                for k, ref in enumerate((gate_ref, up_ref)):
                    weight_ref[c * HALVES + q, target, pl.ds(k * units, units)] = ref[source, :]
            product = jnp.dot(
                parts[c * HALVES + q],
                weight_ref[c * HALVES + q],
                preferred_element_type=F32,
            )
            half_acts += product if q == 0 else pltpu.roll(product, flat - shift, 0)
        acts += half_acts * jnp.concatenate([scales[c]] * 2, axis=1)
    gate_act, up_act = acts[:, :units], acts[:, units:]
    value = (gate_act / (1.0 + jnp.exp(-gate_act)) * up_act).astype(BF16).astype(F32)
    return value * shrink


class Rows:
    def __init__(self, x_ref, shard_rows):
        self.x_ref = x_ref
        self.shard_rows = shard_rows
        self.rows = shard_rows // HALVES
        self.group = -(-self.rows // 8) * 8
        self.chips = x_ref.shape[0] // (HALVES * shard_rows)
        self.flat = self.chips * self.group
        self.columns = x_ref.shape[1] - LANES
        x = x_ref[:, pl.ds(0, self.columns)].astype(F32)
        self.parts = [
            self.part(x, c, q).astype(BF16) for c in range(HALVES) for q in range(HALVES)
        ]
        self.beside = x_ref[:, pl.ds(self.columns, LANES)].astype(F32)
        exponents = [self.part(self.beside, c, 0)[:, :LOW_LANES] for c in range(HALVES)]
        exponents = [jnp.concatenate([e] * (LANES // LOW_LANES), axis=1) for e in exponents]
        self.scales = [jnp.exp2(e - 15.0) for e in exponents]
        self.row_exponent = jnp.maximum(*exponents)

    def part(self, value, c, q):
        value = value.reshape(self.chips, HALVES, self.shard_rows, value.shape[-1])[:, c]
        value = value[:, : self.group] if q == 0 else value[:, self.shard_rows - self.group :]
        return value.reshape(self.flat, value.shape[-1])

    def aligned(self, value, q):
        return value if q == 0 else pltpu.roll(value, self.flat - (self.group - self.rows), 0)

    def of_chip(self, chip):
        source = slice(chip * self.group, chip * self.group + self.rows)
        return source, pl.ds(chip * self.rows, self.rows)


def near_kernel(
    shard_rows,
    block,
    own_ref,
    x_ref,
    gate_ref,
    up_ref,
    adapter_ref,
    hidden_ref,
    factor_ref,
    base_ref,
    combiner_ref,
    part_ref,
    row_ref,
    weight_ref,
    note_ref,
):
    r = Rows(x_ref, shard_rows)
    task_rows = adapter_ref.shape[0]
    own_core, own_quarter = own_ref[0], own_ref[1]
    own_column = pl.multiple_of(own_ref[2], LANES)
    task, tensor, expert = own_ref[3], own_ref[4], own_ref[5]
    shrink = jnp.exp2(-2.0 * r.row_exponent - 2.0)
    for k in range(len(r.parts)):
        part_ref[k] = r.parts[k]
    for k, value in enumerate(r.scales + [shrink]):
        row_ref[k] = value
    hidden = hidden_rows(
        r.parts, r.scales, shrink, r.group - r.rows, weight_ref, gate_ref, up_ref
    )

    own = x_ref[:, pl.ds(own_column, LANES)].astype(F32)
    low = jnp.zeros((r.flat, LOW_LANES), F32)
    residual = jnp.zeros((r.flat, LANES), F32)
    for c in range(HALVES):
        tile = r.part(r.beside, c, 0)
        low_part = tile[:, LOW_LANES : 2 * LOW_LANES] + (
            tile[:, 2 * LOW_LANES : 3 * LOW_LANES] + tile[:, 3 * LOW_LANES :] / PART_STEP
        ) / PART_STEP
        low += low_part * jnp.exp2(tile[:, :LOW_LANES] - 7.0)
        for q in range(HALVES):
            mine = (own_core == c) & (own_quarter == q)
            residual += jnp.where(mine, r.aligned(r.part(own, c, q), q) * r.scales[c], 0.0)
    low_lane = lax.broadcasted_iota(jnp.int32, low.shape, 1) // (task_rows // TASK_COUNT)
    low = jnp.where(low_lane == task, low, 0.0).astype(BF16)
    base = residual + ADAPTER_SCALE * jnp.dot(
        low, adapter_ref[...], preferred_element_type=F32
    )
    up_scale = jnp.exp2(2.0 * r.row_exponent + 2.0)

    notes = sum(r.aligned(r.part(r.beside, c, 1), 1) for c in range(HALVES))
    notes = notes.reshape(r.chips, r.group, LANES)[:, :NOTE_ROWS]
    note_ref[...] = notes
    first, second = notes[:, 0, :].astype(jnp.int32), notes[:, 1, :].astype(jnp.int32)
    weight = [
        notes[:, k + 2, :] + (notes[:, k + 4, :] + notes[:, k + 6, :] / PART_STEP) / PART_STEP
        for k in range(2)
    ]
    set_slots = r.rows // HALVES
    slot = slots_of((first == expert) | (second == expert), block)
    slot = slot - (tensor * set_slots).astype(F32)
    in_set = (slot >= 0.0) & (slot < set_slots)
    place = jnp.where(in_set, slot + set_slots * block_of(slot.shape, block), -1.0)
    weight = jnp.where(first == expert, weight[0], weight[1])
    row = lax.broadcasted_iota(jnp.int32, (r.group, LANES), 0).astype(F32)
    for chip in range(r.chips):
        source, target = r.of_chip(chip)
        slot_weight = jnp.sum(
            jnp.where(place[chip : chip + 1] == row, weight[chip : chip + 1], 0.0),
            axis=1,
            keepdims=True,
        )[: r.rows]
        hidden_ref[target, :] = hidden[source]
        factor_ref[target, :] = slot_weight * up_scale[source]
        base_ref[target, :] = 0.5 * base[source]

    ids = note_ref[own_ref[6]][:2].astype(jnp.int32)
    experts = combiner_ref.shape[0] // (2 * r.rows)
    named = lax.broadcasted_iota(jnp.int32, (experts, LANES), 0)
    slot = slots_of((ids[:1] == named) | (ids[1:] == named), block)
    slot_set = jnp.floor(slot / set_slots)
    place = jnp.where(
        slot >= 0.0,
        slot + slot_set * (r.rows - set_slots) + set_slots * block_of(slot.shape, block),
        -1.0,
    )
    row = lax.broadcasted_iota(jnp.int32, (2 * r.rows, LANES), 0).astype(F32)
    for e in range(experts):
        combiner_ref[pl.ds(e * 2 * r.rows, 2 * r.rows), :] = (place[e : e + 1] == row).astype(F32)


def far_kernel(
    rows, group, own_ref, part_ref, row_ref, gate_ref, up_ref, near_ref, hidden_ref, weight_ref
):
    parts = [part_ref[k] for k in range(part_ref.shape[0])]
    scales = [row_ref[k] for k in range(HALVES)]
    far = hidden_rows(
        parts, scales, row_ref[HALVES], group - rows, weight_ref, gate_ref, up_ref
    )
    chips = far.shape[0] // group
    slots = chips * rows
    near_at = own_ref[0] * slots
    far_at = slots - near_at
    hidden_ref[pl.ds(pl.multiple_of(near_at, 8), slots), :] = near_ref[...]
    for chip in range(0, chips, 2):
        pair = [far[k * group : k * group + rows] for k in (chip, chip + 1)]
        start = pl.multiple_of(far_at + chip * rows, 8)
        hidden_ref[pl.ds(start, 2 * rows), :] = jnp.concatenate(pair, axis=0)


def near_layer(gathered, weights, adapter_up, own, shard_rows, block, experts):
    rows = gathered.shape[0]
    columns = gathered.shape[1] - LANES
    units = weights[0].shape[1]
    chips = rows // (HALVES * shard_rows)
    flat = chips * (-(-shard_rows // HALVES // 8) * 8)
    out = jax.ShapeDtypeStruct((rows // 4, units), F32)
    vmem = pl.BlockSpec(memory_space=pltpu.VMEM)
    return pl.pallas_call(
        functools.partial(near_kernel, shard_rows, block),
        out_shape=(
            out,
            out,
            out,
            jax.ShapeDtypeStruct((experts * shard_rows, LANES), F32),
            jax.ShapeDtypeStruct((2 * HALVES, flat, columns), BF16),
            jax.ShapeDtypeStruct((HALVES + 1, flat, LANES), F32),
        ),
        in_specs=[pl.BlockSpec(memory_space=pltpu.SMEM)] + [vmem] * 4,
        out_specs=(vmem,) * 6,
        scratch_shapes=[
            pltpu.VMEM((2 * HALVES, columns, 2 * units), BF16),
            pltpu.VMEM((chips, NOTE_ROWS, LANES), F32),
        ],
        compiler_params=pltpu.CompilerParams(vmem_limit_bytes=16 * 2**20),
        cost_estimate=pl.CostEstimate(
            flops=4 * rows * columns * units,
            bytes_accessed=4 * rows * columns + 4 * columns * units,
            transcendentals=2 * rows * units,
        ),
    )(own, gathered, *weights, adapter_up)


def far_layer(parts, row_scales, weights, near, tensor, shard_rows):
    _, flat, columns = parts.shape
    slots, units = near.shape
    rows = shard_rows // HALVES
    vmem = pl.BlockSpec(memory_space=pltpu.VMEM)
    return pl.pallas_call(
        functools.partial(far_kernel, rows, flat * rows // slots),
        out_shape=jax.ShapeDtypeStruct((2 * slots, units), F32),
        in_specs=[pl.BlockSpec(memory_space=pltpu.SMEM)] + [vmem] * 5,
        out_specs=vmem,
        scratch_shapes=[pltpu.VMEM((2 * HALVES, columns, 2 * units), BF16)],
        compiler_params=pltpu.CompilerParams(vmem_limit_bytes=10 * 2**20),
        cost_estimate=pl.CostEstimate(
            flops=16 * flat * columns * units,
            bytes_accessed=8 * flat * columns + 16 * columns * units,
            transcendentals=2 * flat * units,
        ),
    )(tensor[None], parts, row_scales, *weights, near)


def norm_kernel(x_ref, out_ref):
    x = x_ref[...]
    mean = jnp.sum(jnp.sum(x * x, axis=0, keepdims=True), axis=1, keepdims=True) / x.size
    x = x * lax.rsqrt(mean + 1e-06)
    for k in range(x.shape[0]):
        out_ref[:, pl.ds(k * LANES, LANES)] = x[k : k + 1, :]


def norm_layer(pooled):
    vmem = pl.BlockSpec(memory_space=pltpu.VMEM)
    return pl.pallas_call(
        norm_kernel,
        out_shape=jax.ShapeDtypeStruct((1, pooled.size), F32),
        in_specs=[vmem],
        out_specs=vmem,
        compiler_params=pltpu.CompilerParams(vmem_limit_bytes=4 * 2**20),
    )(pooled)


def local(
    tokens,
    routes,
    chosen_expert_weight,
    expert_gate_weight,
    expert_up_weight,
    expert_down_weight,
    adapter_down_weight,
    adapter_up_weight,
    document_task_index,
    counts,
    final_norm_scale,
):
    rows, feats = tokens.shape
    seq = lax.axis_size(SEQ)
    experts = lax.axis_size(EXPERT)
    cores = lax.axis_size("c")
    groups = lax.axis_size(GROUP)
    tensors = lax.axis_size("t")
    capacity = rows * 5 // 16
    set_slots = capacity // tensors
    chip_rows = cores * set_slots
    shard_rows = HALVES * chip_rows
    width = feats * experts
    half = feats // cores
    columns = experts * half // HALVES
    slice_width = width // seq
    task_rows = adapter_down_weight.shape[0]
    s = lax.axis_index(SEQ)
    t = lax.axis_index("t")
    g = lax.axis_index(GROUP)
    per_feature_group = feats // slice_width
    own_group = s // per_feature_group

    ids = routes.T
    outgoing, notes = dispatch_layer(
        ids,
        chosen_expert_weight.T,
        tokens,
        adapter_down_weight,
        adapter_up_weight,
        final_norm_scale[None],
        experts,
        set_slots,
    )
    later_weights, _ = lax.optimization_barrier(
        ((expert_gate_weight[0], expert_up_weight[0]), outgoing)
    )
    other = [(k, tensors - 1 - k) for k in range(tensors)]
    far_weights = [lax.ppermute(w, "t", other) for w in later_weights]
    received = swap(outgoing, EXPERT + ("c",))

    sent, adapter_up, norm_scale = rows_layer(own_group, received, task_rows)
    sent = (sent + jnp.pad(notes, ((chip_rows, 0), (columns, 0)))).astype(F16)
    gathered = lax.all_gather(sent, SEQ, axis=0, tiled=False)
    gathered = gathered.astype(BF16).reshape(seq * shard_rows, columns + LANES)
    per_half = half // slice_width
    own_column = own_group * half + (s % per_half) * slice_width
    near, factor, base, combiner, parts, row_scales = near_layer(
        gathered,
        (expert_gate_weight[0], expert_up_weight[0]),
        adapter_up,
        jnp.stack(
            [
                (s // per_half) % cores,
                own_column // columns,
                own_column % columns,
                document_task_index[0],
                t,
                lax.axis_index(EXPERT),
                g,
            ]
        ),
        shard_rows,
        rows,
        experts,
    )
    hidden = far_layer(parts, row_scales, far_weights, near, t, shard_rows)

    units = hidden.shape[-1]
    hidden = hidden.astype(F16).reshape(tensors, -1, units)
    hidden = lax.all_gather(hidden, SEQ, axis=0, tiled=True)
    hidden, down = lax.optimization_barrier((hidden, expert_down_weight[0]))
    part = lax.dot_general(
        hidden.astype(BF16),
        down.reshape(seq * tensors, units, slice_width),
        (((0, 2), (0, 1)), ((), ())),
        preferred_element_type=F32,
    )
    payload = (part * factor + base).reshape(groups, chip_rows, slice_width)

    group_rows = cores * rows
    position = g * group_rows + jnp.arange(group_rows, dtype=jnp.int32)[None, :]
    counted = (position < counts[0]).astype(F32)
    payload, combiner, counted, norm_scale = lax.optimization_barrier(
        (payload, combiner, counted, norm_scale)
    )

    returned = swap(payload, GROUP)
    mixed = lax.dot_general(
        combiner,
        returned.reshape(groups * chip_rows, slice_width),
        (((0,), (0,)), ((), ())),
        precision=HIGH,
    )
    squares = jnp.sum(spread(jnp.sum(mixed * mixed, axis=1)[None], SEQ), axis=0)
    factor = counted * lax.rsqrt(squares / width + 1e-05)
    pooled = jnp.dot(factor, mixed, precision=HIGH) * norm_scale
    pooled = jnp.sum(spread(pooled, GROUP), axis=0)
    return norm_layer(spread(pooled, SEQ).reshape(seq, slice_width))


def solution(mesh):
    seq, experts, tensors = mesh.devices.shape
    parts = Mesh(
        mesh.devices.reshape(seq // 2, 2, experts // 2, 2, tensors), ("z", "c", "y", "h", "t")
    )
    return jax.shard_map(
        local,
        mesh=parts,
        in_specs=(
            P(SEQ, EXPERT),
            P(SEQ, None),
            P(SEQ, None),
            P(EXPERT, None, SEQ + ("t",)),
            P(EXPERT, None, SEQ + ("t",)),
            P(EXPERT, None, SEQ),
            P(None, EXPERT),
            P(None, EXPERT),
            P(),
            P(),
            P(EXPERT),
        ),
        out_specs=P(),
        check_vma=False,
    )
```

```python
import functools

import jax
import jax.numpy as jnp
from jax import lax
from jax.experimental import pallas as pl
from jax.experimental.pallas import tpu as pltpu
from jax.sharding import Mesh
from jax.sharding import PartitionSpec as P

TASK_COUNT = 2
ADAPTER_SCALE = 0.5

SEQ = ("z", "c")
EXPERT = ("y", "h")
GROUP = ("y", "h", "t")
HALVES = 2

BF16 = jnp.bfloat16
F16 = jnp.float16
F32 = jnp.float32
HIGH = lax.Precision.HIGHEST
LANES = 128
LEAST_EXPONENT = -40.0
NOTE_ROWS = 8
PART_STEP = 256.0
LOW_LANES = 32


def swap(x, axes):
    return lax.all_to_all(x, axes, split_axis=0, concat_axis=0, tiled=True)


def spread(x, axes):
    return swap(jnp.broadcast_to(x[None], (lax.axis_size(axes),) + x.shape), axes)


def rounded_parts(x):
    first = x.astype(BF16).astype(F32)
    rest = (x - first) * PART_STEP
    second = rest.astype(BF16).astype(F32)
    return first, second, (rest - second) * PART_STEP


def earlier_in_block(lanes, block):
    i = lax.broadcasted_iota(jnp.int32, (lanes, lanes), 0)
    j = lax.broadcasted_iota(jnp.int32, (lanes, lanes), 1)
    return ((i < j) & (i // block == j // block)).astype(F32).astype(BF16)


def slots_of(named, block):
    before = jnp.dot(
        named.astype(F32).astype(BF16),
        earlier_in_block(named.shape[1], block),
        preferred_element_type=F32,
    )
    return jnp.where(named, before, -1.0)


def block_of(shape, block):
    return (lax.broadcasted_iota(jnp.int32, shape, 1) // block).astype(F32)


def dispatch_kernel(*refs):
    out_ref, note_ref, held, sem = refs[6], refs[7], refs[8:14], refs[14]
    core, chip = lax.axis_index("c"), lax.axis_index("z")
    copies = [pltpu.make_async_copy(refs[k], held[k], sem.at[k]) for k in range(6)]
    for copy in copies:
        copy.start()
    for copy in copies:
        copy.wait()
    routes_ref, chosen_ref, tokens_ref, down_ref, up_ref, norm_ref = held
    targets, set_slots, _ = out_ref.shape
    experts = targets // HALVES
    rows, feats = tokens_ref.shape
    half = feats // HALVES
    ranks = down_ref.shape[0] // HALVES
    first_slot = (lax.axis_index("t") * set_slots).astype(F32)
    ids = routes_ref[...]
    notes = jnp.concatenate([ids.astype(F32)] + list(rounded_parts(chosen_ref[...])), axis=0)
    notes = jnp.concatenate([jnp.where(core == k, notes, 0.0) for k in range(HALVES)], axis=1)
    note_ref[...] = jnp.zeros_like(note_ref)
    note_ref[pl.ds(0, NOTE_ROWS), :] = notes
    expert = lax.broadcasted_iota(jnp.int32, (experts, rows), 0)
    place = slots_of((ids[:1] == expert) | (ids[1:] == expert), rows)
    padded = 16
    row = lax.broadcasted_iota(jnp.int32, (padded, rows), 0)
    slot = jnp.where(row < set_slots, row.astype(F32) + first_slot, -2.0)
    chooser = jnp.concatenate(
        [(place[e : e + 1] == slot).astype(F32) for e in range(experts)], axis=0
    ).astype(BF16)
    for c in range(HALVES):
        lanes = pl.ds(c * half, half)
        x = tokens_ref[:, lanes]
        low = lax.dot_general(
            x, down_ref[:, lanes], (((1,), (1,)), ((), ())), preferred_element_type=F32
        )
        first = low.astype(BF16)
        rest = low - first.astype(F32)
        second = rest.astype(BF16)
        third = (rest - second.astype(F32)).astype(BF16)
        x = jnp.concatenate([x, jnp.zeros_like(first), first, second, third], axis=1)
        chosen = jnp.dot(chooser, x, preferred_element_type=F32)
        column = pl.multiple_of((chip * HALVES + c) % (feats // LANES) * LANES, LANES)
        norm = norm_ref[:, pl.ds(column, LANES)]
        norm_first = norm.astype(BF16).astype(F32)
        norm_rest = norm - norm_first
        norm_second = norm_rest.astype(BF16).astype(F32)
        up_rows = up_ref[pl.ds(pl.multiple_of(core * ranks, ranks), ranks), pl.ds(column, LANES)]
        up_rows = up_rows.astype(F32)
        small = [
            up_rows[:set_slots],
            jnp.concatenate(
                [
                    up_rows[set_slots:],
                    norm_first,
                    norm_second,
                    norm_rest - norm_second,
                    jnp.zeros((2 * set_slots - ranks - 3, LANES), F32),
                ],
                axis=0,
            ),
        ]
        small = jnp.concatenate(small, axis=1).astype(BF16)
        for e in range(experts):
            out_ref[e * HALVES + c, :, pl.ds(0, half + LANES)] = chosen[
                e * padded : e * padded + set_slots
            ].astype(BF16)
            out_ref[e * HALVES + c, :, pl.ds(half + LANES, 2 * LANES)] = small


def dispatch_layer(
    routes, chosen, tokens, adapter_down, adapter_up, norm_scale, experts, set_slots
):
    rows, feats = tokens.shape
    lanes = feats // HALVES + 3 * LANES
    operands = (routes, chosen, tokens, adapter_down, adapter_up, norm_scale)
    return pl.pallas_call(
        dispatch_kernel,
        out_shape=(
            jax.ShapeDtypeStruct((experts * HALVES, set_slots, lanes), BF16),
            jax.ShapeDtypeStruct((HALVES * set_slots, LANES), F32),
        ),
        in_specs=[pl.BlockSpec(memory_space=pltpu.HBM)] * len(operands),
        out_specs=(pl.BlockSpec(memory_space=pltpu.VMEM),) * 2,
        scratch_shapes=[pltpu.VMEM(x.shape, x.dtype) for x in operands]
        + [pltpu.SemaphoreType.DMA((len(operands),))],
        compiler_params=pltpu.CompilerParams(vmem_limit_bytes=57 * 2**20),
        cost_estimate=pl.CostEstimate(
            flops=4 * rows * feats * experts * set_slots,
            bytes_accessed=2 * rows * feats + 2 * experts * HALVES * set_slots * lanes,
            transcendentals=0,
        ),
    )(*operands)


def rows_kernel(own_ref, received_ref, sent_ref, adapter_ref, norm_ref):
    messages, set_slots, _ = received_ref.shape
    groups = messages // HALVES
    half = 2 * LANES
    rows = HALVES * set_slots
    columns = sent_ref.shape[1] - LANES
    ranks = adapter_ref.shape[0] // HALVES

    def both(e, first, lanes):
        return jnp.concatenate(
            [
                received_ref[e * HALVES + c, :, pl.ds(first, lanes)].astype(F32)
                for c in range(HALVES)
            ],
            axis=0,
        )

    x = jnp.concatenate([both(e, 0, half) for e in range(groups)], axis=1)
    largest = jnp.max(jnp.abs(x), axis=1, keepdims=True)
    exponent = jnp.maximum(
        jnp.floor(jnp.log2(jnp.maximum(largest, 1e-30)) + 1.01), LEAST_EXPONENT
    )
    x = x * jnp.exp2(15.0 - exponent)
    low = sum(both(e, half, LANES) for e in range(groups))
    low = sum(low[:, k * LOW_LANES : (k + 1) * LOW_LANES] for k in range(1, 4))
    low = low * jnp.exp2(7.0 - exponent)
    beside = jnp.concatenate(
        [jnp.broadcast_to(exponent, low.shape)] + list(rounded_parts(low)), axis=1
    )
    sent_ref[:, pl.ds(0, columns)] = jnp.concatenate([x[:, :columns], x[:, columns:]], axis=0)
    sent_ref[:, pl.ds(columns, LANES)] = jnp.concatenate(
        [beside, jnp.zeros_like(beside)], axis=0
    )

    adapter = []
    for c in range(HALVES):
        small = received_ref[own_ref[0] * HALVES + c, :, pl.ds(half + LANES, 2 * LANES)]
        small = small.astype(F32)
        small = jnp.concatenate([small[:, :LANES], small[:, LANES:]], axis=0)
        adapter.append(small[:ranks])
        if c == 0:
            norm_ref[...] = (
                small[ranks : ranks + 1] + small[ranks + 1 : ranks + 2]
            ) + small[ranks + 2 : ranks + 3]
    adapter_ref[...] = jnp.concatenate(adapter, axis=0).astype(BF16)


def rows_layer(own_group, received, task_rows):
    messages, set_slots, _ = received.shape
    rows = HALVES * set_slots
    vmem = pl.BlockSpec(memory_space=pltpu.VMEM)
    columns = messages // HALVES * 2 * LANES // HALVES
    return pl.pallas_call(
        rows_kernel,
        out_shape=(
            jax.ShapeDtypeStruct((HALVES * rows, columns + LANES), F32),
            jax.ShapeDtypeStruct((task_rows, LANES), BF16),
            jax.ShapeDtypeStruct((1, LANES), F32),
        ),
        in_specs=[pl.BlockSpec(memory_space=pltpu.SMEM), vmem],
        out_specs=(vmem, vmem, vmem),
        compiler_params=pltpu.CompilerParams(vmem_limit_bytes=8 * 2**20),
        cost_estimate=pl.CostEstimate(
            flops=8 * rows * columns, bytes_accessed=8 * rows * columns, transcendentals=4 * rows
        ),
    )(own_group[None], received)


def hidden_rows(parts, scales, shrink, shift, weight_ref, gate_ref, up_ref):
    units = gate_ref.shape[1]
    half = 2 * LANES
    flat, columns = parts[0].shape
    blocks = columns // half
    acts = jnp.zeros((flat, 2 * units), F32)
    for c in range(HALVES):
        half_acts = jnp.zeros((flat, 2 * units), F32)
        for q in range(HALVES):
            for n in range(blocks):
                source = pl.ds(((q * blocks + n) * HALVES + c) * half, half)
                target = pl.ds(n * half, half)
                for k, ref in enumerate((gate_ref, up_ref)):
                    weight_ref[c * HALVES + q, target, pl.ds(k * units, units)] = ref[source, :]
            product = jnp.dot(
                parts[c * HALVES + q],
                weight_ref[c * HALVES + q],
                preferred_element_type=F32,
            )
            half_acts += product if q == 0 else pltpu.roll(product, flat - shift, 0)
        acts += half_acts * jnp.concatenate([scales[c]] * 2, axis=1)
    gate_act, up_act = acts[:, :units], acts[:, units:]
    value = (gate_act / (1.0 + jnp.exp(-gate_act)) * up_act).astype(BF16).astype(F32)
    return value * shrink


class Rows:
    def __init__(self, x_ref, shard_rows):
        self.x_ref = x_ref
        self.shard_rows = shard_rows
        self.rows = shard_rows // HALVES
        self.group = -(-self.rows // 8) * 8
        self.chips = x_ref.shape[0] // (HALVES * shard_rows)
        self.flat = self.chips * self.group
        self.columns = x_ref.shape[1] - LANES
        x = x_ref[:, pl.ds(0, self.columns)].astype(F32)
        self.parts = [
            self.part(x, c, q).astype(BF16) for c in range(HALVES) for q in range(HALVES)
        ]
        self.beside = x_ref[:, pl.ds(self.columns, LANES)].astype(F32)
        exponents = [self.part(self.beside, c, 0)[:, :LOW_LANES] for c in range(HALVES)]
        exponents = [jnp.concatenate([e] * (LANES // LOW_LANES), axis=1) for e in exponents]
        self.scales = [jnp.exp2(e - 15.0) for e in exponents]
        self.row_exponent = jnp.maximum(*exponents)

    def part(self, value, c, q):
        value = value.reshape(self.chips, HALVES, self.shard_rows, value.shape[-1])[:, c]
        value = value[:, : self.group] if q == 0 else value[:, self.shard_rows - self.group :]
        return value.reshape(self.flat, value.shape[-1])

    def aligned(self, value, q):
        return value if q == 0 else pltpu.roll(value, self.flat - (self.group - self.rows), 0)

    def of_chips(self, value, chips):
        return jnp.concatenate(
            [value[k * self.group : k * self.group + self.rows] for k in chips], axis=0
        )


def near_kernel(
    shard_rows,
    block,
    own_ref,
    x_ref,
    gate_ref,
    up_ref,
    adapter_ref,
    hidden_ref,
    factor_ref,
    base_ref,
    combiner_ref,
    part_ref,
    row_ref,
    weight_ref,
    note_ref,
):
    r = Rows(x_ref, shard_rows)
    task_rows = adapter_ref.shape[0]
    own_core, own_quarter = own_ref[0], own_ref[1]
    own_column = pl.multiple_of(own_ref[2], LANES)
    task, tensor, expert = own_ref[3], own_ref[4], own_ref[5]
    shrink = jnp.exp2(-2.0 * r.row_exponent - 2.0)
    for k in range(len(r.parts)):
        part_ref[k] = r.parts[k]
    for k, value in enumerate(r.scales + [shrink]):
        row_ref[k] = value
    hidden = hidden_rows(
        r.parts, r.scales, shrink, r.group - r.rows, weight_ref, gate_ref, up_ref
    )

    own = x_ref[:, pl.ds(own_column, LANES)].astype(F32)
    low = jnp.zeros((r.flat, LOW_LANES), F32)
    residual = jnp.zeros((r.flat, LANES), F32)
    for c in range(HALVES):
        tile = r.part(r.beside, c, 0)
        low_part = tile[:, LOW_LANES : 2 * LOW_LANES] + (
            tile[:, 2 * LOW_LANES : 3 * LOW_LANES] + tile[:, 3 * LOW_LANES :] / PART_STEP
        ) / PART_STEP
        low += low_part * jnp.exp2(tile[:, :LOW_LANES] - 7.0)
        for q in range(HALVES):
            mine = (own_core == c) & (own_quarter == q)
            residual += jnp.where(mine, r.aligned(r.part(own, c, q), q) * r.scales[c], 0.0)
    low_lane = lax.broadcasted_iota(jnp.int32, low.shape, 1) // (task_rows // TASK_COUNT)
    low = jnp.where(low_lane == task, low, 0.0).astype(BF16)
    base = residual + ADAPTER_SCALE * jnp.dot(
        low, adapter_ref[...], preferred_element_type=F32
    )
    up_scale = jnp.exp2(2.0 * r.row_exponent + 2.0)

    notes = sum(r.aligned(r.part(r.beside, c, 1), 1) for c in range(HALVES))
    notes = notes.reshape(r.chips, r.group, LANES)[:, :NOTE_ROWS]
    note_ref[...] = notes
    first, second = notes[:, 0, :].astype(jnp.int32), notes[:, 1, :].astype(jnp.int32)
    weight = [
        notes[:, k + 2, :] + (notes[:, k + 4, :] + notes[:, k + 6, :] / PART_STEP) / PART_STEP
        for k in range(2)
    ]
    set_slots = r.rows // HALVES
    slot = slots_of((first == expert) | (second == expert), block)
    slot = slot - (tensor * set_slots).astype(F32)
    in_set = (slot >= 0.0) & (slot < set_slots)
    place = jnp.where(in_set, slot + set_slots * block_of(slot.shape, block), -1.0)
    weight = jnp.where(first == expert, weight[0], weight[1])
    row = lax.broadcasted_iota(jnp.int32, (r.group, LANES), 0).astype(F32)
    for chip in range(0, r.chips, 2):
        pair = (chip, chip + 1)
        slot_weight = [
            jnp.sum(
                jnp.where(place[k : k + 1] == row, weight[k : k + 1], 0.0), axis=1, keepdims=True
            )
            for k in pair
        ]
        target = pl.ds(chip * r.rows, 2 * r.rows)
        hidden_ref[target, :] = r.of_chips(hidden, pair)
        factor_ref[target, :] = jnp.concatenate(
            [w[: r.rows] for w in slot_weight], axis=0
        ) * r.of_chips(up_scale, pair)
        base_ref[target, :] = 0.5 * r.of_chips(base, pair)

    ids = note_ref[own_ref[6]][:2].astype(jnp.int32)
    experts = combiner_ref.shape[0] // (2 * r.rows)
    named = lax.broadcasted_iota(jnp.int32, (experts, LANES), 0)
    slot = slots_of((ids[:1] == named) | (ids[1:] == named), block)
    slot_set = jnp.floor(slot / set_slots)
    place = jnp.where(
        slot >= 0.0,
        slot + slot_set * (r.rows - set_slots) + set_slots * block_of(slot.shape, block),
        -1.0,
    )
    row = lax.broadcasted_iota(jnp.int32, (2 * r.rows, LANES), 0).astype(F32)
    for e in range(experts):
        combiner_ref[pl.ds(e * 2 * r.rows, 2 * r.rows), :] = (place[e : e + 1] == row).astype(F32)


def far_kernel(
    rows, group, own_ref, part_ref, row_ref, gate_ref, up_ref, near_ref, hidden_ref, weight_ref
):
    parts = [part_ref[k] for k in range(part_ref.shape[0])]
    scales = [row_ref[k] for k in range(HALVES)]
    far = hidden_rows(
        parts, scales, row_ref[HALVES], group - rows, weight_ref, gate_ref, up_ref
    )
    chips = far.shape[0] // group
    slots = chips * rows
    near_at = own_ref[0] * slots
    far_at = slots - near_at
    hidden_ref[pl.ds(pl.multiple_of(near_at, 8), slots), :] = near_ref[...]
    for chip in range(0, chips, 2):
        pair = [far[k * group : k * group + rows] for k in (chip, chip + 1)]
        start = pl.multiple_of(far_at + chip * rows, 8)
        hidden_ref[pl.ds(start, 2 * rows), :] = jnp.concatenate(pair, axis=0)


def near_layer(gathered, weights, adapter_up, own, shard_rows, block, experts):
    rows = gathered.shape[0]
    columns = gathered.shape[1] - LANES
    units = weights[0].shape[1]
    chips = rows // (HALVES * shard_rows)
    flat = chips * (-(-shard_rows // HALVES // 8) * 8)
    out = jax.ShapeDtypeStruct((rows // 4, units), F32)
    vmem = pl.BlockSpec(memory_space=pltpu.VMEM)
    return pl.pallas_call(
        functools.partial(near_kernel, shard_rows, block),
        out_shape=(
            out,
            out,
            out,
            jax.ShapeDtypeStruct((experts * shard_rows, LANES), F32),
            jax.ShapeDtypeStruct((2 * HALVES, flat, columns), BF16),
            jax.ShapeDtypeStruct((HALVES + 1, flat, LANES), F32),
        ),
        in_specs=[pl.BlockSpec(memory_space=pltpu.SMEM)] + [vmem] * 4,
        out_specs=(vmem,) * 6,
        scratch_shapes=[
            pltpu.VMEM((2 * HALVES, columns, 2 * units), BF16),
            pltpu.VMEM((chips, NOTE_ROWS, LANES), F32),
        ],
        compiler_params=pltpu.CompilerParams(vmem_limit_bytes=16 * 2**20),
        cost_estimate=pl.CostEstimate(
            flops=4 * rows * columns * units,
            bytes_accessed=4 * rows * columns + 4 * columns * units,
            transcendentals=2 * rows * units,
        ),
    )(own, gathered, *weights, adapter_up)


def far_layer(parts, row_scales, weights, near, tensor, shard_rows):
    _, flat, columns = parts.shape
    slots, units = near.shape
    rows = shard_rows // HALVES
    vmem = pl.BlockSpec(memory_space=pltpu.VMEM)
    return pl.pallas_call(
        functools.partial(far_kernel, rows, flat * rows // slots),
        out_shape=jax.ShapeDtypeStruct((2 * slots, units), F32),
        in_specs=[pl.BlockSpec(memory_space=pltpu.SMEM)] + [vmem] * 5,
        out_specs=vmem,
        scratch_shapes=[pltpu.VMEM((2 * HALVES, columns, 2 * units), BF16)],
        compiler_params=pltpu.CompilerParams(vmem_limit_bytes=10 * 2**20),
        cost_estimate=pl.CostEstimate(
            flops=16 * flat * columns * units,
            bytes_accessed=8 * flat * columns + 16 * columns * units,
            transcendentals=2 * flat * units,
        ),
    )(tensor[None], parts, row_scales, *weights, near)


def norm_kernel(x_ref, out_ref):
    x = x_ref[...]
    mean = jnp.sum(jnp.sum(x * x, axis=0, keepdims=True), axis=1, keepdims=True) / x.size
    x = x * lax.rsqrt(mean + 1e-06)
    for k in range(x.shape[0]):
        out_ref[:, pl.ds(k * LANES, LANES)] = x[k : k + 1, :]


def norm_layer(pooled):
    vmem = pl.BlockSpec(memory_space=pltpu.VMEM)
    return pl.pallas_call(
        norm_kernel,
        out_shape=jax.ShapeDtypeStruct((1, pooled.size), F32),
        in_specs=[vmem],
        out_specs=vmem,
        compiler_params=pltpu.CompilerParams(vmem_limit_bytes=4 * 2**20),
    )(pooled)


def local(
    tokens,
    routes,
    chosen_expert_weight,
    expert_gate_weight,
    expert_up_weight,
    expert_down_weight,
    adapter_down_weight,
    adapter_up_weight,
    document_task_index,
    counts,
    final_norm_scale,
):
    rows, feats = tokens.shape
    seq = lax.axis_size(SEQ)
    experts = lax.axis_size(EXPERT)
    cores = lax.axis_size("c")
    groups = lax.axis_size(GROUP)
    tensors = lax.axis_size("t")
    capacity = rows * 5 // 16
    set_slots = capacity // tensors
    chip_rows = cores * set_slots
    shard_rows = HALVES * chip_rows
    width = feats * experts
    half = feats // cores
    columns = experts * half // HALVES
    slice_width = width // seq
    task_rows = adapter_down_weight.shape[0]
    s = lax.axis_index(SEQ)
    t = lax.axis_index("t")
    g = lax.axis_index(GROUP)
    per_feature_group = feats // slice_width
    own_group = s // per_feature_group

    ids = routes.T
    outgoing, notes = dispatch_layer(
        ids,
        chosen_expert_weight.T,
        tokens,
        adapter_down_weight,
        adapter_up_weight,
        final_norm_scale[None],
        experts,
        set_slots,
    )
    later_weights, _ = lax.optimization_barrier(
        ((expert_gate_weight[0], expert_up_weight[0]), outgoing)
    )
    other = [(k, tensors - 1 - k) for k in range(tensors)]
    far_weights = [lax.ppermute(w, "t", other) for w in later_weights]
    received = swap(outgoing, EXPERT + ("c",))

    sent, adapter_up, norm_scale = rows_layer(own_group, received, task_rows)
    sent = (sent + jnp.pad(notes, ((chip_rows, 0), (columns, 0)))).astype(F16)
    gathered = lax.all_gather(sent, SEQ, axis=0, tiled=False)
    gathered = gathered.astype(BF16).reshape(seq * shard_rows, columns + LANES)
    per_half = half // slice_width
    own_column = own_group * half + (s % per_half) * slice_width
    near, factor, base, combiner, parts, row_scales = near_layer(
        gathered,
        (expert_gate_weight[0], expert_up_weight[0]),
        adapter_up,
        jnp.stack(
            [
                (s // per_half) % cores,
                own_column // columns,
                own_column % columns,
                document_task_index[0],
                t,
                lax.axis_index(EXPERT),
                g,
            ]
        ),
        shard_rows,
        rows,
        experts,
    )
    hidden = far_layer(parts, row_scales, far_weights, near, t, shard_rows)

    units = hidden.shape[-1]
    hidden = hidden.astype(F16).reshape(tensors, -1, units)
    hidden = lax.all_gather(hidden, SEQ, axis=0, tiled=True)
    hidden, down = lax.optimization_barrier((hidden, expert_down_weight[0]))
    part = lax.dot_general(
        hidden.astype(BF16),
        down.reshape(seq * tensors, units, slice_width),
        (((0, 2), (0, 1)), ((), ())),
        preferred_element_type=F32,
    )
    payload = (part * factor + base).reshape(groups, chip_rows, slice_width)

    group_rows = cores * rows
    position = g * group_rows + jnp.arange(group_rows, dtype=jnp.int32)[None, :]
    counted = (position < counts[0]).astype(F32)
    payload, combiner, counted, norm_scale = lax.optimization_barrier(
        (payload, combiner, counted, norm_scale)
    )

    returned = swap(payload, GROUP)
    mixed = lax.dot_general(
        combiner,
        returned.reshape(groups * chip_rows, slice_width),
        (((0,), (0,)), ((), ())),
        precision=HIGH,
    )
    squares = jnp.sum(spread(jnp.sum(mixed * mixed, axis=1)[None], SEQ), axis=0)
    factor = counted * lax.rsqrt(squares / width + 1e-05)
    pooled = jnp.dot(factor, mixed, precision=HIGH) * norm_scale
    pooled = jnp.sum(spread(pooled, GROUP), axis=0)
    return norm_layer(spread(pooled, SEQ).reshape(seq, slice_width))


def solution(mesh):
    seq, experts, tensors = mesh.devices.shape
    parts = Mesh(
        mesh.devices.reshape(seq // 2, 2, experts // 2, 2, tensors), ("z", "c", "y", "h", "t")
    )
    return jax.shard_map(
        local,
        mesh=parts,
        in_specs=(
            P(SEQ, EXPERT),
            P(SEQ, None),
            P(SEQ, None),
            P(EXPERT, None, SEQ + ("t",)),
            P(EXPERT, None, SEQ + ("t",)),
            P(EXPERT, None, SEQ),
            P(None, EXPERT),
            P(None, EXPERT),
            P(),
            P(),
            P(EXPERT),
        ),
        out_specs=P(),
        check_vma=False,
    )
```

```python
import functools

import jax
import jax.numpy as jnp
from jax import lax
from jax.experimental import pallas as pl
from jax.experimental.pallas import tpu as pltpu
from jax.sharding import Mesh
from jax.sharding import PartitionSpec as P

TASK_COUNT = 2
ADAPTER_SCALE = 0.5

SEQ = ("z", "c")
EXPERT = ("y", "h")
GROUP = ("y", "h", "t")
HALVES = 2

BF16 = jnp.bfloat16
F16 = jnp.float16
F32 = jnp.float32
HIGH = lax.Precision.HIGHEST
LANES = 128
LEAST_EXPONENT = -40.0
NOTE_ROWS = 8
PART_STEP = 256.0
LOW_LANES = 32


def swap(x, axes):
    return lax.all_to_all(x, axes, split_axis=0, concat_axis=0, tiled=True)


def spread(x, axes):
    return swap(jnp.broadcast_to(x[None], (lax.axis_size(axes),) + x.shape), axes)


def rounded_parts(x):
    first = x.astype(BF16).astype(F32)
    rest = (x - first) * PART_STEP
    second = rest.astype(BF16).astype(F32)
    return first, second, (rest - second) * PART_STEP


def earlier_in_block(lanes, block):
    i = lax.broadcasted_iota(jnp.int32, (lanes, lanes), 0)
    j = lax.broadcasted_iota(jnp.int32, (lanes, lanes), 1)
    return ((i < j) & (i // block == j // block)).astype(F32).astype(BF16)


def slots_of(named, block):
    before = jnp.dot(
        named.astype(F32).astype(BF16),
        earlier_in_block(named.shape[1], block),
        preferred_element_type=F32,
    )
    return jnp.where(named, before, -1.0)


def block_of(shape, block):
    return (lax.broadcasted_iota(jnp.int32, shape, 1) // block).astype(F32)


def dispatch_kernel(*refs):
    out_ref, note_ref, held, sem = refs[6], refs[7], refs[8:14], refs[14]
    core, chip = lax.axis_index("c"), lax.axis_index("z")
    copies = [pltpu.make_async_copy(refs[k], held[k], sem.at[k]) for k in range(6)]
    for copy in copies:
        copy.start()
    for copy in copies:
        copy.wait()
    routes_ref, chosen_ref, tokens_ref, down_ref, up_ref, norm_ref = held
    targets, set_slots, _ = out_ref.shape
    experts = targets // HALVES
    rows, feats = tokens_ref.shape
    half = feats // HALVES
    ranks = down_ref.shape[0] // HALVES
    first_slot = (lax.axis_index("t") * set_slots).astype(F32)
    ids = routes_ref[...]
    notes = jnp.concatenate([ids.astype(F32)] + list(rounded_parts(chosen_ref[...])), axis=0)
    notes = jnp.concatenate([jnp.where(core == k, notes, 0.0) for k in range(HALVES)], axis=1)
    note_ref[...] = jnp.zeros_like(note_ref)
    note_ref[pl.ds(0, NOTE_ROWS), :] = notes
    expert = lax.broadcasted_iota(jnp.int32, (experts, rows), 0)
    place = slots_of((ids[:1] == expert) | (ids[1:] == expert), rows)
    padded = 16
    row = lax.broadcasted_iota(jnp.int32, (padded, rows), 0)
    slot = jnp.where(row < set_slots, row.astype(F32) + first_slot, -2.0)
    chooser = jnp.concatenate(
        [(place[e : e + 1] == slot).astype(F32) for e in range(experts)], axis=0
    ).astype(BF16)
    for c in range(HALVES):
        lanes = pl.ds(c * half, half)
        x = tokens_ref[:, lanes]
        low = lax.dot_general(
            x, down_ref[:, lanes], (((1,), (1,)), ((), ())), preferred_element_type=F32
        )
        first = low.astype(BF16)
        rest = low - first.astype(F32)
        second = rest.astype(BF16)
        third = (rest - second.astype(F32)).astype(BF16)
        x = jnp.concatenate([x, jnp.zeros_like(first), first, second, third], axis=1)
        chosen = jnp.dot(chooser, x, preferred_element_type=F32)
        column = pl.multiple_of((chip * HALVES + c) % (feats // LANES) * LANES, LANES)
        norm = norm_ref[:, pl.ds(column, LANES)]
        norm_first = norm.astype(BF16).astype(F32)
        norm_rest = norm - norm_first
        norm_second = norm_rest.astype(BF16).astype(F32)
        up_rows = up_ref[pl.ds(pl.multiple_of(core * ranks, ranks), ranks), pl.ds(column, LANES)]
        up_rows = up_rows.astype(F32)
        small = [
            up_rows[:set_slots],
            jnp.concatenate(
                [
                    up_rows[set_slots:],
                    norm_first,
                    norm_second,
                    norm_rest - norm_second,
                    jnp.zeros((2 * set_slots - ranks - 3, LANES), F32),
                ],
                axis=0,
            ),
        ]
        small = jnp.concatenate(small, axis=1).astype(BF16)
        for e in range(experts):
            out_ref[e * HALVES + c, :, pl.ds(0, half + LANES)] = chosen[
                e * padded : e * padded + set_slots
            ].astype(BF16)
            out_ref[e * HALVES + c, :, pl.ds(half + LANES, 2 * LANES)] = small


def dispatch_layer(
    routes, chosen, tokens, adapter_down, adapter_up, norm_scale, experts, set_slots
):
    rows, feats = tokens.shape
    lanes = feats // HALVES + 3 * LANES
    operands = (routes, chosen, tokens, adapter_down, adapter_up, norm_scale)
    return pl.pallas_call(
        dispatch_kernel,
        out_shape=(
            jax.ShapeDtypeStruct((experts * HALVES, set_slots, lanes), BF16),
            jax.ShapeDtypeStruct((HALVES * set_slots, LANES), F32),
        ),
        in_specs=[pl.BlockSpec(memory_space=pltpu.HBM)] * len(operands),
        out_specs=(pl.BlockSpec(memory_space=pltpu.VMEM),) * 2,
        scratch_shapes=[pltpu.VMEM(x.shape, x.dtype) for x in operands]
        + [pltpu.SemaphoreType.DMA((len(operands),))],
        compiler_params=pltpu.CompilerParams(vmem_limit_bytes=57 * 2**20),
        cost_estimate=pl.CostEstimate(
            flops=4 * rows * feats * experts * set_slots,
            bytes_accessed=2 * rows * feats + 2 * experts * HALVES * set_slots * lanes,
            transcendentals=0,
        ),
    )(*operands)


def rows_kernel(own_ref, received_ref, sent_ref, adapter_ref, norm_ref):
    messages, set_slots, _ = received_ref.shape
    groups = messages // HALVES
    half = 2 * LANES
    rows = HALVES * set_slots
    columns = sent_ref.shape[1] - LANES
    ranks = adapter_ref.shape[0] // HALVES

    def both(e, first, lanes):
        return jnp.concatenate(
            [
                received_ref[e * HALVES + c, :, pl.ds(first, lanes)].astype(F32)
                for c in range(HALVES)
            ],
            axis=0,
        )

    x = jnp.concatenate([both(e, 0, half) for e in range(groups)], axis=1)
    largest = jnp.max(jnp.abs(x), axis=1, keepdims=True)
    exponent = jnp.maximum(
        jnp.floor(jnp.log2(jnp.maximum(largest, 1e-30)) + 1.01), LEAST_EXPONENT
    )
    x = x * jnp.exp2(15.0 - exponent)
    low = sum(both(e, half, LANES) for e in range(groups))
    low = sum(low[:, k * LOW_LANES : (k + 1) * LOW_LANES] for k in range(1, 4))
    low = low * jnp.exp2(7.0 - exponent)
    beside = jnp.concatenate(
        [jnp.broadcast_to(exponent, low.shape)] + list(rounded_parts(low)), axis=1
    )
    sent_ref[:, pl.ds(0, columns)] = jnp.concatenate([x[:, :columns], x[:, columns:]], axis=0)
    sent_ref[:, pl.ds(columns, LANES)] = jnp.concatenate(
        [beside, jnp.zeros_like(beside)], axis=0
    )

    adapter = []
    for c in range(HALVES):
        small = received_ref[own_ref[0] * HALVES + c, :, pl.ds(half + LANES, 2 * LANES)]
        small = small.astype(F32)
        small = jnp.concatenate([small[:, :LANES], small[:, LANES:]], axis=0)
        adapter.append(small[:ranks])
        if c == 0:
            norm_ref[...] = (
                small[ranks : ranks + 1] + small[ranks + 1 : ranks + 2]
            ) + small[ranks + 2 : ranks + 3]
    adapter_ref[...] = jnp.concatenate(adapter, axis=0).astype(BF16)


def rows_layer(own_group, received, task_rows):
    messages, set_slots, _ = received.shape
    rows = HALVES * set_slots
    vmem = pl.BlockSpec(memory_space=pltpu.VMEM)
    columns = messages // HALVES * 2 * LANES // HALVES
    return pl.pallas_call(
        rows_kernel,
        out_shape=(
            jax.ShapeDtypeStruct((HALVES * rows, columns + LANES), F32),
            jax.ShapeDtypeStruct((task_rows, LANES), BF16),
            jax.ShapeDtypeStruct((1, LANES), F32),
        ),
        in_specs=[pl.BlockSpec(memory_space=pltpu.SMEM), vmem],
        out_specs=(vmem, vmem, vmem),
        compiler_params=pltpu.CompilerParams(vmem_limit_bytes=8 * 2**20),
        cost_estimate=pl.CostEstimate(
            flops=8 * rows * columns, bytes_accessed=8 * rows * columns, transcendentals=4 * rows
        ),
    )(own_group[None], received)


def hidden_rows(parts, scales, shrink, shift, weight_ref, gate_ref, up_ref):
    units = gate_ref.shape[1]
    half = 2 * LANES
    flat, columns = parts[0].shape
    blocks = columns // half
    acts = jnp.zeros((flat, 2 * units), F32)
    for c in range(HALVES):
        half_acts = jnp.zeros((flat, 2 * units), F32)
        for q in range(HALVES):
            for n in range(blocks):
                source = pl.ds(((q * blocks + n) * HALVES + c) * half, half)
                target = pl.ds(n * half, half)
                for k, ref in enumerate((gate_ref, up_ref)):
                    weight_ref[c * HALVES + q, target, pl.ds(k * units, units)] = ref[source, :]
            product = jnp.dot(
                parts[c * HALVES + q],
                weight_ref[c * HALVES + q],
                preferred_element_type=F32,
            )
            half_acts += product if q == 0 else pltpu.roll(product, flat - shift, 0)
        acts += half_acts * jnp.concatenate([scales[c]] * 2, axis=1)
    gate_act, up_act = acts[:, :units], acts[:, units:]
    value = (gate_act / (1.0 + jnp.exp(-gate_act)) * up_act).astype(BF16).astype(F32)
    return value * shrink


class Rows:
    def __init__(self, x_ref, shard_rows):
        self.x_ref = x_ref
        self.shard_rows = shard_rows
        self.rows = shard_rows // HALVES
        self.group = -(-self.rows // 8) * 8
        self.chips = x_ref.shape[0] // (HALVES * shard_rows)
        self.flat = self.chips * self.group
        self.columns = x_ref.shape[1] - LANES
        self.beside = x_ref[:, pl.ds(self.columns, LANES)].astype(F32)
        exponents = [self.part(self.beside, c, 0)[:, :LOW_LANES] for c in range(HALVES)]
        exponents = [jnp.concatenate([e] * (LANES // LOW_LANES), axis=1) for e in exponents]
        self.scales = [jnp.exp2(e - 15.0) for e in exponents]
        self.row_exponent = jnp.maximum(*exponents)

    def part(self, value, c, q):
        value = value.reshape(self.chips, HALVES, self.shard_rows, value.shape[-1])[:, c]
        value = value[:, : self.group] if q == 0 else value[:, self.shard_rows - self.group :]
        return value.reshape(self.flat, value.shape[-1])

    def parts(self):
        x = self.x_ref[:, pl.ds(0, self.columns)].astype(F32)
        return [self.part(x, c, q).astype(BF16) for c in range(HALVES) for q in range(HALVES)]

    def aligned(self, value, q):
        return value if q == 0 else pltpu.roll(value, self.flat - (self.group - self.rows), 0)

    def of_chips(self, value, chips):
        return jnp.concatenate(
            [value[k * self.group : k * self.group + self.rows] for k in chips], axis=0
        )


def slots_kernel(
    shard_rows,
    block,
    own_ref,
    x_ref,
    adapter_ref,
    factor_ref,
    base_ref,
    combiner_ref,
    note_ref,
):
    r = Rows(x_ref, shard_rows)
    task_rows = adapter_ref.shape[0]
    own_core, own_quarter = own_ref[0], own_ref[1]
    own_column = pl.multiple_of(own_ref[2], LANES)
    task, tensor, expert = own_ref[3], own_ref[4], own_ref[5]
    own = x_ref[:, pl.ds(own_column, LANES)].astype(F32)
    low = jnp.zeros((r.flat, LOW_LANES), F32)
    residual = jnp.zeros((r.flat, LANES), F32)
    for c in range(HALVES):
        tile = r.part(r.beside, c, 0)
        low_part = tile[:, LOW_LANES : 2 * LOW_LANES] + (
            tile[:, 2 * LOW_LANES : 3 * LOW_LANES] + tile[:, 3 * LOW_LANES :] / PART_STEP
        ) / PART_STEP
        low += low_part * jnp.exp2(tile[:, :LOW_LANES] - 7.0)
        for q in range(HALVES):
            mine = (own_core == c) & (own_quarter == q)
            residual += jnp.where(mine, r.aligned(r.part(own, c, q), q) * r.scales[c], 0.0)
    low_lane = lax.broadcasted_iota(jnp.int32, low.shape, 1) // (task_rows // TASK_COUNT)
    low = jnp.where(low_lane == task, low, 0.0).astype(BF16)
    base = residual + ADAPTER_SCALE * jnp.dot(
        low, adapter_ref[...], preferred_element_type=F32
    )
    up_scale = jnp.exp2(2.0 * r.row_exponent + 2.0)

    notes = sum(r.aligned(r.part(r.beside, c, 1), 1) for c in range(HALVES))
    notes = notes.reshape(r.chips, r.group, LANES)[:, :NOTE_ROWS]
    note_ref[...] = notes
    first, second = notes[:, 0, :].astype(jnp.int32), notes[:, 1, :].astype(jnp.int32)
    weight = [
        notes[:, k + 2, :] + (notes[:, k + 4, :] + notes[:, k + 6, :] / PART_STEP) / PART_STEP
        for k in range(2)
    ]
    set_slots = r.rows // HALVES
    slot = slots_of((first == expert) | (second == expert), block)
    slot = slot - (tensor * set_slots).astype(F32)
    in_set = (slot >= 0.0) & (slot < set_slots)
    place = jnp.where(in_set, slot + set_slots * block_of(slot.shape, block), -1.0)
    weight = jnp.where(first == expert, weight[0], weight[1])
    row = lax.broadcasted_iota(jnp.int32, (r.group, LANES), 0).astype(F32)
    for chip in range(0, r.chips, 2):
        pair = (chip, chip + 1)
        slot_weight = [
            jnp.sum(
                jnp.where(place[k : k + 1] == row, weight[k : k + 1], 0.0), axis=1, keepdims=True
            )
            for k in pair
        ]
        target = pl.ds(chip * r.rows, 2 * r.rows)
        factor_ref[target, :] = jnp.concatenate(
            [w[: r.rows] for w in slot_weight], axis=0
        ) * r.of_chips(up_scale, pair)
        base_ref[target, :] = 0.5 * r.of_chips(base, pair)

    ids = note_ref[own_ref[6]][:2].astype(jnp.int32)
    experts = combiner_ref.shape[0] // (2 * r.rows)
    named = lax.broadcasted_iota(jnp.int32, (experts, LANES), 0)
    slot = slots_of((ids[:1] == named) | (ids[1:] == named), block)
    slot_set = jnp.floor(slot / set_slots)
    place = jnp.where(
        slot >= 0.0,
        slot + slot_set * (r.rows - set_slots) + set_slots * block_of(slot.shape, block),
        -1.0,
    )
    row = lax.broadcasted_iota(jnp.int32, (2 * r.rows, LANES), 0).astype(F32)
    for e in range(experts):
        combiner_ref[pl.ds(e * 2 * r.rows, 2 * r.rows), :] = (place[e : e + 1] == row).astype(F32)


def near_kernel(
    shard_rows, x_ref, gate_ref, up_ref, hidden_ref, part_ref, row_ref, weight_ref
):
    r = Rows(x_ref, shard_rows)
    parts = r.parts()
    shrink = jnp.exp2(-2.0 * r.row_exponent - 2.0)
    for k, value in enumerate(parts):
        part_ref[k] = value
    for k, value in enumerate(r.scales + [shrink]):
        row_ref[k] = value
    hidden = hidden_rows(
        parts, r.scales, shrink, r.group - r.rows, weight_ref, gate_ref, up_ref
    )
    for chip in range(0, r.chips, 2):
        target = pl.ds(chip * r.rows, 2 * r.rows)
        hidden_ref[target, :] = r.of_chips(hidden, (chip, chip + 1))


def far_kernel(
    rows, group, own_ref, part_ref, row_ref, gate_ref, up_ref, near_ref, hidden_ref, weight_ref
):
    parts = [part_ref[k] for k in range(part_ref.shape[0])]
    scales = [row_ref[k] for k in range(HALVES)]
    far = hidden_rows(
        parts, scales, row_ref[HALVES], group - rows, weight_ref, gate_ref, up_ref
    )
    chips = far.shape[0] // group
    slots = chips * rows
    near_at = own_ref[0] * slots
    far_at = slots - near_at
    hidden_ref[pl.ds(pl.multiple_of(near_at, 8), slots), :] = near_ref[...]
    for chip in range(0, chips, 2):
        pair = [far[k * group : k * group + rows] for k in (chip, chip + 1)]
        start = pl.multiple_of(far_at + chip * rows, 8)
        hidden_ref[pl.ds(start, 2 * rows), :] = jnp.concatenate(pair, axis=0)


def slots_layer(gathered, adapter_up, own, shard_rows, block, experts):
    rows = gathered.shape[0]
    chips = rows // (HALVES * shard_rows)
    out = jax.ShapeDtypeStruct((rows // 4, LANES), F32)
    vmem = pl.BlockSpec(memory_space=pltpu.VMEM)
    return pl.pallas_call(
        functools.partial(slots_kernel, shard_rows, block),
        out_shape=(out, out, jax.ShapeDtypeStruct((experts * shard_rows, LANES), F32)),
        in_specs=[pl.BlockSpec(memory_space=pltpu.SMEM), vmem, vmem],
        out_specs=(vmem,) * 3,
        scratch_shapes=[pltpu.VMEM((chips, NOTE_ROWS, LANES), F32)],
        compiler_params=pltpu.CompilerParams(vmem_limit_bytes=12 * 2**20),
        cost_estimate=pl.CostEstimate(
            flops=64 * rows * LANES, bytes_accessed=16 * rows * LANES, transcendentals=rows * LANES
        ),
    )(own, gathered, adapter_up)


def near_layer(gathered, weights, shard_rows):
    rows = gathered.shape[0]
    columns = gathered.shape[1] - LANES
    units = weights[0].shape[1]
    chips = rows // (HALVES * shard_rows)
    flat = chips * (-(-shard_rows // HALVES // 8) * 8)
    vmem = pl.BlockSpec(memory_space=pltpu.VMEM)
    return pl.pallas_call(
        functools.partial(near_kernel, shard_rows),
        out_shape=(
            jax.ShapeDtypeStruct((rows // 4, units), F32),
            jax.ShapeDtypeStruct((2 * HALVES, flat, columns), BF16),
            jax.ShapeDtypeStruct((HALVES + 1, flat, LANES), F32),
        ),
        in_specs=[vmem] * 3,
        out_specs=(vmem,) * 3,
        scratch_shapes=[pltpu.VMEM((2 * HALVES, columns, 2 * units), BF16)],
        compiler_params=pltpu.CompilerParams(vmem_limit_bytes=16 * 2**20),
        cost_estimate=pl.CostEstimate(
            flops=4 * rows * columns * units,
            bytes_accessed=4 * rows * columns + 4 * columns * units,
            transcendentals=2 * rows * units,
        ),
    )(gathered, *weights)


def far_layer(parts, row_scales, weights, near, tensor, shard_rows):
    _, flat, columns = parts.shape
    slots, units = near.shape
    rows = shard_rows // HALVES
    vmem = pl.BlockSpec(memory_space=pltpu.VMEM)
    return pl.pallas_call(
        functools.partial(far_kernel, rows, flat * rows // slots),
        out_shape=jax.ShapeDtypeStruct((2 * slots, units), F32),
        in_specs=[pl.BlockSpec(memory_space=pltpu.SMEM)] + [vmem] * 5,
        out_specs=vmem,
        scratch_shapes=[pltpu.VMEM((2 * HALVES, columns, 2 * units), BF16)],
        compiler_params=pltpu.CompilerParams(vmem_limit_bytes=10 * 2**20),
        cost_estimate=pl.CostEstimate(
            flops=16 * flat * columns * units,
            bytes_accessed=8 * flat * columns + 16 * columns * units,
            transcendentals=2 * flat * units,
        ),
    )(tensor[None], parts, row_scales, *weights, near)


def norm_kernel(x_ref, out_ref):
    x = x_ref[...]
    mean = jnp.sum(jnp.sum(x * x, axis=0, keepdims=True), axis=1, keepdims=True) / x.size
    x = x * lax.rsqrt(mean + 1e-06)
    for k in range(x.shape[0]):
        out_ref[:, pl.ds(k * LANES, LANES)] = x[k : k + 1, :]


def norm_layer(pooled):
    vmem = pl.BlockSpec(memory_space=pltpu.VMEM)
    return pl.pallas_call(
        norm_kernel,
        out_shape=jax.ShapeDtypeStruct((1, pooled.size), F32),
        in_specs=[vmem],
        out_specs=vmem,
        compiler_params=pltpu.CompilerParams(vmem_limit_bytes=4 * 2**20),
    )(pooled)


def local(
    tokens,
    routes,
    chosen_expert_weight,
    expert_gate_weight,
    expert_up_weight,
    expert_down_weight,
    adapter_down_weight,
    adapter_up_weight,
    document_task_index,
    counts,
    final_norm_scale,
):
    rows, feats = tokens.shape
    seq = lax.axis_size(SEQ)
    experts = lax.axis_size(EXPERT)
    cores = lax.axis_size("c")
    groups = lax.axis_size(GROUP)
    tensors = lax.axis_size("t")
    capacity = rows * 5 // 16
    set_slots = capacity // tensors
    chip_rows = cores * set_slots
    shard_rows = HALVES * chip_rows
    width = feats * experts
    half = feats // cores
    columns = experts * half // HALVES
    slice_width = width // seq
    task_rows = adapter_down_weight.shape[0]
    s = lax.axis_index(SEQ)
    t = lax.axis_index("t")
    g = lax.axis_index(GROUP)
    per_feature_group = feats // slice_width
    own_group = s // per_feature_group

    ids = routes.T
    outgoing, notes = dispatch_layer(
        ids,
        chosen_expert_weight.T,
        tokens,
        adapter_down_weight,
        adapter_up_weight,
        final_norm_scale[None],
        experts,
        set_slots,
    )
    later_weights, _ = lax.optimization_barrier(
        ((expert_gate_weight[0], expert_up_weight[0]), outgoing)
    )
    other = [(k, tensors - 1 - k) for k in range(tensors)]
    far_weights = [lax.ppermute(w, "t", other) for w in later_weights]
    received = swap(outgoing, EXPERT + ("c",))

    sent, adapter_up, norm_scale = rows_layer(own_group, received, task_rows)
    sent = (sent + jnp.pad(notes, ((chip_rows, 0), (columns, 0)))).astype(F16)
    gathered = lax.all_gather(sent, SEQ, axis=0, tiled=False)
    gathered = gathered.astype(BF16).reshape(seq * shard_rows, columns + LANES)
    per_half = half // slice_width
    own_column = own_group * half + (s % per_half) * slice_width
    factor, base, combiner = slots_layer(
        gathered,
        adapter_up,
        jnp.stack(
            [
                (s // per_half) % cores,
                own_column // columns,
                own_column % columns,
                document_task_index[0],
                t,
                lax.axis_index(EXPERT),
                g,
            ]
        ),
        shard_rows,
        rows,
        experts,
    )
    near, parts, row_scales = near_layer(
        gathered, (expert_gate_weight[0], expert_up_weight[0]), shard_rows
    )
    hidden = far_layer(parts, row_scales, far_weights, near, t, shard_rows)

    units = hidden.shape[-1]
    hidden = hidden.astype(F16).reshape(tensors, -1, units)
    hidden = lax.all_gather(hidden, SEQ, axis=0, tiled=True)
    hidden, down = lax.optimization_barrier((hidden, expert_down_weight[0]))
    part = lax.dot_general(
        hidden.astype(BF16),
        down.reshape(seq * tensors, units, slice_width),
        (((0, 2), (0, 1)), ((), ())),
        preferred_element_type=F32,
    )
    payload = (part * factor + base).reshape(groups, chip_rows, slice_width)

    group_rows = cores * rows
    position = g * group_rows + jnp.arange(group_rows, dtype=jnp.int32)[None, :]
    counted = (position < counts[0]).astype(F32)
    payload, combiner, counted, norm_scale = lax.optimization_barrier(
        (payload, combiner, counted, norm_scale)
    )

    returned = swap(payload, GROUP)
    mixed = lax.dot_general(
        combiner,
        returned.reshape(groups * chip_rows, slice_width),
        (((0,), (0,)), ((), ())),
        precision=HIGH,
    )
    squares = jnp.sum(spread(jnp.sum(mixed * mixed, axis=1)[None], SEQ), axis=0)
    factor = counted * lax.rsqrt(squares / width + 1e-05)
    pooled = jnp.dot(factor, mixed, precision=HIGH) * norm_scale
    pooled = jnp.sum(spread(pooled, GROUP), axis=0)
    return norm_layer(spread(pooled, SEQ).reshape(seq, slice_width))


def solution(mesh):
    seq, experts, tensors = mesh.devices.shape
    parts = Mesh(
        mesh.devices.reshape(seq // 2, 2, experts // 2, 2, tensors), ("z", "c", "y", "h", "t")
    )
    return jax.shard_map(
        local,
        mesh=parts,
        in_specs=(
            P(SEQ, EXPERT),
            P(SEQ, None),
            P(SEQ, None),
            P(EXPERT, None, SEQ + ("t",)),
            P(EXPERT, None, SEQ + ("t",)),
            P(EXPERT, None, SEQ),
            P(None, EXPERT),
            P(None, EXPERT),
            P(),
            P(),
            P(EXPERT),
        ),
        out_specs=P(),
        check_vma=False,
    )
```

```python
import functools

import jax
import jax.numpy as jnp
from jax import lax
from jax.experimental import pallas as pl
from jax.experimental.pallas import tpu as pltpu
from jax.sharding import Mesh
from jax.sharding import PartitionSpec as P

TASK_COUNT = 2
ADAPTER_SCALE = 0.5

SEQ = ("z", "c")
EXPERT = ("y", "h")
GROUP = ("y", "h", "t")
HALVES = 2

BF16 = jnp.bfloat16
F16 = jnp.float16
F32 = jnp.float32
HIGH = lax.Precision.HIGHEST
LANES = 128
LEAST_EXPONENT = -40.0
NOTE_ROWS = 8
PART_STEP = 256.0
LOW_LANES = 32


def swap(x, axes):
    return lax.all_to_all(x, axes, split_axis=0, concat_axis=0, tiled=True)


def spread(x, axes):
    return swap(jnp.broadcast_to(x[None], (lax.axis_size(axes),) + x.shape), axes)


def rounded_parts(x):
    first = x.astype(BF16).astype(F32)
    rest = (x - first) * PART_STEP
    second = rest.astype(BF16).astype(F32)
    return first, second, (rest - second) * PART_STEP


def earlier_in_block(lanes, block):
    i = lax.broadcasted_iota(jnp.int32, (lanes, lanes), 0)
    j = lax.broadcasted_iota(jnp.int32, (lanes, lanes), 1)
    return ((i < j) & (i // block == j // block)).astype(F32).astype(BF16)


def slots_of(named, block):
    before = jnp.dot(
        named.astype(F32).astype(BF16),
        earlier_in_block(named.shape[1], block),
        preferred_element_type=F32,
    )
    return jnp.where(named, before, -1.0)


def block_of(shape, block):
    return (lax.broadcasted_iota(jnp.int32, shape, 1) // block).astype(F32)


def dispatch_kernel(*refs):
    out_ref, held, sem = refs[6], refs[7:13], refs[13]
    core, chip = lax.axis_index("c"), lax.axis_index("z")
    copies = [pltpu.make_async_copy(refs[k], held[k], sem.at[k]) for k in range(6)]
    for copy in copies:
        copy.start()
    for copy in copies:
        copy.wait()
    routes_ref, chosen_ref, tokens_ref, down_ref, up_ref, norm_ref = held
    targets, set_slots, _ = out_ref.shape
    experts = targets // HALVES
    rows, feats = tokens_ref.shape
    half = feats // HALVES
    ranks = down_ref.shape[0] // HALVES
    first_slot = (lax.axis_index("t") * set_slots).astype(F32)
    ids = routes_ref[...]
    notes = jnp.concatenate([ids.astype(F32)] + list(rounded_parts(chosen_ref[...])), axis=0)
    group = lax.axis_index("y") * lax.axis_size("h") + lax.axis_index("h")
    mine = lax.broadcasted_iota(jnp.int32, notes.shape, 0) == group
    note = jnp.sum(jnp.where(mine, notes, 0.0), axis=0, keepdims=True)
    note = jnp.concatenate(
        [note[:, :LOW_LANES], note[:, LOW_LANES:], jnp.zeros((set_slots - 2, LOW_LANES), F32)],
        axis=0,
    )
    note = jnp.concatenate(
        [
            jnp.zeros((set_slots, half), F32),
            note,
            jnp.zeros((set_slots, LANES - LOW_LANES), F32),
        ],
        axis=1,
    )
    expert = lax.broadcasted_iota(jnp.int32, (experts, rows), 0)
    place = slots_of((ids[:1] == expert) | (ids[1:] == expert), rows)
    padded = 16
    row = lax.broadcasted_iota(jnp.int32, (padded, rows), 0)
    slot = jnp.where(row < set_slots, row.astype(F32) + first_slot, -2.0)
    chooser = jnp.concatenate(
        [(place[e : e + 1] == slot).astype(F32) for e in range(experts)], axis=0
    ).astype(BF16)
    for c in range(HALVES):
        lanes = pl.ds(c * half, half)
        x = tokens_ref[:, lanes]
        low = lax.dot_general(
            x, down_ref[:, lanes], (((1,), (1,)), ((), ())), preferred_element_type=F32
        )
        first = low.astype(BF16)
        rest = low - first.astype(F32)
        second = rest.astype(BF16)
        third = (rest - second.astype(F32)).astype(BF16)
        x = jnp.concatenate([x, jnp.zeros_like(first), first, second, third], axis=1)
        chosen = jnp.dot(chooser, x, preferred_element_type=F32)
        column = pl.multiple_of((chip * HALVES + c) % (feats // LANES) * LANES, LANES)
        norm = norm_ref[:, pl.ds(column, LANES)]
        norm_first = norm.astype(BF16).astype(F32)
        norm_rest = norm - norm_first
        norm_second = norm_rest.astype(BF16).astype(F32)
        up_rows = up_ref[pl.ds(pl.multiple_of(core * ranks, ranks), ranks), pl.ds(column, LANES)]
        up_rows = up_rows.astype(F32)
        small = [
            up_rows[:set_slots],
            jnp.concatenate(
                [
                    up_rows[set_slots:],
                    norm_first,
                    norm_second,
                    norm_rest - norm_second,
                    jnp.zeros((2 * set_slots - ranks - 3, LANES), F32),
                ],
                axis=0,
            ),
        ]
        small = jnp.concatenate(small, axis=1).astype(BF16)
        for e in range(experts):
            message = chosen[e * padded : e * padded + set_slots] + note
            out_ref[e * HALVES + c, :, pl.ds(0, half + LANES)] = message.astype(BF16)
            out_ref[e * HALVES + c, :, pl.ds(half + LANES, 2 * LANES)] = small


def dispatch_layer(
    routes, chosen, tokens, adapter_down, adapter_up, norm_scale, experts, set_slots
):
    rows, feats = tokens.shape
    lanes = feats // HALVES + 3 * LANES
    operands = (routes, chosen, tokens, adapter_down, adapter_up, norm_scale)
    return pl.pallas_call(
        dispatch_kernel,
        out_shape=jax.ShapeDtypeStruct((experts * HALVES, set_slots, lanes), BF16),
        in_specs=[pl.BlockSpec(memory_space=pltpu.HBM)] * len(operands),
        out_specs=pl.BlockSpec(memory_space=pltpu.VMEM),
        scratch_shapes=[pltpu.VMEM(x.shape, x.dtype) for x in operands]
        + [pltpu.SemaphoreType.DMA((len(operands),))],
        compiler_params=pltpu.CompilerParams(vmem_limit_bytes=57 * 2**20),
        cost_estimate=pl.CostEstimate(
            flops=4 * rows * feats * experts * set_slots,
            bytes_accessed=2 * rows * feats + 2 * experts * HALVES * set_slots * lanes,
            transcendentals=0,
        ),
    )(*operands)


def rows_kernel(own_ref, received_ref, sent_ref, adapter_ref, norm_ref):
    messages, set_slots, _ = received_ref.shape
    groups = messages // HALVES
    half = 2 * LANES
    rows = HALVES * set_slots
    columns = sent_ref.shape[1] - LANES
    ranks = adapter_ref.shape[0] // HALVES

    def both(e, first, lanes):
        return jnp.concatenate(
            [
                received_ref[e * HALVES + c, :, pl.ds(first, lanes)].astype(F32)
                for c in range(HALVES)
            ],
            axis=0,
        )

    x = jnp.concatenate([both(e, 0, half) for e in range(groups)], axis=1)
    largest = jnp.max(jnp.abs(x), axis=1, keepdims=True)
    exponent = jnp.maximum(
        jnp.floor(jnp.log2(jnp.maximum(largest, 1e-30)) + 1.01), LEAST_EXPONENT
    )
    x = x * jnp.exp2(15.0 - exponent)
    sides = [both(e, half, LANES) for e in range(groups)]
    low = sum(sides)
    notes = jnp.concatenate(
        [
            jnp.concatenate(
                [side[r : r + 1, :LOW_LANES] for r in (0, 1, set_slots, set_slots + 1)], axis=1
            )
            for side in sides
        ]
        + [jnp.zeros((rows - groups, LANES), F32)],
        axis=0,
    )
    low = sum(low[:, k * LOW_LANES : (k + 1) * LOW_LANES] for k in range(1, 4))
    low = low * jnp.exp2(7.0 - exponent)
    beside = jnp.concatenate(
        [jnp.broadcast_to(exponent, low.shape)] + list(rounded_parts(low)), axis=1
    )
    sent_ref[:, pl.ds(0, columns)] = jnp.concatenate([x[:, :columns], x[:, columns:]], axis=0)
    sent_ref[:, pl.ds(columns, LANES)] = jnp.concatenate(
        [beside, notes], axis=0
    )

    adapter = []
    for c in range(HALVES):
        small = received_ref[own_ref[0] * HALVES + c, :, pl.ds(half + LANES, 2 * LANES)]
        small = small.astype(F32)
        small = jnp.concatenate([small[:, :LANES], small[:, LANES:]], axis=0)
        adapter.append(small[:ranks])
        if c == 0:
            norm_ref[...] = (
                small[ranks : ranks + 1] + small[ranks + 1 : ranks + 2]
            ) + small[ranks + 2 : ranks + 3]
    adapter_ref[...] = jnp.concatenate(adapter, axis=0).astype(BF16)


def rows_layer(own_group, received, task_rows):
    messages, set_slots, _ = received.shape
    rows = HALVES * set_slots
    vmem = pl.BlockSpec(memory_space=pltpu.VMEM)
    columns = messages // HALVES * 2 * LANES // HALVES
    return pl.pallas_call(
        rows_kernel,
        out_shape=(
            jax.ShapeDtypeStruct((HALVES * rows, columns + LANES), F32),
            jax.ShapeDtypeStruct((task_rows, LANES), BF16),
            jax.ShapeDtypeStruct((1, LANES), F32),
        ),
        in_specs=[pl.BlockSpec(memory_space=pltpu.SMEM), vmem],
        out_specs=(vmem, vmem, vmem),
        compiler_params=pltpu.CompilerParams(vmem_limit_bytes=8 * 2**20),
        cost_estimate=pl.CostEstimate(
            flops=8 * rows * columns, bytes_accessed=8 * rows * columns, transcendentals=4 * rows
        ),
    )(own_group[None], received)


def hidden_rows(parts, scales, shrink, shift, weight_ref, gate_ref, up_ref):
    units = gate_ref.shape[1]
    half = 2 * LANES
    flat, columns = parts[0].shape
    blocks = columns // half
    acts = jnp.zeros((flat, 2 * units), F32)
    for c in range(HALVES):
        half_acts = jnp.zeros((flat, 2 * units), F32)
        for q in range(HALVES):
            for n in range(blocks):
                source = pl.ds(((q * blocks + n) * HALVES + c) * half, half)
                target = pl.ds(n * half, half)
                for k, ref in enumerate((gate_ref, up_ref)):
                    weight_ref[c * HALVES + q, target, pl.ds(k * units, units)] = ref[source, :]
            product = jnp.dot(
                parts[c * HALVES + q],
                weight_ref[c * HALVES + q],
                preferred_element_type=F32,
            )
            half_acts += product if q == 0 else pltpu.roll(product, flat - shift, 0)
        acts += half_acts * jnp.concatenate([scales[c]] * 2, axis=1)
    gate_act, up_act = acts[:, :units], acts[:, units:]
    value = (gate_act / (1.0 + jnp.exp(-gate_act)) * up_act).astype(BF16).astype(F32)
    return value * shrink


class Rows:
    def __init__(self, x_ref, shard_rows):
        self.x_ref = x_ref
        self.shard_rows = shard_rows
        self.rows = shard_rows // HALVES
        self.group = -(-self.rows // 8) * 8
        self.chips = x_ref.shape[0] // (HALVES * shard_rows)
        self.flat = self.chips * self.group
        self.columns = x_ref.shape[1] - LANES
        self.beside = x_ref[:, pl.ds(self.columns, LANES)].astype(F32)
        exponents = [self.part(self.beside, c, 0)[:, :LOW_LANES] for c in range(HALVES)]
        exponents = [jnp.concatenate([e] * (LANES // LOW_LANES), axis=1) for e in exponents]
        self.scales = [jnp.exp2(e - 15.0) for e in exponents]
        self.row_exponent = jnp.maximum(*exponents)

    def part(self, value, c, q):
        value = value.reshape(self.chips, HALVES, self.shard_rows, value.shape[-1])[:, c]
        value = value[:, : self.group] if q == 0 else value[:, self.shard_rows - self.group :]
        return value.reshape(self.flat, value.shape[-1])

    def parts(self):
        x = self.x_ref[:, pl.ds(0, self.columns)].astype(F32)
        return [self.part(x, c, q).astype(BF16) for c in range(HALVES) for q in range(HALVES)]

    def aligned(self, value, q):
        return value if q == 0 else pltpu.roll(value, self.flat - (self.group - self.rows), 0)

    def of_chips(self, value, chips):
        return jnp.concatenate(
            [value[k * self.group : k * self.group + self.rows] for k in chips], axis=0
        )


def slots_kernel(
    shard_rows,
    block,
    own_ref,
    x_ref,
    adapter_ref,
    factor_ref,
    base_ref,
    combiner_ref,
    note_ref,
):
    r = Rows(x_ref, shard_rows)
    task_rows = adapter_ref.shape[0]
    own_core, own_quarter = own_ref[0], own_ref[1]
    own_column = pl.multiple_of(own_ref[2], LANES)
    task, tensor, expert = own_ref[3], own_ref[4], own_ref[5]
    own = x_ref[:, pl.ds(own_column, LANES)].astype(F32)
    low = jnp.zeros((r.flat, LOW_LANES), F32)
    residual = jnp.zeros((r.flat, LANES), F32)
    for c in range(HALVES):
        tile = r.part(r.beside, c, 0)
        low_part = tile[:, LOW_LANES : 2 * LOW_LANES] + (
            tile[:, 2 * LOW_LANES : 3 * LOW_LANES] + tile[:, 3 * LOW_LANES :] / PART_STEP
        ) / PART_STEP
        low += low_part * jnp.exp2(tile[:, :LOW_LANES] - 7.0)
        for q in range(HALVES):
            mine = (own_core == c) & (own_quarter == q)
            residual += jnp.where(mine, r.aligned(r.part(own, c, q), q) * r.scales[c], 0.0)
    low_lane = lax.broadcasted_iota(jnp.int32, low.shape, 1) // (task_rows // TASK_COUNT)
    low = jnp.where(low_lane == task, low, 0.0).astype(BF16)
    base = residual + ADAPTER_SCALE * jnp.dot(
        low, adapter_ref[...], preferred_element_type=F32
    )
    up_scale = jnp.exp2(2.0 * r.row_exponent + 2.0)

    notes = r.aligned(r.part(r.beside, 0, 1), 1)
    notes = notes.reshape(r.chips, r.group, LANES)[:, :NOTE_ROWS]
    note_ref[...] = notes
    first, second = notes[:, 0, :].astype(jnp.int32), notes[:, 1, :].astype(jnp.int32)
    weight = [
        notes[:, k + 2, :] + (notes[:, k + 4, :] + notes[:, k + 6, :] / PART_STEP) / PART_STEP
        for k in range(2)
    ]
    set_slots = r.rows // HALVES
    slot = slots_of((first == expert) | (second == expert), block)
    slot = slot - (tensor * set_slots).astype(F32)
    in_set = (slot >= 0.0) & (slot < set_slots)
    place = jnp.where(in_set, slot + set_slots * block_of(slot.shape, block), -1.0)
    weight = jnp.where(first == expert, weight[0], weight[1])
    row = lax.broadcasted_iota(jnp.int32, (r.group, LANES), 0).astype(F32)
    for chip in range(0, r.chips, 2):
        pair = (chip, chip + 1)
        slot_weight = [
            jnp.sum(
                jnp.where(place[k : k + 1] == row, weight[k : k + 1], 0.0), axis=1, keepdims=True
            )
            for k in pair
        ]
        target = pl.ds(chip * r.rows, 2 * r.rows)
        factor_ref[target, :] = jnp.concatenate(
            [w[: r.rows] for w in slot_weight], axis=0
        ) * r.of_chips(up_scale, pair)
        base_ref[target, :] = 0.5 * r.of_chips(base, pair)

    ids = note_ref[own_ref[6]][:2].astype(jnp.int32)
    experts = combiner_ref.shape[0] // (2 * r.rows)
    named = lax.broadcasted_iota(jnp.int32, (experts, LANES), 0)
    slot = slots_of((ids[:1] == named) | (ids[1:] == named), block)
    slot_set = jnp.floor(slot / set_slots)
    place = jnp.where(
        slot >= 0.0,
        slot + slot_set * (r.rows - set_slots) + set_slots * block_of(slot.shape, block),
        -1.0,
    )
    row = lax.broadcasted_iota(jnp.int32, (2 * r.rows, LANES), 0).astype(F32)
    for e in range(experts):
        combiner_ref[pl.ds(e * 2 * r.rows, 2 * r.rows), :] = (place[e : e + 1] == row).astype(F32)


def near_kernel(
    shard_rows, x_ref, gate_ref, up_ref, hidden_ref, part_ref, row_ref, weight_ref
):
    r = Rows(x_ref, shard_rows)
    parts = r.parts()
    shrink = jnp.exp2(-2.0 * r.row_exponent - 2.0)
    for k, value in enumerate(parts):
        part_ref[k] = value
    for k, value in enumerate(r.scales + [shrink]):
        row_ref[k] = value
    hidden = hidden_rows(
        parts, r.scales, shrink, r.group - r.rows, weight_ref, gate_ref, up_ref
    )
    for chip in range(0, r.chips, 2):
        target = pl.ds(chip * r.rows, 2 * r.rows)
        hidden_ref[target, :] = r.of_chips(hidden, (chip, chip + 1))


def far_kernel(
    rows, group, own_ref, part_ref, row_ref, gate_ref, up_ref, near_ref, hidden_ref, weight_ref
):
    parts = [part_ref[k] for k in range(part_ref.shape[0])]
    scales = [row_ref[k] for k in range(HALVES)]
    far = hidden_rows(
        parts, scales, row_ref[HALVES], group - rows, weight_ref, gate_ref, up_ref
    )
    chips = far.shape[0] // group
    slots = chips * rows
    near_at = own_ref[0] * slots
    far_at = slots - near_at
    hidden_ref[pl.ds(pl.multiple_of(near_at, 8), slots), :] = near_ref[...]
    for chip in range(0, chips, 2):
        pair = [far[k * group : k * group + rows] for k in (chip, chip + 1)]
        start = pl.multiple_of(far_at + chip * rows, 8)
        hidden_ref[pl.ds(start, 2 * rows), :] = jnp.concatenate(pair, axis=0)


def slots_layer(gathered, adapter_up, own, shard_rows, block, experts):
    rows = gathered.shape[0]
    chips = rows // (HALVES * shard_rows)
    out = jax.ShapeDtypeStruct((rows // 4, LANES), F32)
    vmem = pl.BlockSpec(memory_space=pltpu.VMEM)
    return pl.pallas_call(
        functools.partial(slots_kernel, shard_rows, block),
        out_shape=(out, out, jax.ShapeDtypeStruct((experts * shard_rows, LANES), F32)),
        in_specs=[pl.BlockSpec(memory_space=pltpu.SMEM), vmem, vmem],
        out_specs=(vmem,) * 3,
        scratch_shapes=[pltpu.VMEM((chips, NOTE_ROWS, LANES), F32)],
        compiler_params=pltpu.CompilerParams(vmem_limit_bytes=12 * 2**20),
        cost_estimate=pl.CostEstimate(
            flops=64 * rows * LANES, bytes_accessed=16 * rows * LANES, transcendentals=rows * LANES
        ),
    )(own, gathered, adapter_up)


def near_layer(gathered, weights, shard_rows):
    rows = gathered.shape[0]
    columns = gathered.shape[1] - LANES
    units = weights[0].shape[1]
    chips = rows // (HALVES * shard_rows)
    flat = chips * (-(-shard_rows // HALVES // 8) * 8)
    vmem = pl.BlockSpec(memory_space=pltpu.VMEM)
    return pl.pallas_call(
        functools.partial(near_kernel, shard_rows),
        out_shape=(
            jax.ShapeDtypeStruct((rows // 4, units), F32),
            jax.ShapeDtypeStruct((2 * HALVES, flat, columns), BF16),
            jax.ShapeDtypeStruct((HALVES + 1, flat, LANES), F32),
        ),
        in_specs=[vmem] * 3,
        out_specs=(vmem,) * 3,
        scratch_shapes=[pltpu.VMEM((2 * HALVES, columns, 2 * units), BF16)],
        compiler_params=pltpu.CompilerParams(vmem_limit_bytes=16 * 2**20),
        cost_estimate=pl.CostEstimate(
            flops=4 * rows * columns * units,
            bytes_accessed=4 * rows * columns + 4 * columns * units,
            transcendentals=2 * rows * units,
        ),
    )(gathered, *weights)


def far_layer(parts, row_scales, weights, near, tensor, shard_rows):
    _, flat, columns = parts.shape
    slots, units = near.shape
    rows = shard_rows // HALVES
    vmem = pl.BlockSpec(memory_space=pltpu.VMEM)
    return pl.pallas_call(
        functools.partial(far_kernel, rows, flat * rows // slots),
        out_shape=jax.ShapeDtypeStruct((2 * slots, units), F32),
        in_specs=[pl.BlockSpec(memory_space=pltpu.SMEM)] + [vmem] * 5,
        out_specs=vmem,
        scratch_shapes=[pltpu.VMEM((2 * HALVES, columns, 2 * units), BF16)],
        compiler_params=pltpu.CompilerParams(vmem_limit_bytes=10 * 2**20),
        cost_estimate=pl.CostEstimate(
            flops=16 * flat * columns * units,
            bytes_accessed=8 * flat * columns + 16 * columns * units,
            transcendentals=2 * flat * units,
        ),
    )(tensor[None], parts, row_scales, *weights, near)


def norm_kernel(x_ref, out_ref):
    x = x_ref[...]
    mean = jnp.sum(jnp.sum(x * x, axis=0, keepdims=True), axis=1, keepdims=True) / x.size
    x = x * lax.rsqrt(mean + 1e-06)
    for k in range(x.shape[0]):
        out_ref[:, pl.ds(k * LANES, LANES)] = x[k : k + 1, :]


def norm_layer(pooled):
    vmem = pl.BlockSpec(memory_space=pltpu.VMEM)
    return pl.pallas_call(
        norm_kernel,
        out_shape=jax.ShapeDtypeStruct((1, pooled.size), F32),
        in_specs=[vmem],
        out_specs=vmem,
        compiler_params=pltpu.CompilerParams(vmem_limit_bytes=4 * 2**20),
    )(pooled)


def local(
    tokens,
    routes,
    chosen_expert_weight,
    expert_gate_weight,
    expert_up_weight,
    expert_down_weight,
    adapter_down_weight,
    adapter_up_weight,
    document_task_index,
    counts,
    final_norm_scale,
):
    rows, feats = tokens.shape
    seq = lax.axis_size(SEQ)
    experts = lax.axis_size(EXPERT)
    cores = lax.axis_size("c")
    groups = lax.axis_size(GROUP)
    tensors = lax.axis_size("t")
    capacity = rows * 5 // 16
    set_slots = capacity // tensors
    chip_rows = cores * set_slots
    shard_rows = HALVES * chip_rows
    width = feats * experts
    half = feats // cores
    columns = experts * half // HALVES
    slice_width = width // seq
    task_rows = adapter_down_weight.shape[0]
    s = lax.axis_index(SEQ)
    t = lax.axis_index("t")
    g = lax.axis_index(GROUP)
    per_feature_group = feats // slice_width
    own_group = s // per_feature_group

    ids = routes.T
    outgoing = dispatch_layer(
        ids,
        chosen_expert_weight.T,
        tokens,
        adapter_down_weight,
        adapter_up_weight,
        final_norm_scale[None],
        experts,
        set_slots,
    )
    later_weights, _ = lax.optimization_barrier(
        ((expert_gate_weight[0], expert_up_weight[0]), outgoing)
    )
    other = [(k, tensors - 1 - k) for k in range(tensors)]
    far_weights = [lax.ppermute(w, "t", other) for w in later_weights]
    received = swap(outgoing, EXPERT + ("c",))

    sent, adapter_up, norm_scale = rows_layer(own_group, received, task_rows)
    sent = sent.astype(F16)
    gathered = lax.all_gather(sent, SEQ, axis=0, tiled=False)
    gathered = gathered.astype(BF16).reshape(seq * shard_rows, columns + LANES)
    per_half = half // slice_width
    own_column = own_group * half + (s % per_half) * slice_width
    factor, base, combiner = slots_layer(
        gathered,
        adapter_up,
        jnp.stack(
            [
                (s // per_half) % cores,
                own_column // columns,
                own_column % columns,
                document_task_index[0],
                t,
                lax.axis_index(EXPERT),
                g,
            ]
        ),
        shard_rows,
        rows,
        experts,
    )
    near, parts, row_scales = near_layer(
        gathered, (expert_gate_weight[0], expert_up_weight[0]), shard_rows
    )
    hidden = far_layer(parts, row_scales, far_weights, near, t, shard_rows)

    units = hidden.shape[-1]
    hidden = hidden.astype(F16).reshape(tensors, -1, units)
    hidden = lax.all_gather(hidden, SEQ, axis=0, tiled=True)
    hidden, down = lax.optimization_barrier((hidden, expert_down_weight[0]))
    part = lax.dot_general(
        hidden.astype(BF16),
        down.reshape(seq * tensors, units, slice_width),
        (((0, 2), (0, 1)), ((), ())),
        preferred_element_type=F32,
    )
    payload = (part * factor + base).reshape(groups, chip_rows, slice_width)

    group_rows = cores * rows
    position = g * group_rows + jnp.arange(group_rows, dtype=jnp.int32)[None, :]
    counted = (position < counts[0]).astype(F32)
    payload, combiner, counted, norm_scale = lax.optimization_barrier(
        (payload, combiner, counted, norm_scale)
    )

    returned = swap(payload, GROUP)
    mixed = lax.dot_general(
        combiner,
        returned.reshape(groups * chip_rows, slice_width),
        (((0,), (0,)), ((), ())),
        precision=HIGH,
    )
    squares = jnp.sum(spread(jnp.sum(mixed * mixed, axis=1)[None], SEQ), axis=0)
    factor = counted * lax.rsqrt(squares / width + 1e-05)
    pooled = jnp.dot(factor, mixed, precision=HIGH) * norm_scale
    pooled = jnp.sum(spread(pooled, GROUP), axis=0)
    return norm_layer(spread(pooled, SEQ).reshape(seq, slice_width))


def solution(mesh):
    seq, experts, tensors = mesh.devices.shape
    parts = Mesh(
        mesh.devices.reshape(seq // 2, 2, experts // 2, 2, tensors), ("z", "c", "y", "h", "t")
    )
    return jax.shard_map(
        local,
        mesh=parts,
        in_specs=(
            P(SEQ, EXPERT),
            P(SEQ, None),
            P(SEQ, None),
            P(EXPERT, None, SEQ + ("t",)),
            P(EXPERT, None, SEQ + ("t",)),
            P(EXPERT, None, SEQ),
            P(None, EXPERT),
            P(None, EXPERT),
            P(),
            P(),
            P(EXPERT),
        ),
        out_specs=P(),
        check_vma=False,
    )
```

```python
import functools

import jax
import jax.numpy as jnp
from jax import lax
from jax.experimental import pallas as pl
from jax.experimental.pallas import tpu as pltpu
from jax.sharding import Mesh
from jax.sharding import PartitionSpec as P

TASK_COUNT = 2
ADAPTER_SCALE = 0.5

SEQ = ("z", "c")
EXPERT = ("y", "h")
GROUP = ("y", "h", "t")
HALVES = 2

BF16 = jnp.bfloat16
F16 = jnp.float16
F32 = jnp.float32
HIGH = lax.Precision.HIGHEST
LANES = 128
LEAST_EXPONENT = -40.0
NOTE_ROWS = 8
PART_STEP = 256.0
LOW_LANES = 32


def swap(x, axes):
    return lax.all_to_all(x, axes, split_axis=0, concat_axis=0, tiled=True)


def spread(x, axes):
    return swap(jnp.broadcast_to(x[None], (lax.axis_size(axes),) + x.shape), axes)


def rounded_parts(x):
    first = x.astype(BF16).astype(F32)
    rest = (x - first) * PART_STEP
    second = rest.astype(BF16).astype(F32)
    return first, second, (rest - second) * PART_STEP


def earlier_in_block(lanes, block):
    i = lax.broadcasted_iota(jnp.int32, (lanes, lanes), 0)
    j = lax.broadcasted_iota(jnp.int32, (lanes, lanes), 1)
    return ((i < j) & (i // block == j // block)).astype(F32).astype(BF16)


def slots_of(named, block):
    before = jnp.dot(
        named.astype(F32).astype(BF16),
        earlier_in_block(named.shape[1], block),
        preferred_element_type=F32,
    )
    return jnp.where(named, before, -1.0)


def block_of(shape, block):
    return (lax.broadcasted_iota(jnp.int32, shape, 1) // block).astype(F32)


def dispatch_kernel(*refs):
    out_ref, held, sem = refs[6], refs[7:13], refs[13]
    core, chip = lax.axis_index("c"), lax.axis_index("z")
    copies = [pltpu.make_async_copy(refs[k], held[k], sem.at[k]) for k in range(6)]
    for copy in copies:
        copy.start()
    for copy in copies:
        copy.wait()
    routes_ref, chosen_ref, tokens_ref, down_ref, up_ref, norm_ref = held
    targets, set_slots, _ = out_ref.shape
    experts = targets // HALVES
    rows, feats = tokens_ref.shape
    half = feats // HALVES
    ranks = down_ref.shape[0] // HALVES
    first_slot = (lax.axis_index("t") * set_slots).astype(F32)
    ids = routes_ref[...]
    notes = jnp.concatenate([ids.astype(F32)] + list(rounded_parts(chosen_ref[...])), axis=0)
    group = lax.axis_index("y") * lax.axis_size("h") + lax.axis_index("h")
    mine = lax.broadcasted_iota(jnp.int32, notes.shape, 0) == group
    note = jnp.sum(jnp.where(mine, notes, 0.0), axis=0, keepdims=True)
    note = jnp.concatenate(
        [note[:, :LOW_LANES], note[:, LOW_LANES:], jnp.zeros((set_slots - 2, LOW_LANES), F32)],
        axis=0,
    )
    note = jnp.concatenate(
        [
            jnp.zeros((set_slots, half), F32),
            note,
            jnp.zeros((set_slots, LANES - LOW_LANES), F32),
        ],
        axis=1,
    )
    expert = lax.broadcasted_iota(jnp.int32, (experts, rows), 0)
    place = slots_of((ids[:1] == expert) | (ids[1:] == expert), rows)
    padded = 16
    row = lax.broadcasted_iota(jnp.int32, (padded, rows), 0)
    slot = jnp.where(row < set_slots, row.astype(F32) + first_slot, -2.0)
    chooser = jnp.concatenate(
        [(place[e : e + 1] == slot).astype(F32) for e in range(experts)], axis=0
    ).astype(BF16)
    for c in range(HALVES):
        lanes = pl.ds(c * half, half)
        x = tokens_ref[:, lanes]
        low = lax.dot_general(
            x, down_ref[:, lanes], (((1,), (1,)), ((), ())), preferred_element_type=F32
        )
        first = low.astype(BF16)
        rest = low - first.astype(F32)
        second = rest.astype(BF16)
        third = (rest - second.astype(F32)).astype(BF16)
        x = jnp.concatenate([x, jnp.zeros_like(first), first, second, third], axis=1)
        chosen = jnp.dot(chooser, x, preferred_element_type=F32)
        column = pl.multiple_of((chip * HALVES + c) % (feats // LANES) * LANES, LANES)
        norm = norm_ref[:, pl.ds(column, LANES)]
        norm_first = norm.astype(BF16).astype(F32)
        norm_rest = norm - norm_first
        norm_second = norm_rest.astype(BF16).astype(F32)
        up_rows = up_ref[pl.ds(pl.multiple_of(core * ranks, ranks), ranks), pl.ds(column, LANES)]
        up_rows = up_rows.astype(F32)
        small = [
            up_rows[:set_slots],
            jnp.concatenate(
                [
                    up_rows[set_slots:],
                    norm_first,
                    norm_second,
                    norm_rest - norm_second,
                    jnp.zeros((2 * set_slots - ranks - 3, LANES), F32),
                ],
                axis=0,
            ),
        ]
        small = jnp.concatenate(small, axis=1).astype(BF16)
        for e in range(experts):
            message = chosen[e * padded : e * padded + set_slots] + note
            out_ref[e * HALVES + c, :, pl.ds(0, half + LANES)] = message.astype(BF16)
            out_ref[e * HALVES + c, :, pl.ds(half + LANES, 2 * LANES)] = small


def dispatch_layer(
    routes, chosen, tokens, adapter_down, adapter_up, norm_scale, experts, set_slots
):
    rows, feats = tokens.shape
    lanes = feats // HALVES + 3 * LANES
    operands = (routes, chosen, tokens, adapter_down, adapter_up, norm_scale)
    return pl.pallas_call(
        dispatch_kernel,
        out_shape=jax.ShapeDtypeStruct((experts * HALVES, set_slots, lanes), BF16),
        in_specs=[pl.BlockSpec(memory_space=pltpu.HBM)] * len(operands),
        out_specs=pl.BlockSpec(memory_space=pltpu.VMEM),
        scratch_shapes=[pltpu.VMEM(x.shape, x.dtype) for x in operands]
        + [pltpu.SemaphoreType.DMA((len(operands),))],
        compiler_params=pltpu.CompilerParams(vmem_limit_bytes=57 * 2**20),
        cost_estimate=pl.CostEstimate(
            flops=4 * rows * feats * experts * set_slots,
            bytes_accessed=2 * rows * feats + 2 * experts * HALVES * set_slots * lanes,
            transcendentals=0,
        ),
    )(*operands)


def rows_kernel(own_ref, received_ref, sent_ref, adapter_ref, norm_ref):
    messages, set_slots, _ = received_ref.shape
    groups = messages // HALVES
    half = 2 * LANES
    rows = HALVES * set_slots
    columns = sent_ref.shape[1] - LANES
    ranks = adapter_ref.shape[0] // HALVES

    def both(e, first, lanes):
        return jnp.concatenate(
            [
                received_ref[e * HALVES + c, :, pl.ds(first, lanes)].astype(F32)
                for c in range(HALVES)
            ],
            axis=0,
        )

    x = jnp.concatenate([both(e, 0, half) for e in range(groups)], axis=1)
    largest = jnp.max(jnp.abs(x), axis=1, keepdims=True)
    exponent = jnp.maximum(
        jnp.floor(jnp.log2(jnp.maximum(largest, 1e-30)) + 1.01), LEAST_EXPONENT
    )
    x = x * jnp.exp2(15.0 - exponent)
    sides = [both(e, half, LANES) for e in range(groups)]
    low = sum(sides)
    notes = jnp.concatenate(
        [
            jnp.concatenate(
                [side[r : r + 1, :LOW_LANES] for r in (0, 1, set_slots, set_slots + 1)], axis=1
            )
            for side in sides
        ]
        + [jnp.zeros((rows - groups, LANES), F32)],
        axis=0,
    )
    low = sum(low[:, k * LOW_LANES : (k + 1) * LOW_LANES] for k in range(1, 4))
    low = low * jnp.exp2(7.0 - exponent)
    beside = jnp.concatenate(
        [jnp.broadcast_to(exponent, low.shape)] + list(rounded_parts(low)), axis=1
    )
    sent_ref[:, pl.ds(0, columns)] = jnp.concatenate([x[:, :columns], x[:, columns:]], axis=0)
    sent_ref[:, pl.ds(columns, LANES)] = jnp.concatenate(
        [beside, notes], axis=0
    )

    adapter = []
    for c in range(HALVES):
        small = received_ref[own_ref[0] * HALVES + c, :, pl.ds(half + LANES, 2 * LANES)]
        small = small.astype(F32)
        small = jnp.concatenate([small[:, :LANES], small[:, LANES:]], axis=0)
        adapter.append(small[:ranks])
        if c == 0:
            norm_ref[...] = (
                small[ranks : ranks + 1] + small[ranks + 1 : ranks + 2]
            ) + small[ranks + 2 : ranks + 3]
    adapter_ref[...] = jnp.concatenate(adapter, axis=0).astype(BF16)


def rows_layer(own_group, received, task_rows):
    messages, set_slots, _ = received.shape
    rows = HALVES * set_slots
    vmem = pl.BlockSpec(memory_space=pltpu.VMEM)
    columns = messages // HALVES * 2 * LANES // HALVES
    return pl.pallas_call(
        rows_kernel,
        out_shape=(
            jax.ShapeDtypeStruct((HALVES * rows, columns + LANES), F32),
            jax.ShapeDtypeStruct((task_rows, LANES), BF16),
            jax.ShapeDtypeStruct((1, LANES), F32),
        ),
        in_specs=[pl.BlockSpec(memory_space=pltpu.SMEM), vmem],
        out_specs=(vmem, vmem, vmem),
        compiler_params=pltpu.CompilerParams(vmem_limit_bytes=8 * 2**20),
        cost_estimate=pl.CostEstimate(
            flops=8 * rows * columns, bytes_accessed=8 * rows * columns, transcendentals=4 * rows
        ),
    )(own_group[None], received)


def hidden_rows(parts, scales, shrink, shift, weight_ref, gate_ref, up_ref):
    units = gate_ref.shape[1]
    half = 2 * LANES
    flat, columns = parts[0].shape
    blocks = columns // half
    acts = jnp.zeros((flat, 2 * units), F32)
    for c in range(HALVES):
        half_acts = jnp.zeros((flat, 2 * units), F32)
        for q in range(HALVES):
            for n in range(blocks):
                source = pl.ds(((q * blocks + n) * HALVES + c) * half, half)
                target = pl.ds(n * half, half)
                for k, ref in enumerate((gate_ref, up_ref)):
                    weight_ref[c * HALVES + q, target, pl.ds(k * units, units)] = ref[source, :]
            product = jnp.dot(
                parts[c * HALVES + q],
                weight_ref[c * HALVES + q],
                preferred_element_type=F32,
            )
            half_acts += product if q == 0 else pltpu.roll(product, flat - shift, 0)
        acts += half_acts * jnp.concatenate([scales[c]] * 2, axis=1)
    gate_act, up_act = acts[:, :units], acts[:, units:]
    value = (gate_act / (1.0 + jnp.exp(-gate_act)) * up_act).astype(BF16).astype(F32)
    return value * shrink


class Rows:
    def __init__(self, x_ref, shard_rows):
        self.x_ref = x_ref
        self.shard_rows = shard_rows
        self.rows = shard_rows // HALVES
        self.group = -(-self.rows // 8) * 8
        self.chips = x_ref.shape[0] // (HALVES * shard_rows)
        self.flat = self.chips * self.group
        self.columns = x_ref.shape[1] - LANES
        self.beside = x_ref[:, pl.ds(self.columns, LANES)].astype(F32)
        exponents = [self.part(self.beside, c, 0)[:, :LOW_LANES] for c in range(HALVES)]
        exponents = [jnp.concatenate([e] * (LANES // LOW_LANES), axis=1) for e in exponents]
        self.scales = [jnp.exp2(e - 15.0) for e in exponents]
        self.row_exponent = jnp.maximum(*exponents)

    def part(self, value, c, q):
        value = value.reshape(self.chips, HALVES, self.shard_rows, value.shape[-1])[:, c]
        value = value[:, : self.group] if q == 0 else value[:, self.shard_rows - self.group :]
        return value.reshape(self.flat, value.shape[-1])

    def parts(self):
        x = self.x_ref[:, pl.ds(0, self.columns)].astype(F32)
        return [self.part(x, c, q).astype(BF16) for c in range(HALVES) for q in range(HALVES)]

    def aligned(self, value, q):
        return value if q == 0 else pltpu.roll(value, self.flat - (self.group - self.rows), 0)

    def of_chips(self, value, chips):
        return jnp.concatenate(
            [value[k * self.group : k * self.group + self.rows] for k in chips], axis=0
        )


def slots_kernel(
    shard_rows,
    block,
    own_ref,
    x_ref,
    adapter_ref,
    factor_ref,
    base_ref,
    combiner_ref,
    note_ref,
):
    r = Rows(x_ref, shard_rows)
    task_rows = adapter_ref.shape[0]
    own_core, own_quarter = own_ref[0], own_ref[1]
    own_column = pl.multiple_of(own_ref[2], LANES)
    task, tensor, expert = own_ref[3], own_ref[4], own_ref[5]
    own = x_ref[:, pl.ds(own_column, LANES)].astype(F32)
    low = jnp.zeros((r.flat, LOW_LANES), F32)
    residual = jnp.zeros((r.flat, LANES), F32)
    for c in range(HALVES):
        tile = r.part(r.beside, c, 0)
        low_part = tile[:, LOW_LANES : 2 * LOW_LANES] + (
            tile[:, 2 * LOW_LANES : 3 * LOW_LANES] + tile[:, 3 * LOW_LANES :] / PART_STEP
        ) / PART_STEP
        low += low_part * jnp.exp2(tile[:, :LOW_LANES] - 7.0)
        for q in range(HALVES):
            mine = (own_core == c) & (own_quarter == q)
            residual += jnp.where(mine, r.aligned(r.part(own, c, q), q) * r.scales[c], 0.0)
    low_lane = lax.broadcasted_iota(jnp.int32, low.shape, 1) // (task_rows // TASK_COUNT)
    low = jnp.where(low_lane == task, low, 0.0).astype(BF16)
    base = residual + ADAPTER_SCALE * jnp.dot(
        low, adapter_ref[...], preferred_element_type=F32
    )
    up_scale = jnp.exp2(2.0 * r.row_exponent + 2.0)

    notes = r.aligned(r.part(r.beside, 0, 1), 1)
    notes = notes.reshape(r.chips, r.group, LANES)[:, :NOTE_ROWS]
    note_ref[...] = notes
    first, second = notes[:, 0, :].astype(jnp.int32), notes[:, 1, :].astype(jnp.int32)
    weight = [
        notes[:, k + 2, :] + (notes[:, k + 4, :] + notes[:, k + 6, :] / PART_STEP) / PART_STEP
        for k in range(2)
    ]
    set_slots = r.rows // HALVES
    slot = slots_of((first == expert) | (second == expert), block)
    slot = slot - (tensor * set_slots).astype(F32)
    in_set = (slot >= 0.0) & (slot < set_slots)
    place = jnp.where(in_set, slot + set_slots * block_of(slot.shape, block), -1.0)
    weight = jnp.where(first == expert, weight[0], weight[1])
    row = lax.broadcasted_iota(jnp.int32, (r.group, LANES), 0).astype(F32)
    for chip in range(0, r.chips, 2):
        pair = (chip, chip + 1)
        slot_weight = [
            jnp.sum(
                jnp.where(place[k : k + 1] == row, weight[k : k + 1], 0.0), axis=1, keepdims=True
            )
            for k in pair
        ]
        target = pl.ds(chip * r.rows, 2 * r.rows)
        factor_ref[target, :] = jnp.concatenate(
            [w[: r.rows] for w in slot_weight], axis=0
        ) * r.of_chips(up_scale, pair)
        base_ref[target, :] = 0.5 * r.of_chips(base, pair)

    ids = note_ref[own_ref[6]][:2].astype(jnp.int32)
    experts = combiner_ref.shape[0] // (2 * r.rows)
    named = lax.broadcasted_iota(jnp.int32, (experts, LANES), 0)
    slot = slots_of((ids[:1] == named) | (ids[1:] == named), block)
    slot_set = jnp.floor(slot / set_slots)
    place = jnp.where(
        slot >= 0.0,
        slot + slot_set * (r.rows - set_slots) + set_slots * block_of(slot.shape, block),
        -1.0,
    )
    row = lax.broadcasted_iota(jnp.int32, (2 * r.rows, LANES), 0).astype(F32)
    for e in range(experts):
        combiner_ref[pl.ds(e * 2 * r.rows, 2 * r.rows), :] = (place[e : e + 1] == row).astype(F32)


def near_kernel(
    shard_rows, x_ref, gate_ref, up_ref, hidden_ref, part_ref, row_ref, weight_ref
):
    r = Rows(x_ref, shard_rows)
    parts = r.parts()
    shrink = jnp.exp2(-2.0 * r.row_exponent - 2.0)
    for k, value in enumerate(parts):
        part_ref[k] = value
    for k, value in enumerate(r.scales + [shrink]):
        row_ref[k] = value
    hidden = hidden_rows(
        parts, r.scales, shrink, r.group - r.rows, weight_ref, gate_ref, up_ref
    )
    for chip in range(0, r.chips, 2):
        target = pl.ds(chip * r.rows, 2 * r.rows)
        hidden_ref[target, :] = r.of_chips(hidden, (chip, chip + 1))


def far_kernel(
    rows, group, own_ref, part_ref, row_ref, gate_ref, up_ref, near_ref, hidden_ref, weight_ref
):
    parts = [part_ref[k] for k in range(part_ref.shape[0])]
    scales = [row_ref[k] for k in range(HALVES)]
    far = hidden_rows(
        parts, scales, row_ref[HALVES], group - rows, weight_ref, gate_ref, up_ref
    )
    chips = far.shape[0] // group
    units = near_ref.shape[1]
    near_at = pl.multiple_of(own_ref[0] * units, LANES)
    far_at = pl.multiple_of((1 - own_ref[0]) * units, LANES)
    hidden_ref[:, pl.ds(near_at, units)] = near_ref[...]
    for chip in range(0, chips, 2):
        pair = [far[k * group : k * group + rows] for k in (chip, chip + 1)]
        hidden_ref[pl.ds(chip * rows, 2 * rows), pl.ds(far_at, units)] = jnp.concatenate(
            pair, axis=0
        )


def slots_layer(gathered, adapter_up, own, shard_rows, block, experts):
    rows = gathered.shape[0]
    chips = rows // (HALVES * shard_rows)
    out = jax.ShapeDtypeStruct((rows // 4, LANES), F32)
    vmem = pl.BlockSpec(memory_space=pltpu.VMEM)
    return pl.pallas_call(
        functools.partial(slots_kernel, shard_rows, block),
        out_shape=(out, out, jax.ShapeDtypeStruct((experts * shard_rows, LANES), F32)),
        in_specs=[pl.BlockSpec(memory_space=pltpu.SMEM), vmem, vmem],
        out_specs=(vmem,) * 3,
        scratch_shapes=[pltpu.VMEM((chips, NOTE_ROWS, LANES), F32)],
        compiler_params=pltpu.CompilerParams(vmem_limit_bytes=12 * 2**20),
        cost_estimate=pl.CostEstimate(
            flops=64 * rows * LANES, bytes_accessed=16 * rows * LANES, transcendentals=rows * LANES
        ),
    )(own, gathered, adapter_up)


def near_layer(gathered, weights, shard_rows):
    rows = gathered.shape[0]
    columns = gathered.shape[1] - LANES
    units = weights[0].shape[1]
    chips = rows // (HALVES * shard_rows)
    flat = chips * (-(-shard_rows // HALVES // 8) * 8)
    vmem = pl.BlockSpec(memory_space=pltpu.VMEM)
    return pl.pallas_call(
        functools.partial(near_kernel, shard_rows),
        out_shape=(
            jax.ShapeDtypeStruct((rows // 4, units), F32),
            jax.ShapeDtypeStruct((2 * HALVES, flat, columns), BF16),
            jax.ShapeDtypeStruct((HALVES + 1, flat, LANES), F32),
        ),
        in_specs=[vmem] * 3,
        out_specs=(vmem,) * 3,
        scratch_shapes=[pltpu.VMEM((2 * HALVES, columns, 2 * units), BF16)],
        compiler_params=pltpu.CompilerParams(vmem_limit_bytes=16 * 2**20),
        cost_estimate=pl.CostEstimate(
            flops=4 * rows * columns * units,
            bytes_accessed=4 * rows * columns + 4 * columns * units,
            transcendentals=2 * rows * units,
        ),
    )(gathered, *weights)


def far_layer(parts, row_scales, weights, near, tensor, shard_rows):
    _, flat, columns = parts.shape
    slots, units = near.shape
    rows = shard_rows // HALVES
    vmem = pl.BlockSpec(memory_space=pltpu.VMEM)
    return pl.pallas_call(
        functools.partial(far_kernel, rows, flat * rows // slots),
        out_shape=jax.ShapeDtypeStruct((slots, 2 * units), F32),
        in_specs=[pl.BlockSpec(memory_space=pltpu.SMEM)] + [vmem] * 5,
        out_specs=vmem,
        scratch_shapes=[pltpu.VMEM((2 * HALVES, columns, 2 * units), BF16)],
        compiler_params=pltpu.CompilerParams(vmem_limit_bytes=10 * 2**20),
        cost_estimate=pl.CostEstimate(
            flops=16 * flat * columns * units,
            bytes_accessed=8 * flat * columns + 16 * columns * units,
            transcendentals=2 * flat * units,
        ),
    )(tensor[None], parts, row_scales, *weights, near)


def norm_kernel(x_ref, out_ref):
    x = x_ref[...]
    mean = jnp.sum(jnp.sum(x * x, axis=0, keepdims=True), axis=1, keepdims=True) / x.size
    x = x * lax.rsqrt(mean + 1e-06)
    for k in range(x.shape[0]):
        out_ref[:, pl.ds(k * LANES, LANES)] = x[k : k + 1, :]


def norm_layer(pooled):
    vmem = pl.BlockSpec(memory_space=pltpu.VMEM)
    return pl.pallas_call(
        norm_kernel,
        out_shape=jax.ShapeDtypeStruct((1, pooled.size), F32),
        in_specs=[vmem],
        out_specs=vmem,
        compiler_params=pltpu.CompilerParams(vmem_limit_bytes=4 * 2**20),
    )(pooled)


def local(
    tokens,
    routes,
    chosen_expert_weight,
    expert_gate_weight,
    expert_up_weight,
    expert_down_weight,
    adapter_down_weight,
    adapter_up_weight,
    document_task_index,
    counts,
    final_norm_scale,
):
    rows, feats = tokens.shape
    seq = lax.axis_size(SEQ)
    experts = lax.axis_size(EXPERT)
    cores = lax.axis_size("c")
    groups = lax.axis_size(GROUP)
    tensors = lax.axis_size("t")
    capacity = rows * 5 // 16
    set_slots = capacity // tensors
    chip_rows = cores * set_slots
    shard_rows = HALVES * chip_rows
    width = feats * experts
    half = feats // cores
    columns = experts * half // HALVES
    slice_width = width // seq
    task_rows = adapter_down_weight.shape[0]
    s = lax.axis_index(SEQ)
    t = lax.axis_index("t")
    g = lax.axis_index(GROUP)
    per_feature_group = feats // slice_width
    own_group = s // per_feature_group

    ids = routes.T
    outgoing = dispatch_layer(
        ids,
        chosen_expert_weight.T,
        tokens,
        adapter_down_weight,
        adapter_up_weight,
        final_norm_scale[None],
        experts,
        set_slots,
    )
    later_weights, _ = lax.optimization_barrier(
        ((expert_gate_weight[0], expert_up_weight[0]), outgoing)
    )
    other = [(k, tensors - 1 - k) for k in range(tensors)]
    far_weights = [lax.ppermute(w, "t", other) for w in later_weights]
    received = swap(outgoing, EXPERT + ("c",))

    sent, adapter_up, norm_scale = rows_layer(own_group, received, task_rows)
    sent = sent.astype(F16)
    gathered = lax.all_gather(sent, SEQ, axis=0, tiled=False)
    gathered = gathered.astype(BF16).reshape(seq * shard_rows, columns + LANES)
    per_half = half // slice_width
    own_column = own_group * half + (s % per_half) * slice_width
    factor, base, combiner = slots_layer(
        gathered,
        adapter_up,
        jnp.stack(
            [
                (s // per_half) % cores,
                own_column // columns,
                own_column % columns,
                document_task_index[0],
                t,
                lax.axis_index(EXPERT),
                g,
            ]
        ),
        shard_rows,
        rows,
        experts,
    )
    near, parts, row_scales = near_layer(
        gathered, (expert_gate_weight[0], expert_up_weight[0]), shard_rows
    )
    hidden = far_layer(parts, row_scales, far_weights, near, t, shard_rows)

    units = hidden.shape[-1]
    hidden = lax.all_gather(hidden.astype(F16), SEQ, axis=0, tiled=False)
    hidden, down = lax.optimization_barrier((hidden, expert_down_weight[0]))
    part = lax.dot_general(
        hidden.astype(BF16),
        down.reshape(seq, units, slice_width),
        (((0, 2), (0, 1)), ((), ())),
        preferred_element_type=F32,
    )
    payload = (part * factor + base).reshape(groups, chip_rows, slice_width)

    group_rows = cores * rows
    position = g * group_rows + jnp.arange(group_rows, dtype=jnp.int32)[None, :]
    counted = (position < counts[0]).astype(F32)
    payload, combiner, counted, norm_scale = lax.optimization_barrier(
        (payload, combiner, counted, norm_scale)
    )

    returned = swap(payload, GROUP)
    mixed = lax.dot_general(
        combiner,
        returned.reshape(groups * chip_rows, slice_width),
        (((0,), (0,)), ((), ())),
        precision=HIGH,
    )
    squares = jnp.sum(spread(jnp.sum(mixed * mixed, axis=1)[None], SEQ), axis=0)
    factor = counted * lax.rsqrt(squares / width + 1e-05)
    pooled = jnp.dot(factor, mixed, precision=HIGH) * norm_scale
    pooled = jnp.sum(spread(pooled, GROUP), axis=0)
    return norm_layer(spread(pooled, SEQ).reshape(seq, slice_width))


def solution(mesh):
    seq, experts, tensors = mesh.devices.shape
    parts = Mesh(
        mesh.devices.reshape(seq // 2, 2, experts // 2, 2, tensors), ("z", "c", "y", "h", "t")
    )
    return jax.shard_map(
        local,
        mesh=parts,
        in_specs=(
            P(SEQ, EXPERT),
            P(SEQ, None),
            P(SEQ, None),
            P(EXPERT, None, SEQ + ("t",)),
            P(EXPERT, None, SEQ + ("t",)),
            P(EXPERT, None, SEQ),
            P(None, EXPERT),
            P(None, EXPERT),
            P(),
            P(),
            P(EXPERT),
        ),
        out_specs=P(),
        check_vma=False,
    )
```
